32 devices in a mesh: section: 2 (over x), dp: 4 (over z), tensor: 4 (over y, core).
Axes of the slice: x: 2, y: 2, z: 4, core: 2. Of those that a mesh axis runs over, the one named last changes fastest.
Arguments:
- boundary: float32 [2, 8, 1024, 1024], P('section', 'dp', 'tensor'), may hold values from -6 to 6
- w_qkv: bfloat16 [2, 1024, 3, 1024], P('section', 'dp', None, 'tensor'), may hold values from -0.1875 to 0.1875
- w_out: bfloat16 [2, 1024, 1024], P('section', 'tensor', 'dp'), may hold values from -1.5 to 1.5
- w_gate_up: bfloat16 [2, 1024, 2, 2752], P('section', 'dp', None, 'tensor'), may hold values from -0.1875 to 0.1875
- w_down: bfloat16 [2, 2752, 1024], P('section', 'tensor', 'dp'), may hold values from -0.109375 to 0.109375
- norm_gains: bfloat16 [2, 2, 1024], P('section', None, 'dp'), may hold values from 0.099609375 to 1.8984375
- variate_bias: bfloat16 [2, 16, 2], P('section', 'tensor'), may hold values from -1 to 1
- segment_ids: int32 [8, 1024], P('dp'), may hold values from 0 to 8, as said below
- variate_ids: int32 [8, 1024], P('dp'), may hold values from 0 to 3
- time_ids: int32 [8, 1024], P('dp'), may hold values from 0 to 1023
- padding_mask: int32 [8, 1024], P('dp'), may hold values from 0 to 1, as said below
Outputs:
- boundary_out: float32 [2, 8, 1024, 1024], P('section', 'dp', 'tensor')
- grad_qkv: float32 [2, 1024, 3, 1024], P('section', 'dp', None, 'tensor')
- grad_out: float32 [2, 1024, 1024], P('section', 'tensor', 'dp')
- grad_gate_up: float32 [2, 1024, 2, 2752], P('section', 'dp', None, 'tensor')
- grad_down: float32 [2, 2752, 1024], P('section', 'tensor', 'dp')
- grad_gains: float32 [2, 2, 1024], P('section', None, ('dp', 'tensor'))
- grad_bias: float32 [2, 16, 2], P('section', 'tensor')
The draws below stay inside these ranges and needn't reach their ends.
Inputs may be any that keep to these rules, and one draw needn't show every extreme that they name: `segment_ids`: along each sequence the ids never fall. `padding_mask`: in each sequence the 1s form a prefix of 512 positions or more; in each group of 2 consecutive sequences one sequence has no 0.
All inputs are finite; a program needn't handle non-finite values.
Results may differ from the reference program's by a relative error of at most 0.028.
Values may be sent and summed in bfloat16 or wider, within the bound.
No kernel may reach another device: no remote copies, remote signals or barrier semaphores. Data moves between devices by JAX's collectives and lax.ppermute only.
A program may use at most 256 MiB of HBM per device.

```python
import math
import jax
import jax.numpy as jnp
from jax import lax

D = 1024
H = 16
FF = 2752
SEQ_LEN = 1024
MB = 2
CUTS = 8
N_SECTIONS = 2
SEQS = 8


def packing(key):
    cut_key, len_key, pick_key = jax.random.split(key, 3)
    groups = SEQS // MB
    seq_index = jnp.arange(SEQS, dtype=jnp.int32)
    picked = jax.random.randint(pick_key, (groups,), 0, MB)
    chosen = seq_index % MB == picked[seq_index // MB]
    cut_points = jax.random.randint(cut_key, (SEQS, CUTS), 1, SEQ_LEN)
    cut_points = jnp.where(chosen[:, None], SEQ_LEN - 1 - cut_points % (SEQ_LEN // 16), cut_points)
    valid_len = jax.random.randint(len_key, (SEQS,), SEQ_LEN // 2, SEQ_LEN + 1)
    short_row = seq_index == (picked[0] + 1) % MB
    valid_len = jnp.where(chosen, SEQ_LEN, jnp.where(short_row, SEQ_LEN // 2, valid_len))
    positions = jnp.arange(SEQ_LEN, dtype=jnp.int32)
    segment = jnp.sum((positions[None, :, None] >= cut_points[:, None, :]).astype(jnp.int32), axis=-1)
    pad_mask = (positions[None, :] < valid_len[:, None]).astype(jnp.int32)
    return (segment.astype(jnp.int32), pad_mask)


def draw_segment_ids(key, part):
    return packing(key)[0]


def draw_padding_mask(key, part):
    return packing(key)[1]


def set_ends(values, rng, low, top_value):
    index_at = [jax.random.randint(jax.random.fold_in(rng, axis), (), 0, length) for axis, length in enumerate(values.shape)]
    longest = values.shape.index(max(values.shape))
    beside = index_at[:longest] + [(index_at[longest] + 1) % values.shape[longest]] + index_at[longest + 1:]
    return values.at[tuple(index_at)].set(low).at[tuple(beside)].set(top_value)


def steps_of(rng, shape, pieces, least, largest):
    factor_of, own = 1.0, jax.random.fold_in(rng, 6)
    for dim, parts in pieces:
        steps = jnp.exp(jax.random.uniform(jax.random.fold_in(own, dim), (parts,), jnp.float32, least / len(pieces), largest / len(pieces)))
        factor_of = factor_of * jnp.repeat(steps, shape[dim] // parts).reshape([-1 if axis == dim else 1 for axis in range(len(shape))])
    return factor_of


def bell_draw(key, shape, deviation, most, cuts=(), kind=jnp.bfloat16):
    level = steps_of(key, shape, cuts, -0.22, 0.18) if cuts else 1.0
    array = jax.random.normal(key, shape, jnp.float32) * deviation * level
    return jnp.minimum(jnp.maximum(array, -most), most).astype(kind)


def setup_inputs(seed: int = 0) -> dict:
    seeds = jax.random.split(jax.random.key(seed), 12)
    return {
        "boundary": bell_draw(seeds[0], (2, SEQS, SEQ_LEN, D), 1.0, 6.0, ((0, 2), (1, 4), (2, 4)), jnp.float32),
        "w_qkv": bell_draw(seeds[1], (N_SECTIONS, D, 3, D), D ** -0.5, 0.1875, ((0, 2), (1, 4), (3, 4))),
        "w_out": bell_draw(seeds[2], (N_SECTIONS, D, D), (D // 64) ** -0.5, 1.5, ((0, 2), (1, 4), (2, 4))),
        "w_gate_up": bell_draw(seeds[3], (N_SECTIONS, D, 2, FF), D ** -0.5, 0.1875, ((0, 2), (1, 4), (3, 4))),
        "w_down": bell_draw(seeds[4], (N_SECTIONS, FF, D), FF ** -0.5, 0.109375, ((0, 2), (1, 4), (2, 4))),
        "norm_gains": jnp.clip(1.0 + 0.18 * jax.random.normal(seeds[5], (N_SECTIONS, 2, D), jnp.float32), 0.099609375, 1.8984375).astype(jnp.bfloat16),
        "variate_bias": jnp.clip(jax.random.uniform(seeds[6], (N_SECTIONS, H, 2), jnp.float32, -1.0, 1.0) * steps_of(seeds[6], (N_SECTIONS, H, 2), ((0, 2), (1, 4)), -0.4, 0.0), -1.0, 1.0).astype(jnp.bfloat16),
        "segment_ids": draw_segment_ids(jax.random.fold_in(seeds[11], 71), 0),
        "variate_ids": set_ends(jax.random.randint(seeds[8], (SEQS, SEQ_LEN), 0, 4), jax.random.fold_in(seeds[8], 1), 0, 3).astype(jnp.int32),
        "time_ids": set_ends(jax.random.randint(seeds[9], (SEQS, SEQ_LEN), 0, SEQ_LEN), jax.random.fold_in(seeds[9], 1), 0, SEQ_LEN - 1).astype(jnp.int32),
        "padding_mask": draw_padding_mask(jax.random.fold_in(seeds[11], 71), 0),
    }


EPS = 1e-05
NEG = -1e+30
HIGHEST = lax.Precision.HIGHEST

@jax.custom_vjp
def low(v):
    return lax.optimization_barrier(v.astype(jnp.bfloat16)).astype(jnp.float32)

@jax.custom_vjp
def low_back(v):
    return v

def low_keep(v):
    return (low(v), None)

def low_pass(kept, grad):
    return (grad,)

def back_keep(v):
    return (v, None)

def back_low(kept, grad):
    return (low(grad),)
low.defvjp(low_keep, low_pass)
low_back.defvjp(back_keep, back_low)

def rms_scale(x):
    return x * lax.rsqrt(lax.optimization_barrier(jnp.mean(x * x, axis=-1, keepdims=True)) + EPS)

def angles(time_row, head_dim):
    half_dim = head_dim // 2
    frequency = jnp.exp(-jnp.log(10000.0) * jnp.arange(half_dim, dtype=jnp.float32) / half_dim)
    phases = time_row.astype(jnp.float32)[:, None] * frequency[None, :]
    return (jnp.cos(phases)[:, None, :], jnp.sin(phases)[:, None, :])

def rotate(t, cos_part, sin_part):
    half_dim = t.shape[-1] // 2
    first_half = t[..., :half_dim]
    second = t[..., half_dim:]
    return jnp.concatenate([first_half * cos_part - second * sin_part, first_half * sin_part + second * cos_part], axis=-1)

def attention(q, k, v, var_bias, segment, variate, valid_keys):
    head_dim = q.shape[-1]
    block_rows = min(512, SEQ_LEN)
    blocks = SEQ_LEN // block_rows
    positions = jnp.arange(SEQ_LEN, dtype=jnp.int32)

    def attend_block(block_args):
        q_block, seg_block, var_block, pos_block = block_args
        scores = jnp.einsum('qhd,khd->hqk', q_block, k, precision=HIGHEST) * (1.0 / math.sqrt(head_dim))
        same_var = var_block[:, None] == variate[None, :]
        scores = scores + jnp.where(same_var[None], var_bias[:, 0][:, None, None], var_bias[:, 1][:, None, None])
        scores = low_back(scores)
        allowed = (seg_block[:, None] == segment[None, :]) & ((valid_keys[None, :] == 1) | (pos_block[:, None] == positions[None, :]))
        masked = jnp.where(allowed[None], scores, NEG)
        row_max = lax.optimization_barrier(jnp.max(masked, axis=-1, keepdims=True))
        weights = jnp.exp(masked - row_max)
        probability = weights / lax.optimization_barrier(jnp.sum(weights, axis=-1, keepdims=True))
        return jnp.einsum('hqk,khd->qhd', low(probability), v, precision=HIGHEST)
    block_parts = (q.reshape(blocks, block_rows, H, head_dim), segment.reshape(blocks, block_rows), variate.reshape(blocks, block_rows), positions.reshape(blocks, block_rows))
    result = lax.map(jax.checkpoint(attend_block), block_parts)
    return result.reshape(SEQ_LEN, H, head_dim)

def residual_block(x, weights, segment, variate, time_row, valid_keys):
    w_qkv, w_out, w_gate_up, w_down, gain_pair, var_bias = weights
    head_dim = D // H
    cos_part, sin_part = angles(time_row, head_dim)
    normed_one = low(rms_scale(x) * gain_pair[0])
    projected = low_back(jnp.dot(normed_one, w_qkv.reshape(D, 3 * D), precision=HIGHEST)).reshape(SEQ_LEN, 3, H, head_dim)
    q = low(rotate(rms_scale(projected[:, 0]), cos_part, sin_part))
    k = low(rotate(rms_scale(projected[:, 1]), cos_part, sin_part))
    v = low(projected[:, 2])
    attended = low_back(low(attention(q, k, v, var_bias, segment, variate, valid_keys))).reshape(SEQ_LEN, D)
    h = x + low_back(jnp.dot(attended, w_out, precision=HIGHEST))
    normed_two = low(rms_scale(h) * gain_pair[1])
    gate_up = low_back(jnp.dot(normed_two, w_gate_up.reshape(D, 2 * FF), precision=HIGHEST))
    hidden = low(jax.nn.silu(gate_up[:, :FF]) * gate_up[:, FF:])
    return h + low_back(jnp.dot(hidden, w_down, precision=HIGHEST))

def reference(boundary, w_qkv, w_out, w_gate_up, w_down, norm_gains, variate_bias, segment_ids, variate_ids, time_ids, padding_mask):
    params = tuple((a.astype(jnp.float32) for a in (w_qkv, w_out, w_gate_up, w_down, norm_gains, variate_bias)))

    def two_blocks(weights, x, segment, variate, time_row, valid_keys):
        first_set = tuple((w[0] for w in weights))
        second_set = tuple((w[1] for w in weights))
        middle = low_back(low(residual_block(x, first_set, segment, variate, time_row, valid_keys)))
        return residual_block(middle, second_set, segment, variate, time_row, valid_keys)

    def per_sequence(running, sequence):
        x, cotangent, segment, variate, time_row, valid_keys = sequence
        output, pullback = jax.vjp(lambda w, u: two_blocks(w, u, segment, variate, time_row, valid_keys), params, x)
        grad_w, grad_x = pullback(cotangent)
        return (tuple((a + b for a, b in zip(running, grad_w))), (output, grad_x))
    initial = tuple((jnp.zeros_like(a) for a in params))
    summed, (outputs, input_grads) = lax.scan(per_sequence, initial, (boundary[0], boundary[1], segment_ids, variate_ids, time_ids, padding_mask))
    boundary_out = jnp.stack([input_grads, outputs])
    return (boundary_out, summed[0], summed[1], summed[2], summed[3], summed[4], summed[5])
```

```python
import functools
import math

import jax
import jax.numpy as jnp
from jax import lax
from jax.experimental import pallas as pl
from jax.experimental.pallas import tpu as pltpu
from jax.sharding import PartitionSpec as P

EPS = 1e-05
BIG = 8192.0
LOG2E = 1.4426950408889634
BF = jnp.bfloat16
F32 = jnp.float32
HD = 64
ZB = 256
VMEM_MB = 56
N_VAR = 4
L_SEG = 8
L_PAD = 24
L_LSE = 25


def dot(a, b):
    return lax.dot_general(a, b, (((1,), (0,)), ((), ())), preferred_element_type=F32)


def dot_nt(a, b):
    return lax.dot_general(a, b, (((1,), (1,)), ((), ())), preferred_element_type=F32)


def dot_tn(a, b):
    return lax.dot_general(a, b, (((0,), (0,)), ((), ())), preferred_element_type=F32)


def params(mb=VMEM_MB):
    return pltpu.CompilerParams(
        dimension_semantics=("arbitrary",), vmem_limit_bytes=mb * 1024 * 1024
    )


def cost(flops, nbytes, trans=0):
    return pl.CostEstimate(flops=int(flops), bytes_accessed=int(nbytes), transcendentals=int(trans))


def sds(shape, dtype):
    return jax.ShapeDtypeStruct(shape, dtype)


def whole(shape):
    zeros = (0,) * len(shape)
    return pl.BlockSpec(shape, lambda *_: zeros)


def head_sum(u):
    hi = u.astype(BF)
    lo = (u - hi.astype(F32)).astype(BF)
    row = lax.broadcasted_iota(jnp.int32, (128, 128), 0) // HD
    col = lax.broadcasted_iota(jnp.int32, (128, 128), 1) // HD
    same = jnp.where(row == col, 1.0, 0.0).astype(BF)
    return dot(hi, same) + dot(lo, same)


def half_swap(u):
    lane = lax.broadcasted_iota(jnp.int32, u.shape, 1) % HD
    return jnp.where(lane < HD // 2, pltpu.roll(u, 128 - HD // 2, 1), pltpu.roll(u, HD // 2, 1))


def row_rms(x):
    return lax.rsqrt(jnp.mean(x * x, axis=-1, keepdims=True) + EPS)


def qkv_kernel(save, x_ref, gain_ref, w_ref, cos_ref, sin_ref, *refs):
    if save:
        n_ref, q_ref, k_ref, v_ref, q0_ref, k0_ref, n_scr = refs
    else:
        q_ref, k_ref, v_ref, n_scr = refs

    @pl.when(pl.program_id(0) == 0)
    def _():
        x = x_ref[...]
        n = (x * row_rms(x) * gain_ref[...]).astype(BF)
        n_scr[...] = n
        if save:
            n_ref[...] = n

    width = q_ref.shape[1]
    blocks = w_ref.shape[0]
    proj = dot_nt(n_scr[:, :ZB], w_ref[0, 0])
    for z in range(1, blocks):
        proj = proj + dot_nt(n_scr[:, z * ZB : (z + 1) * ZB], w_ref[z, 0])
    v_ref[...] = proj[:, 2 * width :].astype(BF)
    cos, sin = cos_ref[...], sin_ref[...]
    for which, out in ((0, q_ref), (1, k_ref)):
        if save:
            kept = q0_ref if which == 0 else k0_ref
            kept[...] = proj[:, which * width : (which + 1) * width].astype(BF)
        for pair in range(width // 128):
            u = proj[:, which * width + pair * 128 : which * width + (pair + 1) * 128]
            un = u * lax.rsqrt(head_sum(u * u) * (1.0 / HD) + EPS)
            out[:, pair * 128 : (pair + 1) * 128] = (un * cos + half_swap(un) * sin).astype(BF)


def qkv_call(save, x, gain, w, cos, sin):
    rows, model = x.shape
    zb, tn, feats, _ = w.shape
    width = feats // 3
    total = tn * width
    col = pl.BlockSpec((rows, width), lambda t: (0, t))
    outs = [sds((rows, total), BF)] * 3
    specs = [col] * 3
    if save:
        outs = [sds((rows, model), BF)] + outs + [sds((rows, total), BF)] * 2
        specs = [whole((rows, model))] + specs + [col] * 2
    return pl.pallas_call(
        functools.partial(qkv_kernel, save),
        grid=(tn,),
        in_specs=[
            whole((rows, model)),
            whole((1, model)),
            pl.BlockSpec((zb, 1, feats, ZB), lambda t: (0, t, 0, 0)),
            whole((rows, 128)),
            whole((rows, 128)),
        ],
        out_specs=specs,
        out_shape=outs,
        scratch_shapes=[pltpu.VMEM((rows, model), BF)],
        compiler_params=params(),
        cost_estimate=cost(2 * rows * model * 3 * total, 2 * w.size + 16 * x.size),
    )(x, gain, w, cos, sin)


def pick(first, h, a, b):
    return jnp.where(first, a, b) if h == 0 else jnp.where(first, b, a)


def attend_kernel(
    scale, q_ref, ko_ref, kx_ref, vo_ref, vx_ref, aq_ref, ak_ref, hs_ref, add_ref, o_ref, l_ref
):
    rows = q_ref.shape[0]
    kb = 256
    first = lax.broadcasted_iota(jnp.int32, (1, 128), 1) < HD
    q = q_ref[...].astype(F32)
    base = aq_ref[...]
    raws = []
    for h in range(2):
        qh = pick(first, h, q, base * hs_ref[0, h : h + 1, :]).astype(BF)
        parts = [None] * (rows // kb)
        for half, (k_ref, v_ref) in enumerate(((ko_ref, vo_ref), (kx_ref, vx_ref))):
            for block in range(rows // kb):
                at = slice(block * kb, (block + 1) * kb)
                kk = slice(half * rows + block * kb, half * rows + (block + 1) * kb)
                kh = pick(first, h, k_ref[at, :].astype(F32), ak_ref[kk, :].astype(F32)).astype(BF)
                vh = pick(first, h, v_ref[at, :].astype(F32), 1.0).astype(BF)
                for qb in range(rows // kb):
                    qs = slice(qb * kb, (qb + 1) * kb)
                    s = dot_nt(qh[qs], kh)
                    if half == 0:
                        s = s + add_ref[qs, at]
                    p = jnp.exp2(s * scale).astype(BF)
                    r = dot(p, vh)
                    parts[qb] = r if parts[qb] is None else parts[qb] + r
        raws.append(jnp.concatenate(parts, axis=0))
    sums = jnp.where(first, raws[1], raws[0])
    l_ref[...] = sums
    o_ref[...] = (jnp.where(first, raws[0], raws[1]) / pltpu.roll(sums, HD, 1)).astype(BF)


def attend_call(scale, q, k_own, k_oth, v_own, v_oth, aug_q, aug_k, head_scale, add_own):
    rows, total = q.shape
    pairs = total // 128
    col = pl.BlockSpec((rows, 128), lambda p: (0, p))
    return pl.pallas_call(
        functools.partial(attend_kernel, scale),
        grid=(pairs,),
        in_specs=[
            col,
            col,
            col,
            col,
            col,
            whole(aug_q.shape),
            whole(aug_k.shape),
            pl.BlockSpec((1, 2, 128), lambda p: (p, 0, 0)),
            whole(add_own.shape),
        ],
        out_specs=[col, col],
        out_shape=[sds((rows, total), BF), sds((rows, total), F32)],
        compiler_params=params(),
        cost_estimate=cost(
            4 * 2 * rows * rows * 2 * total, 20 * rows * total, rows * rows * 2 * pairs * 2
        ),
    )(q, k_own, k_oth, v_own, v_oth, aug_q, aug_k, head_scale, add_own)


def ffn_kernel(save, x_ref, o_ref, wo_ref, gain_ref, wgu_ref, wd_ref, *refs):
    if save:
        y_ref, h_ref, n_ref, g_ref, u_ref, z_ref, n_scr, acc = refs
    else:
        y_ref, n_scr, acc = refs
    blocks = wgu_ref.shape[0]
    hidden = wd_ref.shape[2]
    step = pl.program_id(0)

    @pl.when(step == 0)
    def _():
        tn, width = wo_ref.shape[1], wo_ref.shape[2]
        total = jnp.zeros((x_ref.shape[0], 1), F32)
        for z in range(blocks):
            at = slice(z * ZB, (z + 1) * ZB)
            h = x_ref[:, at]
            for t in range(tn):
                h = h + dot(o_ref[:, t * width : (t + 1) * width], wo_ref[z, t])
            acc[:, at] = h
            total = total + jnp.sum(h * h, axis=-1, keepdims=True)
        h = acc[...]
        n = (h * lax.rsqrt(total * (1.0 / h.shape[1]) + EPS) * gain_ref[...]).astype(BF)
        n_scr[...] = n
        if save:
            h_ref[...] = h
            n_ref[...] = n

    gate = dot_nt(n_scr[:, :ZB], wgu_ref[0, 0, :hidden])
    up = dot_nt(n_scr[:, :ZB], wgu_ref[0, 0, hidden:])
    for z in range(1, blocks):
        n = n_scr[:, z * ZB : (z + 1) * ZB]
        gate = gate + dot_nt(n, wgu_ref[z, 0, :hidden])
        up = up + dot_nt(n, wgu_ref[z, 0, hidden:])
    hid = (gate / (1.0 + jnp.exp(-gate)) * up).astype(BF)
    if save:
        g_ref[0] = gate.astype(BF)
        u_ref[0] = up.astype(BF)
        z_ref[0] = hid
    for z in range(blocks):
        at = slice(z * ZB, (z + 1) * ZB)
        acc[:, at] = acc[:, at] + dot(hid, wd_ref[z, 0])

    @pl.when(step == pl.num_programs(0) - 1)
    def _():
        y_ref[...] = acc[...].astype(y_ref.dtype)


def ffn_call(save, x, o, wo, gain, wgu, wd):
    rows, model = x.shape
    zb, tn, hidden, _ = wd.shape
    big = whole((rows, model))
    outs = [sds((rows, model), F32 if save else BF)]
    specs = [big]
    if save:
        part = pl.BlockSpec((1, rows, hidden), lambda t: (t, 0, 0))
        outs += [sds((rows, model), F32), sds((rows, model), BF)] + [
            sds((tn, rows, hidden), BF)
        ] * 3
        specs += [big, big, part, part, part]
    return pl.pallas_call(
        functools.partial(ffn_kernel, save),
        grid=(tn,),
        in_specs=[
            big,
            whole(o.shape),
            whole(wo.shape),
            whole((1, model)),
            pl.BlockSpec((zb, 1, 2 * hidden, ZB), lambda t: (0, t, 0, 0)),
            pl.BlockSpec((zb, 1, hidden, ZB), lambda t: (0, t, 0, 0)),
        ],
        out_specs=specs,
        out_shape=outs,
        scratch_shapes=[pltpu.VMEM((rows, model), BF), pltpu.VMEM((rows, model), F32)],
        compiler_params=params(),
        cost_estimate=cost(
            2 * rows * model * (3 * tn * hidden + model), 6 * wd.size + 2 * wo.size + 20 * x.size
        ),
    )(x, o, wo, gain, wgu, wd)


def ffn_back_kernel(
    dy_ref, h_ref, g_ref, u_ref, wgu_ref, wd_ref, wo_ref, gain_ref,
    dh_ref, da_ref, do_ref, dg_ref, gg_ref, df_scr, acc,
):
    blocks = wgu_ref.shape[0]
    hidden = wd_ref.shape[2]
    step = pl.program_id(0)

    @pl.when(step == 0)
    def _():
        df_scr[...] = dy_ref[...].astype(BF)
        acc[...] = jnp.zeros_like(acc)

    dz = dot_nt(df_scr[:, :ZB], wd_ref[0, 0])
    for z in range(1, blocks):
        dz = dz + dot_nt(df_scr[:, z * ZB : (z + 1) * ZB], wd_ref[z, 0])
    gate = g_ref[0].astype(F32)
    up = u_ref[0].astype(F32)
    s = 1.0 / (1.0 + jnp.exp(-gate))
    dgate = (dz * up * s * (1.0 + gate * (1.0 - s))).astype(BF)
    dup = (dz * gate * s).astype(BF)
    dg_ref[0, 0] = dgate
    dg_ref[0, 1] = dup
    for z in range(blocks):
        at = slice(z * ZB, (z + 1) * ZB)
        acc[:, at] = acc[:, at] + (
            dot(dgate, wgu_ref[z, 0, :hidden]) + dot(dup, wgu_ref[z, 0, hidden:])
        )

    @pl.when(step == pl.num_programs(0) - 1)
    def _():
        h = h_ref[...]
        r = row_rms(h)
        hn = h * r
        dn = acc[...]
        gg_ref[...] = jnp.sum(dn * hn, axis=0, keepdims=True)
        dhat = dn * gain_ref[...]
        dh = dy_ref[...] + r * (dhat - hn * jnp.mean(dhat * hn, axis=-1, keepdims=True))
        dh_ref[...] = dh
        da = dh.astype(BF)
        da_ref[...] = da
        tn, width = wo_ref.shape[1], wo_ref.shape[2]
        for t in range(tn):
            part = dot_nt(da[:, :ZB], wo_ref[0, t])
            for z in range(1, blocks):
                part = part + dot_nt(da[:, z * ZB : (z + 1) * ZB], wo_ref[z, t])
            do_ref[:, t * width : (t + 1) * width] = part.astype(BF)


def ffn_back_call(dy, h, g, u, wgu, wd, wo, gain):
    rows, model = dy.shape
    zb, tn, hidden, _ = wd.shape
    big = whole((rows, model))
    part = pl.BlockSpec((1, rows, hidden), lambda t: (t, 0, 0))
    return pl.pallas_call(
        ffn_back_kernel,
        grid=(tn,),
        in_specs=[
            big,
            big,
            part,
            part,
            pl.BlockSpec((zb, 1, 2 * hidden, ZB), lambda t: (0, t, 0, 0)),
            pl.BlockSpec((zb, 1, hidden, ZB), lambda t: (0, t, 0, 0)),
            whole(wo.shape),
            whole((1, model)),
        ],
        out_specs=[
            big,
            big,
            big,
            pl.BlockSpec((1, 2, rows, hidden), lambda t: (t, 0, 0, 0)),
            whole((1, model)),
        ],
        out_shape=[
            sds((rows, model), F32),
            sds((rows, model), BF),
            sds((rows, model), BF),
            sds((tn, 2, rows, hidden), BF),
            sds((1, model), F32),
        ],
        scratch_shapes=[pltpu.VMEM((rows, model), BF), pltpu.VMEM((rows, model), F32)],
        compiler_params=params(),
        cost_estimate=cost(
            2 * rows * model * (3 * tn * hidden + model), 6 * wd.size + 2 * wo.size + 20 * dy.size
        ),
    )(dy, h, g, u, wgu, wd, wo, gain)


def split3(value):
    hi = value.astype(BF).astype(F32)
    mid = (value - hi).astype(BF).astype(F32)
    return hi, mid, value - hi - mid


def attend_back_kernel(
    scale, q_ref, ko_ref, kx_ref, vo_ref, vx_ref, do_ref, o_ref, l_ref, aq_ref, ak_ref, hs_ref,
    add_ref, var_ref, dq_ref, dko_ref, dkx_ref, dvo_ref, dvx_ref, bias_ref,
):
    rows = q_ref.shape[0]
    kb = 256
    first = lax.broadcasted_iota(jnp.int32, (1, 128), 1) < HD
    lane = lax.broadcasted_iota(jnp.int32, (1, 128), 1) % HD
    q = q_ref[...].astype(F32)
    do = do_ref[...].astype(F32)
    inner = do * o_ref[...].astype(F32)
    base = aq_ref[...]
    hi, mid, low = split3(jnp.log2(l_ref[...]) * (-1.0 / scale))
    lse = jnp.where(lane == L_LSE, hi, 0.0)
    lse = jnp.where(lane == L_LSE + 1, mid, lse)
    lse = jnp.where(lane == L_LSE + 2, low, lse)
    dq_t = []
    dk = [[], []]
    dv = [[], []]
    for h in range(2):
        qh = pick(first, h, q, base * hs_ref[0, h : h + 1, :] + lse).astype(BF)
        d = jnp.sum(pick(first, h, inner, 0.0), axis=-1, keepdims=True)
        dhi, dmid, dlow = split3(-d)
        d_aug = jnp.where(lane == 0, dhi, 0.0)
        d_aug = jnp.where(lane == 1, dmid, d_aug)
        d_aug = jnp.where(lane == 2, dlow, d_aug)
        doh = pick(first, h, do, d_aug).astype(BF)
        total = None
        for half, (k_ref, v_ref) in enumerate(((ko_ref, vo_ref), (kx_ref, vx_ref))):
            for block in range(rows // kb):
                at = slice(block * kb, (block + 1) * kb)
                kk = slice(half * rows + block * kb, half * rows + (block + 1) * kb)
                kh = pick(first, h, k_ref[at, :].astype(F32), ak_ref[kk, :].astype(F32)).astype(BF)
                vh = pick(first, h, v_ref[at, :].astype(F32), 1.0).astype(BF)
                s = dot_nt(kh, qh)
                if half == 0:
                    s = s + add_ref[at, :]
                p = jnp.exp2(s * scale)
                ds = (p * dot_nt(vh, doh)).astype(BF)
                dv[h].append(dot(p.astype(BF), doh))
                dk[h].append(dot(ds, qh))
                part = dot_tn(kh, ds)
                total = part if total is None else total + part
        dq_t.append(total)
    scale_back = 1.0 / math.sqrt(HD)
    count = rows // kb
    for half, (dk_ref, dv_ref) in enumerate(((dko_ref, dvo_ref), (dkx_ref, dvx_ref))):
        for block in range(count):
            at = slice(block * kb, (block + 1) * kb)
            i = half * count + block
            dk_ref[at, :] = (jnp.where(first, dk[0][i], dk[1][i]) * scale_back).astype(dk_ref.dtype)
            dv_ref[at, :] = jnp.where(first, dv[0][i], dv[1][i]).astype(dv_ref.dtype)
    joined = jnp.concatenate([dq_t[0][:HD], dq_t[1][HD:]], axis=0)
    dq_ref[...] = joined.T * scale_back
    mine = var_ref[...]
    for h in range(2):
        begin = HD if h == 0 else 0
        r = dq_t[h][begin : begin + 8]
        same = jnp.sum(r * mine, axis=0, keepdims=True)
        every = jnp.sum(r[:N_VAR], axis=0, keepdims=True)
        bias_ref[0, 2 * h : 2 * h + 1, :] = same
        bias_ref[0, 2 * h + 1 : 2 * h + 2, :] = every - same


def attend_back_call(
    scale, q, k_own, k_oth, v_own, v_oth, do, o, sums, aug_q, aug_k, head_scale, add_own, var_q
):
    rows, total = q.shape
    pairs = total // 128
    col = pl.BlockSpec((rows, 128), lambda p: (0, p))
    return pl.pallas_call(
        functools.partial(attend_back_kernel, scale),
        grid=(pairs,),
        in_specs=[col] * 8
        + [
            whole(aug_q.shape),
            whole(aug_k.shape),
            pl.BlockSpec((1, 2, 128), lambda p: (p, 0, 0)),
            whole(add_own.shape),
            whole(var_q.shape),
        ],
        out_specs=[col] * 5 + [pl.BlockSpec((1, 4, rows), lambda p: (p, 0, 0))],
        out_shape=[
            sds((rows, total), F32),
            sds((rows, total), F32),
            sds((rows, total), BF),
            sds((rows, total), F32),
            sds((rows, total), BF),
            sds((pairs, 4, rows), F32),
        ],
        compiler_params=params(),
        cost_estimate=cost(
            10 * 2 * rows * rows * 2 * total, 40 * rows * total, rows * rows * 2 * pairs * 2
        ),
    )(q, k_own, k_oth, v_own, v_oth, do, o, sums, aug_q, aug_k, head_scale, add_own, var_q)


def qkv_back_kernel(
    dq_ref, dk_ref, dkr_ref, dv_ref, dvr_ref, q0_ref, k0_ref, cos_ref, sin_ref, w_ref, x_ref,
    dh_ref, gain_ref, dp_ref, dx_ref, gg_ref, acc,
):
    blocks = w_ref.shape[0]
    width = dq_ref.shape[1]
    step = pl.program_id(0)

    @pl.when(step == 0)
    def _():
        acc[...] = jnp.zeros_like(acc)

    cos, sin = cos_ref[...], sin_ref[...]
    for pair in range(width // 128):
        at = slice(pair * 128, (pair + 1) * 128)
        for which in range(2):
            grad = dq_ref[:, at] if which == 0 else dk_ref[:, at] + dkr_ref[:, at].astype(F32)
            u = (q0_ref if which == 0 else k0_ref)[:, at].astype(F32)
            r = lax.rsqrt(head_sum(u * u) * (1.0 / HD) + EPS)
            un = u * r
            grad = grad * cos - half_swap(grad) * sin
            out = r * (grad - un * (head_sum(grad * un) * (1.0 / HD)))
            dp_ref[0, :, which * width + pair * 128 : which * width + (pair + 1) * 128] = out.astype(
                BF
            )
    dp_ref[0, :, 2 * width :] = (dv_ref[...] + dvr_ref[...].astype(F32)).astype(BF)
    dp = dp_ref[0]
    for z in range(blocks):
        at = slice(z * ZB, (z + 1) * ZB)
        acc[:, at] = acc[:, at] + dot(dp, w_ref[z, 0])

    @pl.when(step == pl.num_programs(0) - 1)
    def _():
        x = x_ref[...]
        r = row_rms(x)
        xn = x * r
        dn = acc[...]
        gg_ref[...] = jnp.sum(dn * xn, axis=0, keepdims=True)
        dhat = dn * gain_ref[...]
        dx_ref[...] = dh_ref[...] + r * (dhat - xn * jnp.mean(dhat * xn, axis=-1, keepdims=True))


def qkv_back_call(dq, dk, dkr, dv, dvr, q0, k0, cos, sin, w, x, dh, gain):
    rows, model = x.shape
    zb, tn, feats, _ = w.shape
    width = feats // 3
    big = whole((rows, model))
    col = pl.BlockSpec((rows, width), lambda t: (0, t))
    return pl.pallas_call(
        qkv_back_kernel,
        grid=(tn,),
        in_specs=[col] * 7
        + [
            whole((rows, 128)),
            whole((rows, 128)),
            pl.BlockSpec((zb, 1, feats, ZB), lambda t: (0, t, 0, 0)),
            big,
            big,
            whole((1, model)),
        ],
        out_specs=[pl.BlockSpec((1, rows, feats), lambda t: (t, 0, 0)), big, whole((1, model))],
        out_shape=[sds((tn, rows, feats), BF), sds((rows, model), F32), sds((1, model), F32)],
        scratch_shapes=[pltpu.VMEM((rows, model), F32)],
        compiler_params=params(),
        cost_estimate=cost(2 * rows * model * tn * feats, 2 * w.size + 40 * x.size),
    )(dq, dk, dkr, dv, dvr, q0, k0, cos, sin, w, x, dh, gain)


def wgrad_kernel(ao_ref, bo_ref, ax_ref, bx_ref, g_ref):
    a = ao_ref[0]
    ax = ax_ref[0]
    for z in range(g_ref.shape[1]):
        at = slice(z * ZB, (z + 1) * ZB)
        g_ref[0, z] = (dot_tn(a, bo_ref[:, at]) + dot_tn(ax, bx_ref[:, at])).astype(BF)


def wgrad_call(a_own, b_own, a_oth, b_oth):
    n, rows, feats = a_own.shape
    model = b_own.shape[1]
    part = pl.BlockSpec((1, rows, feats), lambda i: (i, 0, 0))
    big = whole((rows, model))
    return pl.pallas_call(
        wgrad_kernel,
        grid=(n,),
        in_specs=[part, big, part, big],
        out_specs=pl.BlockSpec((1, model // ZB, feats, ZB), lambda i: (i, 0, 0, 0)),
        out_shape=sds((n, model // ZB, feats, ZB), BF),
        compiler_params=params(),
        cost_estimate=cost(4 * n * rows * feats * model, 2 * n * feats * model),
    )(a_own, b_own, a_oth, b_oth)


def core_swap(value):
    n = lax.axis_size("tensor")
    return lax.ppermute(value, "tensor", [(i, i ^ 1) for i in range(n)])


def y_swap(value):
    n = lax.axis_size("tensor")
    return lax.ppermute(value, "tensor", [(i, i ^ 2) for i in range(n)])


def ring(value):
    n = lax.axis_size("dp")
    return lax.ppermute(value, "dp", [(i, (i + 1) % n) for i in range(n)])


def gather_weight(piece):
    n = lax.axis_size("dp")
    tn = lax.axis_size("tensor")
    zi = lax.axis_index("dp")
    ti = lax.axis_index("tensor")
    feats, cols = piece.shape
    if n > 8:
        every = lax.all_gather(lax.all_gather(piece, "dp"), "tensor")
        every = every.transpose(0, 2, 1, 3).reshape(tn, feats, n * cols // ZB, ZB)
        return every.transpose(2, 0, 1, 3)
    out = jnp.zeros((n, tn, feats, cols), piece.dtype)
    held = piece
    for step in range(n):
        if step:
            held = ring(held)
        across = y_swap(held)
        both = core_swap(jnp.stack([held, across]))
        at = lax.rem(zi - step + n, n)
        for t, part in ((ti, held), (ti ^ 2, across), (ti ^ 1, both[0]), (ti ^ 3, both[1])):
            out = lax.dynamic_update_slice(out, part[None, None], (at, t, 0, 0))
    return out


def scatter_grad(grad):
    n = lax.axis_size("dp")
    zi = lax.axis_index("dp")
    yi = lax.axis_index("tensor") // 2
    mine = lax.dynamic_index_in_dim(grad, yi, 0, keepdims=False)
    other = lax.dynamic_index_in_dim(grad, 1 - yi, 0, keepdims=False)
    got = y_swap(other)
    total = mine.astype(F32) + got.astype(F32)
    blocks, feats, cols = total.shape
    if n > 8:
        flat = total.transpose(1, 0, 2).reshape(feats, blocks * cols).astype(BF)
        return lax.psum_scatter(flat, "dp", scatter_dimension=1, tiled=True).astype(F32)

    def chunk(index):
        return lax.dynamic_index_in_dim(total, lax.rem(index + 2 * n, n), 0, keepdims=False)

    running = chunk(zi - 1)
    for step in range(2, n + 1):
        running = ring(running.astype(BF)).astype(F32) + chunk(zi - step)
    return running


def small_sum(value):
    n = lax.axis_size("dp")
    value = value + core_swap(value)
    value = value + y_swap(value)
    if n & (n - 1):
        return lax.psum(value, "dp")
    bit = 1
    while bit < n:
        value = value + lax.ppermute(value, "dp", [(i, i ^ bit) for i in range(n)])
        bit *= 2
    return value


def own_rows(row, core):
    quarters = row.reshape(2, 2, row.shape[0] // 4)
    own = lax.dynamic_index_in_dim(quarters, core, 1, keepdims=False).reshape(-1)
    oth = lax.dynamic_index_in_dim(quarters, 1 - core, 1, keepdims=False).reshape(-1)
    return own, oth


def tables(segment, variate, time_row, pad, var_bias, core):
    seg_own, seg_oth = own_rows(segment, core)
    var_own, var_oth = own_rows(variate, core)
    pad_own, pad_oth = own_rows(pad, core)
    time_own, _ = own_rows(time_row, core)
    rows = seg_own.shape[0]
    half = HD // 2
    frequency = jnp.exp(-jnp.log(10000.0) * jnp.arange(half, dtype=F32) / half)
    phases = time_own.astype(F32)[:, None] * frequency[None, :]
    cos, sin = jnp.cos(phases), jnp.sin(phases)
    cos = jnp.concatenate([cos] * 4, axis=1)
    sin = jnp.concatenate([-sin, sin, -sin, sin], axis=1)
    lane = (jnp.arange(128, dtype=jnp.int32) % HD)[None, :]
    seg_k = jnp.concatenate([seg_own, seg_oth])[:, None]
    var_k = jnp.concatenate([var_own, var_oth])[:, None]
    pad_k = jnp.concatenate([jnp.ones_like(pad_own), pad_oth])[:, None]
    is_var = lane < 2 * N_VAR
    is_seg = (lane >= L_SEG) & (lane < L_PAD)
    is_lse = (lane >= L_LSE) & (lane < L_LSE + 3)
    aug_k = jnp.where(
        is_var,
        jnp.where(var_k == lane % N_VAR, 1.0, 0.0),
        jnp.where(
            is_seg,
            jnp.where(seg_k == lane - L_SEG, 0.0, -BIG),
            jnp.where(
                lane == L_PAD, jnp.where(pad_k == 1, 0.0, -BIG), jnp.where(is_lse, 1.0, 0.0)
            ),
        ),
    ).astype(BF)
    aug_q = jnp.where(
        is_var,
        jnp.where(var_own[:, None] == lane % N_VAR, 1.0, 0.0),
        jnp.where(
            is_seg,
            jnp.where(seg_own[:, None] == lane - L_SEG, 1.0, 0.0),
            jnp.where(lane == L_PAD, 1.0, 0.0),
        ),
    ).astype(F32)
    delta = (var_bias[:, 0] - var_bias[:, 1]) * math.sqrt(HD)
    hi = delta.astype(BF).astype(F32)
    low = (delta - hi).astype(BF).astype(F32)
    head_scale = jnp.where(
        lane < N_VAR, hi[:, None], jnp.where(lane < 2 * N_VAR, low[:, None], 1.0)
    ).reshape(-1, 2, 128)
    place = jnp.arange(rows, dtype=jnp.int32)
    neg = jnp.where(pad_own == 1, 0.0, -BIG).astype(F32)
    eye = place[:, None] == place[None, :]
    add_q = jnp.where(eye, 0.0, neg[None, :])
    add_k = jnp.where(eye, 0.0, neg[:, None])
    var_q = jnp.where(
        var_own[None, :] == jnp.arange(8, dtype=jnp.int32)[:, None], 1.0, 0.0
    ).astype(F32)
    return cos, sin, aug_q, aug_k, head_scale, add_q, add_k, var_q


def forward(save, x, weights, gains, tab, scale):
    w_qkv, w_out, w_gu, w_down = weights
    cos, sin, aug_q, aug_k, head_scale, add_q, _, _ = tab
    res = qkv_call(save, x, gains[0], w_qkv, cos, sin)
    if save:
        n1, q, k, v, q0, k0 = res
    else:
        q, k, v = res
    k_oth, v_oth = core_swap(k), core_swap(v)
    o, sums = attend_call(scale, q, k, k_oth, v, v_oth, aug_q, aug_k, head_scale, add_q)
    res = ffn_call(save, x, o, w_out, gains[1], w_gu, w_down)
    if not save:
        return res[0]
    y, h, n2, g, u, z = res
    return y, (x, n1, q, k, v, k_oth, v_oth, q0, k0, o, sums, h, n2, g, u, z)


def backward(dy, state, weights, gains, tab, scale):
    x, n1, q, k, v, k_oth, v_oth, q0, k0, o, sums, h, n2, g, u, z = state
    w_qkv, w_out, w_gu, w_down = weights
    cos, sin, aug_q, aug_k, head_scale, _, add_k, var_q = tab
    dh, da, do, dgu, gain_f = ffn_back_call(dy, h, g, u, w_gu, w_down, w_out, gains[1])
    dq, dk, dk_send, dv, dv_send, bias = attend_back_call(
        scale, q, k, k_oth, v, v_oth, do, o, sums, aug_q, aug_k, head_scale, add_k, var_q
    )
    dk_got, dv_got = core_swap(dk_send), core_swap(dv_send)
    dp, dx, gain_a = qkv_back_call(
        dq, dk, dk_got, dv, dv_got, q0, k0, cos, sin, w_qkv, x, dh, gains[0]
    )
    return dx, da, dgu, dp, jnp.concatenate([gain_a, gain_f], axis=0), bias


def per_device(
    boundary, w_qkv, w_out, w_gate_up, w_down, norm_gains, variate_bias,
    segment_ids, variate_ids, time_ids, padding_mask,
):
    ti = lax.axis_index("tensor")
    tn = lax.axis_size("tensor")
    yi, core = ti // 2, ti % 2
    zi, n = lax.axis_index("dp"), lax.axis_size("dp")
    is_first = lax.axis_index("section") == 0
    local = boundary[0]
    rows, model = local.shape[1:]
    scale = LOG2E / math.sqrt(HD)

    own = lax.dynamic_index_in_dim(local, yi, 0, keepdims=False)
    away = lax.dynamic_index_in_dim(local, 1 - yi, 0, keepdims=False)
    came = y_swap(away.astype(BF)).astype(F32)
    ends = jnp.where(
        yi == 0, jnp.concatenate([own, came], axis=0), jnp.concatenate([came, own], axis=0)
    )

    cols = w_qkv.shape[1]
    width = w_qkv.shape[3]
    hidden = w_gate_up.shape[3]
    p_qkv = w_qkv[0].transpose(1, 2, 0).reshape(3 * width, cols)
    p_gain = jnp.pad(norm_gains[0], ((0, 14), (0, 0)))
    full_qkv = gather_weight(jnp.concatenate([p_qkv, p_gain], axis=0))
    full_out = gather_weight(w_out[0])
    full_gu = gather_weight(w_gate_up[0].transpose(1, 2, 0).reshape(2 * hidden, cols))
    full_down = gather_weight(w_down[0])
    gains_all = full_qkv[:, 0, 3 * width : 3 * width + 2].transpose(1, 0, 2).reshape(2, model)
    gains = [gains_all[i : i + 1].astype(F32) for i in range(2)]
    full_qkv = full_qkv[:, :, : 3 * width]
    weights = (full_qkv, full_out, full_gu, full_down)

    bias_all = lax.all_gather(variate_bias[0], "tensor", axis=0, tiled=True).astype(F32)

    def row_of(array):
        return lax.dynamic_index_in_dim(array, yi, 0, keepdims=False)

    tab = tables(
        row_of(segment_ids), row_of(variate_ids), row_of(time_ids), row_of(padding_mask),
        bias_all, core,
    )

    y_low = forward(False, ends, weights, gains, tab, scale)
    got = lax.ppermute(y_low, "section", [(0, 1)]).astype(F32)
    x_in = jnp.where(is_first, ends, got)
    y, state = forward(True, x_in, weights, gains, tab, scale)
    dx = backward(ends, state, weights, gains, tab, scale)[0]
    got = lax.ppermute(dx.astype(BF), "section", [(1, 0)]).astype(F32)
    dy = jnp.where(is_first, got, ends)
    x, n1, q, k, v, k_oth, v_oth, q0, k0, o, sums, h, n2, g, u, z = state

    def by_core(array, index):
        parts = array.reshape((2, 2) + array.shape[1:])
        return lax.dynamic_index_in_dim(parts, index, 1, keepdims=False)

    def halves(array):
        return by_core(array, core), core_swap(by_core(array, 1 - core))

    def heads(array):
        return array.reshape(array.shape[0], tn, -1).transpose(1, 0, 2)

    df = dy.astype(BF)
    df_oth = core_swap(df)
    z_own, z_oth = halves(z)
    g_down = scatter_grad(wgrad_call(z_own, df, z_oth, df_oth))
    dx, da, dgu, dp, gain_grads, bias = backward(dy, state, weights, gains, tab, scale)
    n2_oth, n1_oth, da_oth = core_swap(n2), core_swap(n1), core_swap(da)
    gu_own, gu_oth = halves(dgu)
    flat = (4, h.shape[0], hidden)
    g_gu = wgrad_call(gu_own.reshape(flat), n2, gu_oth.reshape(flat), n2_oth)
    g_gu = g_gu.reshape(2, 2, model // ZB, hidden, ZB).transpose(0, 2, 1, 3, 4)
    g_gu = scatter_grad(g_gu.reshape(2, model // ZB, 2 * hidden, ZB))
    o_own, o_oth = halves(heads(o))
    g_out = scatter_grad(wgrad_call(o_own, da, o_oth, da_oth))
    dp_own, dp_oth = halves(dp)
    g_qkv = scatter_grad(wgrad_call(dp_own, n1, dp_oth, n1_oth))

    out_rows = jnp.where(is_first, dx, y)
    lower, upper = out_rows[:rows], out_rows[rows:]
    keep = jnp.where(yi == 0, lower, upper)
    send = jnp.where(yi == 0, upper, lower)
    back = y_swap(send.astype(BF)).astype(F32)
    boundary_out = jnp.where(
        yi == 0, jnp.stack([keep, back]), jnp.stack([back, keep])
    )[None]

    bias_sum = bias.sum(axis=-1).reshape(1, -1)
    small = jnp.concatenate(
        [gain_grads, jnp.pad(bias_sum, ((0, 0), (0, model - bias_sum.shape[1])))], axis=0
    )
    small = small_sum(small)
    piece = model // (n * tn)
    gain_piece = lax.dynamic_slice_in_dim(small[:2], (zi * tn + ti) * piece, piece, 1)
    heads_local = variate_bias.shape[1]
    bias_piece = lax.dynamic_slice_in_dim(
        small[2, : bias_sum.shape[1]].reshape(-1, 2), ti * heads_local, heads_local, 0
    )
    return (
        boundary_out,
        g_qkv.reshape(3, width, cols).transpose(2, 0, 1)[None],
        g_out[None],
        g_gu.reshape(2, hidden, cols).transpose(2, 0, 1)[None],
        g_down[None],
        gain_piece[None],
        bias_piece[None],
    )


def solution(mesh):
    placed = (
        P("section", "dp", "tensor", None),
        P("section", "dp", None, "tensor"),
        P("section", "tensor", "dp"),
        P("section", "dp", None, "tensor"),
        P("section", "tensor", "dp"),
        P("section", None, "dp"),
        P("section", "tensor", None),
        P("dp", None),
        P("dp", None),
        P("dp", None),
        P("dp", None),
    )
    return jax.shard_map(
        per_device,
        mesh=mesh,
        in_specs=placed,
        out_specs=(
            P("section", "dp", "tensor", None),
            P("section", "dp", None, "tensor"),
            P("section", "tensor", "dp"),
            P("section", "dp", None, "tensor"),
            P("section", "tensor", "dp"),
            P("section", None, ("dp", "tensor")),
            P("section", "tensor", None),
        ),
        check_vma=False,
    )
```

```python
import functools
import math

import jax
import jax.numpy as jnp
from jax import lax
from jax.experimental import pallas as pl
from jax.experimental.pallas import tpu as pltpu
from jax.sharding import PartitionSpec as P

EPS = 1e-05
BIG = 8192.0
LOG2E = 1.4426950408889634
BF = jnp.bfloat16
F32 = jnp.float32
HD = 64
ZB = 256
VMEM_MB = 56
N_VAR = 4
L_SEG = 8
L_PAD = 24
L_LSE = 25


def dot(a, b):
    return lax.dot_general(a, b, (((1,), (0,)), ((), ())), preferred_element_type=F32)


def dot_nt(a, b):
    return lax.dot_general(a, b, (((1,), (1,)), ((), ())), preferred_element_type=F32)


def dot_tn(a, b):
    return lax.dot_general(a, b, (((0,), (0,)), ((), ())), preferred_element_type=F32)


def params(mb=VMEM_MB):
    return pltpu.CompilerParams(
        dimension_semantics=("arbitrary",), vmem_limit_bytes=mb * 1024 * 1024
    )


def cost(flops, nbytes, trans=0):
    return pl.CostEstimate(flops=1000, bytes_accessed=1000, transcendentals=0)


def sds(shape, dtype):
    return jax.ShapeDtypeStruct(shape, dtype)


def whole(shape):
    zeros = (0,) * len(shape)
    return pl.BlockSpec(shape, lambda *_: zeros)


def head_sum(u):
    row = lax.broadcasted_iota(jnp.int32, (u.shape[1], u.shape[1]), 0) // HD
    col = lax.broadcasted_iota(jnp.int32, (u.shape[1], u.shape[1]), 1) // HD
    return dot(u.astype(BF), jnp.where(row == col, 1.0, 0.0).astype(BF))


def half_swap(u):
    lane = lax.broadcasted_iota(jnp.int32, u.shape, 1) % HD
    return jnp.where(lane < HD // 2, pltpu.roll(u, 128 - HD // 2, 1), pltpu.roll(u, HD // 2, 1))


def row_rms(x):
    return lax.rsqrt(jnp.mean(x * x, axis=-1, keepdims=True) + EPS)


def hbm():
    return pl.BlockSpec(memory_space=pl.ANY)


def smem():
    return pl.BlockSpec(memory_space=pltpu.SMEM)


def copies(refs, low, scratch, sems, t):
    rows = pl.ds(low, scratch.shape[2])
    return [
        pltpu.make_async_copy(
            refs[4 * (t // 2) + r].at[t % 2, rows], scratch.at[r, t], sems.at[r, t]
        )
        for r in range(4)
    ]


def start_all(refs, low, scratch, sems):
    for t in range(4):
        for copy in copies(refs, low, scratch, sems, t):
            copy.start()


def wait_for(refs, low, scratch, sems, t):
    for fixed in range(4):

        @pl.when(t == fixed)
        def _():
            for copy in copies(refs, low, scratch, sems, fixed):
                copy.wait()


def weight_scratch(feats):
    return [pltpu.VMEM((4, 4, feats, ZB), BF), pltpu.SemaphoreType.DMA((4, 4))]


def place(zi_ref, r):
    return lax.rem(zi_ref[0] - r + 4, 4)


def block_store(ref, value):
    for z in range(4):
        ref[z] = value[:, z * ZB : (z + 1) * ZB]


def chunks(wide, step=ZB):
    return [slice(low, min(low + step, wide)) for low in range(0, wide, step)]


def block_load(ref):
    return jnp.concatenate([ref[z] for z in range(4)], axis=1)


def qkv_kernel(save, x_ref, gain_ref, zi_ref, cos_ref, sin_ref, *refs):
    weight, refs = refs[:8], refs[8:]
    if save:
        n_ref, q_ref, k_ref, v_ref, q0_ref, k0_ref, n_scr, w_ref, sems = refs
    else:
        q_ref, k_ref, v_ref, n_scr, w_ref, sems = refs
    t = pl.program_id(0)

    @pl.when(t == 0)
    def _():
        start_all(weight, 0, w_ref, sems)
        x = x_ref[...].astype(F32)
        n = (x * row_rms(x) * gain_ref[...]).astype(BF)
        block_store(n_scr, n)
        if save:
            n_ref[...] = n

    wait_for(weight, 0, w_ref, sems, t)
    width = q_ref.shape[1]

    def project(which):
        cols = slice(which * width, (which + 1) * width)
        total = dot_nt(n_scr[place(zi_ref, 0)], w_ref[0, t, cols])
        for r in range(1, 4):
            total = total + dot_nt(n_scr[place(zi_ref, r)], w_ref[r, t, cols])
        return total

    cos, sin = cos_ref[...], sin_ref[...]
    for which, out in ((0, q_ref), (1, k_ref)):
        u = project(which)
        if save:
            kept = q0_ref if which == 0 else k0_ref
            kept[...] = u.astype(BF)
        un = u * lax.rsqrt(head_sum(u * u) * (1.0 / HD) + EPS)
        for pair in range(width // 128):
            at = slice(pair * 128, (pair + 1) * 128)
            out[:, at] = (un[:, at] * cos + half_swap(un[:, at]) * sin).astype(BF)
    v_ref[...] = project(2).astype(BF)


def qkv_call(save, x, gain, zi, w, feats, cos, sin):
    rows, model = x.shape
    width = feats // 3
    total = 4 * width
    col = pl.BlockSpec((rows, width), lambda t: (0, t))
    outs = [sds((rows, total), BF)] * 3
    specs = [col] * 3
    if save:
        outs = [sds((rows, model), BF)] + outs + [sds((rows, total), BF)] * 2
        specs = [whole((rows, model))] + specs + [col] * 2
    return pl.pallas_call(
        functools.partial(qkv_kernel, save),
        grid=(4,),
        in_specs=[whole((rows, model)), whole((1, model)), smem()]
        + [whole((rows, 128))] * 2
        + [hbm()] * 8,
        out_specs=specs,
        out_shape=outs,
        scratch_shapes=[pltpu.VMEM((4, rows, ZB), BF)] + weight_scratch(feats),
        compiler_params=params(22),
        cost_estimate=cost(2 * rows * model * 3 * total, 6 * total * model + 16 * x.size),
    )(x, gain, zi, cos, sin, *w)


def other_core_spec(rows, pairs):
    half = pairs // 2
    return pl.BlockSpec((rows, 128), lambda p: (0, lax.rem(p + half, pairs)))


def pick(first, h, a, b):
    return jnp.where(first, a, b) if h == 0 else jnp.where(first, b, a)


def pick_low(first, h, a, b):
    mine = jnp.where(first, 1.0, 0.0) if h == 0 else jnp.where(first, 0.0, 1.0)
    low = mine.astype(BF)
    return a * low + b * (1.0 - mine).astype(BF)


def attend_kernel(
    scale, q_ref, ko_ref, kx_ref, vo_ref, vx_ref, aq_ref, ak_ref, hs_ref, add_ref, o_ref, l_ref
):
    rows = q_ref.shape[0]
    kb = 128
    first = lax.broadcasted_iota(jnp.int32, (1, 128), 1) < HD
    q = q_ref[...].astype(F32)
    base = aq_ref[...]
    raws = []
    for h in range(2):
        qh = pick(first, h, q, base * hs_ref[0, h : h + 1, :]).astype(BF)
        total = None
        for half, (k_ref, v_ref) in enumerate(((ko_ref, vo_ref), (kx_ref, vx_ref))):
            for block in range(rows // kb):
                at = slice(block * kb, (block + 1) * kb)
                kk = slice(half * rows + block * kb, half * rows + (block + 1) * kb)
                kh = pick_low(first, h, k_ref[at, :], ak_ref[kk, :])
                vh = pick_low(first, h, v_ref[at, :], BF(1.0))
                s = dot_nt(qh, kh)
                if half == 0:
                    s = s + add_ref[:, at]
                part = dot(jnp.exp2(s * scale).astype(BF), vh)
                total = part if total is None else total + part
        raws.append(total)
    sums = jnp.where(first, raws[1], raws[0])
    l_ref[...] = sums
    o_ref[...] = (jnp.where(first, raws[0], raws[1]) / pltpu.roll(sums, HD, 1)).astype(BF)


def attend_call(scale, q, k_own, k_oth, v_own, v_oth, aug_q, aug_k, head_scale, add_own):
    rows, total = q.shape
    pairs = total // 128
    col = pl.BlockSpec((rows, 128), lambda p: (0, p))
    far = other_core_spec(rows, pairs)
    return pl.pallas_call(
        functools.partial(attend_kernel, scale),
        grid=(pairs,),
        in_specs=[
            col,
            col,
            far,
            col,
            far,
            whole(aug_q.shape),
            whole(aug_k.shape),
            pl.BlockSpec((1, 2, 128), lambda p: (p, 0, 0)),
            whole(add_own.shape),
        ],
        out_specs=[col, col],
        out_shape=[sds((rows, total), BF), sds((rows, total), F32)],
        compiler_params=params(10),
        cost_estimate=cost(
            4 * 2 * rows * rows * 2 * total, 20 * rows * total, rows * rows * 2 * pairs * 2
        ),
    )(q, k_own, k_oth, v_own, v_oth, aug_q, aug_k, head_scale, add_own)


def padded(hidden):
    return -(-2 * hidden // 128) * 128


def pair_scratch(parts, hidden):
    return [
        pltpu.VMEM((4, 2, parts * padded(hidden), ZB), BF),
        pltpu.SemaphoreType.DMA((4, 2, 2, parts)),
    ]


def pair_copies(refs, parts, scratch, sems, half):
    wide = scratch.shape[2] // parts
    hidden = refs[0].shape[1] // parts
    return [
        pltpu.make_async_copy(
            refs[4 * half + r].at[y, pl.ds(part * hidden, hidden)],
            scratch.at[r, half, pl.ds(part * wide + y * hidden, hidden)],
            sems.at[r, half, y, part],
        )
        for r in range(4)
        for y in range(2)
        for part in range(parts)
    ]


def pair_start(refs, parts, scratch, sems):
    wide = scratch.shape[2] // parts
    hidden = refs[0].shape[1] // parts
    for half in range(2):
        for copy in pair_copies(refs, parts, scratch, sems, half):
            copy.start()
    blank = wide - 2 * hidden
    if blank:
        for half in range(2):
            for r in range(4):
                for part in range(parts):
                    low = part * wide + 2 * hidden
                    scratch[r, half, low : low + blank] = jnp.zeros((blank, ZB), BF)


def pair_wait(refs, parts, scratch, sems, half):
    for fixed in range(2):

        @pl.when(half == fixed)
        def _():
            for copy in pair_copies(refs, parts, scratch, sems, fixed):
                copy.wait()


def near_far(rows, feats):
    return (
        pl.BlockSpec((1, rows, feats), lambda t: (jnp.minimum(t, 1), 0, 0)),
        pl.BlockSpec((1, rows, feats), lambda t: (jnp.maximum(t - 2, 0), 0, 0)),
    )


def put(is_near, near_ref, far_ref, value, at=...):
    @pl.when(is_near)
    def _():
        near_ref[at] = value

    @pl.when(jnp.logical_not(is_near))
    def _():
        far_ref[at] = value


def ffn_up_kernel(save, out_low, x_ref, o_ref, gain_ref, zi_ref, *refs):
    wo, wgu, refs = refs[:8], refs[8:16], refs[16:]
    if save:
        h_ref, zn_ref, zf_ref, n_ref, g_ref, u_ref = refs[:6]
    else:
        h_ref, zn_ref, zf_ref = refs[:3]
    n_scr, wo_ref, wo_sems, wgu_ref, wgu_sems, acc, z_scr = refs[-7:]
    wide = wgu_ref.shape[2] // 2
    half = pl.program_id(0)

    @pl.when(half == 0)
    def _():
        start_all(wo, out_low, wo_ref, wo_sems)
        pair_start(wgu, 2, wgu_ref, wgu_sems)
        width = wo_ref.shape[2]
        block_store(acc, x_ref[...].astype(F32))
        for s in range(4):
            for copy in copies(wo, out_low, wo_ref, wo_sems, s):
                copy.wait()
        for r in range(4):
            z = place(zi_ref, r)
            h = acc[z]
            for s in range(4):
                h = h + dot(o_ref[:, s * width : (s + 1) * width], wo_ref[r, s])
            acc[z] = h
        h = block_load(acc)
        n = (h * row_rms(h) * gain_ref[...]).astype(BF)
        block_store(n_scr, n)
        h_ref[...] = h
        if save:
            n_ref[...] = n

    pair_wait(wgu, 2, wgu_ref, wgu_sems, half)
    for at in chunks(wide):
        total = []
        for part in range(2):
            cols = slice(part * wide + at.start, part * wide + at.stop)
            one = dot_nt(n_scr[place(zi_ref, 0)], wgu_ref[0, half, cols])
            for r in range(1, 4):
                one = one + dot_nt(n_scr[place(zi_ref, r)], wgu_ref[r, half, cols])
            total.append(one)
        gate, up = total
        z_scr[:, at] = (gate / (1.0 + jnp.exp(-gate)) * up).astype(BF)
        if save:
            g_ref[0, :, at] = gate.astype(BF)
            u_ref[0, :, at] = up.astype(BF)
    put(half == 0, zn_ref, zf_ref, z_scr[...])


def ffn_up_call(save, out_low, width, x, o, gain, zi, wo, wgu):
    rows, model = x.shape
    hidden = wgu[0].shape[1] // 2
    wide = padded(hidden)
    big = whole((rows, model))
    part = pl.BlockSpec((1, rows, wide), lambda t: (t, 0, 0))
    outs = [sds((rows, model), F32)] + [sds((rows, wide), BF)] * 2
    specs = [big, whole((rows, wide)), whole((rows, wide))]
    if save:
        outs += [sds((rows, model), BF)] + [sds((2, rows, wide), BF)] * 2
        specs += [big, part, part]
    return pl.pallas_call(
        functools.partial(ffn_up_kernel, save, out_low),
        grid=(2,),
        in_specs=[big, whole(o.shape), whole((1, model)), smem()] + [hbm()] * 16,
        out_specs=specs,
        out_shape=outs,
        scratch_shapes=[pltpu.VMEM((4, rows, ZB), BF)]
        + weight_scratch(width)
        + pair_scratch(2, hidden)
        + [pltpu.VMEM((4, rows, ZB), F32), pltpu.VMEM((rows, wide), BF)],
        compiler_params=params(30),
        cost_estimate=cost(
            2 * rows * model * (8 * hidden + model), 16 * hidden * model + 20 * x.size
        ),
    )(x, o, gain, zi, *wo, *wgu)


def ffn_down_kernel(h_ref, zn_ref, zf_ref, zi_ref, *refs):
    weight, (y_ref, w_ref, sems) = refs[:8], refs[8:]
    pair_start(weight, 1, w_ref, sems)
    for half, z_ref in enumerate((zn_ref, zf_ref)):
        for copy in pair_copies(weight, 1, w_ref, sems, half):
            copy.wait()
    for z in range(4):
        r = lax.rem(zi_ref[0] - z + 4, 4)
        at = slice(z * ZB, (z + 1) * ZB)
        y = h_ref[:, at] + dot(zn_ref[...], w_ref[r, 0]) + dot(zf_ref[...], w_ref[r, 1])
        y_ref[:, at] = y.astype(y_ref.dtype)


def ffn_down_call(dtype, h, z_near, z_far, zi, wd):
    rows, model = h.shape
    hidden = wd[0].shape[1]
    vmem = pl.BlockSpec(memory_space=pltpu.VMEM)
    return pl.pallas_call(
        ffn_down_kernel,
        in_specs=[vmem] * 3 + [smem()] + [hbm()] * 8,
        out_specs=vmem,
        out_shape=sds((rows, model), dtype),
        scratch_shapes=pair_scratch(1, hidden),
        compiler_params=pltpu.CompilerParams(vmem_limit_bytes=18 * 1024 * 1024),
        cost_estimate=cost(2 * rows * model * 4 * hidden, 8 * hidden * model + 8 * h.size),
    )(h, z_near, z_far, zi, *wd)


def ffn_back_kernel(out_low, dy_ref, h_ref, g_ref, u_ref, gain_ref, zi_ref, *refs):
    wo, wgu, wd, refs = refs[:8], refs[8:16], refs[16:24], refs[24:]
    dh_ref, da_ref, do_ref, dgn_ref, dgf_ref, dun_ref, duf_ref, gg_ref = refs[:8]
    df_scr, acc, wo_ref, wo_sems, wgu_ref, wgu_sems, wd_ref, wd_sems, dg_scr, du_scr = refs[8:]
    wide = wd_ref.shape[2]
    half = pl.program_id(0)

    @pl.when(half == 0)
    def _():
        pair_start(wd, 1, wd_ref, wd_sems)
        pair_start(wgu, 2, wgu_ref, wgu_sems)
        start_all(wo, out_low, wo_ref, wo_sems)
        block_store(df_scr, dy_ref[...])
        acc[...] = jnp.zeros_like(acc)

    pair_wait(wd, 1, wd_ref, wd_sems, half)
    for at in chunks(wide):
        dz = dot_nt(df_scr[place(zi_ref, 0)], wd_ref[0, half, at])
        for r in range(1, 4):
            dz = dz + dot_nt(df_scr[place(zi_ref, r)], wd_ref[r, half, at])
        gate = g_ref[0, :, at].astype(F32)
        up = u_ref[0, :, at].astype(F32)
        s = 1.0 / (1.0 + jnp.exp(-gate))
        dg_scr[:, at] = (dz * up * s * (1.0 + gate * (1.0 - s))).astype(BF)
        du_scr[:, at] = (dz * gate * s).astype(BF)
    dgate, dup = dg_scr[...], du_scr[...]
    put(half == 0, dgn_ref, dgf_ref, dgate)
    put(half == 0, dun_ref, duf_ref, dup)
    pair_wait(wgu, 2, wgu_ref, wgu_sems, half)
    for r in range(4):
        z = place(zi_ref, r)
        acc[z] = acc[z] + (
            dot(dgate, wgu_ref[r, half, :wide]) + dot(dup, wgu_ref[r, half, wide:])
        )

    @pl.when(half == 1)
    def _():
        h = h_ref[...]
        r = row_rms(h)
        hn = h * r
        dn = block_load(acc)
        gg_ref[...] = jnp.sum(dn * hn, axis=0, keepdims=True)
        dhat = dn * gain_ref[...]
        dh = dy_ref[...].astype(F32) + r * (
            dhat - hn * jnp.mean(dhat * hn, axis=-1, keepdims=True)
        )
        dh_ref[...] = dh
        da = dh.astype(BF)
        da_ref[...] = da
        block_store(df_scr, da)
        width = wo_ref.shape[2]
        for s in range(4):
            for copy in copies(wo, out_low, wo_ref, wo_sems, s):
                copy.wait()
        for s in range(4):
            part = dot_nt(df_scr[place(zi_ref, 0)], wo_ref[0, s])
            for q in range(1, 4):
                part = part + dot_nt(df_scr[place(zi_ref, q)], wo_ref[q, s])
            do_ref[:, s * width : (s + 1) * width] = part.astype(BF)


def ffn_back_call(out_low, width, dy, h, g, u, gain, zi, wo, wgu, wd):
    rows, model = dy.shape
    hidden = wd[0].shape[1]
    wide = g.shape[2]
    big = whole((rows, model))
    part = pl.BlockSpec((1, rows, wide), lambda t: (t, 0, 0))
    return pl.pallas_call(
        functools.partial(ffn_back_kernel, out_low),
        grid=(2,),
        in_specs=[big, big, part, part, whole((1, model)), smem()] + [hbm()] * 24,
        out_specs=[big, big, big] + [whole((rows, wide))] * 4 + [whole((1, model))],
        out_shape=[sds((rows, model), F32), sds((rows, model), BF), sds((rows, model), BF)]
        + [sds((rows, wide), BF)] * 4
        + [sds((1, model), F32)],
        scratch_shapes=[pltpu.VMEM((4, rows, ZB), BF), pltpu.VMEM((4, rows, ZB), F32)]
        + weight_scratch(width)
        + pair_scratch(2, hidden)
        + pair_scratch(1, hidden)
        + [pltpu.VMEM((rows, wide), BF)] * 2,
        compiler_params=params(57),
        cost_estimate=cost(
            2 * rows * model * (12 * hidden + model), 24 * hidden * model + 20 * dy.size
        ),
    )(dy, h, g, u, gain, zi, *wo, *wgu, *wd)


def split3(value):
    hi = value.astype(BF).astype(F32)
    mid = (value - hi).astype(BF).astype(F32)
    return hi, mid, value - hi - mid


def attend_back_kernel(
    scale, q_ref, ko_ref, kx_ref, vo_ref, vx_ref, do_ref, o_ref, l_ref, aq_ref, ak_ref, hs_ref,
    add_ref, var_ref, dq_ref, dko_ref, dkx_ref, dvo_ref, dvx_ref, bias_ref,
):
    rows = q_ref.shape[0]
    kb = 256
    first = lax.broadcasted_iota(jnp.int32, (1, 128), 1) < HD
    lane = lax.broadcasted_iota(jnp.int32, (1, 128), 1) % HD
    q = q_ref[...].astype(F32)
    do = do_ref[...].astype(F32)
    inner = do * o_ref[...].astype(F32)
    base = aq_ref[...]
    hi, mid, low = split3(jnp.log2(l_ref[...]) * (-1.0 / scale))
    lse = jnp.where(lane == L_LSE, hi, 0.0)
    lse = jnp.where(lane == L_LSE + 1, mid, lse)
    lse = jnp.where(lane == L_LSE + 2, low, lse)
    dq_t = []
    dk = [[], []]
    dv = [[], []]
    for h in range(2):
        qh = pick(first, h, q, base * hs_ref[0, h : h + 1, :] + lse).astype(BF)
        d = jnp.sum(pick(first, h, inner, 0.0), axis=-1, keepdims=True)
        dhi, dmid, dlow = split3(-d)
        d_aug = jnp.where(lane == 0, dhi, 0.0)
        d_aug = jnp.where(lane == 1, dmid, d_aug)
        d_aug = jnp.where(lane == 2, dlow, d_aug)
        doh = pick(first, h, do, d_aug).astype(BF)
        total = None
        for half, (k_ref, v_ref) in enumerate(((ko_ref, vo_ref), (kx_ref, vx_ref))):
            for block in range(rows // kb):
                at = slice(block * kb, (block + 1) * kb)
                kk = slice(half * rows + block * kb, half * rows + (block + 1) * kb)
                kh = pick_low(first, h, k_ref[at, :], ak_ref[kk, :])
                vh = pick_low(first, h, v_ref[at, :], BF(1.0))
                s = dot_nt(kh, qh)
                if half == 0:
                    s = s + add_ref[at, :]
                p = jnp.exp2(s * scale)
                ds = (p * dot_nt(vh, doh)).astype(BF)
                dv[h].append(dot(p.astype(BF), doh))
                dk[h].append(dot(ds, qh))
                part = dot_tn(kh, ds)
                total = part if total is None else total + part
        dq_t.append(total)
    scale_back = 1.0 / math.sqrt(HD)
    count = rows // kb
    for half, (dk_ref, dv_ref) in enumerate(((dko_ref, dvo_ref), (dkx_ref, dvx_ref))):
        for block in range(count):
            at = slice(block * kb, (block + 1) * kb)
            i = half * count + block
            dk_ref[at, :] = (jnp.where(first, dk[0][i], dk[1][i]) * scale_back).astype(dk_ref.dtype)
            dv_ref[at, :] = jnp.where(first, dv[0][i], dv[1][i]).astype(dv_ref.dtype)
    joined = jnp.concatenate([dq_t[0][:HD], dq_t[1][HD:]], axis=0)
    dq_ref[...] = (joined.T * scale_back).astype(BF)
    mine = var_ref[...]
    for h in range(2):
        begin = HD if h == 0 else 0
        r = dq_t[h][begin : begin + 8]
        same = jnp.sum(r * mine, axis=0, keepdims=True)
        every = jnp.sum(r[:N_VAR], axis=0, keepdims=True)
        bias_ref[0, 2 * h : 2 * h + 1, :] = same
        bias_ref[0, 2 * h + 1 : 2 * h + 2, :] = every - same


def attend_back_call(
    scale, span, q, k_own, k_oth, v_own, v_oth, do, o, sums, aug_q, aug_k, head_scale, add_own, var_q
):
    rows, total = q.shape
    every = total // 128
    low, high = span or (0, every)
    pairs = high - low
    total = pairs * 128
    col = pl.BlockSpec((rows, 128), lambda p: (0, p + low))
    far = pl.BlockSpec((rows, 128), lambda p: (0, lax.rem(p + low + every // 2, every)))
    out = pl.BlockSpec((rows, 128), lambda p: (0, p))
    out_far = other_core_spec(rows, pairs) if span is None else out
    return pl.pallas_call(
        functools.partial(attend_back_kernel, scale),
        grid=(pairs,),
        in_specs=[col, col, far, col, far, col, col, col]
        + [
            whole(aug_q.shape),
            whole(aug_k.shape),
            pl.BlockSpec((1, 2, 128), lambda p: (p + low, 0, 0)),
            whole(add_own.shape),
            whole(var_q.shape),
        ],
        out_specs=[out, out, out_far, out, out_far] + [pl.BlockSpec((1, 4, rows), lambda p: (p, 0, 0))],
        out_shape=[
            sds((rows, total), BF),
            sds((rows, total), BF),
            sds((rows, total), BF),
            sds((rows, total), BF),
            sds((rows, total), BF),
            sds((pairs, 4, rows), F32),
        ],
        compiler_params=params(14),
        cost_estimate=cost(
            10 * 2 * rows * rows * 2 * total, 40 * rows * total, rows * rows * 2 * pairs * 2
        ),
    )(q, k_own, k_oth, v_own, v_oth, do, o, sums, aug_q, aug_k, head_scale, add_own, var_q)


def qkv_back_kernel(
    dq_ref, dk_ref, dkr_ref, dv_ref, dvr_ref, q0_ref, k0_ref, cos_ref, sin_ref, x_ref, dh_ref,
    gain_ref, zi_ref, *refs,
):
    weight, refs = refs[:8], refs[8:]
    dpn_ref, dpf_ref, dx_ref, dxl_ref, gg_ref, dp_scr, acc, w_ref, sems = refs
    width = dq_ref.shape[1]
    t = pl.program_id(0)

    @pl.when(t == 0)
    def _():
        start_all(weight, 0, w_ref, sems)
        acc[...] = jnp.zeros_like(acc)

    cos, sin = cos_ref[...], sin_ref[...]
    for which in range(2):
        u = (q0_ref if which == 0 else k0_ref)[...].astype(F32)
        r = lax.rsqrt(head_sum(u * u) * (1.0 / HD) + EPS)
        un = u * r
        turned = []
        for pair in range(width // 128):
            at = slice(pair * 128, (pair + 1) * 128)
            if which == 0:
                grad = dq_ref[:, at].astype(F32)
            else:
                grad = dk_ref[:, at].astype(F32) + dkr_ref[:, at].astype(F32)
            turned.append(grad * cos - half_swap(grad) * sin)
        grad = jnp.concatenate(turned, axis=1)
        out = r * (grad - un * (head_sum(grad * un) * (1.0 / HD)))
        dp_scr[:, which * width : (which + 1) * width] = out.astype(BF)
    dp_scr[:, 2 * width :] = (dv_ref[...].astype(F32) + dvr_ref[...].astype(F32)).astype(BF)
    wait_for(weight, 0, w_ref, sems, t)
    dp = dp_scr[...]
    put(t < 2, dpn_ref, dpf_ref, dp, 0)
    for r in range(4):
        z = place(zi_ref, r)
        acc[z] = acc[z] + dot(dp, w_ref[r, t])

    @pl.when(t == 3)
    def _():
        x = x_ref[...].astype(F32)
        r = row_rms(x)
        xn = x * r
        dn = block_load(acc)
        gg_ref[...] = jnp.sum(dn * xn, axis=0, keepdims=True)
        dhat = dn * gain_ref[...]
        dx = dh_ref[...] + r * (dhat - xn * jnp.mean(dhat * xn, axis=-1, keepdims=True))
        dx_ref[...] = dx
        dxl_ref[...] = dx.astype(BF)


def qkv_back_call(dq, dk, dkr, dv, dvr, q0, k0, cos, sin, x, dh, gain, zi, w, feats):
    rows, model = x.shape
    width = feats // 3
    big = whole((rows, model))
    col = pl.BlockSpec((rows, width), lambda t: (0, t))
    return pl.pallas_call(
        qkv_back_kernel,
        grid=(4,),
        in_specs=[col] * 7
        + [whole((rows, 128)), whole((rows, 128)), big, big, whole((1, model)), smem()]
        + [hbm()] * 8,
        out_specs=[*near_far(rows, feats), big, big, whole((1, model))],
        out_shape=[sds((2, rows, feats), BF)] * 2
        + [sds((rows, model), F32), sds((rows, model), BF), sds((1, model), F32)],
        scratch_shapes=[pltpu.VMEM((rows, feats), BF), pltpu.VMEM((4, rows, ZB), F32)]
        + weight_scratch(feats),
        compiler_params=params(24),
        cost_estimate=cost(8 * rows * model * feats, 8 * feats * model + 40 * x.size),
    )(dq, dk, dkr, dv, dvr, q0, k0, cos, sin, x, dh, gain, zi, *w)


def wgrad_kernel(feats, zi_ref, ao_ref, bo_ref, ax_ref, bx_ref, keep_ref, send_ref):
    if len(ao_ref.shape) == 3:
        for i, out in ((1, send_ref), (0, keep_ref)):
            g = dot_tn(ao_ref[i], bo_ref[...]) + dot_tn(ax_ref[i], bx_ref[...])
            for z in range(4):
                out[lax.rem(zi_ref[0] - z + 4, 4)] = g[:, z * ZB : (z + 1) * ZB].astype(BF)
    else:
        g = dot_tn(ao_ref[...], bo_ref[...]) + dot_tn(ax_ref[...], bx_ref[...])
        for z in range(4):
            r = lax.rem(zi_ref[0] - z + 4, 4)
            at = slice(z * ZB, (z + 1) * ZB)
            keep_ref[r] = g[:feats, at].astype(BF)
            send_ref[r] = g[feats : 2 * feats, at].astype(BF)


def wgrad_call(zi, feats, a_own, b_own, a_oth, b_oth):
    rows, model = b_own.shape
    part = whole(a_oth.shape)
    big = whole((rows, model))
    out = whole((4, feats, ZB))
    return pl.pallas_call(
        functools.partial(wgrad_kernel, feats),
        grid=(1,),
        in_specs=[smem(), part, big, part, big],
        out_specs=[out, out],
        out_shape=[sds((4, feats, ZB), BF)] * 2,
        compiler_params=params(26),
        cost_estimate=cost(8 * rows * feats * model, 4 * feats * model),
    )(zi, a_own, b_own, a_oth, b_oth)


def core_swap(value):
    n = lax.axis_size("tensor")
    return lax.ppermute(value, "tensor", [(i, i ^ 1) for i in range(n)])


def y_swap(value):
    n = lax.axis_size("tensor")
    return lax.ppermute(value, "tensor", [(i, i ^ 2) for i in range(n)])


def ring(value):
    n = lax.axis_size("dp")
    return lax.ppermute(value, "dp", [(i, (i + 1) % n) for i in range(n)])


def gather_any(piece):
    ti = lax.axis_index("tensor")
    every = lax.all_gather(lax.all_gather(piece, "dp"), "tensor")
    tn, n, feats, cols = every.shape
    every = every.transpose(0, 2, 1, 3).reshape(tn, feats, n * cols // ZB, ZB)
    every = jnp.take(every, ti ^ jnp.array([0, 2, 1, 3]), axis=0)
    every = jnp.take(every, jnp.array([0, 3, 2, 1]), axis=2).transpose(2, 0, 1, 3)
    return [every[r, :2] for r in range(4)] + [every[r, 2:] for r in range(4)]


def meet(*values):
    return lax.optimization_barrier(values)


def after(value, *others):
    return lax.optimization_barrier((value, others))[0]


def scatter_any(keep, send):
    total = keep.astype(F32) + y_swap(send).astype(F32)
    total = jnp.take(total, jnp.array([0, 3, 2, 1]), axis=0)
    flat = total.transpose(1, 0, 2).reshape(total.shape[1], -1).astype(BF)
    return lax.psum_scatter(flat, "dp", scatter_dimension=1, tiled=True).astype(F32)


def plus(a, b):
    return (a.astype(F32) + b.astype(F32)).astype(BF)


def small_sum(value):
    n = lax.axis_size("dp")
    value = value + core_swap(value)
    value = value + y_swap(value)
    if n & (n - 1):
        return lax.psum(value, "dp")
    bit = 1
    while bit < n:
        value = value + lax.ppermute(value, "dp", [(i, i ^ bit) for i in range(n)])
        bit *= 2
    return value


def own_rows(row, core):
    quarters = row.reshape(2, 2, row.shape[0] // 4)
    own = lax.dynamic_index_in_dim(quarters, core, 1, keepdims=False).reshape(-1)
    oth = lax.dynamic_index_in_dim(quarters, 1 - core, 1, keepdims=False).reshape(-1)
    return own, oth


def tables(segment, variate, time_row, pad, var_bias, core):
    seg_own, seg_oth = own_rows(segment, core)
    var_own, var_oth = own_rows(variate, core)
    pad_own, pad_oth = own_rows(pad, core)
    time_own, _ = own_rows(time_row, core)
    rows = seg_own.shape[0]
    half = HD // 2
    frequency = jnp.exp(-jnp.log(10000.0) * jnp.arange(half, dtype=F32) / half)
    phases = time_own.astype(F32)[:, None] * frequency[None, :]
    cos, sin = jnp.cos(phases), jnp.sin(phases)
    cos = jnp.concatenate([cos] * 4, axis=1)
    sin = jnp.concatenate([-sin, sin, -sin, sin], axis=1)
    lane = (jnp.arange(128, dtype=jnp.int32) % HD)[None, :]
    seg_k = jnp.concatenate([seg_own, seg_oth])[:, None]
    var_k = jnp.concatenate([var_own, var_oth])[:, None]
    pad_k = jnp.concatenate([jnp.ones_like(pad_own), pad_oth])[:, None]
    is_var = lane < 2 * N_VAR
    is_seg = (lane >= L_SEG) & (lane < L_PAD)
    is_lse = (lane >= L_LSE) & (lane < L_LSE + 3)
    aug_k = jnp.where(
        is_var,
        jnp.where(var_k == lane % N_VAR, 1.0, 0.0),
        jnp.where(
            is_seg,
            jnp.where(seg_k == lane - L_SEG, 0.0, -BIG),
            jnp.where(
                lane == L_PAD, jnp.where(pad_k == 1, 0.0, -BIG), jnp.where(is_lse, 1.0, 0.0)
            ),
        ),
    ).astype(BF)
    aug_q = jnp.where(
        is_var,
        jnp.where(var_own[:, None] == lane % N_VAR, 1.0, 0.0),
        jnp.where(
            is_seg,
            jnp.where(seg_own[:, None] == lane - L_SEG, 1.0, 0.0),
            jnp.where(lane == L_PAD, 1.0, 0.0),
        ),
    ).astype(F32)
    delta = (var_bias[:, 0] - var_bias[:, 1]) * math.sqrt(HD)
    hi = delta.astype(BF).astype(F32)
    low = (delta - hi).astype(BF).astype(F32)
    head_scale = jnp.where(
        lane < N_VAR, hi[:, None], jnp.where(lane < 2 * N_VAR, low[:, None], 1.0)
    ).reshape(-1, 2, 128)
    place = jnp.arange(rows, dtype=jnp.int32)
    neg = jnp.where(pad_own == 1, 0.0, -BIG).astype(F32)
    eye = place[:, None] == place[None, :]
    add_q = jnp.where(eye, 0.0, neg[None, :])
    add_k = jnp.where(eye, 0.0, neg[:, None])
    var_q = jnp.where(
        var_own[None, :] == jnp.arange(8, dtype=jnp.int32)[:, None], 1.0, 0.0
    ).astype(F32)
    return cos, sin, aug_q, aug_k, head_scale, add_q, add_k, var_q


def small_rows(gg_a, gg_f, bias, ti, heads_local):
    bias = bias.sum(axis=-1).reshape(4, 2 * heads_local)
    bias = jnp.take(bias, jnp.array([0, 2, 1, 3])[jnp.arange(4) ^ ti], axis=0).reshape(1, -1)
    bias = jnp.pad(bias, ((0, 0), (0, gg_a.shape[1] - bias.shape[1])))
    return jnp.concatenate([gg_a, gg_f, bias], axis=0)


def attend_part(scale, state, tab):
    q, k, v, k_oth, v_oth = state
    _, _, aug_q, aug_k, head_scale, add_q, _, _ = tab
    return attend_call(scale, q, k, k_oth, v, v_oth, aug_q, aug_k, head_scale, add_q)


def per_device(
    boundary, w_qkv, w_out, w_gate_up, w_down, norm_gains, variate_bias,
    segment_ids, variate_ids, time_ids, padding_mask,
):
    ti = lax.axis_index("tensor")
    tn = lax.axis_size("tensor")
    yi, core = ti // 2, ti % 2
    n = lax.axis_size("dp")
    is_first = lax.axis_index("section") == 0
    local = boundary[0]
    rows, model = local.shape[1:]
    scale = LOG2E / math.sqrt(HD)
    cols = w_qkv.shape[1]
    near = cols == ZB
    width = w_qkv.shape[3]
    hidden = w_gate_up.shape[3]
    heads_local = variate_bias.shape[1]
    zi = (lax.axis_index("dp") if near else 0) * jnp.ones((1,), jnp.int32)

    def row_of(array):
        return lax.dynamic_index_in_dim(array, yi, 0, keepdims=False)

    away = lax.dynamic_index_in_dim(local, 1 - yi, 0, keepdims=False).astype(BF)
    own = row_of(local).astype(BF)
    p_qkv = w_qkv[0].transpose(1, 2, 0).reshape(3 * width, cols)
    p_bias = jnp.pad(variate_bias[0].reshape(1, -1), ((0, 0), (0, cols - 2 * heads_local)))
    p_small = jnp.pad(jnp.concatenate([norm_gains[0], p_bias], axis=0), ((0, 13), (0, 0)))
    low = 3 * width
    out_low = low + 16
    p1 = jnp.concatenate([p_qkv, p_small, w_out[0]], axis=0)
    p2 = w_gate_up[0].transpose(1, 2, 0).reshape(2 * hidden, cols)
    p3 = w_down[0]

    if near:
        a1, came = ring(p1), y_swap(away)
        a1, came, p1, p2, p3 = meet(a1, came, p1, p2, p3)
        a2, y0 = ring(a1), y_swap(p1)
        a1, a2, y0, p2, p3 = meet(a1, a2, y0, p2, p3)
        a3, y1 = ring(a2), y_swap(a1)
        n1 = [jnp.stack([p1, y0])]
        f1 = [core_swap(n1[0])]
        a2, a3, y1, p2, p3 = meet(a2, a3, y1, p2, p3)
        b1, y2, d0 = ring(p2), y_swap(a2), y_swap(p3)
        n1.append(jnp.stack([a1, y1]))
        f1.append(core_swap(n1[1]))
        a3, b1, y2, d0, p2 = meet(a3, b1, y2, d0, p2)
        b2, y3 = ring(b1), y_swap(a3)
        n1.append(jnp.stack([a2, y2]))
        f1.append(core_swap(n1[2]))
        b1, b2, y3, p2, d0 = meet(b1, b2, y3, p2, d0)
        n1.append(jnp.stack([a3, y3]))
        f1.append(core_swap(n1[3]))
        w1 = n1 + f1
        b3, g0 = ring(b2), y_swap(p2)
    else:
        w1 = gather_any(p1)
        came = y_swap(away)
    ends = jnp.where(
        yi == 0, jnp.concatenate([own, came], axis=0), jnp.concatenate([came, own], axis=0)
    )
    gains = jnp.stack([w[0, low : low + 2] for w in w1[:4]])
    gains = jnp.take(gains, (zi[0] - jnp.arange(4)) % 4, axis=0)
    gains = gains.transpose(1, 0, 2).reshape(2, model).astype(F32)
    gain_a, gain_f = gains[:1], gains[1:]
    bias = [w[:, low + 2, : 2 * heads_local] for w in (w1[0], w1[4])]
    bias = jnp.concatenate(bias).reshape(4 * heads_local, 2).astype(F32)
    tab = tables(
        row_of(segment_ids), row_of(variate_ids), row_of(time_ids), row_of(padding_mask),
        bias, core,
    )
    cos, sin, aug_q, aug_k, head_scale, add_q, add_k, var_q = tab

    q, k, v = qkv_call(False, ends, gain_a, zi, w1, low, cos, sin)
    if near:
        b1, b2, b3, g0, d0, q, k, v = meet(b1, b2, b3, g0, d0, q, k, v)
        n3 = [jnp.stack([p3, d0])]
        c1, g1 = ring(n3[0]), y_swap(b1)
        n2 = [jnp.stack([p2, g0])]
        f2 = [core_swap(n2[0])]
        f3 = [core_swap(n3[0])]
    k_oth, v_oth = core_swap(k), core_swap(v)
    o, _ = attend_part(scale, (q, k, v, k_oth, v_oth), tab)
    if near:
        b2, b3, c1, g1, o = meet(b2, b3, c1, g1, o)
        c2, g2 = ring(c1), y_swap(b2)
        n2.append(jnp.stack([b1, g1]))
        f2.append(core_swap(n2[1]))
        f3.append(core_swap(c1))
        b3, c2, g2 = meet(b3, c2, g2)
        c3, g3 = ring(c2), y_swap(b3)
        n2.append(jnp.stack([b2, g2]))
        f2.append(core_swap(n2[2]))
        f3.append(core_swap(c2))
        n2.append(jnp.stack([b3, g3]))
        f2.append(core_swap(n2[3]))
        f3.append(core_swap(c3))
        w2, w3 = n2 + f2, n3 + [c1, c2, c3] + f3
    else:
        w2, w3 = gather_any(p2), gather_any(p3)
    h, z_near, z_far = ffn_up_call(False, out_low, width, ends, o, gain_f, zi, w1, w2)
    y_low = ffn_down_call(BF, h, z_near, z_far, zi, w3)
    got = lax.ppermute(y_low, "section", [(0, 1)])

    x = jnp.where(is_first, ends, got)
    n1, q, k, v, q0, k0 = qkv_call(True, x, gain_a, zi, w1, low, cos, sin)
    k_oth, v_oth = core_swap(k), core_swap(v)
    o, sums = attend_part(scale, (q, k, v, k_oth, v_oth), tab)
    h, z_near, z_far, n2, g, u = ffn_up_call(True, out_low, width, x, o, gain_f, zi, w1, w2)
    y = ffn_down_call(F32, h, z_near, z_far, zi, w3)

    def qkv_back(dq, dk, dk_got, dv, dv_got, dh):
        return qkv_back_call(
            dq, dk, dk_got, dv, dv_got, q0, k0, cos, sin, x, dh, gain_a, zi, w1, low
        )

    dh, _, do = ffn_back_call(out_low, width, ends, h, g, u, gain_f, zi, w1, w2, w3)[:3]
    dq, dk, dk_send, dv, dv_send, _ = attend_back_call(
        scale, None, q, k, k_oth, v, v_oth, do, o, sums, aug_q, aug_k, head_scale, add_k, var_q
    )
    dx_low = qkv_back(dq, dk, core_swap(dk_send), dv, core_swap(dv_send), dh)[3]
    got = lax.ppermute(dx_low, "section", [(1, 0)])
    z_oth, n2_oth, n1_oth = core_swap(z_far), core_swap(n2), core_swap(n1)
    o_oth = core_swap(o[:, 2 * width :])

    df = jnp.where(is_first, got, ends)
    down_keep, down_send = wgrad_call(zi, hidden, z_near, df, z_oth, core_swap(df))
    df, down_keep, down_send = meet(df, down_keep, down_send)
    down_got = y_swap(down_send)
    dh, da, do, dg_near, dg_far, du_near, du_far, gg_f = ffn_back_call(
        out_low, width, df, h, g, u, gain_f, zi, w1, w2, w3
    )
    gate_keep, gate_send = wgrad_call(zi, hidden, dg_near, n2, core_swap(dg_far), n2_oth)
    du_oth, da_oth = core_swap(du_far), core_swap(da)
    cut = width * 3 // 2
    if near:
        down_keep, down_got, gate_keep, gate_send, du_oth, da_oth, do = meet(
            down_keep, down_got, gate_keep, gate_send, du_oth, da_oth, do
        )
        gate_got = y_swap(gate_send)
        down = [plus(down_keep[r], down_got[r]) for r in range(4)]
        down_run = ring(down[1])
    up_keep, up_send = wgrad_call(zi, hidden, du_near, n2, du_oth, n2_oth)
    out_keep, out_send = wgrad_call(zi, width, o, da, o_oth, da_oth)

    def attend_back(do, low, high):
        return attend_back_call(
            scale, (low, high), q, k, k_oth, v, v_oth, do, o, sums, aug_q, aug_k, head_scale,
            add_k, var_q,
        )

    pairs = do.shape[1] // 128
    if near:
        up = [jnp.stack([up_keep[r], up_send[r]]) for r in range(4)]
        down_run, do, *up = meet(down_run, do, *up, out_send)[:6]
        down_run = ring(plus(down_run, down[2]))
        up_run = ring(up[1])
        first = attend_back(do, 0, pairs // 2)
        down_run, up_run, gate_got, do, out_send, *first = meet(
            down_run, up_run, gate_got, do, out_send, *first
        )
        out_got = y_swap(out_send)
        down_run = ring(plus(down_run, down[3]))
        up_run = ring(plus(up_run, up[2]))
        gate = [plus(gate_keep[r], gate_got[r]) for r in range(4)]
    else:
        first = attend_back(do, 0, pairs // 2)
    second = attend_back(do, pairs // 2, pairs)
    if near:
        down_run, up_run, out_got, first, second, *gate = meet(
            down_run, up_run, out_got, first, second, *gate
        )
        gate_run = ring(gate[1])
        up_run = ring(plus(up_run, up[3]))
        g_down = down_run.astype(F32) + down[0].astype(F32)
        out = [plus(out_keep[r], out_got[r]) for r in range(4)]
    dq, dk, dk_send, dv, dv_send, bias = (
        jnp.concatenate([b, a] if i in (2, 4) else [a, b], axis=0 if i == 5 else 1)
        for i, (a, b) in enumerate(zip(first, second))
    )
    dp_near, dp_far, dx, dx_low, gg_a = qkv_back(
        dq, dk, core_swap(dk_send), dv, core_swap(dv_send), dh
    )
    out_low_rows = jnp.where(is_first, dx_low, y.astype(BF))
    send = jnp.where(yi == 0, out_low_rows[rows:], out_low_rows[:rows])
    if near:
        gate_run, up_run, send, dp_near, dp_far, *out = meet(
            gate_run, up_run, send, dp_near, dp_far, *out
        )
        rows_got = y_swap(send)
        gate_run = ring(plus(gate_run, gate[2]))
        out_run = ring(out[1])
        up_run = plus(up_run, up[0])
    qkv_keep, qkv_send = wgrad_call(zi, 3 * width, dp_near, n1, core_swap(dp_far), n1_oth)
    small = small_rows(gg_a, gg_f, bias, ti, heads_local)
    if near:
        rows_got, gate_run, out_run, up_run, qkv_keep, qkv_send, small = meet(
            rows_got, gate_run, out_run, up_run, qkv_keep, qkv_send, small
        )
        head_got = y_swap(qkv_send[:, :cut])
        up_got = y_swap(up_run[1])
        tails = [jnp.stack([qkv_keep[r, cut:], qkv_send[r, cut:]]) for r in range(4)]
        tail_run = ring(tails[1])
        gate_run = ring(plus(gate_run, gate[3]))
        out_run = ring(plus(out_run, out[2]))
        g_gu_up = up_run[0].astype(F32)
        tail_run, gate_run, out_run, head_got = meet(tail_run, gate_run, out_run, head_got)
        tail_run = ring(plus(tail_run, tails[2]))
        out_run = ring(plus(out_run, out[3]))
        heads_sum = [plus(qkv_keep[r, :cut], head_got[r]) for r in range(4)]
        head_run = ring(heads_sum[1])
        tail_run, head_run, out_run = meet(tail_run, head_run, out_run)
        tail_run = ring(plus(tail_run, tails[3]))
        head_run = ring(plus(head_run, heads_sum[2]))
        tail_run, head_run, small = meet(tail_run, head_run, small)
        tail_run = plus(tail_run, tails[0])
        tail_got = y_swap(tail_run[1])
        head_run = ring(plus(head_run, heads_sum[3]))
        small = small_sum(small)
        g_qkv = jnp.concatenate(
            [
                head_run.astype(F32) + heads_sum[0].astype(F32),
                tail_run[0].astype(F32) + tail_got.astype(F32),
            ],
            axis=0,
        )
        g_out = out_run.astype(F32) + out[0].astype(F32)
        g_gu = jnp.stack(
            [gate_run.astype(F32) + gate[0].astype(F32), g_gu_up + up_got.astype(F32)]
        )
    else:
        rows_got = y_swap(send)
        g_down = scatter_any(down_keep, down_send)
        g_gu = jnp.stack([scatter_any(gate_keep, gate_send), scatter_any(up_keep, up_send)])
        g_out = scatter_any(out_keep, out_send)
        g_qkv = scatter_any(qkv_keep, qkv_send)
        small = small_sum(small)

    out_rows = jnp.where(is_first, dx, y)
    keep = jnp.where(yi == 0, out_rows[:rows], out_rows[rows:])
    back = rows_got.astype(F32)
    boundary_out = jnp.where(yi == 0, jnp.stack([keep, back]), jnp.stack([back, keep]))[None]
    piece = model // (n * tn)
    gain_piece = lax.dynamic_slice_in_dim(
        small[:2], (lax.axis_index("dp") * tn + ti) * piece, piece, 1
    )
    bias_piece = lax.dynamic_slice_in_dim(
        small[2, : 8 * heads_local].reshape(-1, 2), ti * heads_local, heads_local, 0
    )
    return (
        boundary_out,
        g_qkv.reshape(3, width, cols).transpose(2, 0, 1)[None],
        g_out[None],
        g_gu.transpose(2, 0, 1)[None],
        g_down[None],
        gain_piece[None],
        bias_piece[None],
    )


def solution(mesh):
    placed = (
        P("section", "dp", "tensor", None),
        P("section", "dp", None, "tensor"),
        P("section", "tensor", "dp"),
        P("section", "dp", None, "tensor"),
        P("section", "tensor", "dp"),
        P("section", None, "dp"),
        P("section", "tensor", None),
        P("dp", None),
        P("dp", None),
        P("dp", None),
        P("dp", None),
    )
    return jax.shard_map(
        per_device,
        mesh=mesh,
        in_specs=placed,
        out_specs=(
            P("section", "dp", "tensor", None),
            P("section", "dp", None, "tensor"),
            P("section", "tensor", "dp"),
            P("section", "dp", None, "tensor"),
            P("section", "tensor", "dp"),
            P("section", None, ("dp", "tensor")),
            P("section", "tensor", None),
        ),
        check_vma=False,
    )
```

```python
import functools
import math

import jax
import jax.numpy as jnp
from jax import lax
from jax.experimental import pallas as pl
from jax.experimental.pallas import tpu as pltpu
from jax.sharding import PartitionSpec as P

EPS = 1e-05
BIG = 8192.0
LOG2E = 1.4426950408889634
BF = jnp.bfloat16
F32 = jnp.float32
HD = 64
ZB = 256
VMEM_MB = 56
N_VAR = 4
L_SEG = 8
L_PAD = 24
L_LSE = 25


def dot(a, b):
    return lax.dot_general(a, b, (((1,), (0,)), ((), ())), preferred_element_type=F32)


def dot_nt(a, b):
    return lax.dot_general(a, b, (((1,), (1,)), ((), ())), preferred_element_type=F32)


def dot_tn(a, b):
    return lax.dot_general(a, b, (((0,), (0,)), ((), ())), preferred_element_type=F32)


def params(mb=VMEM_MB):
    return pltpu.CompilerParams(
        dimension_semantics=("arbitrary",), vmem_limit_bytes=mb * 1024 * 1024
    )


def cost(flops, nbytes, trans=0):
    return pl.CostEstimate(flops=int(flops), bytes_accessed=int(nbytes), transcendentals=0)


def sds(shape, dtype):
    return jax.ShapeDtypeStruct(shape, dtype)


def whole(shape):
    zeros = (0,) * len(shape)
    return pl.BlockSpec(shape, lambda *_: zeros)


def head_sum(u):
    row = lax.broadcasted_iota(jnp.int32, (u.shape[1], u.shape[1]), 0) // HD
    col = lax.broadcasted_iota(jnp.int32, (u.shape[1], u.shape[1]), 1) // HD
    return dot(u.astype(BF), jnp.where(row == col, 1.0, 0.0).astype(BF))


def half_swap(u):
    lane = lax.broadcasted_iota(jnp.int32, u.shape, 1) % HD
    return jnp.where(lane < HD // 2, pltpu.roll(u, 128 - HD // 2, 1), pltpu.roll(u, HD // 2, 1))


def row_rms(x):
    return lax.rsqrt(jnp.mean(x * x, axis=-1, keepdims=True) + EPS)


def hbm():
    return pl.BlockSpec(memory_space=pl.ANY)


def smem():
    return pl.BlockSpec(memory_space=pltpu.SMEM)


def copies(refs, low, scratch, sems, t):
    rows = pl.ds(low, scratch.shape[2])
    return [
        pltpu.make_async_copy(
            refs[4 * (t // 2) + r].at[t % 2, rows], scratch.at[r, t], sems.at[r, t]
        )
        for r in range(4)
    ]


def start_all(refs, low, scratch, sems):
    for t in range(4):
        for copy in copies(refs, low, scratch, sems, t):
            copy.start()


def wait_for(refs, low, scratch, sems, t):
    for fixed in range(4):

        @pl.when(t == fixed)
        def _():
            for copy in copies(refs, low, scratch, sems, fixed):
                copy.wait()


def weight_scratch(feats):
    return [pltpu.VMEM((4, 4, feats, ZB), BF), pltpu.SemaphoreType.DMA((4, 4))]


def place(zi_ref, r):
    return lax.rem(zi_ref[0] - r + 4, 4)


def block_store(ref, value):
    for z in range(4):
        ref[z] = value[:, z * ZB : (z + 1) * ZB]


def chunks(wide, step=ZB):
    return [slice(low, min(low + step, wide)) for low in range(0, wide, step)]


def block_load(ref):
    return jnp.concatenate([ref[z] for z in range(4)], axis=1)


def qkv_kernel(save, x_ref, gain_ref, zi_ref, cos_ref, sin_ref, *refs):
    weight, refs = refs[:8], refs[8:]
    if save:
        n_ref, q_ref, k_ref, v_ref, q0_ref, k0_ref, n_scr, w_ref, sems = refs
    else:
        q_ref, k_ref, v_ref, n_scr, w_ref, sems = refs
    t = pl.program_id(0)

    @pl.when(t == 0)
    def _():
        start_all(weight, 0, w_ref, sems)
        x = x_ref[...].astype(F32)
        n = (x * row_rms(x) * gain_ref[...]).astype(BF)
        block_store(n_scr, n)
        if save:
            n_ref[...] = n

    wait_for(weight, 0, w_ref, sems, t)
    width = q_ref.shape[1]

    def project(which):
        cols = slice(which * width, (which + 1) * width)
        total = dot_nt(n_scr[place(zi_ref, 0)], w_ref[0, t, cols])
        for r in range(1, 4):
            total = total + dot_nt(n_scr[place(zi_ref, r)], w_ref[r, t, cols])
        return total

    cos, sin = cos_ref[...], sin_ref[...]
    for which, out in ((0, q_ref), (1, k_ref)):
        u = project(which)
        if save:
            kept = q0_ref if which == 0 else k0_ref
            kept[...] = u.astype(BF)
        un = u * lax.rsqrt(head_sum(u * u) * (1.0 / HD) + EPS)
        for pair in range(width // 128):
            at = slice(pair * 128, (pair + 1) * 128)
            out[:, at] = (un[:, at] * cos + half_swap(un[:, at]) * sin).astype(BF)
    v_ref[...] = project(2).astype(BF)


def qkv_call(save, x, gain, zi, w, feats, cos, sin):
    rows, model = x.shape
    width = feats // 3
    total = 4 * width
    col = pl.BlockSpec((rows, width), lambda t: (0, t))
    outs = [sds((rows, total), BF)] * 3
    specs = [col] * 3
    if save:
        outs = [sds((rows, model), BF)] + outs + [sds((rows, total), BF)] * 2
        specs = [whole((rows, model))] + specs + [col] * 2
    return pl.pallas_call(
        functools.partial(qkv_kernel, save),
        grid=(4,),
        in_specs=[whole((rows, model)), whole((1, model)), smem()]
        + [whole((rows, 128))] * 2
        + [hbm()] * 8,
        out_specs=specs,
        out_shape=outs,
        scratch_shapes=[pltpu.VMEM((4, rows, ZB), BF)] + weight_scratch(feats),
        compiler_params=params(),
        cost_estimate=cost(2 * rows * model * 3 * total, 6 * total * model + 16 * x.size),
    )(x, gain, zi, cos, sin, *w)


def other_core_spec(rows, pairs):
    half = pairs // 2
    return pl.BlockSpec((rows, 128), lambda p: (0, lax.rem(p + half, pairs)))


def pick(first, h, a, b):
    return jnp.where(first, a, b) if h == 0 else jnp.where(first, b, a)


def pick_low(first, h, a, b):
    mine = jnp.where(first, 1.0, 0.0) if h == 0 else jnp.where(first, 0.0, 1.0)
    low = mine.astype(BF)
    return a * low + b * (1.0 - mine).astype(BF)


def attend_kernel(
    scale, q_ref, ko_ref, kx_ref, vo_ref, vx_ref, aq_ref, ak_ref, hs_ref, add_ref, o_ref, l_ref
):
    rows = q_ref.shape[0]
    kb = 128
    first = lax.broadcasted_iota(jnp.int32, (1, 128), 1) < HD
    q = q_ref[...].astype(F32)
    base = aq_ref[...]
    raws = []
    for h in range(2):
        qh = pick(first, h, q, base * hs_ref[0, h : h + 1, :]).astype(BF)
        total = None
        for half, (k_ref, v_ref) in enumerate(((ko_ref, vo_ref), (kx_ref, vx_ref))):
            for block in range(rows // kb):
                at = slice(block * kb, (block + 1) * kb)
                kk = slice(half * rows + block * kb, half * rows + (block + 1) * kb)
                kh = pick_low(first, h, k_ref[at, :], ak_ref[kk, :])
                vh = pick_low(first, h, v_ref[at, :], BF(1.0))
                s = dot_nt(qh, kh)
                if half == 0:
                    s = s + add_ref[:, at]
                part = dot(jnp.exp2(s * scale).astype(BF), vh)
                total = part if total is None else total + part
        raws.append(total)
    sums = jnp.where(first, raws[1], raws[0])
    l_ref[...] = sums
    o_ref[...] = (jnp.where(first, raws[0], raws[1]) / pltpu.roll(sums, HD, 1)).astype(BF)


def attend_call(scale, q, k_own, k_oth, v_own, v_oth, aug_q, aug_k, head_scale, add_own):
    rows, total = q.shape
    pairs = total // 128
    col = pl.BlockSpec((rows, 128), lambda p: (0, p))
    far = other_core_spec(rows, pairs)
    return pl.pallas_call(
        functools.partial(attend_kernel, scale),
        grid=(pairs,),
        in_specs=[
            col,
            col,
            far,
            col,
            far,
            whole(aug_q.shape),
            whole(aug_k.shape),
            pl.BlockSpec((1, 2, 128), lambda p: (p, 0, 0)),
            whole(add_own.shape),
        ],
        out_specs=[col, col],
        out_shape=[sds((rows, total), BF), sds((rows, total), F32)],
        compiler_params=params(),
        cost_estimate=cost(
            4 * 2 * rows * rows * 2 * total, 20 * rows * total, rows * rows * 2 * pairs * 2
        ),
    )(q, k_own, k_oth, v_own, v_oth, aug_q, aug_k, head_scale, add_own)


def padded(hidden):
    return -(-2 * hidden // 128) * 128


def pair_scratch(parts, hidden):
    return [
        pltpu.VMEM((4, 2, parts * padded(hidden), ZB), BF),
        pltpu.SemaphoreType.DMA((4, 2, 2, parts)),
    ]


def pair_copies(refs, parts, scratch, sems, half):
    wide = scratch.shape[2] // parts
    hidden = refs[0].shape[1] // parts
    return [
        pltpu.make_async_copy(
            refs[4 * half + r].at[y, pl.ds(part * hidden, hidden)],
            scratch.at[r, half, pl.ds(part * wide + y * hidden, hidden)],
            sems.at[r, half, y, part],
        )
        for r in range(4)
        for y in range(2)
        for part in range(parts)
    ]


def pair_start(refs, parts, scratch, sems):
    wide = scratch.shape[2] // parts
    hidden = refs[0].shape[1] // parts
    for half in range(2):
        for copy in pair_copies(refs, parts, scratch, sems, half):
            copy.start()
    blank = wide - 2 * hidden
    if blank:
        for half in range(2):
            for r in range(4):
                for part in range(parts):
                    low = part * wide + 2 * hidden
                    scratch[r, half, low : low + blank] = jnp.zeros((blank, ZB), BF)


def pair_wait(refs, parts, scratch, sems, half):
    for fixed in range(2):

        @pl.when(half == fixed)
        def _():
            for copy in pair_copies(refs, parts, scratch, sems, fixed):
                copy.wait()


def near_far(rows, feats):
    return (
        pl.BlockSpec((1, rows, feats), lambda t: (jnp.minimum(t, 1), 0, 0)),
        pl.BlockSpec((1, rows, feats), lambda t: (jnp.maximum(t - 2, 0), 0, 0)),
    )


def put(is_near, near_ref, far_ref, value, at=...):
    @pl.when(is_near)
    def _():
        near_ref[at] = value

    @pl.when(jnp.logical_not(is_near))
    def _():
        far_ref[at] = value


def ffn_up_kernel(save, out_low, x_ref, o_ref, gain_ref, zi_ref, *refs):
    wo, wgu, refs = refs[:8], refs[8:16], refs[16:]
    if save:
        h_ref, zn_ref, zf_ref, n_ref, g_ref, u_ref = refs[:6]
    else:
        h_ref, zn_ref, zf_ref = refs[:3]
    n_scr, wo_ref, wo_sems, wgu_ref, wgu_sems, acc, z_scr = refs[-7:]
    wide = wgu_ref.shape[2] // 2
    half = pl.program_id(0)

    @pl.when(half == 0)
    def _():
        start_all(wo, out_low, wo_ref, wo_sems)
        pair_start(wgu, 2, wgu_ref, wgu_sems)
        width = wo_ref.shape[2]
        block_store(acc, x_ref[...].astype(F32))
        for s in range(4):
            for copy in copies(wo, out_low, wo_ref, wo_sems, s):
                copy.wait()
        for r in range(4):
            z = place(zi_ref, r)
            h = acc[z]
            for s in range(4):
                h = h + dot(o_ref[:, s * width : (s + 1) * width], wo_ref[r, s])
            acc[z] = h
        h = block_load(acc)
        n = (h * row_rms(h) * gain_ref[...]).astype(BF)
        block_store(n_scr, n)
        h_ref[...] = h
        if save:
            n_ref[...] = n

    pair_wait(wgu, 2, wgu_ref, wgu_sems, half)
    for at in chunks(wide):
        total = []
        for part in range(2):
            cols = slice(part * wide + at.start, part * wide + at.stop)
            one = dot_nt(n_scr[place(zi_ref, 0)], wgu_ref[0, half, cols])
            for r in range(1, 4):
                one = one + dot_nt(n_scr[place(zi_ref, r)], wgu_ref[r, half, cols])
            total.append(one)
        gate, up = total
        z_scr[:, at] = (gate / (1.0 + jnp.exp(-gate)) * up).astype(BF)
        if save:
            g_ref[0, :, at] = gate.astype(BF)
            u_ref[0, :, at] = up.astype(BF)
    put(half == 0, zn_ref, zf_ref, z_scr[...])


def ffn_up_call(save, out_low, width, x, o, gain, zi, wo, wgu):
    rows, model = x.shape
    hidden = wgu[0].shape[1] // 2
    wide = padded(hidden)
    big = whole((rows, model))
    part = pl.BlockSpec((1, rows, wide), lambda t: (t, 0, 0))
    outs = [sds((rows, model), F32)] + [sds((rows, wide), BF)] * 2
    specs = [big, whole((rows, wide)), whole((rows, wide))]
    if save:
        outs += [sds((rows, model), BF)] + [sds((2, rows, wide), BF)] * 2
        specs += [big, part, part]
    return pl.pallas_call(
        functools.partial(ffn_up_kernel, save, out_low),
        grid=(2,),
        in_specs=[big, whole(o.shape), whole((1, model)), smem()] + [hbm()] * 16,
        out_specs=specs,
        out_shape=outs,
        scratch_shapes=[pltpu.VMEM((4, rows, ZB), BF)]
        + weight_scratch(width)
        + pair_scratch(2, hidden)
        + [pltpu.VMEM((4, rows, ZB), F32), pltpu.VMEM((rows, wide), BF)],
        compiler_params=params(),
        cost_estimate=cost(
            2 * rows * model * (8 * hidden + model), 16 * hidden * model + 20 * x.size
        ),
    )(x, o, gain, zi, *wo, *wgu)


def ffn_down_kernel(h_ref, zn_ref, zf_ref, zi_ref, *refs):
    weight, (y_ref, w_ref, sems) = refs[:8], refs[8:]
    pair_start(weight, 1, w_ref, sems)
    for half, z_ref in enumerate((zn_ref, zf_ref)):
        for copy in pair_copies(weight, 1, w_ref, sems, half):
            copy.wait()
    for z in range(4):
        r = lax.rem(zi_ref[0] - z + 4, 4)
        at = slice(z * ZB, (z + 1) * ZB)
        y = h_ref[:, at] + dot(zn_ref[...], w_ref[r, 0]) + dot(zf_ref[...], w_ref[r, 1])
        y_ref[:, at] = y.astype(y_ref.dtype)


def ffn_down_call(dtype, h, z_near, z_far, zi, wd):
    rows, model = h.shape
    hidden = wd[0].shape[1]
    vmem = pl.BlockSpec(memory_space=pltpu.VMEM)
    return pl.pallas_call(
        ffn_down_kernel,
        in_specs=[vmem] * 3 + [smem()] + [hbm()] * 8,
        out_specs=vmem,
        out_shape=sds((rows, model), dtype),
        scratch_shapes=pair_scratch(1, hidden),
        compiler_params=pltpu.CompilerParams(vmem_limit_bytes=18 * 1024 * 1024),
        cost_estimate=cost(2 * rows * model * 4 * hidden, 8 * hidden * model + 8 * h.size),
    )(h, z_near, z_far, zi, *wd)


def ffn_back_kernel(out_low, dy_ref, h_ref, g_ref, u_ref, gain_ref, zi_ref, *refs):
    wo, wgu, wd, refs = refs[:8], refs[8:16], refs[16:24], refs[24:]
    dh_ref, da_ref, do_ref, dgn_ref, dgf_ref, dun_ref, duf_ref, gg_ref = refs[:8]
    df_scr, acc, wo_ref, wo_sems, wgu_ref, wgu_sems, wd_ref, wd_sems, dg_scr, du_scr = refs[8:]
    wide = wd_ref.shape[2]
    half = pl.program_id(0)

    @pl.when(half == 0)
    def _():
        pair_start(wd, 1, wd_ref, wd_sems)
        pair_start(wgu, 2, wgu_ref, wgu_sems)
        start_all(wo, out_low, wo_ref, wo_sems)
        block_store(df_scr, dy_ref[...])
        acc[...] = jnp.zeros_like(acc)

    pair_wait(wd, 1, wd_ref, wd_sems, half)
    for at in chunks(wide):
        dz = dot_nt(df_scr[place(zi_ref, 0)], wd_ref[0, half, at])
        for r in range(1, 4):
            dz = dz + dot_nt(df_scr[place(zi_ref, r)], wd_ref[r, half, at])
        gate = g_ref[0, :, at].astype(F32)
        up = u_ref[0, :, at].astype(F32)
        s = 1.0 / (1.0 + jnp.exp(-gate))
        dg_scr[:, at] = (dz * up * s * (1.0 + gate * (1.0 - s))).astype(BF)
        du_scr[:, at] = (dz * gate * s).astype(BF)
    dgate, dup = dg_scr[...], du_scr[...]
    put(half == 0, dgn_ref, dgf_ref, dgate)
    put(half == 0, dun_ref, duf_ref, dup)
    pair_wait(wgu, 2, wgu_ref, wgu_sems, half)
    for r in range(4):
        z = place(zi_ref, r)
        acc[z] = acc[z] + (
            dot(dgate, wgu_ref[r, half, :wide]) + dot(dup, wgu_ref[r, half, wide:])
        )

    @pl.when(half == 1)
    def _():
        h = h_ref[...]
        r = row_rms(h)
        hn = h * r
        dn = block_load(acc)
        gg_ref[...] = jnp.sum(dn * hn, axis=0, keepdims=True)
        dhat = dn * gain_ref[...]
        dh = dy_ref[...].astype(F32) + r * (
            dhat - hn * jnp.mean(dhat * hn, axis=-1, keepdims=True)
        )
        dh_ref[...] = dh
        da = dh.astype(BF)
        da_ref[...] = da
        block_store(df_scr, da)
        width = wo_ref.shape[2]
        for s in range(4):
            for copy in copies(wo, out_low, wo_ref, wo_sems, s):
                copy.wait()
        for s in range(4):
            part = dot_nt(df_scr[place(zi_ref, 0)], wo_ref[0, s])
            for q in range(1, 4):
                part = part + dot_nt(df_scr[place(zi_ref, q)], wo_ref[q, s])
            do_ref[:, s * width : (s + 1) * width] = part.astype(BF)


def ffn_back_call(out_low, width, dy, h, g, u, gain, zi, wo, wgu, wd):
    rows, model = dy.shape
    hidden = wd[0].shape[1]
    wide = g.shape[2]
    big = whole((rows, model))
    part = pl.BlockSpec((1, rows, wide), lambda t: (t, 0, 0))
    return pl.pallas_call(
        functools.partial(ffn_back_kernel, out_low),
        grid=(2,),
        in_specs=[big, big, part, part, whole((1, model)), smem()] + [hbm()] * 24,
        out_specs=[big, big, big] + [whole((rows, wide))] * 4 + [whole((1, model))],
        out_shape=[sds((rows, model), F32), sds((rows, model), BF), sds((rows, model), BF)]
        + [sds((rows, wide), BF)] * 4
        + [sds((1, model), F32)],
        scratch_shapes=[pltpu.VMEM((4, rows, ZB), BF), pltpu.VMEM((4, rows, ZB), F32)]
        + weight_scratch(width)
        + pair_scratch(2, hidden)
        + pair_scratch(1, hidden)
        + [pltpu.VMEM((rows, wide), BF)] * 2,
        compiler_params=params(57),
        cost_estimate=cost(
            2 * rows * model * (12 * hidden + model), 24 * hidden * model + 20 * dy.size
        ),
    )(dy, h, g, u, gain, zi, *wo, *wgu, *wd)


def split3(value):
    hi = value.astype(BF).astype(F32)
    mid = (value - hi).astype(BF).astype(F32)
    return hi, mid, value - hi - mid


def attend_back_kernel(
    scale, q_ref, ko_ref, kx_ref, vo_ref, vx_ref, do_ref, o_ref, l_ref, aq_ref, ak_ref, hs_ref,
    add_ref, var_ref, dq_ref, dko_ref, dkx_ref, dvo_ref, dvx_ref, bias_ref,
):
    rows = q_ref.shape[0]
    kb = 256
    first = lax.broadcasted_iota(jnp.int32, (1, 128), 1) < HD
    lane = lax.broadcasted_iota(jnp.int32, (1, 128), 1) % HD
    q = q_ref[...].astype(F32)
    do = do_ref[...].astype(F32)
    inner = do * o_ref[...].astype(F32)
    base = aq_ref[...]
    hi, mid, low = split3(jnp.log2(l_ref[...]) * (-1.0 / scale))
    lse = jnp.where(lane == L_LSE, hi, 0.0)
    lse = jnp.where(lane == L_LSE + 1, mid, lse)
    lse = jnp.where(lane == L_LSE + 2, low, lse)
    dq_t = []
    dk = [[], []]
    dv = [[], []]
    for h in range(2):
        qh = pick(first, h, q, base * hs_ref[0, h : h + 1, :] + lse).astype(BF)
        d = jnp.sum(pick(first, h, inner, 0.0), axis=-1, keepdims=True)
        dhi, dmid, dlow = split3(-d)
        d_aug = jnp.where(lane == 0, dhi, 0.0)
        d_aug = jnp.where(lane == 1, dmid, d_aug)
        d_aug = jnp.where(lane == 2, dlow, d_aug)
        doh = pick(first, h, do, d_aug).astype(BF)
        total = None
        for half, (k_ref, v_ref) in enumerate(((ko_ref, vo_ref), (kx_ref, vx_ref))):
            for block in range(rows // kb):
                at = slice(block * kb, (block + 1) * kb)
                kk = slice(half * rows + block * kb, half * rows + (block + 1) * kb)
                kh = pick_low(first, h, k_ref[at, :], ak_ref[kk, :])
                vh = pick_low(first, h, v_ref[at, :], BF(1.0))
                s = dot_nt(kh, qh)
                if half == 0:
                    s = s + add_ref[at, :]
                p = jnp.exp2(s * scale)
                ds = (p * dot_nt(vh, doh)).astype(BF)
                dv[h].append(dot(p.astype(BF), doh))
                dk[h].append(dot(ds, qh))
                part = dot_tn(kh, ds)
                total = part if total is None else total + part
        dq_t.append(total)
    scale_back = 1.0 / math.sqrt(HD)
    count = rows // kb
    for half, (dk_ref, dv_ref) in enumerate(((dko_ref, dvo_ref), (dkx_ref, dvx_ref))):
        for block in range(count):
            at = slice(block * kb, (block + 1) * kb)
            i = half * count + block
            dk_ref[at, :] = (jnp.where(first, dk[0][i], dk[1][i]) * scale_back).astype(dk_ref.dtype)
            dv_ref[at, :] = jnp.where(first, dv[0][i], dv[1][i]).astype(dv_ref.dtype)
    joined = jnp.concatenate([dq_t[0][:HD], dq_t[1][HD:]], axis=0)
    dq_ref[...] = (joined.T * scale_back).astype(BF)
    mine = var_ref[...]
    for h in range(2):
        begin = HD if h == 0 else 0
        r = dq_t[h][begin : begin + 8]
        same = jnp.sum(r * mine, axis=0, keepdims=True)
        every = jnp.sum(r[:N_VAR], axis=0, keepdims=True)
        bias_ref[0, 2 * h : 2 * h + 1, :] = same
        bias_ref[0, 2 * h + 1 : 2 * h + 2, :] = every - same


def attend_back_call(
    scale, span, q, k_own, k_oth, v_own, v_oth, do, o, sums, aug_q, aug_k, head_scale, add_own, var_q
):
    rows, total = q.shape
    every = total // 128
    low, high = span or (0, every)
    pairs = high - low
    total = pairs * 128
    col = pl.BlockSpec((rows, 128), lambda p: (0, p + low))
    far = pl.BlockSpec((rows, 128), lambda p: (0, lax.rem(p + low + every // 2, every)))
    out = pl.BlockSpec((rows, 128), lambda p: (0, p))
    out_far = other_core_spec(rows, pairs) if span is None else out
    return pl.pallas_call(
        functools.partial(attend_back_kernel, scale),
        grid=(pairs,),
        in_specs=[col, col, far, col, far, col, col, col]
        + [
            whole(aug_q.shape),
            whole(aug_k.shape),
            pl.BlockSpec((1, 2, 128), lambda p: (p + low, 0, 0)),
            whole(add_own.shape),
            whole(var_q.shape),
        ],
        out_specs=[out, out, out_far, out, out_far] + [pl.BlockSpec((1, 4, rows), lambda p: (p, 0, 0))],
        out_shape=[
            sds((rows, total), BF),
            sds((rows, total), BF),
            sds((rows, total), BF),
            sds((rows, total), BF),
            sds((rows, total), BF),
            sds((pairs, 4, rows), F32),
        ],
        compiler_params=params(),
        cost_estimate=cost(
            10 * 2 * rows * rows * 2 * total, 40 * rows * total, rows * rows * 2 * pairs * 2
        ),
    )(q, k_own, k_oth, v_own, v_oth, do, o, sums, aug_q, aug_k, head_scale, add_own, var_q)


def qkv_back_kernel(
    dq_ref, dk_ref, dkr_ref, dv_ref, dvr_ref, q0_ref, k0_ref, cos_ref, sin_ref, x_ref, dh_ref,
    gain_ref, zi_ref, *refs,
):
    weight, refs = refs[:8], refs[8:]
    dpn_ref, dpf_ref, dx_ref, dxl_ref, gg_ref, dp_scr, acc, w_ref, sems = refs
    width = dq_ref.shape[1]
    t = pl.program_id(0)

    @pl.when(t == 0)
    def _():
        start_all(weight, 0, w_ref, sems)
        acc[...] = jnp.zeros_like(acc)

    cos, sin = cos_ref[...], sin_ref[...]
    for which in range(2):
        u = (q0_ref if which == 0 else k0_ref)[...].astype(F32)
        r = lax.rsqrt(head_sum(u * u) * (1.0 / HD) + EPS)
        un = u * r
        turned = []
        for pair in range(width // 128):
            at = slice(pair * 128, (pair + 1) * 128)
            if which == 0:
                grad = dq_ref[:, at].astype(F32)
            else:
                grad = dk_ref[:, at].astype(F32) + dkr_ref[:, at].astype(F32)
            turned.append(grad * cos - half_swap(grad) * sin)
        grad = jnp.concatenate(turned, axis=1)
        out = r * (grad - un * (head_sum(grad * un) * (1.0 / HD)))
        dp_scr[:, which * width : (which + 1) * width] = out.astype(BF)
    dp_scr[:, 2 * width :] = (dv_ref[...].astype(F32) + dvr_ref[...].astype(F32)).astype(BF)
    wait_for(weight, 0, w_ref, sems, t)
    dp = dp_scr[...]
    put(t < 2, dpn_ref, dpf_ref, dp, 0)
    for r in range(4):
        z = place(zi_ref, r)
        acc[z] = acc[z] + dot(dp, w_ref[r, t])

    @pl.when(t == 3)
    def _():
        x = x_ref[...].astype(F32)
        r = row_rms(x)
        xn = x * r
        dn = block_load(acc)
        gg_ref[...] = jnp.sum(dn * xn, axis=0, keepdims=True)
        dhat = dn * gain_ref[...]
        dx = dh_ref[...] + r * (dhat - xn * jnp.mean(dhat * xn, axis=-1, keepdims=True))
        dx_ref[...] = dx
        dxl_ref[...] = dx.astype(BF)


def qkv_back_call(dq, dk, dkr, dv, dvr, q0, k0, cos, sin, x, dh, gain, zi, w, feats):
    rows, model = x.shape
    width = feats // 3
    big = whole((rows, model))
    col = pl.BlockSpec((rows, width), lambda t: (0, t))
    return pl.pallas_call(
        qkv_back_kernel,
        grid=(4,),
        in_specs=[col] * 7
        + [whole((rows, 128)), whole((rows, 128)), big, big, whole((1, model)), smem()]
        + [hbm()] * 8,
        out_specs=[*near_far(rows, feats), big, big, whole((1, model))],
        out_shape=[sds((2, rows, feats), BF)] * 2
        + [sds((rows, model), F32), sds((rows, model), BF), sds((1, model), F32)],
        scratch_shapes=[pltpu.VMEM((rows, feats), BF), pltpu.VMEM((4, rows, ZB), F32)]
        + weight_scratch(feats),
        compiler_params=params(),
        cost_estimate=cost(8 * rows * model * feats, 8 * feats * model + 40 * x.size),
    )(dq, dk, dkr, dv, dvr, q0, k0, cos, sin, x, dh, gain, zi, *w)


def wgrad_kernel(feats, zi_ref, ao_ref, bo_ref, ax_ref, bx_ref, keep_ref, send_ref):
    if len(ao_ref.shape) == 3:
        for i, out in ((1, send_ref), (0, keep_ref)):
            g = dot_tn(ao_ref[i], bo_ref[...]) + dot_tn(ax_ref[i], bx_ref[...])
            for z in range(4):
                out[lax.rem(zi_ref[0] - z + 4, 4)] = g[:, z * ZB : (z + 1) * ZB].astype(BF)
    else:
        g = dot_tn(ao_ref[...], bo_ref[...]) + dot_tn(ax_ref[...], bx_ref[...])
        for z in range(4):
            r = lax.rem(zi_ref[0] - z + 4, 4)
            at = slice(z * ZB, (z + 1) * ZB)
            keep_ref[r] = g[:feats, at].astype(BF)
            send_ref[r] = g[feats : 2 * feats, at].astype(BF)


def wgrad_call(zi, feats, a_own, b_own, a_oth, b_oth):
    rows, model = b_own.shape
    part = whole(a_oth.shape)
    big = whole((rows, model))
    out = whole((4, feats, ZB))
    return pl.pallas_call(
        functools.partial(wgrad_kernel, feats),
        grid=(1,),
        in_specs=[smem(), part, big, part, big],
        out_specs=[out, out],
        out_shape=[sds((4, feats, ZB), BF)] * 2,
        compiler_params=params(26),
        cost_estimate=cost(8 * rows * feats * model, 4 * feats * model),
    )(zi, a_own, b_own, a_oth, b_oth)


def core_swap(value):
    n = lax.axis_size("tensor")
    return lax.ppermute(value, "tensor", [(i, i ^ 1) for i in range(n)])


def y_swap(value):
    n = lax.axis_size("tensor")
    return lax.ppermute(value, "tensor", [(i, i ^ 2) for i in range(n)])


def ring(value):
    n = lax.axis_size("dp")
    return lax.ppermute(value, "dp", [(i, (i + 1) % n) for i in range(n)])


def gather_any(piece):
    ti = lax.axis_index("tensor")
    every = lax.all_gather(lax.all_gather(piece, "dp"), "tensor")
    tn, n, feats, cols = every.shape
    every = every.transpose(0, 2, 1, 3).reshape(tn, feats, n * cols // ZB, ZB)
    every = jnp.take(every, ti ^ jnp.array([0, 2, 1, 3]), axis=0)
    every = jnp.take(every, jnp.array([0, 3, 2, 1]), axis=2).transpose(2, 0, 1, 3)
    return [every[r, :2] for r in range(4)] + [every[r, 2:] for r in range(4)]


def meet(*values):
    return list(lax.optimization_barrier(values))


def after(value, *others):
    return lax.optimization_barrier((value, others))[0]


def to_owner(part, r):
    n = lax.axis_size("dp")
    return lax.ppermute(part, "dp", [(i, (i - r) % n) for i in range(n)])


def add_all(own, others):
    total = own.astype(F32)
    for other in others:
        total = total + other.astype(F32)
    return total


def scatter_any(keep, send):
    total = keep.astype(F32) + y_swap(send).astype(F32)
    total = jnp.take(total, jnp.array([0, 3, 2, 1]), axis=0)
    flat = total.transpose(1, 0, 2).reshape(total.shape[1], -1).astype(BF)
    return lax.psum_scatter(flat, "dp", scatter_dimension=1, tiled=True).astype(F32)


def plus(a, b):
    return (a.astype(F32) + b.astype(F32)).astype(BF)


def small_sum(value):
    n = lax.axis_size("dp")
    value = value + core_swap(value)
    value = value + y_swap(value)
    if n & (n - 1):
        return lax.psum(value, "dp")
    bit = 1
    while bit < n:
        value = value + lax.ppermute(value, "dp", [(i, i ^ bit) for i in range(n)])
        bit *= 2
    return value


def own_rows(row, core):
    quarters = row.reshape(2, 2, row.shape[0] // 4)
    own = lax.dynamic_index_in_dim(quarters, core, 1, keepdims=False).reshape(-1)
    oth = lax.dynamic_index_in_dim(quarters, 1 - core, 1, keepdims=False).reshape(-1)
    return own, oth


def tables(segment, variate, time_row, pad, core):
    seg_own, seg_oth = own_rows(segment, core)
    var_own, var_oth = own_rows(variate, core)
    pad_own, pad_oth = own_rows(pad, core)
    time_own, _ = own_rows(time_row, core)
    rows = seg_own.shape[0]
    half = HD // 2
    frequency = jnp.exp(-jnp.log(10000.0) * jnp.arange(half, dtype=F32) / half)
    phases = time_own.astype(F32)[:, None] * frequency[None, :]
    cos, sin = jnp.cos(phases), jnp.sin(phases)
    cos = jnp.concatenate([cos] * 4, axis=1)
    sin = jnp.concatenate([-sin, sin, -sin, sin], axis=1)
    lane = (jnp.arange(128, dtype=jnp.int32) % HD)[None, :]
    seg_k = jnp.concatenate([seg_own, seg_oth])[:, None]
    var_k = jnp.concatenate([var_own, var_oth])[:, None]
    pad_k = jnp.concatenate([jnp.ones_like(pad_own), pad_oth])[:, None]
    is_var = lane < 2 * N_VAR
    is_seg = (lane >= L_SEG) & (lane < L_PAD)
    is_lse = (lane >= L_LSE) & (lane < L_LSE + 3)
    aug_k = jnp.where(
        is_var,
        jnp.where(var_k == lane % N_VAR, 1.0, 0.0),
        jnp.where(
            is_seg,
            jnp.where(seg_k == lane - L_SEG, 0.0, -BIG),
            jnp.where(
                lane == L_PAD, jnp.where(pad_k == 1, 0.0, -BIG), jnp.where(is_lse, 1.0, 0.0)
            ),
        ),
    ).astype(BF)
    aug_q = jnp.where(
        is_var,
        jnp.where(var_own[:, None] == lane % N_VAR, 1.0, 0.0),
        jnp.where(
            is_seg,
            jnp.where(seg_own[:, None] == lane - L_SEG, 1.0, 0.0),
            jnp.where(lane == L_PAD, 1.0, 0.0),
        ),
    ).astype(F32)
    place = jnp.arange(rows, dtype=jnp.int32)
    neg = jnp.where(pad_own == 1, 0.0, -BIG).astype(F32)
    eye = place[:, None] == place[None, :]
    add_q = jnp.where(eye, 0.0, neg[None, :])
    add_k = jnp.where(eye, 0.0, neg[:, None])
    var_q = jnp.where(
        var_own[None, :] == jnp.arange(8, dtype=jnp.int32)[:, None], 1.0, 0.0
    ).astype(F32)
    return cos, sin, aug_q, aug_k, add_q, add_k, var_q


def head_scales(var_bias):
    lane = (jnp.arange(128, dtype=jnp.int32) % HD)[None, :]
    delta = (var_bias[:, 0] - var_bias[:, 1]) * math.sqrt(HD)
    hi = delta.astype(BF).astype(F32)
    low = (delta - hi).astype(BF).astype(F32)
    return jnp.where(
        lane < N_VAR, hi[:, None], jnp.where(lane < 2 * N_VAR, low[:, None], 1.0)
    ).reshape(-1, 2, 128)


def small_rows(gg_a, gg_f, bias, ti, heads_local):
    bias = bias.sum(axis=-1).reshape(4, 2 * heads_local)
    bias = jnp.take(bias, jnp.array([0, 2, 1, 3])[jnp.arange(4) ^ ti], axis=0).reshape(1, -1)
    bias = jnp.pad(bias, ((0, 0), (0, gg_a.shape[1] - bias.shape[1])))
    return jnp.concatenate([gg_a, gg_f, bias], axis=0)


def attend_part(scale, state, tab):
    q, k, v, k_oth, v_oth = state
    _, _, aug_q, aug_k, head_scale, add_q, _, _ = tab
    return attend_call(scale, q, k, k_oth, v, v_oth, aug_q, aug_k, head_scale, add_q)


def per_device(
    boundary, w_qkv, w_out, w_gate_up, w_down, norm_gains, variate_bias,
    segment_ids, variate_ids, time_ids, padding_mask,
):
    ti = lax.axis_index("tensor")
    tn = lax.axis_size("tensor")
    yi, core = ti // 2, ti % 2
    n = lax.axis_size("dp")
    is_first = lax.axis_index("section") == 0
    local = boundary[0]
    rows, model = local.shape[1:]
    scale = LOG2E / math.sqrt(HD)
    cols = w_qkv.shape[1]
    near = cols == ZB
    width = w_qkv.shape[3]
    hidden = w_gate_up.shape[3]
    heads_local = variate_bias.shape[1]
    zi = (lax.axis_index("dp") if near else 0) * jnp.ones((1,), jnp.int32)

    def row_of(array):
        return lax.dynamic_index_in_dim(array, yi, 0, keepdims=False)

    away = lax.dynamic_index_in_dim(local, 1 - yi, 0, keepdims=False).astype(BF)
    own = row_of(local).astype(BF)
    p_qkv = w_qkv[0].transpose(1, 2, 0).reshape(3 * width, cols)
    p_bias = jnp.pad(variate_bias[0].reshape(1, -1), ((0, 0), (0, cols - 2 * heads_local)))
    p_small = jnp.pad(jnp.concatenate([norm_gains[0], p_bias], axis=0), ((0, 13), (0, 0)))
    low = 3 * width
    out_low = low + 16
    p1 = jnp.concatenate([p_qkv, p_small, w_out[0]], axis=0)
    p2 = w_gate_up[0].transpose(1, 2, 0).reshape(2 * hidden, cols)
    p3 = w_down[0]

    def both_ends(came):
        return jnp.where(
            yi == 0, jnp.concatenate([own, came], axis=0), jnp.concatenate([came, own], axis=0)
        )

    tab = tables(
        row_of(segment_ids), row_of(variate_ids), row_of(time_ids), row_of(padding_mask), core
    )

    if near:
        a1, came = ring(p1), y_swap(away)
        a1, came, p1, p2, p3 = meet(a1, came, p1, p2, p3)
        a2, y0 = ring(a1), y_swap(p1)
        a1, a2, y0, p2, p3, *tab = meet(a1, a2, y0, p2, p3, *tab)
        ends = both_ends(came)
        a3, y1 = ring(a2), y_swap(a1)
        n1 = [jnp.stack([p1, y0])]
        f1 = [core_swap(n1[0])]
        a2, a3, y1, p2, p3, ends = meet(a2, a3, y1, p2, p3, ends)
        b1, y2, d0 = ring(p2), y_swap(a2), y_swap(p3)
        n1.append(jnp.stack([a1, y1]))
        f1.append(core_swap(n1[1]))
        a3, b1, y2, d0, p2 = meet(a3, b1, y2, d0, p2)
        b2, y3 = ring(b1), y_swap(a3)
        n1.append(jnp.stack([a2, y2]))
        f1.append(core_swap(n1[2]))
        b1, b2, y3, p2, d0 = meet(b1, b2, y3, p2, d0)
        n1.append(jnp.stack([a3, y3]))
        f1.append(core_swap(n1[3]))
        w1 = n1 + f1
        b3, g0 = ring(b2), y_swap(p2)
    else:
        w1 = gather_any(p1)
        ends = both_ends(y_swap(away))
    gains = jnp.stack([w[0, low : low + 2] for w in w1[:4]])
    gains = jnp.take(gains, (zi[0] - jnp.arange(4)) % 4, axis=0)
    gains = gains.transpose(1, 0, 2).reshape(2, model).astype(F32)
    gain_a, gain_f = gains[:1], gains[1:]
    bias = [w[:, low + 2, : 2 * heads_local] for w in (w1[0], w1[4])]
    bias = jnp.concatenate(bias).reshape(4 * heads_local, 2).astype(F32)
    head_scale = head_scales(bias)
    cos, sin, aug_q, aug_k, add_q, add_k, var_q = tab
    tab = (cos, sin, aug_q, aug_k, head_scale, add_q, add_k, var_q)

    q, k, v = qkv_call(False, ends, gain_a, zi, w1, low, cos, sin)
    if near:
        b1, b2, b3, g0, d0, q, k, v = meet(b1, b2, b3, g0, d0, q, k, v)
        n3 = [jnp.stack([p3, d0])]
        c1, g1 = ring(n3[0]), y_swap(b1)
        n2 = [jnp.stack([p2, g0])]
        f2 = [core_swap(n2[0])]
        f3 = [core_swap(n3[0])]
    k_oth, v_oth = core_swap(k), core_swap(v)
    o, _ = attend_part(scale, (q, k, v, k_oth, v_oth), tab)
    if near:
        b2, b3, c1, g1, o = meet(b2, b3, c1, g1, o)
        c2, g2 = ring(c1), y_swap(b2)
        n2.append(jnp.stack([b1, g1]))
        f2.append(core_swap(n2[1]))
        f3.append(core_swap(c1))
        b3, c2, g2 = meet(b3, c2, g2)
        c3, g3 = ring(c2), y_swap(b3)
        n2.append(jnp.stack([b2, g2]))
        f2.append(core_swap(n2[2]))
        f3.append(core_swap(c2))
        b3, c3, g3 = meet(b3, c3, g3)
        n2.append(jnp.stack([b3, g3]))
        f2.append(core_swap(n2[3]))
        f3.append(core_swap(c3))
        w2, w3 = n2 + f2, n3 + [c1, c2, c3] + f3
    else:
        w2, w3 = gather_any(p2), gather_any(p3)
    h, z_near, z_far = ffn_up_call(False, out_low, width, ends, o, gain_f, zi, w1, w2)
    y_low = ffn_down_call(BF, h, z_near, z_far, zi, w3)
    got = lax.ppermute(y_low, "section", [(0, 1)])

    x = jnp.where(is_first, ends, got)
    n1, q, k, v, q0, k0 = qkv_call(True, x, gain_a, zi, w1, low, cos, sin)
    k_oth, v_oth = core_swap(k), core_swap(v)
    o, sums = attend_part(scale, (q, k, v, k_oth, v_oth), tab)
    h, z_near, z_far, n2, g, u = ffn_up_call(True, out_low, width, x, o, gain_f, zi, w1, w2)
    y = ffn_down_call(F32, h, z_near, z_far, zi, w3)

    def qkv_back(dq, dk, dk_got, dv, dv_got, dh):
        return qkv_back_call(
            dq, dk, dk_got, dv, dv_got, q0, k0, cos, sin, x, dh, gain_a, zi, w1, low
        )

    dh, _, do = ffn_back_call(out_low, width, ends, h, g, u, gain_f, zi, w1, w2, w3)[:3]
    dq, dk, dk_send, dv, dv_send, _ = attend_back_call(
        scale, None, q, k, k_oth, v, v_oth, do, o, sums, aug_q, aug_k, head_scale, add_k, var_q
    )
    dx_low = qkv_back(dq, dk, core_swap(dk_send), dv, core_swap(dv_send), dh)[3]
    got = lax.ppermute(dx_low, "section", [(1, 0)])
    z_oth, n2_oth, n1_oth = core_swap(z_far), core_swap(n2), core_swap(n1)
    o_oth = core_swap(o[:, 2 * width :])

    got, y, z_oth, n2_oth, n1_oth, o_oth = meet(got, y, z_oth, n2_oth, n1_oth, o_oth)

    df = jnp.where(is_first, got, ends)
    down_keep, down_send = wgrad_call(zi, hidden, z_near, df, z_oth, core_swap(df))
    df, down_keep, down_send = meet(df, down_keep, down_send)
    down_got = y_swap(down_send)
    back = ffn_back_call(out_low, width, df, h, g, u, gain_f, zi, w1, w2, w3)
    down_keep, down_got, *back = meet(down_keep, down_got, *back)
    dh, da, do, dg_near, dg_far, du_near, du_far, gg_f = back
    dg_oth, du_oth, da_oth = core_swap(dg_far), core_swap(du_far), core_swap(da)
    if near:
        down = [plus(down_keep[r], down_got[r]) for r in range(4)]
        down_run = ring(down[1])
        dg_oth, du_oth, da_oth, down_run = meet(dg_oth, du_oth, da_oth, down_run)
        down_run = ring(plus(down_run, down[2]))
    else:
        down_run = down_got
    gate_keep, gate_send = wgrad_call(zi, hidden, dg_near, n2, dg_oth, n2_oth)
    out_keep, out_send = wgrad_call(zi, width, o, da, o_oth, da_oth)
    do, gate_keep, gate_send, out_keep, out_send, down_run = meet(
        do, gate_keep, gate_send, out_keep, out_send, down_run
    )
    back = attend_back_call(
        scale, None, q, k, k_oth, v, v_oth, do, o, sums, aug_q, aug_k, head_scale, add_k, var_q
    )
    half = hidden // 32 * 16
    cut = width * 3 // 2
    if near:
        gate_got = y_swap(gate_send)
        down_run = ring(plus(down_run, down[3]))
        out = [jnp.stack([out_keep[r], out_send[r]]) for r in range(4)]
        out_run = [to_owner(out[r], r) for r in (1, 2, 3)]
        gate_got, down_run, *rest = meet(gate_got, down_run, *out_run, *back)
        out_run, back = rest[:3], rest[3:]
        g_down = down_run.astype(F32) + down[0].astype(F32)
        out_sum = add_all(out[0], out_run)
    dq, dk, dk_send, dv, dv_send, bias = back
    dk_got, dv_got = core_swap(dk_send), core_swap(dv_send)
    up_keep, up_send = wgrad_call(zi, hidden, du_near, n2, du_oth, n2_oth)
    dk_got, dv_got, up_keep, up_send = meet(dk_got, dv_got, up_keep, up_send)
    if near:
        up_got = [y_swap(up_send[:, :half])]
        gate = [plus(gate_keep[r], gate_got[r]) for r in range(4)]
        gate_run = [to_owner(gate[r][:half], r) for r in (1, 2, 3)]
    back = qkv_back(dq, dk, dk_got, dv, dv_got, dh)
    if near:
        rest = meet(*up_got, *gate_run, *back)
        up_got, gate_run, back = rest[:1], rest[1:4], rest[4:]
        up_got.append(y_swap(up_send[:, half:]))
        gate_more = [to_owner(gate[r][half:], r) for r in (1, 2, 3)]
    dp_near, dp_far, dx, dx_low, gg_a = back
    dp_oth = core_swap(dp_far)
    qkv_keep, qkv_send = wgrad_call(zi, 3 * width, dp_near, n1, dp_oth, n1_oth)
    small = small_rows(gg_a, gg_f, bias, ti, heads_local)
    out_low_rows = jnp.where(is_first, dx_low, y.astype(BF))
    send = jnp.where(yi == 0, out_low_rows[rows:], out_low_rows[:rows])
    if near:
        up_last, qkv_keep, qkv_send, small, send, *gate_more = meet(
            up_got[1], qkv_keep, qkv_send, small, send, *gate_more
        )
        g_gate = jnp.concatenate(
            [
                add_all(gate[0][:half], gate_run),
                add_all(gate[0][half:], gate_more),
            ],
            axis=0,
        )
        head_got = y_swap(qkv_send[:, :cut])
        rows_got = y_swap(send)
        up = [
            plus(up_keep[r], jnp.concatenate([up_got[0][r], up_last[r]], axis=0))
            for r in range(4)
        ]
        up_run = [to_owner(up[r], r) for r in (1, 2, 3)]
        head_got, rows_got, *up_run = meet(head_got, rows_got, *up_run)
        tail_got = y_swap(qkv_send[:, cut:])
        head = [plus(qkv_keep[r, :cut], head_got[r]) for r in range(4)]
        head_run = [to_owner(head[r], r) for r in (1, 2, 3)]
        tail_got, small, out_sum, *head_run = meet(tail_got, small, out_sum, *head_run)
        small = small + core_swap(small)
        small = small + y_swap(small)
        tail = [plus(qkv_keep[r, cut:], tail_got[r]) for r in range(4)]
        tail_run = [to_owner(tail[r], r) for r in (1, 2, 3)]
        out_got = y_swap(out_sum[1].astype(BF))
        for bit in (1, 2):
            small = small + lax.ppermute(small, "dp", [(i, i ^ bit) for i in range(4)])
        g_gu = jnp.stack([g_gate, add_all(up[0], up_run)])
        g_out = out_sum[0] + out_got.astype(F32)
        g_qkv = jnp.concatenate([add_all(head[0], head_run), add_all(tail[0], tail_run)], axis=0)
    else:
        rows_got = y_swap(send)
        g_down = scatter_any(down_keep, down_send)
        g_gu = jnp.stack([scatter_any(gate_keep, gate_send), scatter_any(up_keep, up_send)])
        g_out = scatter_any(out_keep, out_send)
        g_qkv = scatter_any(qkv_keep, qkv_send)
        small = small_sum(small)

    out_rows = jnp.where(is_first, dx, y)
    keep = jnp.where(yi == 0, out_rows[:rows], out_rows[rows:])
    back = rows_got.astype(F32)
    boundary_out = jnp.where(yi == 0, jnp.stack([keep, back]), jnp.stack([back, keep]))[None]
    piece = model // (n * tn)
    gain_piece = lax.dynamic_slice_in_dim(
        small[:2], (lax.axis_index("dp") * tn + ti) * piece, piece, 1
    )
    bias_piece = lax.dynamic_slice_in_dim(
        small[2, : 8 * heads_local].reshape(-1, 2), ti * heads_local, heads_local, 0
    )
    return (
        boundary_out,
        g_qkv.reshape(3, width, cols).transpose(2, 0, 1)[None],
        g_out[None],
        g_gu.transpose(2, 0, 1)[None],
        g_down[None],
        gain_piece[None],
        bias_piece[None],
    )


def solution(mesh):
    placed = (
        P("section", "dp", "tensor", None),
        P("section", "dp", None, "tensor"),
        P("section", "tensor", "dp"),
        P("section", "dp", None, "tensor"),
        P("section", "tensor", "dp"),
        P("section", None, "dp"),
        P("section", "tensor", None),
        P("dp", None),
        P("dp", None),
        P("dp", None),
        P("dp", None),
    )
    return jax.shard_map(
        per_device,
        mesh=mesh,
        in_specs=placed,
        out_specs=(
            P("section", "dp", "tensor", None),
            P("section", "dp", None, "tensor"),
            P("section", "tensor", "dp"),
            P("section", "dp", None, "tensor"),
            P("section", "tensor", "dp"),
            P("section", None, ("dp", "tensor")),
            P("section", "tensor", None),
        ),
        check_vma=False,
    )
```

```python
import functools
import math

import jax
import jax.numpy as jnp
from jax import lax
from jax.experimental import pallas as pl
from jax.experimental.pallas import tpu as pltpu
from jax.sharding import PartitionSpec as P

EPS = 1e-05
BIG = 8192.0
LOG2E = 1.4426950408889634
BF = jnp.bfloat16
F32 = jnp.float32
HD = 64
ZB = 256
VMEM_MB = 56
N_VAR = 4
L_SEG = 8
L_PAD = 24
L_LSE = 25


def dot(a, b):
    return lax.dot_general(a, b, (((1,), (0,)), ((), ())), preferred_element_type=F32)


def dot_nt(a, b):
    return lax.dot_general(a, b, (((1,), (1,)), ((), ())), preferred_element_type=F32)


def dot_tn(a, b):
    return lax.dot_general(a, b, (((0,), (0,)), ((), ())), preferred_element_type=F32)


def params(mb=VMEM_MB):
    return pltpu.CompilerParams(
        dimension_semantics=("arbitrary",), vmem_limit_bytes=mb * 1024 * 1024
    )


def cost(flops, nbytes, trans=0):
    return pl.CostEstimate(flops=int(flops), bytes_accessed=int(nbytes), transcendentals=0)


def sds(shape, dtype):
    return jax.ShapeDtypeStruct(shape, dtype)


def whole(shape):
    zeros = (0,) * len(shape)
    return pl.BlockSpec(shape, lambda *_: zeros)


def head_sum(u):
    row = lax.broadcasted_iota(jnp.int32, (u.shape[1], u.shape[1]), 0) // HD
    col = lax.broadcasted_iota(jnp.int32, (u.shape[1], u.shape[1]), 1) // HD
    return dot(u.astype(BF), jnp.where(row == col, 1.0, 0.0).astype(BF))


def half_swap(u):
    lane = lax.broadcasted_iota(jnp.int32, u.shape, 1) % HD
    return jnp.where(lane < HD // 2, pltpu.roll(u, 128 - HD // 2, 1), pltpu.roll(u, HD // 2, 1))


def row_rms(x):
    return lax.rsqrt(jnp.mean(x * x, axis=-1, keepdims=True) + EPS)


def hbm():
    return pl.BlockSpec(memory_space=pl.ANY)


def smem():
    return pl.BlockSpec(memory_space=pltpu.SMEM)


def copies(refs, low, scratch, sems, t):
    rows = pl.ds(low, scratch.shape[2])
    return [
        pltpu.make_async_copy(
            refs[4 * (t // 2) + r].at[t % 2, rows], scratch.at[r, t], sems.at[r, t]
        )
        for r in range(4)
    ]


def start_all(refs, low, scratch, sems):
    for t in range(4):
        for copy in copies(refs, low, scratch, sems, t):
            copy.start()


def wait_for(refs, low, scratch, sems, t):
    for fixed in range(4):

        @pl.when(t == fixed)
        def _():
            for copy in copies(refs, low, scratch, sems, fixed):
                copy.wait()


def weight_scratch(feats):
    return [pltpu.VMEM((4, 4, feats, ZB), BF), pltpu.SemaphoreType.DMA((4, 4))]


def place(zi_ref, r):
    return lax.rem(zi_ref[0] - r + 4, 4)


def block_store(ref, value):
    for z in range(4):
        ref[z] = value[:, z * ZB : (z + 1) * ZB]


def chunks(wide, step=ZB):
    return [slice(low, min(low + step, wide)) for low in range(0, wide, step)]


def block_load(ref):
    return jnp.concatenate([ref[z] for z in range(4)], axis=1)


def qkv_kernel(save, x_ref, gain_ref, zi_ref, cos_ref, sin_ref, *refs):
    weight, refs = refs[:8], refs[8:]
    if save:
        n_ref, q_ref, k_ref, v_ref, q0_ref, k0_ref, n_scr, w_ref, sems = refs
    else:
        q_ref, k_ref, v_ref, n_scr, w_ref, sems = refs
    t = pl.program_id(0)

    @pl.when(t == 0)
    def _():
        start_all(weight, 0, w_ref, sems)
        x = x_ref[...].astype(F32)
        n = (x * row_rms(x) * gain_ref[...]).astype(BF)
        block_store(n_scr, n)
        if save:
            n_ref[...] = n

    wait_for(weight, 0, w_ref, sems, t)
    width = q_ref.shape[1]

    def project(which):
        cols = slice(which * width, (which + 1) * width)
        total = dot_nt(n_scr[place(zi_ref, 0)], w_ref[0, t, cols])
        for r in range(1, 4):
            total = total + dot_nt(n_scr[place(zi_ref, r)], w_ref[r, t, cols])
        return total

    cos, sin = cos_ref[...], sin_ref[...]
    for which, out in ((0, q_ref), (1, k_ref)):
        u = project(which)
        if save:
            kept = q0_ref if which == 0 else k0_ref
            kept[...] = u.astype(BF)
        un = u * lax.rsqrt(head_sum(u * u) * (1.0 / HD) + EPS)
        for pair in range(width // 128):
            at = slice(pair * 128, (pair + 1) * 128)
            out[:, at] = (un[:, at] * cos + half_swap(un[:, at]) * sin).astype(BF)
    v_ref[...] = project(2).astype(BF)


def qkv_call(save, x, gain, zi, w, feats, cos, sin):
    rows, model = x.shape
    width = feats // 3
    total = 4 * width
    col = pl.BlockSpec((rows, width), lambda t: (0, t))
    outs = [sds((rows, total), BF)] * 3
    specs = [col] * 3
    if save:
        outs = [sds((rows, model), BF)] + outs + [sds((rows, total), BF)] * 2
        specs = [whole((rows, model))] + specs + [col] * 2
    return pl.pallas_call(
        functools.partial(qkv_kernel, save),
        grid=(4,),
        in_specs=[whole((rows, model)), whole((1, model)), smem()]
        + [whole((rows, 128))] * 2
        + [hbm()] * 8,
        out_specs=specs,
        out_shape=outs,
        scratch_shapes=[pltpu.VMEM((4, rows, ZB), BF)] + weight_scratch(feats),
        compiler_params=params(),
        cost_estimate=cost(2 * rows * model * 3 * total, 6 * total * model + 16 * x.size),
    )(x, gain, zi, cos, sin, *w)


def other_core_spec(rows, pairs):
    half = pairs // 2
    return pl.BlockSpec((rows, 128), lambda p: (0, lax.rem(p + half, pairs)))


def pick(first, h, a, b):
    return jnp.where(first, a, b) if h == 0 else jnp.where(first, b, a)


def pick_low(first, h, a, b):
    mine = jnp.where(first, 1.0, 0.0) if h == 0 else jnp.where(first, 0.0, 1.0)
    low = mine.astype(BF)
    return a * low + b * (1.0 - mine).astype(BF)


def attend_kernel(
    scale, q_ref, ko_ref, kx_ref, vo_ref, vx_ref, aq_ref, ak_ref, hs_ref, add_ref, o_ref, l_ref
):
    rows = q_ref.shape[0]
    kb = 128
    first = lax.broadcasted_iota(jnp.int32, (1, 128), 1) < HD
    q = q_ref[...].astype(F32)
    base = aq_ref[...]
    raws = []
    for h in range(2):
        qh = pick(first, h, q, base * hs_ref[0, h : h + 1, :]).astype(BF)
        total = None
        for half, (k_ref, v_ref) in enumerate(((ko_ref, vo_ref), (kx_ref, vx_ref))):
            for block in range(rows // kb):
                at = slice(block * kb, (block + 1) * kb)
                kk = slice(half * rows + block * kb, half * rows + (block + 1) * kb)
                kh = pick_low(first, h, k_ref[at, :], ak_ref[kk, :])
                vh = pick_low(first, h, v_ref[at, :], BF(1.0))
                s = dot_nt(qh, kh)
                if half == 0:
                    s = s + add_ref[:, at]
                part = dot(jnp.exp2(s * scale).astype(BF), vh)
                total = part if total is None else total + part
        raws.append(total)
    sums = jnp.where(first, raws[1], raws[0])
    l_ref[...] = sums
    o_ref[...] = (jnp.where(first, raws[0], raws[1]) / pltpu.roll(sums, HD, 1)).astype(BF)


def attend_call(scale, q, k_own, k_oth, v_own, v_oth, aug_q, aug_k, head_scale, add_own):
    rows, total = q.shape
    pairs = total // 128
    col = pl.BlockSpec((rows, 128), lambda p: (0, p))
    far = other_core_spec(rows, pairs)
    return pl.pallas_call(
        functools.partial(attend_kernel, scale),
        grid=(pairs,),
        in_specs=[
            col,
            col,
            far,
            col,
            far,
            whole(aug_q.shape),
            whole(aug_k.shape),
            pl.BlockSpec((1, 2, 128), lambda p: (p, 0, 0)),
            whole(add_own.shape),
        ],
        out_specs=[col, col],
        out_shape=[sds((rows, total), BF), sds((rows, total), F32)],
        compiler_params=params(),
        cost_estimate=cost(
            4 * 2 * rows * rows * 2 * total, 20 * rows * total, rows * rows * 2 * pairs * 2
        ),
    )(q, k_own, k_oth, v_own, v_oth, aug_q, aug_k, head_scale, add_own)


def padded(hidden):
    return -(-2 * hidden // 128) * 128


def pair_scratch(parts, hidden):
    return [
        pltpu.VMEM((4, 2, parts * padded(hidden), ZB), BF),
        pltpu.SemaphoreType.DMA((4, 2, 2, parts)),
    ]


def pair_copies(refs, parts, scratch, sems, half):
    wide = scratch.shape[2] // parts
    hidden = refs[0].shape[1] // parts
    return [
        pltpu.make_async_copy(
            refs[4 * half + r].at[y, pl.ds(part * hidden, hidden)],
            scratch.at[r, half, pl.ds(part * wide + y * hidden, hidden)],
            sems.at[r, half, y, part],
        )
        for r in range(4)
        for y in range(2)
        for part in range(parts)
    ]


def pair_start(refs, parts, scratch, sems):
    wide = scratch.shape[2] // parts
    hidden = refs[0].shape[1] // parts
    for half in range(2):
        for copy in pair_copies(refs, parts, scratch, sems, half):
            copy.start()
    blank = wide - 2 * hidden
    if blank:
        for half in range(2):
            for r in range(4):
                for part in range(parts):
                    low = part * wide + 2 * hidden
                    scratch[r, half, low : low + blank] = jnp.zeros((blank, ZB), BF)


def pair_wait(refs, parts, scratch, sems, half):
    for fixed in range(2):

        @pl.when(half == fixed)
        def _():
            for copy in pair_copies(refs, parts, scratch, sems, fixed):
                copy.wait()


def near_far(rows, feats):
    return (
        pl.BlockSpec((1, rows, feats), lambda t: (jnp.minimum(t, 1), 0, 0)),
        pl.BlockSpec((1, rows, feats), lambda t: (jnp.maximum(t - 2, 0), 0, 0)),
    )


def put(is_near, near_ref, far_ref, value, at=...):
    @pl.when(is_near)
    def _():
        near_ref[at] = value

    @pl.when(jnp.logical_not(is_near))
    def _():
        far_ref[at] = value


def ffn_up_kernel(save, out_low, x_ref, o_ref, gain_ref, zi_ref, *refs):
    wo, wgu, refs = refs[:8], refs[8:16], refs[16:]
    if save:
        h_ref, zn_ref, zf_ref, n_ref, g_ref, u_ref = refs[:6]
    else:
        h_ref, zn_ref, zf_ref = refs[:3]
    n_scr, wo_ref, wo_sems, wgu_ref, wgu_sems, acc, z_scr = refs[-7:]
    wide = wgu_ref.shape[2] // 2
    half = pl.program_id(0)

    @pl.when(half == 0)
    def _():
        start_all(wo, out_low, wo_ref, wo_sems)
        pair_start(wgu, 2, wgu_ref, wgu_sems)
        width = wo_ref.shape[2]
        block_store(acc, x_ref[...].astype(F32))
        for s in range(4):
            for copy in copies(wo, out_low, wo_ref, wo_sems, s):
                copy.wait()
        for r in range(4):
            z = place(zi_ref, r)
            h = acc[z]
            for s in range(4):
                h = h + dot(o_ref[:, s * width : (s + 1) * width], wo_ref[r, s])
            acc[z] = h
        h = block_load(acc)
        n = (h * row_rms(h) * gain_ref[...]).astype(BF)
        block_store(n_scr, n)
        h_ref[...] = h
        if save:
            n_ref[...] = n

    pair_wait(wgu, 2, wgu_ref, wgu_sems, half)
    for at in chunks(wide):
        total = []
        for part in range(2):
            cols = slice(part * wide + at.start, part * wide + at.stop)
            one = dot_nt(n_scr[place(zi_ref, 0)], wgu_ref[0, half, cols])
            for r in range(1, 4):
                one = one + dot_nt(n_scr[place(zi_ref, r)], wgu_ref[r, half, cols])
            total.append(one)
        gate, up = total
        z_scr[:, at] = (gate / (1.0 + jnp.exp(-gate)) * up).astype(BF)
        if save:
            g_ref[0, :, at] = gate.astype(BF)
            u_ref[0, :, at] = up.astype(BF)
    put(half == 0, zn_ref, zf_ref, z_scr[...])


def ffn_up_call(save, out_low, width, x, o, gain, zi, wo, wgu):
    rows, model = x.shape
    hidden = wgu[0].shape[1] // 2
    wide = padded(hidden)
    big = whole((rows, model))
    part = pl.BlockSpec((1, rows, wide), lambda t: (t, 0, 0))
    outs = [sds((rows, model), F32)] + [sds((rows, wide), BF)] * 2
    specs = [big, whole((rows, wide)), whole((rows, wide))]
    if save:
        outs += [sds((rows, model), BF)] + [sds((2, rows, wide), BF)] * 2
        specs += [big, part, part]
    return pl.pallas_call(
        functools.partial(ffn_up_kernel, save, out_low),
        grid=(2,),
        in_specs=[big, whole(o.shape), whole((1, model)), smem()] + [hbm()] * 16,
        out_specs=specs,
        out_shape=outs,
        scratch_shapes=[pltpu.VMEM((4, rows, ZB), BF)]
        + weight_scratch(width)
        + pair_scratch(2, hidden)
        + [pltpu.VMEM((4, rows, ZB), F32), pltpu.VMEM((rows, wide), BF)],
        compiler_params=params(),
        cost_estimate=cost(
            2 * rows * model * (8 * hidden + model), 16 * hidden * model + 20 * x.size
        ),
    )(x, o, gain, zi, *wo, *wgu)


def ffn_down_kernel(h_ref, zn_ref, zf_ref, zi_ref, *refs):
    weight, (y_ref, w_ref, sems) = refs[:8], refs[8:]
    pair_start(weight, 1, w_ref, sems)
    for half, z_ref in enumerate((zn_ref, zf_ref)):
        for copy in pair_copies(weight, 1, w_ref, sems, half):
            copy.wait()
    for z in range(4):
        r = lax.rem(zi_ref[0] - z + 4, 4)
        at = slice(z * ZB, (z + 1) * ZB)
        y = h_ref[:, at] + dot(zn_ref[...], w_ref[r, 0]) + dot(zf_ref[...], w_ref[r, 1])
        y_ref[:, at] = y.astype(y_ref.dtype)


def ffn_down_call(dtype, h, z_near, z_far, zi, wd):
    rows, model = h.shape
    hidden = wd[0].shape[1]
    vmem = pl.BlockSpec(memory_space=pltpu.VMEM)
    return pl.pallas_call(
        ffn_down_kernel,
        in_specs=[vmem] * 3 + [smem()] + [hbm()] * 8,
        out_specs=vmem,
        out_shape=sds((rows, model), dtype),
        scratch_shapes=pair_scratch(1, hidden),
        compiler_params=pltpu.CompilerParams(vmem_limit_bytes=VMEM_MB * 1024 * 1024),
        cost_estimate=cost(2 * rows * model * 4 * hidden, 8 * hidden * model + 8 * h.size),
    )(h, z_near, z_far, zi, *wd)


def ffn_back_kernel(out_low, dy_ref, h_ref, g_ref, u_ref, gain_ref, zi_ref, *refs):
    wo, wgu, wd, refs = refs[:8], refs[8:16], refs[16:24], refs[24:]
    dh_ref, da_ref, do_ref, dgn_ref, dgf_ref, dun_ref, duf_ref, gg_ref = refs[:8]
    df_scr, acc, wo_ref, wo_sems, wgu_ref, wgu_sems, wd_ref, wd_sems, dg_scr, du_scr = refs[8:]
    wide = wd_ref.shape[2]
    half = pl.program_id(0)

    @pl.when(half == 0)
    def _():
        pair_start(wd, 1, wd_ref, wd_sems)
        pair_start(wgu, 2, wgu_ref, wgu_sems)
        start_all(wo, out_low, wo_ref, wo_sems)
        block_store(df_scr, dy_ref[...])
        acc[...] = jnp.zeros_like(acc)

    pair_wait(wd, 1, wd_ref, wd_sems, half)
    for at in chunks(wide):
        dz = dot_nt(df_scr[place(zi_ref, 0)], wd_ref[0, half, at])
        for r in range(1, 4):
            dz = dz + dot_nt(df_scr[place(zi_ref, r)], wd_ref[r, half, at])
        gate = g_ref[0, :, at].astype(F32)
        up = u_ref[0, :, at].astype(F32)
        s = 1.0 / (1.0 + jnp.exp(-gate))
        dg_scr[:, at] = (dz * up * s * (1.0 + gate * (1.0 - s))).astype(BF)
        du_scr[:, at] = (dz * gate * s).astype(BF)
    dgate, dup = dg_scr[...], du_scr[...]
    put(half == 0, dgn_ref, dgf_ref, dgate)
    put(half == 0, dun_ref, duf_ref, dup)
    pair_wait(wgu, 2, wgu_ref, wgu_sems, half)
    for r in range(4):
        z = place(zi_ref, r)
        acc[z] = acc[z] + (
            dot(dgate, wgu_ref[r, half, :wide]) + dot(dup, wgu_ref[r, half, wide:])
        )

    @pl.when(half == 1)
    def _():
        h = h_ref[...]
        r = row_rms(h)
        hn = h * r
        dn = block_load(acc)
        gg_ref[...] = jnp.sum(dn * hn, axis=0, keepdims=True)
        dhat = dn * gain_ref[...]
        dh = dy_ref[...].astype(F32) + r * (
            dhat - hn * jnp.mean(dhat * hn, axis=-1, keepdims=True)
        )
        dh_ref[...] = dh
        da = dh.astype(BF)
        da_ref[...] = da
        block_store(df_scr, da)
        width = wo_ref.shape[2]
        for s in range(4):
            for copy in copies(wo, out_low, wo_ref, wo_sems, s):
                copy.wait()
        for s in range(4):
            part = dot_nt(df_scr[place(zi_ref, 0)], wo_ref[0, s])
            for q in range(1, 4):
                part = part + dot_nt(df_scr[place(zi_ref, q)], wo_ref[q, s])
            do_ref[:, s * width : (s + 1) * width] = part.astype(BF)


def ffn_back_call(out_low, width, dy, h, g, u, gain, zi, wo, wgu, wd):
    rows, model = dy.shape
    hidden = wd[0].shape[1]
    wide = g.shape[2]
    big = whole((rows, model))
    part = pl.BlockSpec((1, rows, wide), lambda t: (t, 0, 0))
    return pl.pallas_call(
        functools.partial(ffn_back_kernel, out_low),
        grid=(2,),
        in_specs=[big, big, part, part, whole((1, model)), smem()] + [hbm()] * 24,
        out_specs=[big, big, big] + [whole((rows, wide))] * 4 + [whole((1, model))],
        out_shape=[sds((rows, model), F32), sds((rows, model), BF), sds((rows, model), BF)]
        + [sds((rows, wide), BF)] * 4
        + [sds((1, model), F32)],
        scratch_shapes=[pltpu.VMEM((4, rows, ZB), BF), pltpu.VMEM((4, rows, ZB), F32)]
        + weight_scratch(width)
        + pair_scratch(2, hidden)
        + pair_scratch(1, hidden)
        + [pltpu.VMEM((rows, wide), BF)] * 2,
        compiler_params=params(57),
        cost_estimate=cost(
            2 * rows * model * (12 * hidden + model), 24 * hidden * model + 20 * dy.size
        ),
    )(dy, h, g, u, gain, zi, *wo, *wgu, *wd)


def split3(value):
    hi = value.astype(BF).astype(F32)
    mid = (value - hi).astype(BF).astype(F32)
    return hi, mid, value - hi - mid


def attend_back_kernel(
    scale, q_ref, ko_ref, kx_ref, vo_ref, vx_ref, do_ref, o_ref, l_ref, aq_ref, ak_ref, hs_ref,
    add_ref, var_ref, dq_ref, dko_ref, dkx_ref, dvo_ref, dvx_ref, bias_ref,
):
    rows = q_ref.shape[0]
    kb = 256
    first = lax.broadcasted_iota(jnp.int32, (1, 128), 1) < HD
    lane = lax.broadcasted_iota(jnp.int32, (1, 128), 1) % HD
    q = q_ref[...].astype(F32)
    do = do_ref[...].astype(F32)
    inner = do * o_ref[...].astype(F32)
    base = aq_ref[...]
    hi, mid, low = split3(jnp.log2(l_ref[...]) * (-1.0 / scale))
    lse = jnp.where(lane == L_LSE, hi, 0.0)
    lse = jnp.where(lane == L_LSE + 1, mid, lse)
    lse = jnp.where(lane == L_LSE + 2, low, lse)
    dq_t = []
    dk = [[], []]
    dv = [[], []]
    for h in range(2):
        qh = pick(first, h, q, base * hs_ref[0, h : h + 1, :] + lse).astype(BF)
        d = jnp.sum(pick(first, h, inner, 0.0), axis=-1, keepdims=True)
        dhi, dmid, dlow = split3(-d)
        d_aug = jnp.where(lane == 0, dhi, 0.0)
        d_aug = jnp.where(lane == 1, dmid, d_aug)
        d_aug = jnp.where(lane == 2, dlow, d_aug)
        doh = pick(first, h, do, d_aug).astype(BF)
        total = None
        for half, (k_ref, v_ref) in enumerate(((ko_ref, vo_ref), (kx_ref, vx_ref))):
            for block in range(rows // kb):
                at = slice(block * kb, (block + 1) * kb)
                kk = slice(half * rows + block * kb, half * rows + (block + 1) * kb)
                kh = pick_low(first, h, k_ref[at, :], ak_ref[kk, :])
                vh = pick_low(first, h, v_ref[at, :], BF(1.0))
                s = dot_nt(kh, qh)
                if half == 0:
                    s = s + add_ref[at, :]
                p = jnp.exp2(s * scale)
                ds = (p * dot_nt(vh, doh)).astype(BF)
                dv[h].append(dot(p.astype(BF), doh))
                dk[h].append(dot(ds, qh))
                part = dot_tn(kh, ds)
                total = part if total is None else total + part
        dq_t.append(total)
    scale_back = 1.0 / math.sqrt(HD)
    count = rows // kb
    for half, (dk_ref, dv_ref) in enumerate(((dko_ref, dvo_ref), (dkx_ref, dvx_ref))):
        for block in range(count):
            at = slice(block * kb, (block + 1) * kb)
            i = half * count + block
            dk_ref[at, :] = (jnp.where(first, dk[0][i], dk[1][i]) * scale_back).astype(dk_ref.dtype)
            dv_ref[at, :] = jnp.where(first, dv[0][i], dv[1][i]).astype(dv_ref.dtype)
    joined = jnp.concatenate([dq_t[0][:HD], dq_t[1][HD:]], axis=0)
    dq_ref[...] = (joined.T * scale_back).astype(BF)
    mine = var_ref[...]
    for h in range(2):
        begin = HD if h == 0 else 0
        r = dq_t[h][begin : begin + 8]
        same = jnp.sum(r * mine, axis=0, keepdims=True)
        every = jnp.sum(r[:N_VAR], axis=0, keepdims=True)
        bias_ref[0, 2 * h : 2 * h + 1, :] = same
        bias_ref[0, 2 * h + 1 : 2 * h + 2, :] = every - same


def attend_back_call(
    scale, span, q, k_own, k_oth, v_own, v_oth, do, o, sums, aug_q, aug_k, head_scale, add_own, var_q
):
    rows, total = q.shape
    every = total // 128
    low, high = span or (0, every)
    pairs = high - low
    total = pairs * 128
    col = pl.BlockSpec((rows, 128), lambda p: (0, p + low))
    far = pl.BlockSpec((rows, 128), lambda p: (0, lax.rem(p + low + every // 2, every)))
    out = pl.BlockSpec((rows, 128), lambda p: (0, p))
    out_far = other_core_spec(rows, pairs) if span is None else out
    return pl.pallas_call(
        functools.partial(attend_back_kernel, scale),
        grid=(pairs,),
        in_specs=[col, col, far, col, far, col, col, col]
        + [
            whole(aug_q.shape),
            whole(aug_k.shape),
            pl.BlockSpec((1, 2, 128), lambda p: (p + low, 0, 0)),
            whole(add_own.shape),
            whole(var_q.shape),
        ],
        out_specs=[out, out, out_far, out, out_far] + [pl.BlockSpec((1, 4, rows), lambda p: (p, 0, 0))],
        out_shape=[
            sds((rows, total), BF),
            sds((rows, total), BF),
            sds((rows, total), BF),
            sds((rows, total), BF),
            sds((rows, total), BF),
            sds((pairs, 4, rows), F32),
        ],
        compiler_params=params(),
        cost_estimate=cost(
            10 * 2 * rows * rows * 2 * total, 40 * rows * total, rows * rows * 2 * pairs * 2
        ),
    )(q, k_own, k_oth, v_own, v_oth, do, o, sums, aug_q, aug_k, head_scale, add_own, var_q)


def qkv_back_kernel(
    dq_ref, dk_ref, dkr_ref, dv_ref, dvr_ref, q0_ref, k0_ref, cos_ref, sin_ref, x_ref, dh_ref,
    gain_ref, zi_ref, *refs,
):
    weight, refs = refs[:8], refs[8:]
    dpn_ref, dpf_ref, dx_ref, dxl_ref, gg_ref, dp_scr, acc, w_ref, sems = refs
    width = dq_ref.shape[1]
    t = pl.program_id(0)

    @pl.when(t == 0)
    def _():
        start_all(weight, 0, w_ref, sems)
        acc[...] = jnp.zeros_like(acc)

    cos, sin = cos_ref[...], sin_ref[...]
    for which in range(2):
        u = (q0_ref if which == 0 else k0_ref)[...].astype(F32)
        r = lax.rsqrt(head_sum(u * u) * (1.0 / HD) + EPS)
        un = u * r
        turned = []
        for pair in range(width // 128):
            at = slice(pair * 128, (pair + 1) * 128)
            if which == 0:
                grad = dq_ref[:, at].astype(F32)
            else:
                grad = dk_ref[:, at].astype(F32) + dkr_ref[:, at].astype(F32)
            turned.append(grad * cos - half_swap(grad) * sin)
        grad = jnp.concatenate(turned, axis=1)
        out = r * (grad - un * (head_sum(grad * un) * (1.0 / HD)))
        dp_scr[:, which * width : (which + 1) * width] = out.astype(BF)
    dp_scr[:, 2 * width :] = (dv_ref[...].astype(F32) + dvr_ref[...].astype(F32)).astype(BF)
    wait_for(weight, 0, w_ref, sems, t)
    dp = dp_scr[...]
    put(t < 2, dpn_ref, dpf_ref, dp, 0)
    for r in range(4):
        z = place(zi_ref, r)
        acc[z] = acc[z] + dot(dp, w_ref[r, t])

    @pl.when(t == 3)
    def _():
        x = x_ref[...].astype(F32)
        r = row_rms(x)
        xn = x * r
        dn = block_load(acc)
        gg_ref[...] = jnp.sum(dn * xn, axis=0, keepdims=True)
        dhat = dn * gain_ref[...]
        dx = dh_ref[...] + r * (dhat - xn * jnp.mean(dhat * xn, axis=-1, keepdims=True))
        dx_ref[...] = dx
        dxl_ref[...] = dx.astype(BF)


def qkv_back_call(dq, dk, dkr, dv, dvr, q0, k0, cos, sin, x, dh, gain, zi, w, feats):
    rows, model = x.shape
    width = feats // 3
    big = whole((rows, model))
    col = pl.BlockSpec((rows, width), lambda t: (0, t))
    return pl.pallas_call(
        qkv_back_kernel,
        grid=(4,),
        in_specs=[col] * 7
        + [whole((rows, 128)), whole((rows, 128)), big, big, whole((1, model)), smem()]
        + [hbm()] * 8,
        out_specs=[*near_far(rows, feats), big, big, whole((1, model))],
        out_shape=[sds((2, rows, feats), BF)] * 2
        + [sds((rows, model), F32), sds((rows, model), BF), sds((1, model), F32)],
        scratch_shapes=[pltpu.VMEM((rows, feats), BF), pltpu.VMEM((4, rows, ZB), F32)]
        + weight_scratch(feats),
        compiler_params=params(),
        cost_estimate=cost(8 * rows * model * feats, 8 * feats * model + 40 * x.size),
    )(dq, dk, dkr, dv, dvr, q0, k0, cos, sin, x, dh, gain, zi, *w)


def wgrad_kernel(feats, zi_ref, ao_ref, bo_ref, ax_ref, bx_ref, keep_ref, send_ref):
    if len(ao_ref.shape) == 3:
        for i, out in ((1, send_ref), (0, keep_ref)):
            g = dot_tn(ao_ref[i], bo_ref[...]) + dot_tn(ax_ref[i], bx_ref[...])
            for z in range(4):
                out[lax.rem(zi_ref[0] - z + 4, 4)] = g[:, z * ZB : (z + 1) * ZB].astype(BF)
    else:
        g = dot_tn(ao_ref[...], bo_ref[...]) + dot_tn(ax_ref[...], bx_ref[...])
        for z in range(4):
            r = lax.rem(zi_ref[0] - z + 4, 4)
            at = slice(z * ZB, (z + 1) * ZB)
            keep_ref[r] = g[:feats, at].astype(BF)
            send_ref[r] = g[feats : 2 * feats, at].astype(BF)


def wgrad_call(zi, feats, a_own, b_own, a_oth, b_oth):
    rows, model = b_own.shape
    part = whole(a_oth.shape)
    big = whole((rows, model))
    out = whole((4, feats, ZB))
    return pl.pallas_call(
        functools.partial(wgrad_kernel, feats),
        grid=(1,),
        in_specs=[smem(), part, big, part, big],
        out_specs=[out, out],
        out_shape=[sds((4, feats, ZB), BF)] * 2,
        compiler_params=params(26),
        cost_estimate=cost(8 * rows * feats * model, 4 * feats * model),
    )(zi, a_own, b_own, a_oth, b_oth)


def core_swap(value):
    n = lax.axis_size("tensor")
    return lax.ppermute(value, "tensor", [(i, i ^ 1) for i in range(n)])


def y_swap(value):
    n = lax.axis_size("tensor")
    return lax.ppermute(value, "tensor", [(i, i ^ 2) for i in range(n)])


def ring(value):
    n = lax.axis_size("dp")
    return lax.ppermute(value, "dp", [(i, (i + 1) % n) for i in range(n)])


def gather_any(piece):
    ti = lax.axis_index("tensor")
    every = lax.all_gather(lax.all_gather(piece, "dp"), "tensor")
    tn, n, feats, cols = every.shape
    every = every.transpose(0, 2, 1, 3).reshape(tn, feats, n * cols // ZB, ZB)
    every = jnp.take(every, ti ^ jnp.array([0, 2, 1, 3]), axis=0)
    every = jnp.take(every, jnp.array([0, 3, 2, 1]), axis=2).transpose(2, 0, 1, 3)
    return [every[r, :2] for r in range(4)] + [every[r, 2:] for r in range(4)]


def meet(*values):
    return list(lax.optimization_barrier(values))


def after(value, *others):
    return lax.optimization_barrier((value, others))[0]


def to_owner(part, r):
    n = lax.axis_size("dp")
    return lax.ppermute(part, "dp", [(i, (i - r) % n) for i in range(n)])


def add_all(own, others):
    total = own.astype(F32)
    for other in others:
        total = total + other.astype(F32)
    return total


def scatter_any(keep, send):
    total = keep.astype(F32) + y_swap(send).astype(F32)
    total = jnp.take(total, jnp.array([0, 3, 2, 1]), axis=0)
    flat = total.transpose(1, 0, 2).reshape(total.shape[1], -1).astype(BF)
    return lax.psum_scatter(flat, "dp", scatter_dimension=1, tiled=True).astype(F32)


def plus(a, b):
    return (a.astype(F32) + b.astype(F32)).astype(BF)


def small_sum(value):
    n = lax.axis_size("dp")
    value = value + core_swap(value)
    value = value + y_swap(value)
    if n & (n - 1):
        return lax.psum(value, "dp")
    bit = 1
    while bit < n:
        value = value + lax.ppermute(value, "dp", [(i, i ^ bit) for i in range(n)])
        bit *= 2
    return value


def own_rows(row, core):
    quarters = row.reshape(2, 2, row.shape[0] // 4)
    own = lax.dynamic_index_in_dim(quarters, core, 1, keepdims=False).reshape(-1)
    oth = lax.dynamic_index_in_dim(quarters, 1 - core, 1, keepdims=False).reshape(-1)
    return own, oth


def tables(segment, variate, time_row, pad, core):
    seg_own, seg_oth = own_rows(segment, core)
    var_own, var_oth = own_rows(variate, core)
    pad_own, pad_oth = own_rows(pad, core)
    time_own, _ = own_rows(time_row, core)
    rows = seg_own.shape[0]
    half = HD // 2
    frequency = jnp.exp(-jnp.log(10000.0) * jnp.arange(half, dtype=F32) / half)
    phases = time_own.astype(F32)[:, None] * frequency[None, :]
    cos, sin = jnp.cos(phases), jnp.sin(phases)
    cos = jnp.concatenate([cos] * 4, axis=1)
    sin = jnp.concatenate([-sin, sin, -sin, sin], axis=1)
    lane = (jnp.arange(128, dtype=jnp.int32) % HD)[None, :]
    seg_k = jnp.concatenate([seg_own, seg_oth])[:, None]
    var_k = jnp.concatenate([var_own, var_oth])[:, None]
    pad_k = jnp.concatenate([jnp.ones_like(pad_own), pad_oth])[:, None]
    is_var = lane < 2 * N_VAR
    is_seg = (lane >= L_SEG) & (lane < L_PAD)
    is_lse = (lane >= L_LSE) & (lane < L_LSE + 3)
    aug_k = jnp.where(
        is_var,
        jnp.where(var_k == lane % N_VAR, 1.0, 0.0),
        jnp.where(
            is_seg,
            jnp.where(seg_k == lane - L_SEG, 0.0, -BIG),
            jnp.where(
                lane == L_PAD, jnp.where(pad_k == 1, 0.0, -BIG), jnp.where(is_lse, 1.0, 0.0)
            ),
        ),
    ).astype(BF)
    aug_q = jnp.where(
        is_var,
        jnp.where(var_own[:, None] == lane % N_VAR, 1.0, 0.0),
        jnp.where(
            is_seg,
            jnp.where(seg_own[:, None] == lane - L_SEG, 1.0, 0.0),
            jnp.where(lane == L_PAD, 1.0, 0.0),
        ),
    ).astype(F32)
    place = jnp.arange(rows, dtype=jnp.int32)
    neg = jnp.where(pad_own == 1, 0.0, -BIG).astype(F32)
    eye = place[:, None] == place[None, :]
    add_q = jnp.where(eye, 0.0, neg[None, :])
    add_k = jnp.where(eye, 0.0, neg[:, None])
    var_q = jnp.where(
        var_own[None, :] == jnp.arange(8, dtype=jnp.int32)[:, None], 1.0, 0.0
    ).astype(F32)
    return cos, sin, aug_q, aug_k, add_q, add_k, var_q


def head_scales(var_bias):
    lane = (jnp.arange(128, dtype=jnp.int32) % HD)[None, :]
    delta = (var_bias[:, 0] - var_bias[:, 1]) * math.sqrt(HD)
    hi = delta.astype(BF).astype(F32)
    low = (delta - hi).astype(BF).astype(F32)
    return jnp.where(
        lane < N_VAR, hi[:, None], jnp.where(lane < 2 * N_VAR, low[:, None], 1.0)
    ).reshape(-1, 2, 128)


def small_rows(gg_a, gg_f, bias, ti, heads_local):
    bias = bias.sum(axis=-1).reshape(4, 2 * heads_local)
    bias = jnp.take(bias, jnp.array([0, 2, 1, 3])[jnp.arange(4) ^ ti], axis=0).reshape(1, -1)
    bias = jnp.pad(bias, ((0, 0), (0, gg_a.shape[1] - bias.shape[1])))
    return jnp.concatenate([gg_a, gg_f, bias], axis=0)


def attend_part(scale, state, tab):
    q, k, v, k_oth, v_oth = state
    _, _, aug_q, aug_k, head_scale, add_q, _, _ = tab
    return attend_call(scale, q, k, k_oth, v, v_oth, aug_q, aug_k, head_scale, add_q)


def per_device(
    boundary, w_qkv, w_out, w_gate_up, w_down, norm_gains, variate_bias,
    segment_ids, variate_ids, time_ids, padding_mask,
):
    ti = lax.axis_index("tensor")
    tn = lax.axis_size("tensor")
    yi, core = ti // 2, ti % 2
    n = lax.axis_size("dp")
    is_first = lax.axis_index("section") == 0
    local = boundary[0]
    rows, model = local.shape[1:]
    scale = LOG2E / math.sqrt(HD)
    cols = w_qkv.shape[1]
    near = cols == ZB
    width = w_qkv.shape[3]
    hidden = w_gate_up.shape[3]
    heads_local = variate_bias.shape[1]
    zi = (lax.axis_index("dp") if near else 0) * jnp.ones((1,), jnp.int32)

    def row_of(array):
        return lax.dynamic_index_in_dim(array, yi, 0, keepdims=False)

    away = lax.dynamic_index_in_dim(local, 1 - yi, 0, keepdims=False).astype(BF)
    own = row_of(local).astype(BF)
    p_qkv = w_qkv[0].transpose(1, 2, 0).reshape(3 * width, cols)
    p_bias = jnp.pad(variate_bias[0].reshape(1, -1), ((0, 0), (0, cols - 2 * heads_local)))
    p_small = jnp.pad(jnp.concatenate([norm_gains[0], p_bias], axis=0), ((0, 13), (0, 0)))
    low = 3 * width
    out_low = low + 16
    p1 = jnp.concatenate([p_qkv, p_small, w_out[0]], axis=0)
    p2 = w_gate_up[0].transpose(1, 2, 0).reshape(2 * hidden, cols)
    p3 = w_down[0]

    def both_ends(came):
        return jnp.where(
            yi == 0, jnp.concatenate([own, came], axis=0), jnp.concatenate([came, own], axis=0)
        )

    tab = tables(
        row_of(segment_ids), row_of(variate_ids), row_of(time_ids), row_of(padding_mask), core
    )

    if near:
        a1, came = ring(p1), y_swap(away)
        a1, came, p1, p2, p3 = meet(a1, came, p1, p2, p3)
        a2, y0 = ring(a1), y_swap(p1)
        a1, a2, y0, p2, p3, *tab = meet(a1, a2, y0, p2, p3, *tab)
        ends = both_ends(came)
        a3, y1 = ring(a2), y_swap(a1)
        n1 = [jnp.stack([p1, y0])]
        f1 = [core_swap(n1[0])]
        a2, a3, y1, p2, p3, ends = meet(a2, a3, y1, p2, p3, ends)
        b1, y2, d0 = ring(p2), y_swap(a2), y_swap(p3)
        n1.append(jnp.stack([a1, y1]))
        f1.append(core_swap(n1[1]))
        a3, b1, y2, d0, p2 = meet(a3, b1, y2, d0, p2)
        b2, y3 = ring(b1), y_swap(a3)
        n1.append(jnp.stack([a2, y2]))
        f1.append(core_swap(n1[2]))
        b1, b2, y3, p2, d0 = meet(b1, b2, y3, p2, d0)
        n1.append(jnp.stack([a3, y3]))
        f1.append(core_swap(n1[3]))
        w1 = n1 + f1
        b3, g0 = ring(b2), y_swap(p2)
    else:
        w1 = gather_any(p1)
        ends = both_ends(y_swap(away))
    gains = jnp.stack([w[0, low : low + 2] for w in w1[:4]])
    gains = jnp.take(gains, (zi[0] - jnp.arange(4)) % 4, axis=0)
    gains = gains.transpose(1, 0, 2).reshape(2, model).astype(F32)
    gain_a, gain_f = gains[:1], gains[1:]
    bias = [w[:, low + 2, : 2 * heads_local] for w in (w1[0], w1[4])]
    bias = jnp.concatenate(bias).reshape(4 * heads_local, 2).astype(F32)
    head_scale = head_scales(bias)
    cos, sin, aug_q, aug_k, add_q, add_k, var_q = tab
    tab = (cos, sin, aug_q, aug_k, head_scale, add_q, add_k, var_q)

    q, k, v = qkv_call(False, ends, gain_a, zi, w1, low, cos, sin)
    if near:
        b1, b2, b3, g0, d0, q, k, v = meet(b1, b2, b3, g0, d0, q, k, v)
        n3 = [jnp.stack([p3, d0])]
        c1, g1 = ring(n3[0]), y_swap(b1)
        n2 = [jnp.stack([p2, g0])]
        f2 = [core_swap(n2[0])]
        f3 = [core_swap(n3[0])]
    k_oth, v_oth = core_swap(k), core_swap(v)
    o, _ = attend_part(scale, (q, k, v, k_oth, v_oth), tab)
    if near:
        b2, b3, c1, g1, o = meet(b2, b3, c1, g1, o)
        c2, g2 = ring(c1), y_swap(b2)
        n2.append(jnp.stack([b1, g1]))
        f2.append(core_swap(n2[1]))
        f3.append(core_swap(c1))
        b3, c2, g2 = meet(b3, c2, g2)
        c3, g3 = ring(c2), y_swap(b3)
        n2.append(jnp.stack([b2, g2]))
        f2.append(core_swap(n2[2]))
        f3.append(core_swap(c2))
        b3, c3, g3 = meet(b3, c3, g3)
        n2.append(jnp.stack([b3, g3]))
        f2.append(core_swap(n2[3]))
        f3.append(core_swap(c3))
        w2, w3 = n2 + f2, n3 + [c1, c2, c3] + f3
    else:
        w2, w3 = gather_any(p2), gather_any(p3)
    h, z_near, z_far = ffn_up_call(False, out_low, width, ends, o, gain_f, zi, w1, w2)
    y_low = ffn_down_call(BF, h, z_near, z_far, zi, w3)
    got = lax.ppermute(y_low, "section", [(0, 1)])

    x = jnp.where(is_first, ends, got)
    n1, q, k, v, q0, k0 = qkv_call(True, x, gain_a, zi, w1, low, cos, sin)
    k_oth, v_oth = core_swap(k), core_swap(v)
    o, sums = attend_part(scale, (q, k, v, k_oth, v_oth), tab)
    h, z_near, z_far, n2, g, u = ffn_up_call(True, out_low, width, x, o, gain_f, zi, w1, w2)
    y = ffn_down_call(F32, h, z_near, z_far, zi, w3)

    def qkv_back(dq, dk, dk_got, dv, dv_got, dh):
        return qkv_back_call(
            dq, dk, dk_got, dv, dv_got, q0, k0, cos, sin, x, dh, gain_a, zi, w1, low
        )

    dh, _, do = ffn_back_call(out_low, width, ends, h, g, u, gain_f, zi, w1, w2, w3)[:3]
    dq, dk, dk_send, dv, dv_send, _ = attend_back_call(
        scale, None, q, k, k_oth, v, v_oth, do, o, sums, aug_q, aug_k, head_scale, add_k, var_q
    )
    dx_low = qkv_back(dq, dk, core_swap(dk_send), dv, core_swap(dv_send), dh)[3]
    got = lax.ppermute(dx_low, "section", [(1, 0)])
    z_oth, n2_oth, n1_oth = core_swap(z_far), core_swap(n2), core_swap(n1)
    o_oth = core_swap(o[:, 2 * width :])

    got, y, z_oth, n2_oth, n1_oth, o_oth = meet(got, y, z_oth, n2_oth, n1_oth, o_oth)

    df = jnp.where(is_first, got, ends)
    down_keep, down_send = wgrad_call(zi, hidden, z_near, df, z_oth, core_swap(df))
    df, down_keep, down_send = meet(df, down_keep, down_send)
    down_got = y_swap(down_send)
    back = ffn_back_call(out_low, width, df, h, g, u, gain_f, zi, w1, w2, w3)
    down_keep, down_got, *back = meet(down_keep, down_got, *back)
    dh, da, do, dg_near, dg_far, du_near, du_far, gg_f = back
    dg_oth, du_oth, da_oth = core_swap(dg_far), core_swap(du_far), core_swap(da)
    if near:
        down = [plus(down_keep[r], down_got[r]) for r in range(4)]
        down_run = ring(down[1])
    else:
        down_run = down_got
    dg_oth, du_oth, da_oth = meet(dg_oth, du_oth, da_oth)
    gate_keep, gate_send = wgrad_call(zi, hidden, dg_near, n2, dg_oth, n2_oth)
    down_run, do, gate_keep, gate_send, du_oth, da_oth = meet(
        down_run, do, gate_keep, gate_send, du_oth, da_oth
    )
    if near:
        gate_got = y_swap(gate_send)
        down_run = ring(plus(down_run, down[2]))
    out_keep, out_send = wgrad_call(zi, width, o, da, o_oth, da_oth)
    up_keep, up_send = wgrad_call(zi, hidden, du_near, n2, du_oth, n2_oth)
    do, out_keep, out_send, up_keep, up_send, down_run = meet(
        do, out_keep, out_send, up_keep, up_send, down_run
    )
    back = attend_back_call(
        scale, None, q, k, k_oth, v, v_oth, do, o, sums, aug_q, aug_k, head_scale, add_k, var_q
    )
    half = hidden // 32 * 16
    cut = width * 3 // 2
    if near:
        down_run = ring(plus(down_run, down[3]))
        out = [jnp.stack([out_keep[r], out_send[r]]) for r in range(4)]
        out_run = [to_owner(out[r], r) for r in (1, 2, 3)]
        gate_got, down_run, *rest = meet(gate_got, down_run, *out_run, *back)
        out_run, back = rest[:3], rest[3:]
    dq, dk, dk_send, dv, dv_send, bias = back
    dk_got, dv_got = core_swap(dk_send), core_swap(dv_send)
    if near:
        up_got = y_swap(up_send)
        gate = [plus(gate_keep[r], gate_got[r]) for r in range(4)]
        gate_run = [to_owner(gate[r], r) for r in (1, 2, 3)]
    back = qkv_back(dq, dk, dk_got, dv, dv_got, dh)
    if near:
        up_got, *rest = meet(up_got, *gate_run, *back)
        gate_run, back = rest[:3], rest[3:]
    dp_near, dp_far, dx, dx_low, gg_a = back
    dp_oth = core_swap(dp_far)
    qkv_keep, qkv_send = wgrad_call(zi, 3 * width, dp_near, n1, dp_oth, n1_oth)
    small = small_rows(gg_a, gg_f, bias, ti, heads_local)
    out_low_rows = jnp.where(is_first, dx_low, y.astype(BF))
    send = jnp.where(yi == 0, out_low_rows[rows:], out_low_rows[:rows])
    if near:
        up = [plus(up_keep[r, :half], up_got[r, :half]) for r in range(4)]
        up_run = [to_owner(up[r], r) for r in (1, 2, 3)]
        rows_got = y_swap(send)
        out_far = add_all(out[0][1], [run[1] for run in out_run]).astype(BF)
        out_got = y_swap(out_far)
        small = small + core_swap(small)
        rows_got, out_got, qkv_keep, qkv_send, small, *up_run = meet(
            rows_got, out_got, qkv_keep, qkv_send, small, *up_run
        )
        head_got = y_swap(qkv_send[:, :cut])
        more = [plus(up_keep[r, half:], up_got[r, half:]) for r in range(4)]
        more_run = [to_owner(more[r], r) for r in (1, 2, 3)]
        small = small + y_swap(small)
        head_got, small, *more_run = meet(head_got, small, *more_run)
        tail_got = y_swap(qkv_send[:, cut:])
        head = [plus(qkv_keep[r, :cut], head_got[r]) for r in range(4)]
        head_run = [to_owner(head[r], r) for r in (1, 2, 3)]
        small = small + lax.ppermute(small, "dp", [(i, i ^ 1) for i in range(4)])
        tail_got, small, down_run, out_got, *rest = meet(
            tail_got, small, down_run, out_got, *head_run, *gate_run, *out_run, *up_run, *more_run
        )
        head_run, gate_run, out_run, up_run, more_run = (rest[i : i + 3] for i in range(0, 15, 3))
        tail = [plus(qkv_keep[r, cut:], tail_got[r]) for r in range(4)]
        tail_run = [to_owner(tail[r], r) for r in (1, 2, 3)]
        small = small + lax.ppermute(small, "dp", [(i, i ^ 2) for i in range(4)])
        g_down = down_run.astype(F32) + down[0].astype(F32)
        g_up = [add_all(up[0], up_run), add_all(more[0], more_run)]
        g_gu = jnp.stack([add_all(gate[0], gate_run), jnp.concatenate(g_up, axis=0)])
        g_out = add_all(out[0][0], [run[0] for run in out_run] + [out_got])
        g_qkv = jnp.concatenate([add_all(head[0], head_run), add_all(tail[0], tail_run)], axis=0)
    else:
        rows_got = y_swap(send)
        g_down = scatter_any(down_keep, down_send)
        g_gu = jnp.stack([scatter_any(gate_keep, gate_send), scatter_any(up_keep, up_send)])
        g_out = scatter_any(out_keep, out_send)
        g_qkv = scatter_any(qkv_keep, qkv_send)
        small = small_sum(small)

    out_rows = jnp.where(is_first, dx, y)
    keep = jnp.where(yi == 0, out_rows[:rows], out_rows[rows:])
    back = rows_got.astype(F32)
    boundary_out = jnp.where(yi == 0, jnp.stack([keep, back]), jnp.stack([back, keep]))[None]
    piece = model // (n * tn)
    gain_piece = lax.dynamic_slice_in_dim(
        small[:2], (lax.axis_index("dp") * tn + ti) * piece, piece, 1
    )
    bias_piece = lax.dynamic_slice_in_dim(
        small[2, : 8 * heads_local].reshape(-1, 2), ti * heads_local, heads_local, 0
    )
    return (
        boundary_out,
        g_qkv.reshape(3, width, cols).transpose(2, 0, 1)[None],
        g_out[None],
        g_gu.transpose(2, 0, 1)[None],
        g_down[None],
        gain_piece[None],
        bias_piece[None],
    )


def solution(mesh):
    placed = (
        P("section", "dp", "tensor", None),
        P("section", "dp", None, "tensor"),
        P("section", "tensor", "dp"),
        P("section", "dp", None, "tensor"),
        P("section", "tensor", "dp"),
        P("section", None, "dp"),
        P("section", "tensor", None),
        P("dp", None),
        P("dp", None),
        P("dp", None),
        P("dp", None),
    )
    return jax.shard_map(
        per_device,
        mesh=mesh,
        in_specs=placed,
        out_specs=(
            P("section", "dp", "tensor", None),
            P("section", "dp", None, "tensor"),
            P("section", "tensor", "dp"),
            P("section", "dp", None, "tensor"),
            P("section", "tensor", "dp"),
            P("section", None, ("dp", "tensor")),
            P("section", "tensor", None),
        ),
        check_vma=False,
    )
```

```python
import functools
import math

import jax
import jax.numpy as jnp
from jax import lax
from jax.experimental import pallas as pl
from jax.experimental.pallas import tpu as pltpu
from jax.sharding import PartitionSpec as P

EPS = 1e-05
BIG = 8192.0
LOG2E = 1.4426950408889634
BF = jnp.bfloat16
F32 = jnp.float32
HD = 64
ZB = 256
VMEM_MB = 56
N_VAR = 4
L_SEG = 8
L_PAD = 24
L_LSE = 25


def dot(a, b):
    return lax.dot_general(a, b, (((1,), (0,)), ((), ())), preferred_element_type=F32)


def dot_nt(a, b):
    return lax.dot_general(a, b, (((1,), (1,)), ((), ())), preferred_element_type=F32)


def dot_tn(a, b):
    return lax.dot_general(a, b, (((0,), (0,)), ((), ())), preferred_element_type=F32)


def params(mb=VMEM_MB):
    return pltpu.CompilerParams(
        dimension_semantics=("arbitrary",), vmem_limit_bytes=mb * 1024 * 1024
    )


def cost(flops, nbytes, trans=0):
    return pl.CostEstimate(flops=int(flops), bytes_accessed=int(nbytes), transcendentals=0)


def sds(shape, dtype):
    return jax.ShapeDtypeStruct(shape, dtype)


def whole(shape):
    zeros = (0,) * len(shape)
    return pl.BlockSpec(shape, lambda *_: zeros)


def head_sum(u):
    row = lax.broadcasted_iota(jnp.int32, (u.shape[1], u.shape[1]), 0) // HD
    col = lax.broadcasted_iota(jnp.int32, (u.shape[1], u.shape[1]), 1) // HD
    return dot(u.astype(BF), jnp.where(row == col, 1.0, 0.0).astype(BF))


def half_swap(u):
    lane = lax.broadcasted_iota(jnp.int32, u.shape, 1) % HD
    return jnp.where(lane < HD // 2, pltpu.roll(u, 128 - HD // 2, 1), pltpu.roll(u, HD // 2, 1))


def row_rms(x):
    return lax.rsqrt(jnp.mean(x * x, axis=-1, keepdims=True) + EPS)


def hbm():
    return pl.BlockSpec(memory_space=pl.ANY)


def smem():
    return pl.BlockSpec(memory_space=pltpu.SMEM)


def copies(refs, low, scratch, sems, t):
    rows = pl.ds(low, scratch.shape[2])
    return [
        pltpu.make_async_copy(
            refs[4 * (t // 2) + r].at[t % 2, rows], scratch.at[r, t], sems.at[r, t]
        )
        for r in range(4)
    ]


def start_all(refs, low, scratch, sems, shards=range(4)):
    for t in shards:
        for copy in copies(refs, low, scratch, sems, t):
            copy.start()


def wait_for(refs, low, scratch, sems, t):
    for fixed in range(4):

        @pl.when(t == fixed)
        def _():
            for copy in copies(refs, low, scratch, sems, fixed):
                copy.wait()


def weight_scratch(feats):
    return [pltpu.VMEM((4, 4, feats, ZB), BF), pltpu.SemaphoreType.DMA((4, 4))]


def place(zi_ref, r):
    return lax.rem(zi_ref[0] - r + 4, 4)


def block_store(ref, value):
    for z in range(4):
        ref[z] = value[:, z * ZB : (z + 1) * ZB]


def chunks(wide, step=ZB):
    return [slice(low, min(low + step, wide)) for low in range(0, wide, step)]


def block_load(ref):
    return jnp.concatenate([ref[z] for z in range(4)], axis=1)


def qkv_kernel(save, x_ref, gain_ref, zi_ref, cos_ref, sin_ref, *refs):
    weight, refs = refs[:8], refs[8:]
    if save:
        n_ref, q_ref, k_ref, v_ref, q0_ref, k0_ref, n_scr, w_ref, sems = refs
    else:
        q_ref, k_ref, v_ref, n_scr, w_ref, sems = refs
    t = pl.program_id(0)

    @pl.when(t == 0)
    def _():
        start_all(weight, 0, w_ref, sems, range(1))
        x = x_ref[...].astype(F32)
        n = (x * row_rms(x) * gain_ref[...]).astype(BF)
        block_store(n_scr, n)
        if save:
            n_ref[...] = n

    wait_for(weight, 0, w_ref, sems, t)

    @pl.when(t == 0)
    def _():
        start_all(weight, 0, w_ref, sems, range(1, 4))

    width = q_ref.shape[1]

    def project(which):
        cols = slice(which * width, (which + 1) * width)
        total = dot_nt(n_scr[place(zi_ref, 0)], w_ref[0, t, cols])
        for r in range(1, 4):
            total = total + dot_nt(n_scr[place(zi_ref, r)], w_ref[r, t, cols])
        return total

    cos, sin = cos_ref[...], sin_ref[...]
    for which, out in ((0, q_ref), (1, k_ref)):
        u = project(which)
        if save:
            kept = q0_ref if which == 0 else k0_ref
            kept[...] = u.astype(BF)
        un = u * lax.rsqrt(head_sum(u * u) * (1.0 / HD) + EPS)
        for pair in range(width // 128):
            at = slice(pair * 128, (pair + 1) * 128)
            out[:, at] = (un[:, at] * cos + half_swap(un[:, at]) * sin).astype(BF)
    v_ref[...] = project(2).astype(BF)


def qkv_call(save, x, gain, zi, w, feats, cos, sin):
    rows, model = x.shape
    width = feats // 3
    total = 4 * width
    col = pl.BlockSpec((rows, width), lambda t: (0, t))
    outs = [sds((rows, total), BF)] * 3
    specs = [col] * 3
    if save:
        outs = [sds((rows, model), BF)] + outs + [sds((rows, total), BF)] * 2
        specs = [whole((rows, model))] + specs + [col] * 2
    return pl.pallas_call(
        functools.partial(qkv_kernel, save),
        grid=(4,),
        in_specs=[whole((rows, model)), whole((1, model)), smem()]
        + [whole((rows, 128))] * 2
        + [hbm()] * 8,
        out_specs=specs,
        out_shape=outs,
        scratch_shapes=[pltpu.VMEM((4, rows, ZB), BF)] + weight_scratch(feats),
        compiler_params=params(),
        cost_estimate=cost(2 * rows * model * 3 * total, 6 * total * model + 16 * x.size),
    )(x, gain, zi, cos, sin, *w)


def other_core_spec(rows, pairs):
    half = pairs // 2
    return pl.BlockSpec((rows, 128), lambda p: (0, lax.rem(p + half, pairs)))


def pick(first, h, a, b):
    return jnp.where(first, a, b) if h == 0 else jnp.where(first, b, a)


def pick_low(first, h, a, b):
    mine = jnp.where(first, 1.0, 0.0) if h == 0 else jnp.where(first, 0.0, 1.0)
    low = mine.astype(BF)
    return a * low + b * (1.0 - mine).astype(BF)


def attend_kernel(
    scale, q_ref, ko_ref, kx_ref, vo_ref, vx_ref, aq_ref, ak_ref, hs_ref, add_ref, o_ref, l_ref
):
    rows = q_ref.shape[0]
    kb = 128
    first = lax.broadcasted_iota(jnp.int32, (1, 128), 1) < HD
    q = q_ref[...].astype(F32)
    base = aq_ref[...]
    raws = []
    for h in range(2):
        qh = pick(first, h, q, base * hs_ref[0, h : h + 1, :]).astype(BF)
        total = None
        for half, (k_ref, v_ref) in enumerate(((ko_ref, vo_ref), (kx_ref, vx_ref))):
            for block in range(rows // kb):
                at = slice(block * kb, (block + 1) * kb)
                kk = slice(half * rows + block * kb, half * rows + (block + 1) * kb)
                kh = pick_low(first, h, k_ref[at, :], ak_ref[kk, :])
                vh = pick_low(first, h, v_ref[at, :], BF(1.0))
                s = dot_nt(qh, kh)
                if half == 0:
                    s = s + add_ref[:, at]
                part = dot(jnp.exp2(s * scale).astype(BF), vh)
                total = part if total is None else total + part
        raws.append(total)
    sums = jnp.where(first, raws[1], raws[0])
    l_ref[...] = sums
    o_ref[...] = (jnp.where(first, raws[0], raws[1]) / pltpu.roll(sums, HD, 1)).astype(BF)


def attend_call(scale, q, k_own, k_oth, v_own, v_oth, aug_q, aug_k, head_scale, add_own):
    rows, total = q.shape
    pairs = total // 128
    col = pl.BlockSpec((rows, 128), lambda p: (0, p))
    far = other_core_spec(rows, pairs)
    return pl.pallas_call(
        functools.partial(attend_kernel, scale),
        grid=(pairs,),
        in_specs=[
            col,
            col,
            far,
            col,
            far,
            whole(aug_q.shape),
            whole(aug_k.shape),
            pl.BlockSpec((1, 2, 128), lambda p: (p, 0, 0)),
            whole(add_own.shape),
        ],
        out_specs=[col, col],
        out_shape=[sds((rows, total), BF), sds((rows, total), F32)],
        compiler_params=params(),
        cost_estimate=cost(
            4 * 2 * rows * rows * 2 * total, 20 * rows * total, rows * rows * 2 * pairs * 2
        ),
    )(q, k_own, k_oth, v_own, v_oth, aug_q, aug_k, head_scale, add_own)


def padded(hidden):
    return -(-2 * hidden // 128) * 128


def pair_scratch(parts, hidden):
    return [
        pltpu.VMEM((4, 2, parts * padded(hidden), ZB), BF),
        pltpu.SemaphoreType.DMA((4, 2, 2, parts)),
    ]


def pair_copies(refs, parts, scratch, sems, half):
    wide = scratch.shape[2] // parts
    hidden = refs[0].shape[1] // parts
    return [
        pltpu.make_async_copy(
            refs[4 * half + r].at[y, pl.ds(part * hidden, hidden)],
            scratch.at[r, half, pl.ds(part * wide + y * hidden, hidden)],
            sems.at[r, half, y, part],
        )
        for r in range(4)
        for y in range(2)
        for part in range(parts)
    ]


def pair_start(refs, parts, scratch, sems, halves=range(2)):
    wide = scratch.shape[2] // parts
    hidden = refs[0].shape[1] // parts
    for half in halves:
        for copy in pair_copies(refs, parts, scratch, sems, half):
            copy.start()
    blank = wide - 2 * hidden
    if blank:
        for half in halves:
            for r in range(4):
                for part in range(parts):
                    low = part * wide + 2 * hidden
                    scratch[r, half, low : low + blank] = jnp.zeros((blank, ZB), BF)


def pair_wait(refs, parts, scratch, sems, half):
    for fixed in range(2):

        @pl.when(half == fixed)
        def _():
            for copy in pair_copies(refs, parts, scratch, sems, fixed):
                copy.wait()


def near_far(rows, feats):
    return (
        pl.BlockSpec((1, rows, feats), lambda t: (jnp.minimum(t, 1), 0, 0)),
        pl.BlockSpec((1, rows, feats), lambda t: (jnp.maximum(t - 2, 0), 0, 0)),
    )


def put(is_near, near_ref, far_ref, value, at=...):
    @pl.when(is_near)
    def _():
        near_ref[at] = value

    @pl.when(jnp.logical_not(is_near))
    def _():
        far_ref[at] = value


def ffn_up_kernel(save, out_low, x_ref, o_ref, gain_ref, zi_ref, *refs):
    wo, wgu, refs = refs[:8], refs[8:16], refs[16:]
    if save:
        h_ref, zn_ref, zf_ref, n_ref, g_ref, u_ref = refs[:6]
    else:
        h_ref, zn_ref, zf_ref = refs[:3]
    n_scr, wo_ref, wo_sems, wgu_ref, wgu_sems, acc, z_scr = refs[-7:]
    wide = wgu_ref.shape[2] // 2
    half = pl.program_id(0)

    @pl.when(half == 0)
    def _():
        start_all(wo, out_low, wo_ref, wo_sems)
        pair_start(wgu, 2, wgu_ref, wgu_sems, range(1))
        width = wo_ref.shape[2]
        block_store(acc, x_ref[...].astype(F32))
        for s in range(4):
            for copy in copies(wo, out_low, wo_ref, wo_sems, s):
                copy.wait()
        pair_start(wgu, 2, wgu_ref, wgu_sems, range(1, 2))
        for r in range(4):
            z = place(zi_ref, r)
            h = acc[z]
            for s in range(4):
                h = h + dot(o_ref[:, s * width : (s + 1) * width], wo_ref[r, s])
            acc[z] = h
        h = block_load(acc)
        n = (h * row_rms(h) * gain_ref[...]).astype(BF)
        block_store(n_scr, n)
        h_ref[...] = h
        if save:
            n_ref[...] = n

    pair_wait(wgu, 2, wgu_ref, wgu_sems, half)
    for at in chunks(wide):
        total = []
        for part in range(2):
            cols = slice(part * wide + at.start, part * wide + at.stop)
            one = dot_nt(n_scr[place(zi_ref, 0)], wgu_ref[0, half, cols])
            for r in range(1, 4):
                one = one + dot_nt(n_scr[place(zi_ref, r)], wgu_ref[r, half, cols])
            total.append(one)
        gate, up = total
        z_scr[:, at] = (gate / (1.0 + jnp.exp(-gate)) * up).astype(BF)
        if save:
            g_ref[0, :, at] = gate.astype(BF)
            u_ref[0, :, at] = up.astype(BF)
    put(half == 0, zn_ref, zf_ref, z_scr[...])


def ffn_up_call(save, out_low, width, x, o, gain, zi, wo, wgu):
    rows, model = x.shape
    hidden = wgu[0].shape[1] // 2
    wide = padded(hidden)
    big = whole((rows, model))
    part = pl.BlockSpec((1, rows, wide), lambda t: (t, 0, 0))
    outs = [sds((rows, model), F32)] + [sds((rows, wide), BF)] * 2
    specs = [big, whole((rows, wide)), whole((rows, wide))]
    if save:
        outs += [sds((rows, model), BF)] + [sds((2, rows, wide), BF)] * 2
        specs += [big, part, part]
    return pl.pallas_call(
        functools.partial(ffn_up_kernel, save, out_low),
        grid=(2,),
        in_specs=[big, whole(o.shape), whole((1, model)), smem()] + [hbm()] * 16,
        out_specs=specs,
        out_shape=outs,
        scratch_shapes=[pltpu.VMEM((4, rows, ZB), BF)]
        + weight_scratch(width)
        + pair_scratch(2, hidden)
        + [pltpu.VMEM((4, rows, ZB), F32), pltpu.VMEM((rows, wide), BF)],
        compiler_params=params(),
        cost_estimate=cost(
            2 * rows * model * (8 * hidden + model), 16 * hidden * model + 20 * x.size
        ),
    )(x, o, gain, zi, *wo, *wgu)


def ffn_down_kernel(h_ref, zn_ref, zf_ref, zi_ref, *refs):
    weight, (y_ref, w_ref, sems) = refs[:8], refs[8:]
    pair_start(weight, 1, w_ref, sems)
    for half, z_ref in enumerate((zn_ref, zf_ref)):
        for copy in pair_copies(weight, 1, w_ref, sems, half):
            copy.wait()
    for z in range(4):
        r = lax.rem(zi_ref[0] - z + 4, 4)
        at = slice(z * ZB, (z + 1) * ZB)
        y = h_ref[:, at] + dot(zn_ref[...], w_ref[r, 0]) + dot(zf_ref[...], w_ref[r, 1])
        y_ref[:, at] = y.astype(y_ref.dtype)


def ffn_down_call(dtype, h, z_near, z_far, zi, wd):
    rows, model = h.shape
    hidden = wd[0].shape[1]
    vmem = pl.BlockSpec(memory_space=pltpu.VMEM)
    return pl.pallas_call(
        ffn_down_kernel,
        in_specs=[vmem] * 3 + [smem()] + [hbm()] * 8,
        out_specs=vmem,
        out_shape=sds((rows, model), dtype),
        scratch_shapes=pair_scratch(1, hidden),
        compiler_params=pltpu.CompilerParams(vmem_limit_bytes=VMEM_MB * 1024 * 1024),
        cost_estimate=cost(2 * rows * model * 4 * hidden, 8 * hidden * model + 8 * h.size),
    )(h, z_near, z_far, zi, *wd)


def ffn_back_kernel(out_low, dy_ref, h_ref, g_ref, u_ref, gain_ref, zi_ref, *refs):
    wo, wgu, wd, refs = refs[:8], refs[8:16], refs[16:24], refs[24:]
    dh_ref, da_ref, do_ref, dgn_ref, dgf_ref, dun_ref, duf_ref, gg_ref = refs[:8]
    df_scr, acc, wo_ref, wo_sems, wgu_ref, wgu_sems, wd_ref, wd_sems, dg_scr, du_scr = refs[8:]
    wide = wd_ref.shape[2]
    half = pl.program_id(0)

    @pl.when(half == 0)
    def _():
        pair_start(wd, 1, wd_ref, wd_sems, range(1))
        block_store(df_scr, dy_ref[...])
        acc[...] = jnp.zeros_like(acc)

    pair_wait(wd, 1, wd_ref, wd_sems, half)

    @pl.when(half == 0)
    def _():
        pair_start(wgu, 2, wgu_ref, wgu_sems, range(1))
        pair_start(wd, 1, wd_ref, wd_sems, range(1, 2))
        pair_start(wgu, 2, wgu_ref, wgu_sems, range(1, 2))
        start_all(wo, out_low, wo_ref, wo_sems)

    for at in chunks(wide):
        dz = dot_nt(df_scr[place(zi_ref, 0)], wd_ref[0, half, at])
        for r in range(1, 4):
            dz = dz + dot_nt(df_scr[place(zi_ref, r)], wd_ref[r, half, at])
        gate = g_ref[0, :, at].astype(F32)
        up = u_ref[0, :, at].astype(F32)
        s = 1.0 / (1.0 + jnp.exp(-gate))
        dg_scr[:, at] = (dz * up * s * (1.0 + gate * (1.0 - s))).astype(BF)
        du_scr[:, at] = (dz * gate * s).astype(BF)
    dgate, dup = dg_scr[...], du_scr[...]
    put(half == 0, dgn_ref, dgf_ref, dgate)
    put(half == 0, dun_ref, duf_ref, dup)
    pair_wait(wgu, 2, wgu_ref, wgu_sems, half)
    for r in range(4):
        z = place(zi_ref, r)
        acc[z] = acc[z] + (
            dot(dgate, wgu_ref[r, half, :wide]) + dot(dup, wgu_ref[r, half, wide:])
        )

    @pl.when(half == 1)
    def _():
        h = h_ref[...]
        r = row_rms(h)
        hn = h * r
        dn = block_load(acc)
        gg_ref[...] = jnp.sum(dn * hn, axis=0, keepdims=True)
        dhat = dn * gain_ref[...]
        dh = dy_ref[...].astype(F32) + r * (
            dhat - hn * jnp.mean(dhat * hn, axis=-1, keepdims=True)
        )
        dh_ref[...] = dh
        da = dh.astype(BF)
        da_ref[...] = da
        block_store(df_scr, da)
        width = wo_ref.shape[2]
        for s in range(4):
            for copy in copies(wo, out_low, wo_ref, wo_sems, s):
                copy.wait()
        for s in range(4):
            part = dot_nt(df_scr[place(zi_ref, 0)], wo_ref[0, s])
            for q in range(1, 4):
                part = part + dot_nt(df_scr[place(zi_ref, q)], wo_ref[q, s])
            do_ref[:, s * width : (s + 1) * width] = part.astype(BF)


def ffn_back_call(out_low, width, dy, h, g, u, gain, zi, wo, wgu, wd):
    rows, model = dy.shape
    hidden = wd[0].shape[1]
    wide = g.shape[2]
    big = whole((rows, model))
    part = pl.BlockSpec((1, rows, wide), lambda t: (t, 0, 0))
    return pl.pallas_call(
        functools.partial(ffn_back_kernel, out_low),
        grid=(2,),
        in_specs=[big, big, part, part, whole((1, model)), smem()] + [hbm()] * 24,
        out_specs=[big, big, big] + [whole((rows, wide))] * 4 + [whole((1, model))],
        out_shape=[sds((rows, model), F32), sds((rows, model), BF), sds((rows, model), BF)]
        + [sds((rows, wide), BF)] * 4
        + [sds((1, model), F32)],
        scratch_shapes=[pltpu.VMEM((4, rows, ZB), BF), pltpu.VMEM((4, rows, ZB), F32)]
        + weight_scratch(width)
        + pair_scratch(2, hidden)
        + pair_scratch(1, hidden)
        + [pltpu.VMEM((rows, wide), BF)] * 2,
        compiler_params=params(57),
        cost_estimate=cost(
            2 * rows * model * (12 * hidden + model), 24 * hidden * model + 20 * dy.size
        ),
    )(dy, h, g, u, gain, zi, *wo, *wgu, *wd)


def split3(value):
    hi = value.astype(BF).astype(F32)
    mid = (value - hi).astype(BF).astype(F32)
    return hi, mid, value - hi - mid


def attend_back_kernel(
    scale, q_ref, ko_ref, kx_ref, vo_ref, vx_ref, do_ref, o_ref, l_ref, aq_ref, ak_ref, hs_ref,
    add_ref, var_ref, dq_ref, dko_ref, dkx_ref, dvo_ref, dvx_ref, bias_ref,
):
    rows = q_ref.shape[0]
    kb = 512
    first = lax.broadcasted_iota(jnp.int32, (1, 128), 1) < HD
    lane = lax.broadcasted_iota(jnp.int32, (1, 128), 1) % HD
    q = q_ref[...].astype(F32)
    do = do_ref[...].astype(F32)
    inner = do * o_ref[...].astype(F32)
    base = aq_ref[...]
    hi, mid, low = split3(jnp.log2(l_ref[...]) * (-1.0 / scale))
    lse = jnp.where(lane == L_LSE, hi, 0.0)
    lse = jnp.where(lane == L_LSE + 1, mid, lse)
    lse = jnp.where(lane == L_LSE + 2, low, lse)
    dq_t = []
    dk = [[], []]
    dv = [[], []]
    for h in range(2):
        qh = pick(first, h, q, base * hs_ref[0, h : h + 1, :] + lse).astype(BF)
        d = jnp.sum(pick(first, h, inner, 0.0), axis=-1, keepdims=True)
        dhi, dmid, dlow = split3(-d)
        d_aug = jnp.where(lane == 0, dhi, 0.0)
        d_aug = jnp.where(lane == 1, dmid, d_aug)
        d_aug = jnp.where(lane == 2, dlow, d_aug)
        doh = pick(first, h, do, d_aug).astype(BF)
        total = None
        for half, (k_ref, v_ref) in enumerate(((ko_ref, vo_ref), (kx_ref, vx_ref))):
            for block in range(rows // kb):
                at = slice(block * kb, (block + 1) * kb)
                kk = slice(half * rows + block * kb, half * rows + (block + 1) * kb)
                kh = pick_low(first, h, k_ref[at, :], ak_ref[kk, :])
                vh = pick_low(first, h, v_ref[at, :], BF(1.0))
                s = dot_nt(kh, qh)
                if half == 0:
                    s = s + add_ref[at, :]
                p = jnp.exp2(s * scale)
                ds = (p * dot_nt(vh, doh)).astype(BF)
                dv[h].append(dot(p.astype(BF), doh))
                dk[h].append(dot(ds, qh))
                part = dot_tn(kh, ds)
                total = part if total is None else total + part
        dq_t.append(total)
    scale_back = 1.0 / math.sqrt(HD)
    count = rows // kb
    for half, (dk_ref, dv_ref) in enumerate(((dko_ref, dvo_ref), (dkx_ref, dvx_ref))):
        for block in range(count):
            at = slice(block * kb, (block + 1) * kb)
            i = half * count + block
            dk_ref[at, :] = (jnp.where(first, dk[0][i], dk[1][i]) * scale_back).astype(dk_ref.dtype)
            dv_ref[at, :] = jnp.where(first, dv[0][i], dv[1][i]).astype(dv_ref.dtype)
    joined = jnp.concatenate([dq_t[0][:HD], dq_t[1][HD:]], axis=0)
    dq_ref[...] = (joined.T * scale_back).astype(BF)
    mine = var_ref[...]
    for h in range(2):
        begin = HD if h == 0 else 0
        r = dq_t[h][begin : begin + 8]
        same = jnp.sum(r * mine, axis=0, keepdims=True)
        every = jnp.sum(r[:N_VAR], axis=0, keepdims=True)
        bias_ref[0, 2 * h : 2 * h + 1, :] = same
        bias_ref[0, 2 * h + 1 : 2 * h + 2, :] = every - same


def attend_back_call(
    scale, span, q, k_own, k_oth, v_own, v_oth, do, o, sums, aug_q, aug_k, head_scale, add_own, var_q
):
    rows, total = q.shape
    every = total // 128
    low, high = span or (0, every)
    pairs = high - low
    total = pairs * 128
    col = pl.BlockSpec((rows, 128), lambda p: (0, p + low))
    far = pl.BlockSpec((rows, 128), lambda p: (0, lax.rem(p + low + every // 2, every)))
    out = pl.BlockSpec((rows, 128), lambda p: (0, p))
    out_far = other_core_spec(rows, pairs) if span is None else out
    return pl.pallas_call(
        functools.partial(attend_back_kernel, scale),
        grid=(pairs,),
        in_specs=[col, col, far, col, far, col, col, col]
        + [
            whole(aug_q.shape),
            whole(aug_k.shape),
            pl.BlockSpec((1, 2, 128), lambda p: (p + low, 0, 0)),
            whole(add_own.shape),
            whole(var_q.shape),
        ],
        out_specs=[out, out, out_far, out, out_far] + [pl.BlockSpec((1, 4, rows), lambda p: (p, 0, 0))],
        out_shape=[
            sds((rows, total), BF),
            sds((rows, total), BF),
            sds((rows, total), BF),
            sds((rows, total), BF),
            sds((rows, total), BF),
            sds((pairs, 4, rows), F32),
        ],
        compiler_params=params(),
        cost_estimate=cost(
            10 * 2 * rows * rows * 2 * total, 40 * rows * total, rows * rows * 2 * pairs * 2
        ),
    )(q, k_own, k_oth, v_own, v_oth, do, o, sums, aug_q, aug_k, head_scale, add_own, var_q)


def qkv_back_kernel(
    dq_ref, dk_ref, dkr_ref, dv_ref, dvr_ref, q0_ref, k0_ref, cos_ref, sin_ref, x_ref, dh_ref,
    gain_ref, zi_ref, *refs,
):
    weight, refs = refs[:8], refs[8:]
    dpn_ref, dpf_ref, dx_ref, dxl_ref, gg_ref, dp_scr, acc, w_ref, sems = refs
    width = dq_ref.shape[1]
    t = pl.program_id(0)

    @pl.when(t == 0)
    def _():
        start_all(weight, 0, w_ref, sems)
        acc[...] = jnp.zeros_like(acc)

    cos, sin = cos_ref[...], sin_ref[...]
    for which in range(2):
        u = (q0_ref if which == 0 else k0_ref)[...].astype(F32)
        r = lax.rsqrt(head_sum(u * u) * (1.0 / HD) + EPS)
        un = u * r
        turned = []
        for pair in range(width // 128):
            at = slice(pair * 128, (pair + 1) * 128)
            if which == 0:
                grad = dq_ref[:, at].astype(F32)
            else:
                grad = dk_ref[:, at].astype(F32) + dkr_ref[:, at].astype(F32)
            turned.append(grad * cos - half_swap(grad) * sin)
        grad = jnp.concatenate(turned, axis=1)
        out = r * (grad - un * (head_sum(grad * un) * (1.0 / HD)))
        dp_scr[:, which * width : (which + 1) * width] = out.astype(BF)
    dp_scr[:, 2 * width :] = (dv_ref[...].astype(F32) + dvr_ref[...].astype(F32)).astype(BF)
    wait_for(weight, 0, w_ref, sems, t)
    dp = dp_scr[...]
    put(t < 2, dpn_ref, dpf_ref, dp, 0)
    for r in range(4):
        z = place(zi_ref, r)
        acc[z] = acc[z] + dot(dp, w_ref[r, t])

    @pl.when(t == 3)
    def _():
        x = x_ref[...].astype(F32)
        r = row_rms(x)
        xn = x * r
        dn = block_load(acc)
        gg_ref[...] = jnp.sum(dn * xn, axis=0, keepdims=True)
        dhat = dn * gain_ref[...]
        dx = dh_ref[...] + r * (dhat - xn * jnp.mean(dhat * xn, axis=-1, keepdims=True))
        dx_ref[...] = dx
        dxl_ref[...] = dx.astype(BF)


def qkv_back_call(dq, dk, dkr, dv, dvr, q0, k0, cos, sin, x, dh, gain, zi, w, feats):
    rows, model = x.shape
    width = feats // 3
    big = whole((rows, model))
    col = pl.BlockSpec((rows, width), lambda t: (0, t))
    return pl.pallas_call(
        qkv_back_kernel,
        grid=(4,),
        in_specs=[col] * 7
        + [whole((rows, 128)), whole((rows, 128)), big, big, whole((1, model)), smem()]
        + [hbm()] * 8,
        out_specs=[*near_far(rows, feats), big, big, whole((1, model))],
        out_shape=[sds((2, rows, feats), BF)] * 2
        + [sds((rows, model), F32), sds((rows, model), BF), sds((1, model), F32)],
        scratch_shapes=[pltpu.VMEM((rows, feats), BF), pltpu.VMEM((4, rows, ZB), F32)]
        + weight_scratch(feats),
        compiler_params=params(),
        cost_estimate=cost(8 * rows * model * feats, 8 * feats * model + 40 * x.size),
    )(dq, dk, dkr, dv, dvr, q0, k0, cos, sin, x, dh, gain, zi, *w)


def wgrad_kernel(feats, zi_ref, ao_ref, bo_ref, ax_ref, bx_ref, keep_ref, send_ref):
    if len(ao_ref.shape) == 3:
        for i, out in ((1, send_ref), (0, keep_ref)):
            g = dot_tn(ao_ref[i], bo_ref[...]) + dot_tn(ax_ref[i], bx_ref[...])
            for z in range(4):
                out[lax.rem(zi_ref[0] - z + 4, 4)] = g[:, z * ZB : (z + 1) * ZB].astype(BF)
    else:
        g = dot_tn(ao_ref[...], bo_ref[...]) + dot_tn(ax_ref[...], bx_ref[...])
        for z in range(4):
            r = lax.rem(zi_ref[0] - z + 4, 4)
            at = slice(z * ZB, (z + 1) * ZB)
            keep_ref[r] = g[:feats, at].astype(BF)
            send_ref[r] = g[feats : 2 * feats, at].astype(BF)


def wgrad_call(zi, feats, a_own, b_own, a_oth, b_oth):
    rows, model = b_own.shape
    part = whole(a_oth.shape)
    big = whole((rows, model))
    out = whole((4, feats, ZB))
    return pl.pallas_call(
        functools.partial(wgrad_kernel, feats),
        grid=(1,),
        in_specs=[smem(), part, big, part, big],
        out_specs=[out, out],
        out_shape=[sds((4, feats, ZB), BF)] * 2,
        compiler_params=params(26),
        cost_estimate=cost(8 * rows * feats * model, 4 * feats * model),
    )(zi, a_own, b_own, a_oth, b_oth)


def core_swap(value):
    n = lax.axis_size("tensor")
    return lax.ppermute(value, "tensor", [(i, i ^ 1) for i in range(n)])


def y_swap(value):
    n = lax.axis_size("tensor")
    return lax.ppermute(value, "tensor", [(i, i ^ 2) for i in range(n)])


def ring(value):
    n = lax.axis_size("dp")
    return lax.ppermute(value, "dp", [(i, (i + 1) % n) for i in range(n)])


def gather_any(piece):
    ti = lax.axis_index("tensor")
    every = lax.all_gather(lax.all_gather(piece, "dp"), "tensor")
    tn, n, feats, cols = every.shape
    every = every.transpose(0, 2, 1, 3).reshape(tn, feats, n * cols // ZB, ZB)
    every = jnp.take(every, ti ^ jnp.array([0, 2, 1, 3]), axis=0)
    every = jnp.take(every, jnp.array([0, 3, 2, 1]), axis=2).transpose(2, 0, 1, 3)
    return [every[r, :2] for r in range(4)] + [every[r, 2:] for r in range(4)]


def meet(*values):
    return list(lax.optimization_barrier(values))


def after(value, *others):
    return lax.optimization_barrier((value, others))[0]


def to_owner(part, r):
    n = lax.axis_size("dp")
    return lax.ppermute(part, "dp", [(i, (i - r) % n) for i in range(n)])


def add_all(own, others):
    total = own.astype(F32)
    for other in others:
        total = total + other.astype(F32)
    return total


def scatter_any(keep, send):
    total = keep.astype(F32) + y_swap(send).astype(F32)
    total = jnp.take(total, jnp.array([0, 3, 2, 1]), axis=0)
    flat = total.transpose(1, 0, 2).reshape(total.shape[1], -1).astype(BF)
    return lax.psum_scatter(flat, "dp", scatter_dimension=1, tiled=True).astype(F32)


def plus(a, b):
    return (a.astype(F32) + b.astype(F32)).astype(BF)


def small_sum(value):
    n = lax.axis_size("dp")
    value = value + core_swap(value)
    value = value + y_swap(value)
    if n & (n - 1):
        return lax.psum(value, "dp")
    bit = 1
    while bit < n:
        value = value + lax.ppermute(value, "dp", [(i, i ^ bit) for i in range(n)])
        bit *= 2
    return value


def own_rows(row, core):
    quarters = row.reshape(2, 2, row.shape[0] // 4)
    own = lax.dynamic_index_in_dim(quarters, core, 1, keepdims=False).reshape(-1)
    oth = lax.dynamic_index_in_dim(quarters, 1 - core, 1, keepdims=False).reshape(-1)
    return own, oth


def tables(segment, variate, time_row, pad, core):
    seg_own, seg_oth = own_rows(segment, core)
    var_own, var_oth = own_rows(variate, core)
    pad_own, pad_oth = own_rows(pad, core)
    time_own, _ = own_rows(time_row, core)
    rows = seg_own.shape[0]
    half = HD // 2
    frequency = jnp.exp(-jnp.log(10000.0) * jnp.arange(half, dtype=F32) / half)
    phases = time_own.astype(F32)[:, None] * frequency[None, :]
    cos, sin = jnp.cos(phases), jnp.sin(phases)
    cos = jnp.concatenate([cos] * 4, axis=1)
    sin = jnp.concatenate([-sin, sin, -sin, sin], axis=1)
    lane = (jnp.arange(128, dtype=jnp.int32) % HD)[None, :]
    seg_k = jnp.concatenate([seg_own, seg_oth])[:, None]
    var_k = jnp.concatenate([var_own, var_oth])[:, None]
    pad_k = jnp.concatenate([jnp.ones_like(pad_own), pad_oth])[:, None]
    is_var = lane < 2 * N_VAR
    is_seg = (lane >= L_SEG) & (lane < L_PAD)
    is_lse = (lane >= L_LSE) & (lane < L_LSE + 3)
    aug_k = jnp.where(
        is_var,
        jnp.where(var_k == lane % N_VAR, 1.0, 0.0),
        jnp.where(
            is_seg,
            jnp.where(seg_k == lane - L_SEG, 0.0, -BIG),
            jnp.where(
                lane == L_PAD, jnp.where(pad_k == 1, 0.0, -BIG), jnp.where(is_lse, 1.0, 0.0)
            ),
        ),
    ).astype(BF)
    aug_q = jnp.where(
        is_var,
        jnp.where(var_own[:, None] == lane % N_VAR, 1.0, 0.0),
        jnp.where(
            is_seg,
            jnp.where(seg_own[:, None] == lane - L_SEG, 1.0, 0.0),
            jnp.where(lane == L_PAD, 1.0, 0.0),
        ),
    ).astype(F32)
    place = jnp.arange(rows, dtype=jnp.int32)
    neg = jnp.where(pad_own == 1, 0.0, -BIG).astype(F32)
    eye = place[:, None] == place[None, :]
    add_q = jnp.where(eye, 0.0, neg[None, :])
    add_k = jnp.where(eye, 0.0, neg[:, None])
    var_q = jnp.where(
        var_own[None, :] == jnp.arange(8, dtype=jnp.int32)[:, None], 1.0, 0.0
    ).astype(F32)
    return cos, sin, aug_q, aug_k, add_q, add_k, var_q


def head_scales(var_bias):
    lane = (jnp.arange(128, dtype=jnp.int32) % HD)[None, :]
    delta = (var_bias[:, 0] - var_bias[:, 1]) * math.sqrt(HD)
    hi = delta.astype(BF).astype(F32)
    low = (delta - hi).astype(BF).astype(F32)
    return jnp.where(
        lane < N_VAR, hi[:, None], jnp.where(lane < 2 * N_VAR, low[:, None], 1.0)
    ).reshape(-1, 2, 128)


def small_rows(gg_a, gg_f, bias, ti, heads_local):
    bias = bias.sum(axis=-1).reshape(4, 2 * heads_local)
    bias = jnp.take(bias, jnp.array([0, 2, 1, 3])[jnp.arange(4) ^ ti], axis=0).reshape(1, -1)
    bias = jnp.pad(bias, ((0, 0), (0, gg_a.shape[1] - bias.shape[1])))
    return jnp.concatenate([gg_a, gg_f, bias], axis=0)


def attend_part(scale, state, tab):
    q, k, v, k_oth, v_oth = state
    _, _, aug_q, aug_k, head_scale, add_q, _, _ = tab
    return attend_call(scale, q, k, k_oth, v, v_oth, aug_q, aug_k, head_scale, add_q)


def per_device(
    boundary, w_qkv, w_out, w_gate_up, w_down, norm_gains, variate_bias,
    segment_ids, variate_ids, time_ids, padding_mask,
):
    ti = lax.axis_index("tensor")
    tn = lax.axis_size("tensor")
    yi, core = ti // 2, ti % 2
    n = lax.axis_size("dp")
    is_first = lax.axis_index("section") == 0
    local = boundary[0]
    rows, model = local.shape[1:]
    scale = LOG2E / math.sqrt(HD)
    cols = w_qkv.shape[1]
    near = cols == ZB
    width = w_qkv.shape[3]
    hidden = w_gate_up.shape[3]
    heads_local = variate_bias.shape[1]
    zi = (lax.axis_index("dp") if near else 0) * jnp.ones((1,), jnp.int32)

    def row_of(array):
        return lax.dynamic_index_in_dim(array, yi, 0, keepdims=False)

    away = lax.dynamic_index_in_dim(local, 1 - yi, 0, keepdims=False).astype(BF)
    own = row_of(local).astype(BF)
    p_qkv = w_qkv[0].transpose(1, 2, 0).reshape(3 * width, cols)
    p_bias = jnp.pad(variate_bias[0].reshape(1, -1), ((0, 0), (0, cols - 2 * heads_local)))
    p_small = jnp.pad(jnp.concatenate([norm_gains[0], p_bias], axis=0), ((0, 13), (0, 0)))
    low = 3 * width
    out_low = low + 16
    p1 = jnp.concatenate([p_qkv, p_small, w_out[0]], axis=0)
    p2 = w_gate_up[0].transpose(1, 2, 0).reshape(2 * hidden, cols)
    p3 = w_down[0]

    def both_ends(came):
        return jnp.where(
            yi == 0, jnp.concatenate([own, came], axis=0), jnp.concatenate([came, own], axis=0)
        )

    tab = tables(
        row_of(segment_ids), row_of(variate_ids), row_of(time_ids), row_of(padding_mask), core
    )

    if near:
        a1, came = ring(p1), y_swap(away)
        a1, came, p1, p2, p3 = meet(a1, came, p1, p2, p3)
        a2, y0 = ring(a1), y_swap(p1)
        a1, a2, y0, p2, p3, *tab = meet(a1, a2, y0, p2, p3, *tab)
        ends = both_ends(came)
        a3, y1 = ring(a2), y_swap(a1)
        n1 = [jnp.stack([p1, y0])]
        f1 = [core_swap(n1[0])]
        a2, a3, y1, p2, p3, ends = meet(a2, a3, y1, p2, p3, ends)
        b1, y2, d0 = ring(p2), y_swap(a2), y_swap(p3)
        n1.append(jnp.stack([a1, y1]))
        f1.append(core_swap(n1[1]))
        a3, b1, y2, d0, p2 = meet(a3, b1, y2, d0, p2)
        b2, y3 = ring(b1), y_swap(a3)
        n1.append(jnp.stack([a2, y2]))
        f1.append(core_swap(n1[2]))
        b1, b2, y3, p2, d0 = meet(b1, b2, y3, p2, d0)
        n1.append(jnp.stack([a3, y3]))
        f1.append(core_swap(n1[3]))
        w1 = n1 + f1
        b3, g0 = ring(b2), y_swap(p2)
    else:
        w1 = gather_any(p1)
        ends = both_ends(y_swap(away))
    gains = jnp.stack([w[0, low : low + 2] for w in w1[:4]])
    gains = jnp.take(gains, (zi[0] - jnp.arange(4)) % 4, axis=0)
    gains = gains.transpose(1, 0, 2).reshape(2, model).astype(F32)
    gain_a, gain_f = gains[:1], gains[1:]
    bias = [w[:, low + 2, : 2 * heads_local] for w in (w1[0], w1[4])]
    bias = jnp.concatenate(bias).reshape(4 * heads_local, 2).astype(F32)
    head_scale = head_scales(bias)
    cos, sin, aug_q, aug_k, add_q, add_k, var_q = tab
    tab = (cos, sin, aug_q, aug_k, head_scale, add_q, add_k, var_q)

    if near:
        b1, b2, b3, g0, d0 = meet(b1, b2, b3, g0, d0)
        n3 = [jnp.stack([p3, d0])]
        c1, g1 = ring(n3[0]), y_swap(b1)
        n2 = [jnp.stack([p2, g0])]
        f2 = [core_swap(n2[0])]
        f3 = [core_swap(n3[0])]
    q, k, v = qkv_call(False, ends, gain_a, zi, w1, low, cos, sin)
    if near:
        b2, b3, c1, g1, q, k, v = meet(b2, b3, c1, g1, q, k, v)
        c2, g2 = ring(c1), y_swap(b2)
    k_oth, v_oth = core_swap(k), core_swap(v)
    o, _ = attend_part(scale, (q, k, v, k_oth, v_oth), tab)
    if near:
        b3, c1, g1, c2, g2, o = meet(b3, c1, g1, c2, g2, o)
        c3, g3 = ring(c2), y_swap(b3)
        n2.append(jnp.stack([b1, g1]))
        f2.append(core_swap(n2[1]))
        f3.append(core_swap(c1))
        n2.append(jnp.stack([b2, g2]))
        f2.append(core_swap(n2[2]))
        f3.append(core_swap(c2))
        b3, c3, g3 = meet(b3, c3, g3)
        n2.append(jnp.stack([b3, g3]))
        f2.append(core_swap(n2[3]))
        f3.append(core_swap(c3))
        w2, w3 = n2 + f2, n3 + [c1, c2, c3] + f3
    else:
        w2, w3 = gather_any(p2), gather_any(p3)
    h, z_near, z_far = ffn_up_call(False, out_low, width, ends, o, gain_f, zi, w1, w2)
    y_low = ffn_down_call(BF, h, z_near, z_far, zi, w3)
    got = lax.ppermute(y_low, "section", [(0, 1)])

    x = jnp.where(is_first, ends, got)
    n1, q, k, v, q0, k0 = qkv_call(True, x, gain_a, zi, w1, low, cos, sin)
    k_oth, v_oth = core_swap(k), core_swap(v)
    o, sums = attend_part(scale, (q, k, v, k_oth, v_oth), tab)
    h, z_near, z_far, n2, g, u = ffn_up_call(True, out_low, width, x, o, gain_f, zi, w1, w2)
    y = ffn_down_call(F32, h, z_near, z_far, zi, w3)

    def qkv_back(dq, dk, dk_got, dv, dv_got, dh):
        return qkv_back_call(
            dq, dk, dk_got, dv, dv_got, q0, k0, cos, sin, x, dh, gain_a, zi, w1, low
        )

    dh, _, do = ffn_back_call(out_low, width, ends, h, g, u, gain_f, zi, w1, w2, w3)[:3]
    dq, dk, dk_send, dv, dv_send, _ = attend_back_call(
        scale, None, q, k, k_oth, v, v_oth, do, o, sums, aug_q, aug_k, head_scale, add_k, var_q
    )
    dx_low = qkv_back(dq, dk, core_swap(dk_send), dv, core_swap(dv_send), dh)[3]
    dx_low, z_far, n1_far, n2_far, o_far = meet(dx_low, z_far, n1, n2, o[:, 2 * width :])
    got = lax.ppermute(dx_low, "section", [(1, 0)])
    z_oth, n2_oth, n1_oth = core_swap(z_far), core_swap(n2_far), core_swap(n1_far)
    o_oth = core_swap(o_far)

    got, y, z_oth, n2_oth, n1_oth, o_oth = meet(got, y, z_oth, n2_oth, n1_oth, o_oth)

    df = jnp.where(is_first, got, ends)
    down_keep, down_send = wgrad_call(zi, hidden, z_near, df, z_oth, core_swap(df))
    df, down_keep, down_send = meet(df, down_keep, down_send)
    down_got = y_swap(down_send)
    back = ffn_back_call(out_low, width, df, h, g, u, gain_f, zi, w1, w2, w3)
    down_keep, down_got, *back = meet(down_keep, down_got, *back)
    dh, da, do, dg_near, dg_far, du_near, du_far, gg_f = back
    dg_oth, du_oth, da_oth = core_swap(dg_far), core_swap(du_far), core_swap(da)
    if near:
        down = [plus(down_keep[r], down_got[r]) for r in range(4)]
        down_run = ring(down[1])
    else:
        down_run = down_got
    dg_oth, du_oth, da_oth = meet(dg_oth, du_oth, da_oth)
    gate_keep, gate_send = wgrad_call(zi, hidden, dg_near, n2, dg_oth, n2_oth)
    down_run, do, gate_keep, gate_send, du_oth, da_oth = meet(
        down_run, do, gate_keep, gate_send, du_oth, da_oth
    )
    if near:
        gate_got = y_swap(gate_send)
        down_run = ring(plus(down_run, down[2]))
    out_keep, out_send = wgrad_call(zi, width, o, da, o_oth, da_oth)
    up_keep, up_send = wgrad_call(zi, hidden, du_near, n2, du_oth, n2_oth)
    do, out_keep, out_send, up_keep, up_send, down_run = meet(
        do, out_keep, out_send, up_keep, up_send, down_run
    )
    back = attend_back_call(
        scale, None, q, k, k_oth, v, v_oth, do, o, sums, aug_q, aug_k, head_scale, add_k, var_q
    )
    half = hidden // 32 * 16
    cut = width * 3 // 2
    if near:
        down_run = ring(plus(down_run, down[3]))
        out = [jnp.stack([out_keep[r], out_send[r]]) for r in range(4)]
        out_run = [to_owner(out[r], r) for r in (1, 2, 3)]
        gate_got, down_run, *rest = meet(gate_got, down_run, *out_run, *back)
        out_run, back = rest[:3], rest[3:]
    dq, dk, dk_send, dv, dv_send, bias = back
    dk_got, dv_got = core_swap(dk_send), core_swap(dv_send)
    if near:
        up_got = y_swap(up_send)
        gate = [plus(gate_keep[r], gate_got[r]) for r in range(4)]
        gate_run = [to_owner(gate[r], r) for r in (1, 2, 3)]
    back = qkv_back(dq, dk, dk_got, dv, dv_got, dh)
    if near:
        up_got, *rest = meet(up_got, *gate_run, *back)
        gate_run, back = rest[:3], rest[3:]
    dp_near, dp_far, dx, dx_low, gg_a = back
    dp_oth = core_swap(dp_far)
    qkv_keep, qkv_send = wgrad_call(zi, 3 * width, dp_near, n1, dp_oth, n1_oth)
    small = small_rows(gg_a, gg_f, bias, ti, heads_local)
    out_low_rows = jnp.where(is_first, dx_low, y.astype(BF))
    send = jnp.where(yi == 0, out_low_rows[rows:], out_low_rows[:rows])
    if near:
        up = [plus(up_keep[r, :half], up_got[r, :half]) for r in range(4)]
        up_run = [to_owner(up[r], r) for r in (1, 2, 3)]
        rows_got = y_swap(send)
        out_far = add_all(out[0][1], [run[1] for run in out_run]).astype(BF)
        out_got = y_swap(out_far)
        small = small + core_swap(small)
        rows_got, out_got, qkv_keep, qkv_send, small, *up_run = meet(
            rows_got, out_got, qkv_keep, qkv_send, small, *up_run
        )
        head_got = y_swap(qkv_send[:, :cut])
        more = [plus(up_keep[r, half:], up_got[r, half:]) for r in range(4)]
        more_run = [to_owner(more[r], r) for r in (1, 2, 3)]
        small = small + y_swap(small)
        head_got, small, *more_run = meet(head_got, small, *more_run)
        tail_got = y_swap(qkv_send[:, cut:])
        head = [plus(qkv_keep[r, :cut], head_got[r]) for r in range(4)]
        head_run = [to_owner(head[r], r) for r in (1, 2, 3)]
        small = small + lax.ppermute(small, "dp", [(i, i ^ 1) for i in range(4)])
        tail_got, small, down_run, out_got, *rest = meet(
            tail_got, small, down_run, out_got, *head_run, *gate_run, *out_run, *up_run, *more_run
        )
        head_run, gate_run, out_run, up_run, more_run = (rest[i : i + 3] for i in range(0, 15, 3))
        tail = [plus(qkv_keep[r, cut:], tail_got[r]) for r in range(4)]
        tail_run = [to_owner(tail[r], r) for r in (1, 2, 3)]
        small = small + lax.ppermute(small, "dp", [(i, i ^ 2) for i in range(4)])
        g_down = down_run.astype(F32) + down[0].astype(F32)
        g_up = [add_all(up[0], up_run), add_all(more[0], more_run)]
        g_gu = jnp.stack([add_all(gate[0], gate_run), jnp.concatenate(g_up, axis=0)])
        g_out = add_all(out[0][0], [run[0] for run in out_run] + [out_got])
        g_qkv = jnp.concatenate([add_all(head[0], head_run), add_all(tail[0], tail_run)], axis=0)
    else:
        rows_got = y_swap(send)
        g_down = scatter_any(down_keep, down_send)
        g_gu = jnp.stack([scatter_any(gate_keep, gate_send), scatter_any(up_keep, up_send)])
        g_out = scatter_any(out_keep, out_send)
        g_qkv = scatter_any(qkv_keep, qkv_send)
        small = small_sum(small)

    out_rows = jnp.where(is_first, dx, y)
    keep = jnp.where(yi == 0, out_rows[:rows], out_rows[rows:])
    back = rows_got.astype(F32)
    boundary_out = jnp.where(yi == 0, jnp.stack([keep, back]), jnp.stack([back, keep]))[None]
    piece = model // (n * tn)
    gain_piece = lax.dynamic_slice_in_dim(
        small[:2], (lax.axis_index("dp") * tn + ti) * piece, piece, 1
    )
    bias_piece = lax.dynamic_slice_in_dim(
        small[2, : 8 * heads_local].reshape(-1, 2), ti * heads_local, heads_local, 0
    )
    return (
        boundary_out,
        g_qkv.reshape(3, width, cols).transpose(2, 0, 1)[None],
        g_out[None],
        g_gu.transpose(2, 0, 1)[None],
        g_down[None],
        gain_piece[None],
        bias_piece[None],
    )


def solution(mesh):
    placed = (
        P("section", "dp", "tensor", None),
        P("section", "dp", None, "tensor"),
        P("section", "tensor", "dp"),
        P("section", "dp", None, "tensor"),
        P("section", "tensor", "dp"),
        P("section", None, "dp"),
        P("section", "tensor", None),
        P("dp", None),
        P("dp", None),
        P("dp", None),
        P("dp", None),
    )
    return jax.shard_map(
        per_device,
        mesh=mesh,
        in_specs=placed,
        out_specs=(
            P("section", "dp", "tensor", None),
            P("section", "dp", None, "tensor"),
            P("section", "tensor", "dp"),
            P("section", "dp", None, "tensor"),
            P("section", "tensor", "dp"),
            P("section", None, ("dp", "tensor")),
            P("section", "tensor", None),
        ),
        check_vma=False,
    )
```

```python
import functools
import math

import jax
import jax.numpy as jnp
from jax import lax
from jax.experimental import pallas as pl
from jax.experimental.pallas import tpu as pltpu
from jax.sharding import PartitionSpec as P

EPS = 1e-05
BIG = 8192.0
LOG2E = 1.4426950408889634
BF = jnp.bfloat16
F32 = jnp.float32
HD = 64
ZB = 256
VMEM_MB = 56
N_VAR = 4
L_SEG = 8
L_PAD = 24
L_LSE = 25


def dot(a, b):
    return lax.dot_general(a, b, (((1,), (0,)), ((), ())), preferred_element_type=F32)


def dot_nt(a, b):
    return lax.dot_general(a, b, (((1,), (1,)), ((), ())), preferred_element_type=F32)


def dot_tn(a, b):
    return lax.dot_general(a, b, (((0,), (0,)), ((), ())), preferred_element_type=F32)


def params(mb=VMEM_MB):
    return pltpu.CompilerParams(
        dimension_semantics=("arbitrary",), vmem_limit_bytes=mb * 1024 * 1024
    )


def cost(flops, nbytes, trans=0):
    return pl.CostEstimate(flops=int(flops), bytes_accessed=int(nbytes), transcendentals=0)


def sds(shape, dtype):
    return jax.ShapeDtypeStruct(shape, dtype)


def whole(shape):
    zeros = (0,) * len(shape)
    return pl.BlockSpec(shape, lambda *_: zeros)


def head_sum(u):
    row = lax.broadcasted_iota(jnp.int32, (u.shape[1], u.shape[1]), 0) // HD
    col = lax.broadcasted_iota(jnp.int32, (u.shape[1], u.shape[1]), 1) // HD
    return dot(u.astype(BF), jnp.where(row == col, 1.0, 0.0).astype(BF))


def half_swap(u):
    lane = lax.broadcasted_iota(jnp.int32, u.shape, 1) % HD
    return jnp.where(lane < HD // 2, pltpu.roll(u, 128 - HD // 2, 1), pltpu.roll(u, HD // 2, 1))


def row_rms(x):
    return lax.rsqrt(jnp.mean(x * x, axis=-1, keepdims=True) + EPS)


def hbm():
    return pl.BlockSpec(memory_space=pl.ANY)


def smem():
    return pl.BlockSpec(memory_space=pltpu.SMEM)


def copies(refs, low, scratch, sems, t):
    rows = pl.ds(low, scratch.shape[2])
    return [
        pltpu.make_async_copy(
            refs[4 * (t // 2) + r].at[t % 2, rows], scratch.at[r, t], sems.at[r, t]
        )
        for r in range(4)
    ]


def start_all(refs, low, scratch, sems, shards=range(4)):
    for t in shards:
        for copy in copies(refs, low, scratch, sems, t):
            copy.start()


def wait_for(refs, low, scratch, sems, t):
    for fixed in range(4):

        @pl.when(t == fixed)
        def _():
            for copy in copies(refs, low, scratch, sems, fixed):
                copy.wait()


def weight_scratch(feats):
    return [pltpu.VMEM((4, 4, feats, ZB), BF), pltpu.SemaphoreType.DMA((4, 4))]


def place(zi_ref, r):
    return lax.rem(zi_ref[0] - r + 4, 4)


def block_store(ref, value):
    for z in range(4):
        ref[z] = value[:, z * ZB : (z + 1) * ZB]


def chunks(wide, step=ZB):
    return [slice(low, min(low + step, wide)) for low in range(0, wide, step)]


def block_load(ref):
    return jnp.concatenate([ref[z] for z in range(4)], axis=1)


def qkv_kernel(save, x_ref, gain_ref, zi_ref, cos_ref, sin_ref, *refs):
    weight, refs = refs[:8], refs[8:]
    if save:
        n_ref, q_ref, k_ref, v_ref, q0_ref, k0_ref, n_scr, w_ref, sems = refs
    else:
        q_ref, k_ref, v_ref, n_scr, w_ref, sems = refs
    t = pl.program_id(0)

    @pl.when(t == 0)
    def _():
        start_all(weight, 0, w_ref, sems, range(1))
        x = x_ref[...].astype(F32)
        n = (x * row_rms(x) * gain_ref[...]).astype(BF)
        block_store(n_scr, n)
        if save:
            n_ref[...] = n

    wait_for(weight, 0, w_ref, sems, t)

    @pl.when(t == 0)
    def _():
        start_all(weight, 0, w_ref, sems, range(1, 4))

    width = q_ref.shape[1]

    def project(which):
        cols = slice(which * width, (which + 1) * width)
        total = dot_nt(n_scr[place(zi_ref, 0)], w_ref[0, t, cols])
        for r in range(1, 4):
            total = total + dot_nt(n_scr[place(zi_ref, r)], w_ref[r, t, cols])
        return total

    cos, sin = cos_ref[...], sin_ref[...]
    for which, out in ((0, q_ref), (1, k_ref)):
        u = project(which)
        if save:
            kept = q0_ref if which == 0 else k0_ref
            kept[...] = u.astype(BF)
        un = u * lax.rsqrt(head_sum(u * u) * (1.0 / HD) + EPS)
        for pair in range(width // 128):
            at = slice(pair * 128, (pair + 1) * 128)
            out[:, at] = (un[:, at] * cos + half_swap(un[:, at]) * sin).astype(BF)
    v_ref[...] = project(2).astype(BF)


def qkv_call(save, x, gain, zi, w, feats, cos, sin):
    rows, model = x.shape
    width = feats // 3
    total = 4 * width
    col = pl.BlockSpec((rows, width), lambda t: (0, t))
    outs = [sds((rows, total), BF)] * 3
    specs = [col] * 3
    if save:
        outs = [sds((rows, model), BF)] + outs + [sds((rows, total), BF)] * 2
        specs = [whole((rows, model))] + specs + [col] * 2
    return pl.pallas_call(
        functools.partial(qkv_kernel, save),
        grid=(4,),
        in_specs=[whole((rows, model)), whole((1, model)), smem()]
        + [whole((rows, 128))] * 2
        + [hbm()] * 8,
        out_specs=specs,
        out_shape=outs,
        scratch_shapes=[pltpu.VMEM((4, rows, ZB), BF)] + weight_scratch(feats),
        compiler_params=params(),
        cost_estimate=cost(2 * rows * model * 3 * total, 6 * total * model + 16 * x.size),
    )(x, gain, zi, cos, sin, *w)


def other_core_spec(rows, pairs):
    half = pairs // 2
    return pl.BlockSpec((rows, 128), lambda p: (0, lax.rem(p + half, pairs)))


def pick(first, h, a, b):
    return jnp.where(first, a, b) if h == 0 else jnp.where(first, b, a)


def pick_low(first, h, a, b):
    mine = jnp.where(first, 1.0, 0.0) if h == 0 else jnp.where(first, 0.0, 1.0)
    low = mine.astype(BF)
    return a * low + b * (1.0 - mine).astype(BF)


def attend_kernel(
    scale, q_ref, ko_ref, kx_ref, vo_ref, vx_ref, aq_ref, ak_ref, hs_ref, add_ref, o_ref, l_ref
):
    rows = q_ref.shape[0]
    kb = 128
    first = lax.broadcasted_iota(jnp.int32, (1, 128), 1) < HD
    q = q_ref[...].astype(F32)
    base = aq_ref[...]
    raws = []
    for h in range(2):
        qh = pick(first, h, q, base * hs_ref[0, h : h + 1, :]).astype(BF)
        total = None
        for half, (k_ref, v_ref) in enumerate(((ko_ref, vo_ref), (kx_ref, vx_ref))):
            for block in range(rows // kb):
                at = slice(block * kb, (block + 1) * kb)
                kk = slice(half * rows + block * kb, half * rows + (block + 1) * kb)
                kh = pick_low(first, h, k_ref[at, :], ak_ref[kk, :])
                vh = pick_low(first, h, v_ref[at, :], BF(1.0))
                s = dot_nt(qh, kh)
                if half == 0:
                    s = s + add_ref[:, at]
                part = dot(jnp.exp2(s * scale).astype(BF), vh)
                total = part if total is None else total + part
        raws.append(total)
    sums = jnp.where(first, raws[1], raws[0])
    l_ref[...] = sums
    o_ref[...] = (jnp.where(first, raws[0], raws[1]) / pltpu.roll(sums, HD, 1)).astype(BF)


def attend_call(scale, q, k_own, k_oth, v_own, v_oth, aug_q, aug_k, head_scale, add_own):
    rows, total = q.shape
    pairs = total // 128
    col = pl.BlockSpec((rows, 128), lambda p: (0, p))
    far = other_core_spec(rows, pairs)
    return pl.pallas_call(
        functools.partial(attend_kernel, scale),
        grid=(pairs,),
        in_specs=[
            col,
            col,
            far,
            col,
            far,
            whole(aug_q.shape),
            whole(aug_k.shape),
            pl.BlockSpec((1, 2, 128), lambda p: (p, 0, 0)),
            whole(add_own.shape),
        ],
        out_specs=[col, col],
        out_shape=[sds((rows, total), BF), sds((rows, total), F32)],
        compiler_params=params(),
        cost_estimate=cost(
            4 * 2 * rows * rows * 2 * total, 20 * rows * total, rows * rows * 2 * pairs * 2
        ),
    )(q, k_own, k_oth, v_own, v_oth, aug_q, aug_k, head_scale, add_own)


def padded(hidden):
    return -(-2 * hidden // 128) * 128


def pair_scratch(parts, hidden):
    return [
        pltpu.VMEM((4, 2, parts * padded(hidden), ZB), BF),
        pltpu.SemaphoreType.DMA((4, 2, 2, parts)),
    ]


def pair_copies(refs, parts, scratch, sems, half):
    wide = scratch.shape[2] // parts
    hidden = refs[0].shape[1] // parts
    return [
        pltpu.make_async_copy(
            refs[4 * half + r].at[y, pl.ds(part * hidden, hidden)],
            scratch.at[r, half, pl.ds(part * wide + y * hidden, hidden)],
            sems.at[r, half, y, part],
        )
        for r in range(4)
        for y in range(2)
        for part in range(parts)
    ]


def pair_start(refs, parts, scratch, sems, halves=range(2)):
    wide = scratch.shape[2] // parts
    hidden = refs[0].shape[1] // parts
    for half in halves:
        for copy in pair_copies(refs, parts, scratch, sems, half):
            copy.start()
    blank = wide - 2 * hidden
    if blank:
        for half in halves:
            for r in range(4):
                for part in range(parts):
                    low = part * wide + 2 * hidden
                    scratch[r, half, low : low + blank] = jnp.zeros((blank, ZB), BF)


def pair_wait(refs, parts, scratch, sems, half):
    for fixed in range(2):

        @pl.when(half == fixed)
        def _():
            for copy in pair_copies(refs, parts, scratch, sems, fixed):
                copy.wait()


def near_far(rows, feats):
    return (
        pl.BlockSpec((1, rows, feats), lambda t: (jnp.minimum(t, 1), 0, 0)),
        pl.BlockSpec((1, rows, feats), lambda t: (jnp.maximum(t - 2, 0), 0, 0)),
    )


def put(is_near, near_ref, far_ref, value, at=...):
    @pl.when(is_near)
    def _():
        near_ref[at] = value

    @pl.when(jnp.logical_not(is_near))
    def _():
        far_ref[at] = value


def ffn_up_kernel(save, out_low, x_ref, o_ref, gain_ref, zi_ref, *refs):
    wo, wgu, refs = refs[:8], refs[8:16], refs[16:]
    if save:
        h_ref, zn_ref, zf_ref, n_ref, g_ref, u_ref = refs[:6]
    else:
        h_ref, zn_ref, zf_ref = refs[:3]
    n_scr, wo_ref, wo_sems, wgu_ref, wgu_sems, acc, z_scr = refs[-7:]
    wide = wgu_ref.shape[2] // 2
    half = pl.program_id(0)

    @pl.when(half == 0)
    def _():
        start_all(wo, out_low, wo_ref, wo_sems)
        pair_start(wgu, 2, wgu_ref, wgu_sems, range(1))
        width = wo_ref.shape[2]
        block_store(acc, x_ref[...].astype(F32))
        for s in range(4):
            for copy in copies(wo, out_low, wo_ref, wo_sems, s):
                copy.wait()
        pair_start(wgu, 2, wgu_ref, wgu_sems, range(1, 2))
        for r in range(4):
            z = place(zi_ref, r)
            h = acc[z]
            for s in range(4):
                h = h + dot(o_ref[:, s * width : (s + 1) * width], wo_ref[r, s])
            acc[z] = h
        h = block_load(acc)
        n = (h * row_rms(h) * gain_ref[...]).astype(BF)
        block_store(n_scr, n)
        h_ref[...] = h
        if save:
            n_ref[...] = n

    pair_wait(wgu, 2, wgu_ref, wgu_sems, half)
    for at in chunks(wide):
        total = []
        for part in range(2):
            cols = slice(part * wide + at.start, part * wide + at.stop)
            one = dot_nt(n_scr[place(zi_ref, 0)], wgu_ref[0, half, cols])
            for r in range(1, 4):
                one = one + dot_nt(n_scr[place(zi_ref, r)], wgu_ref[r, half, cols])
            total.append(one)
        gate, up = total
        z_scr[:, at] = (gate / (1.0 + jnp.exp(-gate)) * up).astype(BF)
        if save:
            g_ref[0, :, at] = gate.astype(BF)
            u_ref[0, :, at] = up.astype(BF)
    put(half == 0, zn_ref, zf_ref, z_scr[...])


def ffn_up_call(save, out_low, width, x, o, gain, zi, wo, wgu):
    rows, model = x.shape
    hidden = wgu[0].shape[1] // 2
    wide = padded(hidden)
    big = whole((rows, model))
    part = pl.BlockSpec((1, rows, wide), lambda t: (t, 0, 0))
    outs = [sds((rows, model), F32)] + [sds((rows, wide), BF)] * 2
    specs = [big, whole((rows, wide)), whole((rows, wide))]
    if save:
        outs += [sds((rows, model), BF)] + [sds((2, rows, wide), BF)] * 2
        specs += [big, part, part]
    return pl.pallas_call(
        functools.partial(ffn_up_kernel, save, out_low),
        grid=(2,),
        in_specs=[big, whole(o.shape), whole((1, model)), smem()] + [hbm()] * 16,
        out_specs=specs,
        out_shape=outs,
        scratch_shapes=[pltpu.VMEM((4, rows, ZB), BF)]
        + weight_scratch(width)
        + pair_scratch(2, hidden)
        + [pltpu.VMEM((4, rows, ZB), F32), pltpu.VMEM((rows, wide), BF)],
        compiler_params=params(),
        cost_estimate=cost(
            2 * rows * model * (8 * hidden + model), 16 * hidden * model + 20 * x.size
        ),
    )(x, o, gain, zi, *wo, *wgu)


def ffn_down_kernel(h_ref, zn_ref, zf_ref, zi_ref, *refs):
    weight, (y_ref, w_ref, sems) = refs[:8], refs[8:]
    pair_start(weight, 1, w_ref, sems)
    for half, z_ref in enumerate((zn_ref, zf_ref)):
        for copy in pair_copies(weight, 1, w_ref, sems, half):
            copy.wait()
    for z in range(4):
        r = lax.rem(zi_ref[0] - z + 4, 4)
        at = slice(z * ZB, (z + 1) * ZB)
        y = h_ref[:, at] + dot(zn_ref[...], w_ref[r, 0]) + dot(zf_ref[...], w_ref[r, 1])
        y_ref[:, at] = y.astype(y_ref.dtype)


def ffn_down_call(dtype, h, z_near, z_far, zi, wd):
    rows, model = h.shape
    hidden = wd[0].shape[1]
    vmem = pl.BlockSpec(memory_space=pltpu.VMEM)
    return pl.pallas_call(
        ffn_down_kernel,
        in_specs=[vmem] * 3 + [smem()] + [hbm()] * 8,
        out_specs=vmem,
        out_shape=sds((rows, model), dtype),
        scratch_shapes=pair_scratch(1, hidden),
        compiler_params=pltpu.CompilerParams(vmem_limit_bytes=VMEM_MB * 1024 * 1024),
        cost_estimate=cost(2 * rows * model * 4 * hidden, 8 * hidden * model + 8 * h.size),
    )(h, z_near, z_far, zi, *wd)


def ffn_back_kernel(out_low, dy_ref, h_ref, g_ref, u_ref, gain_ref, zi_ref, *refs):
    wo, wgu, wd, refs = refs[:8], refs[8:16], refs[16:24], refs[24:]
    dh_ref, da_ref, do_ref, dgn_ref, dgf_ref, dun_ref, duf_ref, gg_ref = refs[:8]
    df_scr, acc, wo_ref, wo_sems, wgu_ref, wgu_sems, wd_ref, wd_sems, dg_scr, du_scr = refs[8:]
    wide = wd_ref.shape[2]
    half = pl.program_id(0)

    @pl.when(half == 0)
    def _():
        pair_start(wd, 1, wd_ref, wd_sems, range(1))
        block_store(df_scr, dy_ref[...])
        acc[...] = jnp.zeros_like(acc)

    pair_wait(wd, 1, wd_ref, wd_sems, half)

    @pl.when(half == 0)
    def _():
        pair_start(wgu, 2, wgu_ref, wgu_sems, range(1))
        pair_start(wd, 1, wd_ref, wd_sems, range(1, 2))
        pair_start(wgu, 2, wgu_ref, wgu_sems, range(1, 2))
        start_all(wo, out_low, wo_ref, wo_sems)

    for at in chunks(wide):
        dz = dot_nt(df_scr[place(zi_ref, 0)], wd_ref[0, half, at])
        for r in range(1, 4):
            dz = dz + dot_nt(df_scr[place(zi_ref, r)], wd_ref[r, half, at])
        gate = g_ref[0, :, at].astype(F32)
        up = u_ref[0, :, at].astype(F32)
        s = 1.0 / (1.0 + jnp.exp(-gate))
        dg_scr[:, at] = (dz * up * s * (1.0 + gate * (1.0 - s))).astype(BF)
        du_scr[:, at] = (dz * gate * s).astype(BF)
    dgate, dup = dg_scr[...], du_scr[...]
    put(half == 0, dgn_ref, dgf_ref, dgate)
    put(half == 0, dun_ref, duf_ref, dup)
    pair_wait(wgu, 2, wgu_ref, wgu_sems, half)
    for r in range(4):
        z = place(zi_ref, r)
        acc[z] = acc[z] + (
            dot(dgate, wgu_ref[r, half, :wide]) + dot(dup, wgu_ref[r, half, wide:])
        )

    @pl.when(half == 1)
    def _():
        h = h_ref[...]
        r = row_rms(h)
        hn = h * r
        dn = block_load(acc)
        gg_ref[...] = jnp.sum(dn * hn, axis=0, keepdims=True)
        dhat = dn * gain_ref[...]
        dh = dy_ref[...].astype(F32) + r * (
            dhat - hn * jnp.mean(dhat * hn, axis=-1, keepdims=True)
        )
        dh_ref[...] = dh
        da = dh.astype(BF)
        da_ref[...] = da
        block_store(df_scr, da)
        width = wo_ref.shape[2]
        for s in range(4):
            for copy in copies(wo, out_low, wo_ref, wo_sems, s):
                copy.wait()
        for s in range(4):
            part = dot_nt(df_scr[place(zi_ref, 0)], wo_ref[0, s])
            for q in range(1, 4):
                part = part + dot_nt(df_scr[place(zi_ref, q)], wo_ref[q, s])
            do_ref[:, s * width : (s + 1) * width] = part.astype(BF)


def ffn_back_call(out_low, width, dy, h, g, u, gain, zi, wo, wgu, wd):
    rows, model = dy.shape
    hidden = wd[0].shape[1]
    wide = g.shape[2]
    big = whole((rows, model))
    part = pl.BlockSpec((1, rows, wide), lambda t: (t, 0, 0))
    return pl.pallas_call(
        functools.partial(ffn_back_kernel, out_low),
        grid=(2,),
        in_specs=[big, big, part, part, whole((1, model)), smem()] + [hbm()] * 24,
        out_specs=[big, big, big] + [whole((rows, wide))] * 4 + [whole((1, model))],
        out_shape=[sds((rows, model), F32), sds((rows, model), BF), sds((rows, model), BF)]
        + [sds((rows, wide), BF)] * 4
        + [sds((1, model), F32)],
        scratch_shapes=[pltpu.VMEM((4, rows, ZB), BF), pltpu.VMEM((4, rows, ZB), F32)]
        + weight_scratch(width)
        + pair_scratch(2, hidden)
        + pair_scratch(1, hidden)
        + [pltpu.VMEM((rows, wide), BF)] * 2,
        compiler_params=params(57),
        cost_estimate=cost(
            2 * rows * model * (12 * hidden + model), 24 * hidden * model + 20 * dy.size
        ),
    )(dy, h, g, u, gain, zi, *wo, *wgu, *wd)


def split3(value):
    hi = value.astype(BF).astype(F32)
    mid = (value - hi).astype(BF).astype(F32)
    return hi, mid, value - hi - mid


def attend_back_kernel(
    scale, q_ref, ko_ref, kx_ref, vo_ref, vx_ref, do_ref, o_ref, l_ref, aq_ref, ak_ref, hs_ref,
    add_ref, var_ref, dq_ref, dko_ref, dkx_ref, dvo_ref, dvx_ref, bias_ref,
):
    rows = q_ref.shape[0]
    kb = 512
    first = lax.broadcasted_iota(jnp.int32, (1, 128), 1) < HD
    lane = lax.broadcasted_iota(jnp.int32, (1, 128), 1) % HD
    q = q_ref[...].astype(F32)
    do = do_ref[...].astype(F32)
    inner = do * o_ref[...].astype(F32)
    base = aq_ref[...]
    hi, mid, low = split3(jnp.log2(l_ref[...]) * (-1.0 / scale))
    lse = jnp.where(lane == L_LSE, hi, 0.0)
    lse = jnp.where(lane == L_LSE + 1, mid, lse)
    lse = jnp.where(lane == L_LSE + 2, low, lse)
    dq_t = []
    dk = [[], []]
    dv = [[], []]
    for h in range(2):
        qh = pick(first, h, q, base * hs_ref[0, h : h + 1, :] + lse).astype(BF)
        d = jnp.sum(pick(first, h, inner, 0.0), axis=-1, keepdims=True)
        dhi, dmid, dlow = split3(-d)
        d_aug = jnp.where(lane == 0, dhi, 0.0)
        d_aug = jnp.where(lane == 1, dmid, d_aug)
        d_aug = jnp.where(lane == 2, dlow, d_aug)
        doh = pick(first, h, do, d_aug).astype(BF)
        total = None
        for half, (k_ref, v_ref) in enumerate(((ko_ref, vo_ref), (kx_ref, vx_ref))):
            for block in range(rows // kb):
                at = slice(block * kb, (block + 1) * kb)
                kk = slice(half * rows + block * kb, half * rows + (block + 1) * kb)
                kh = pick_low(first, h, k_ref[at, :], ak_ref[kk, :])
                vh = pick_low(first, h, v_ref[at, :], BF(1.0))
                s = dot_nt(kh, qh)
                if half == 0:
                    s = s + add_ref[at, :]
                p = jnp.exp2(s * scale)
                ds = (p * dot_nt(vh, doh)).astype(BF)
                dv[h].append(dot(p.astype(BF), doh))
                dk[h].append(dot(ds, qh))
                part = dot_tn(kh, ds)
                total = part if total is None else total + part
        dq_t.append(total)
    scale_back = 1.0 / math.sqrt(HD)
    count = rows // kb
    for half, (dk_ref, dv_ref) in enumerate(((dko_ref, dvo_ref), (dkx_ref, dvx_ref))):
        for block in range(count):
            at = slice(block * kb, (block + 1) * kb)
            i = half * count + block
            dk_ref[at, :] = (jnp.where(first, dk[0][i], dk[1][i]) * scale_back).astype(dk_ref.dtype)
            dv_ref[at, :] = jnp.where(first, dv[0][i], dv[1][i]).astype(dv_ref.dtype)
    joined = jnp.concatenate([dq_t[0][:HD], dq_t[1][HD:]], axis=0)
    dq_ref[...] = (joined.T * scale_back).astype(BF)
    mine = var_ref[...]
    for h in range(2):
        begin = HD if h == 0 else 0
        r = dq_t[h][begin : begin + 8]
        same = jnp.sum(r * mine, axis=0, keepdims=True)
        every = jnp.sum(r[:N_VAR], axis=0, keepdims=True)
        bias_ref[0, 2 * h : 2 * h + 1, :] = same
        bias_ref[0, 2 * h + 1 : 2 * h + 2, :] = every - same


def attend_back_call(
    scale, span, q, k_own, k_oth, v_own, v_oth, do, o, sums, aug_q, aug_k, head_scale, add_own, var_q
):
    rows, total = q.shape
    every = total // 128
    low, high = span or (0, every)
    pairs = high - low
    total = pairs * 128
    col = pl.BlockSpec((rows, 128), lambda p: (0, p + low))
    far = pl.BlockSpec((rows, 128), lambda p: (0, lax.rem(p + low + every // 2, every)))
    out = pl.BlockSpec((rows, 128), lambda p: (0, p))
    out_far = other_core_spec(rows, pairs) if span is None else out
    return pl.pallas_call(
        functools.partial(attend_back_kernel, scale),
        grid=(pairs,),
        in_specs=[col, col, far, col, far, col, col, col]
        + [
            whole(aug_q.shape),
            whole(aug_k.shape),
            pl.BlockSpec((1, 2, 128), lambda p: (p + low, 0, 0)),
            whole(add_own.shape),
            whole(var_q.shape),
        ],
        out_specs=[out, out, out_far, out, out_far] + [pl.BlockSpec((1, 4, rows), lambda p: (p, 0, 0))],
        out_shape=[
            sds((rows, total), BF),
            sds((rows, total), BF),
            sds((rows, total), BF),
            sds((rows, total), BF),
            sds((rows, total), BF),
            sds((pairs, 4, rows), F32),
        ],
        compiler_params=params(),
        cost_estimate=cost(
            10 * 2 * rows * rows * 2 * total, 40 * rows * total, rows * rows * 2 * pairs * 2
        ),
    )(q, k_own, k_oth, v_own, v_oth, do, o, sums, aug_q, aug_k, head_scale, add_own, var_q)


def qkv_back_kernel(
    dq_ref, dk_ref, dkr_ref, dv_ref, dvr_ref, q0_ref, k0_ref, cos_ref, sin_ref, x_ref, dh_ref,
    gain_ref, zi_ref, *refs,
):
    weight, refs = refs[:8], refs[8:]
    dpn_ref, dpf_ref, dx_ref, dxl_ref, gg_ref, dp_scr, acc, w_ref, sems = refs
    width = dq_ref.shape[1]
    t = pl.program_id(0)

    @pl.when(t == 0)
    def _():
        start_all(weight, 0, w_ref, sems)
        acc[...] = jnp.zeros_like(acc)

    cos, sin = cos_ref[...], sin_ref[...]
    for which in range(2):
        u = (q0_ref if which == 0 else k0_ref)[...].astype(F32)
        r = lax.rsqrt(head_sum(u * u) * (1.0 / HD) + EPS)
        un = u * r
        turned = []
        for pair in range(width // 128):
            at = slice(pair * 128, (pair + 1) * 128)
            if which == 0:
                grad = dq_ref[:, at].astype(F32)
            else:
                grad = dk_ref[:, at].astype(F32) + dkr_ref[:, at].astype(F32)
            turned.append(grad * cos - half_swap(grad) * sin)
        grad = jnp.concatenate(turned, axis=1)
        out = r * (grad - un * (head_sum(grad * un) * (1.0 / HD)))
        dp_scr[:, which * width : (which + 1) * width] = out.astype(BF)
    dp_scr[:, 2 * width :] = (dv_ref[...].astype(F32) + dvr_ref[...].astype(F32)).astype(BF)
    wait_for(weight, 0, w_ref, sems, t)
    dp = dp_scr[...]
    put(t < 2, dpn_ref, dpf_ref, dp, 0)
    for r in range(4):
        z = place(zi_ref, r)
        acc[z] = acc[z] + dot(dp, w_ref[r, t])

    @pl.when(t == 3)
    def _():
        x = x_ref[...].astype(F32)
        r = row_rms(x)
        xn = x * r
        dn = block_load(acc)
        gg_ref[...] = jnp.sum(dn * xn, axis=0, keepdims=True)
        dhat = dn * gain_ref[...]
        dx = dh_ref[...] + r * (dhat - xn * jnp.mean(dhat * xn, axis=-1, keepdims=True))
        dx_ref[...] = dx
        dxl_ref[...] = dx.astype(BF)


def qkv_back_call(dq, dk, dkr, dv, dvr, q0, k0, cos, sin, x, dh, gain, zi, w, feats):
    rows, model = x.shape
    width = feats // 3
    big = whole((rows, model))
    col = pl.BlockSpec((rows, width), lambda t: (0, t))
    return pl.pallas_call(
        qkv_back_kernel,
        grid=(4,),
        in_specs=[col] * 7
        + [whole((rows, 128)), whole((rows, 128)), big, big, whole((1, model)), smem()]
        + [hbm()] * 8,
        out_specs=[*near_far(rows, feats), big, big, whole((1, model))],
        out_shape=[sds((2, rows, feats), BF)] * 2
        + [sds((rows, model), F32), sds((rows, model), BF), sds((1, model), F32)],
        scratch_shapes=[pltpu.VMEM((rows, feats), BF), pltpu.VMEM((4, rows, ZB), F32)]
        + weight_scratch(feats),
        compiler_params=params(),
        cost_estimate=cost(8 * rows * model * feats, 8 * feats * model + 40 * x.size),
    )(dq, dk, dkr, dv, dvr, q0, k0, cos, sin, x, dh, gain, zi, *w)


def wgrad_kernel(feats, zi_ref, ao_ref, bo_ref, ax_ref, bx_ref, keep_ref, send_ref):
    if len(ao_ref.shape) == 3:
        for i, out in ((1, send_ref), (0, keep_ref)):
            g = dot_tn(ao_ref[i], bo_ref[...]) + dot_tn(ax_ref[i], bx_ref[...])
            for z in range(4):
                out[lax.rem(zi_ref[0] - z + 4, 4)] = g[:, z * ZB : (z + 1) * ZB].astype(BF)
    else:
        g = dot_tn(ao_ref[...], bo_ref[...]) + dot_tn(ax_ref[...], bx_ref[...])
        for z in range(4):
            r = lax.rem(zi_ref[0] - z + 4, 4)
            at = slice(z * ZB, (z + 1) * ZB)
            keep_ref[r] = g[:feats, at].astype(BF)
            send_ref[r] = g[feats : 2 * feats, at].astype(BF)


def wgrad_call(zi, feats, a_own, b_own, a_oth, b_oth):
    rows, model = b_own.shape
    part = whole(a_oth.shape)
    big = whole((rows, model))
    out = whole((4, feats, ZB))
    return pl.pallas_call(
        functools.partial(wgrad_kernel, feats),
        grid=(1,),
        in_specs=[smem(), part, big, part, big],
        out_specs=[out, out],
        out_shape=[sds((4, feats, ZB), BF)] * 2,
        compiler_params=params(26),
        cost_estimate=cost(8 * rows * feats * model, 4 * feats * model),
    )(zi, a_own, b_own, a_oth, b_oth)


def core_swap(value):
    n = lax.axis_size("tensor")
    return lax.ppermute(value, "tensor", [(i, i ^ 1) for i in range(n)])


def y_swap(value):
    n = lax.axis_size("tensor")
    return lax.ppermute(value, "tensor", [(i, i ^ 2) for i in range(n)])


def ring(value):
    n = lax.axis_size("dp")
    return lax.ppermute(value, "dp", [(i, (i + 1) % n) for i in range(n)])


def gather_any(piece):
    ti = lax.axis_index("tensor")
    every = lax.all_gather(lax.all_gather(piece, "dp"), "tensor")
    tn, n, feats, cols = every.shape
    every = every.transpose(0, 2, 1, 3).reshape(tn, feats, n * cols // ZB, ZB)
    every = jnp.take(every, ti ^ jnp.array([0, 2, 1, 3]), axis=0)
    every = jnp.take(every, jnp.array([0, 3, 2, 1]), axis=2).transpose(2, 0, 1, 3)
    return [every[r, :2] for r in range(4)] + [every[r, 2:] for r in range(4)]


def meet(*values):
    return list(lax.optimization_barrier(values))


def after(value, *others):
    return lax.optimization_barrier((value, others))[0]


def to_owner(part, r):
    n = lax.axis_size("dp")
    return lax.ppermute(part, "dp", [(i, (i - r) % n) for i in range(n)])


def add_all(own, others):
    total = own.astype(F32)
    for other in others:
        total = total + other.astype(F32)
    return total


def scatter_any(keep, send):
    total = keep.astype(F32) + y_swap(send).astype(F32)
    total = jnp.take(total, jnp.array([0, 3, 2, 1]), axis=0)
    flat = total.transpose(1, 0, 2).reshape(total.shape[1], -1).astype(BF)
    return lax.psum_scatter(flat, "dp", scatter_dimension=1, tiled=True).astype(F32)


def plus(a, b):
    return (a.astype(F32) + b.astype(F32)).astype(BF)


def small_sum(value):
    n = lax.axis_size("dp")
    value = value + core_swap(value)
    value = value + y_swap(value)
    if n & (n - 1):
        return lax.psum(value, "dp")
    bit = 1
    while bit < n:
        value = value + lax.ppermute(value, "dp", [(i, i ^ bit) for i in range(n)])
        bit *= 2
    return value


def own_rows(row, core):
    quarters = row.reshape(2, 2, row.shape[0] // 4)
    own = lax.dynamic_index_in_dim(quarters, core, 1, keepdims=False).reshape(-1)
    oth = lax.dynamic_index_in_dim(quarters, 1 - core, 1, keepdims=False).reshape(-1)
    return own, oth


def tables(segment, variate, time_row, pad, core):
    seg_own, seg_oth = own_rows(segment, core)
    var_own, var_oth = own_rows(variate, core)
    pad_own, pad_oth = own_rows(pad, core)
    time_own, _ = own_rows(time_row, core)
    rows = seg_own.shape[0]
    half = HD // 2
    frequency = jnp.exp(-jnp.log(10000.0) * jnp.arange(half, dtype=F32) / half)
    phases = time_own.astype(F32)[:, None] * frequency[None, :]
    cos, sin = jnp.cos(phases), jnp.sin(phases)
    cos = jnp.concatenate([cos] * 4, axis=1)
    sin = jnp.concatenate([-sin, sin, -sin, sin], axis=1)
    lane = (jnp.arange(128, dtype=jnp.int32) % HD)[None, :]
    seg_k = jnp.concatenate([seg_own, seg_oth])[:, None]
    var_k = jnp.concatenate([var_own, var_oth])[:, None]
    pad_k = jnp.concatenate([jnp.ones_like(pad_own), pad_oth])[:, None]
    is_var = lane < 2 * N_VAR
    is_seg = (lane >= L_SEG) & (lane < L_PAD)
    is_lse = (lane >= L_LSE) & (lane < L_LSE + 3)
    aug_k = jnp.where(
        is_var,
        jnp.where(var_k == lane % N_VAR, 1.0, 0.0),
        jnp.where(
            is_seg,
            jnp.where(seg_k == lane - L_SEG, 0.0, -BIG),
            jnp.where(
                lane == L_PAD, jnp.where(pad_k == 1, 0.0, -BIG), jnp.where(is_lse, 1.0, 0.0)
            ),
        ),
    ).astype(BF)
    aug_q = jnp.where(
        is_var,
        jnp.where(var_own[:, None] == lane % N_VAR, 1.0, 0.0),
        jnp.where(
            is_seg,
            jnp.where(seg_own[:, None] == lane - L_SEG, 1.0, 0.0),
            jnp.where(lane == L_PAD, 1.0, 0.0),
        ),
    ).astype(F32)
    place = jnp.arange(rows, dtype=jnp.int32)
    neg = jnp.where(pad_own == 1, 0.0, -BIG).astype(F32)
    eye = place[:, None] == place[None, :]
    add_q = jnp.where(eye, 0.0, neg[None, :])
    add_k = jnp.where(eye, 0.0, neg[:, None])
    var_q = jnp.where(
        var_own[None, :] == jnp.arange(8, dtype=jnp.int32)[:, None], 1.0, 0.0
    ).astype(F32)
    return cos, sin, aug_q, aug_k, add_q, add_k, var_q


def head_scales(var_bias):
    lane = (jnp.arange(128, dtype=jnp.int32) % HD)[None, :]
    delta = (var_bias[:, 0] - var_bias[:, 1]) * math.sqrt(HD)
    hi = delta.astype(BF).astype(F32)
    low = (delta - hi).astype(BF).astype(F32)
    return jnp.where(
        lane < N_VAR, hi[:, None], jnp.where(lane < 2 * N_VAR, low[:, None], 1.0)
    ).reshape(-1, 2, 128)


def small_rows(gg_a, gg_f, bias, ti, heads_local):
    bias = bias.sum(axis=-1).reshape(4, 2 * heads_local)
    bias = jnp.take(bias, jnp.array([0, 2, 1, 3])[jnp.arange(4) ^ ti], axis=0).reshape(1, -1)
    bias = jnp.pad(bias, ((0, 0), (0, gg_a.shape[1] - bias.shape[1])))
    return jnp.concatenate([gg_a, gg_f, bias], axis=0)


def attend_part(scale, state, tab):
    q, k, v, k_oth, v_oth = state
    _, _, aug_q, aug_k, head_scale, add_q, _, _ = tab
    return attend_call(scale, q, k, k_oth, v, v_oth, aug_q, aug_k, head_scale, add_q)


def per_device(
    boundary, w_qkv, w_out, w_gate_up, w_down, norm_gains, variate_bias,
    segment_ids, variate_ids, time_ids, padding_mask,
):
    ti = lax.axis_index("tensor")
    tn = lax.axis_size("tensor")
    yi, core = ti // 2, ti % 2
    n = lax.axis_size("dp")
    is_first = lax.axis_index("section") == 0
    local = boundary[0]
    rows, model = local.shape[1:]
    scale = LOG2E / math.sqrt(HD)
    cols = w_qkv.shape[1]
    near = cols == ZB
    width = w_qkv.shape[3]
    hidden = w_gate_up.shape[3]
    heads_local = variate_bias.shape[1]
    zi = (lax.axis_index("dp") if near else 0) * jnp.ones((1,), jnp.int32)

    def row_of(array):
        return lax.dynamic_index_in_dim(array, yi, 0, keepdims=False)

    away = lax.dynamic_index_in_dim(local, 1 - yi, 0, keepdims=False).astype(BF)
    own = row_of(local).astype(BF)
    p_qkv = w_qkv[0].transpose(1, 2, 0).reshape(3 * width, cols)
    p_bias = jnp.pad(variate_bias[0].reshape(1, -1), ((0, 0), (0, cols - 2 * heads_local)))
    p_small = jnp.pad(jnp.concatenate([norm_gains[0], p_bias], axis=0), ((0, 13), (0, 0)))
    low = 3 * width
    out_low = low + 16
    p1 = jnp.concatenate([p_qkv, p_small, w_out[0]], axis=0)
    p2 = w_gate_up[0].transpose(1, 2, 0).reshape(2 * hidden, cols)
    p3 = w_down[0]

    def both_ends(came):
        return jnp.where(
            yi == 0, jnp.concatenate([own, came], axis=0), jnp.concatenate([came, own], axis=0)
        )

    tab = tables(
        row_of(segment_ids), row_of(variate_ids), row_of(time_ids), row_of(padding_mask), core
    )

    if near:
        a1, came = ring(p1), y_swap(away)
        a1, came, p1, p2, p3 = meet(a1, came, p1, p2, p3)
        a2, y0 = ring(a1), y_swap(p1)
        a1, a2, y0, p2, p3, *tab = meet(a1, a2, y0, p2, p3, *tab)
        ends = both_ends(came)
        a3, y1 = ring(a2), y_swap(a1)
        n1 = [jnp.stack([p1, y0])]
        f1 = [core_swap(n1[0])]
        a2, a3, y1, p2, p3, ends = meet(a2, a3, y1, p2, p3, ends)
        mid = p3.shape[0] // 32 * 16
        b1, y2, d0 = ring(p2), y_swap(a2), y_swap(p3[:mid])
        n1.append(jnp.stack([a1, y1]))
        f1.append(core_swap(n1[1]))
        a3, b1, y2, d0, p2, p3 = meet(a3, b1, y2, d0, p2, p3)
        b2, y3, d1 = ring(b1), y_swap(a3), y_swap(p3[mid:])
        n1.append(jnp.stack([a2, y2]))
        f1.append(core_swap(n1[2]))
        b1, b2, y3, p2, d0, d1 = meet(b1, b2, y3, p2, d0, d1)
        d0 = jnp.concatenate([d0, d1], axis=0)
        n1.append(jnp.stack([a3, y3]))
        f1.append(core_swap(n1[3]))
        w1 = n1 + f1
        b3, g0 = ring(b2), y_swap(p2)
    else:
        w1 = gather_any(p1)
        ends = both_ends(y_swap(away))
    gains = jnp.stack([w[0, low : low + 2] for w in w1[:4]])
    gains = jnp.take(gains, (zi[0] - jnp.arange(4)) % 4, axis=0)
    gains = gains.transpose(1, 0, 2).reshape(2, model).astype(F32)
    gain_a, gain_f = gains[:1], gains[1:]
    bias = [w[:, low + 2, : 2 * heads_local] for w in (w1[0], w1[4])]
    bias = jnp.concatenate(bias).reshape(4 * heads_local, 2).astype(F32)
    head_scale = head_scales(bias)
    cos, sin, aug_q, aug_k, add_q, add_k, var_q = tab
    tab = (cos, sin, aug_q, aug_k, head_scale, add_q, add_k, var_q)

    if near:
        b1, b2, b3, g0, d0 = meet(b1, b2, b3, g0, d0)
        n3 = [jnp.stack([p3, d0])]
        c1, g1 = ring(n3[0]), y_swap(b1)
        n2 = [jnp.stack([p2, g0])]
        f2 = [core_swap(n2[0])]
        f3 = [core_swap(n3[0])]
    q, k, v = qkv_call(False, ends, gain_a, zi, w1, low, cos, sin)
    if near:
        b2, b3, c1, g1, q, k, v = meet(b2, b3, c1, g1, q, k, v)
        c2, g2 = ring(c1), y_swap(b2)
    k_oth, v_oth = core_swap(k), core_swap(v)
    o, _ = attend_part(scale, (q, k, v, k_oth, v_oth), tab)
    if near:
        b3, c1, g1, c2, g2, o = meet(b3, c1, g1, c2, g2, o)
        c3, g3 = ring(c2), y_swap(b3)
        n2.append(jnp.stack([b1, g1]))
        f2.append(core_swap(n2[1]))
        f3.append(core_swap(c1))
        n2.append(jnp.stack([b2, g2]))
        f2.append(core_swap(n2[2]))
        f3.append(core_swap(c2))
        b3, c3, g3 = meet(b3, c3, g3)
        n2.append(jnp.stack([b3, g3]))
        f2.append(core_swap(n2[3]))
        f3.append(core_swap(c3))
        w2, w3 = n2 + f2, n3 + [c1, c2, c3] + f3
    else:
        w2, w3 = gather_any(p2), gather_any(p3)
    h, z_near, z_far = ffn_up_call(False, out_low, width, ends, o, gain_f, zi, w1, w2)
    y_low = ffn_down_call(BF, h, z_near, z_far, zi, w3)
    got = lax.ppermute(y_low, "section", [(0, 1)])

    x = jnp.where(is_first, ends, got)
    n1, q, k, v, q0, k0 = qkv_call(True, x, gain_a, zi, w1, low, cos, sin)
    k_oth, v_oth = core_swap(k), core_swap(v)
    o, sums = attend_part(scale, (q, k, v, k_oth, v_oth), tab)
    h, z_near, z_far, n2, g, u = ffn_up_call(True, out_low, width, x, o, gain_f, zi, w1, w2)
    y = ffn_down_call(F32, h, z_near, z_far, zi, w3)

    def qkv_back(dq, dk, dk_got, dv, dv_got, dh):
        return qkv_back_call(
            dq, dk, dk_got, dv, dv_got, q0, k0, cos, sin, x, dh, gain_a, zi, w1, low
        )

    dh, _, do = ffn_back_call(out_low, width, ends, h, g, u, gain_f, zi, w1, w2, w3)[:3]
    dq, dk, dk_send, dv, dv_send, _ = attend_back_call(
        scale, None, q, k, k_oth, v, v_oth, do, o, sums, aug_q, aug_k, head_scale, add_k, var_q
    )
    dx_low = qkv_back(dq, dk, core_swap(dk_send), dv, core_swap(dv_send), dh)[3]
    dx_low, z_far, n1_far, n2_far, o_far = meet(dx_low, z_far, n1, n2, o[:, 2 * width :])
    got = lax.ppermute(dx_low, "section", [(1, 0)])
    z_oth, n2_oth, n1_oth = core_swap(z_far), core_swap(n2_far), core_swap(n1_far)
    o_oth = core_swap(o_far)

    got, y, z_oth, n2_oth, n1_oth, o_oth = meet(got, y, z_oth, n2_oth, n1_oth, o_oth)

    df = jnp.where(is_first, got, ends)
    down_keep, down_send = wgrad_call(zi, hidden, z_near, df, z_oth, core_swap(df))
    df, down_keep, down_send = meet(df, down_keep, down_send)
    down_got = y_swap(down_send)
    back = ffn_back_call(out_low, width, df, h, g, u, gain_f, zi, w1, w2, w3)
    down_keep, down_got, *back = meet(down_keep, down_got, *back)
    dh, da, do, dg_near, dg_far, du_near, du_far, gg_f = back
    dg_oth, du_oth, da_oth = core_swap(dg_far), core_swap(du_far), core_swap(da)
    if near:
        down = [plus(down_keep[r], down_got[r]) for r in range(4)]
        down_run = ring(down[1])
    else:
        down_run = down_got
    dg_oth, du_oth, da_oth = meet(dg_oth, du_oth, da_oth)
    gate_keep, gate_send = wgrad_call(zi, hidden, dg_near, n2, dg_oth, n2_oth)
    down_run, do, gate_keep, gate_send, du_oth, da_oth = meet(
        down_run, do, gate_keep, gate_send, du_oth, da_oth
    )
    if near:
        gate_got = y_swap(gate_send)
        down_run = ring(plus(down_run, down[2]))
    out_keep, out_send = wgrad_call(zi, width, o, da, o_oth, da_oth)
    up_keep, up_send = wgrad_call(zi, hidden, du_near, n2, du_oth, n2_oth)
    do, out_keep, out_send, up_keep, up_send, down_run = meet(
        do, out_keep, out_send, up_keep, up_send, down_run
    )
    back = attend_back_call(
        scale, None, q, k, k_oth, v, v_oth, do, o, sums, aug_q, aug_k, head_scale, add_k, var_q
    )
    half = hidden // 32 * 16
    cut = width * 3 // 2
    if near:
        down_run = ring(plus(down_run, down[3]))
        out = [jnp.stack([out_keep[r], out_send[r]]) for r in range(4)]
        out_run = [to_owner(out[r], r) for r in (1, 2, 3)]
        gate_got, down_run, *rest = meet(gate_got, down_run, *out_run, *back)
        out_run, back = rest[:3], rest[3:]
    dq, dk, dk_send, dv, dv_send, bias = back
    dk_got, dv_got = core_swap(dk_send), core_swap(dv_send)
    if near:
        up_got = y_swap(up_send)
        gate = [plus(gate_keep[r], gate_got[r]) for r in range(4)]
        gate_run = [to_owner(gate[r], r) for r in (1, 2, 3)]
    back = qkv_back(dq, dk, dk_got, dv, dv_got, dh)
    if near:
        up_got, *rest = meet(up_got, *gate_run, *back)
        gate_run, back = rest[:3], rest[3:]
    dp_near, dp_far, dx, dx_low, gg_a = back
    dp_oth = core_swap(dp_far)
    qkv_keep, qkv_send = wgrad_call(zi, 3 * width, dp_near, n1, dp_oth, n1_oth)
    if near:
        up = [plus(up_keep[r, :half], up_got[r, :half]) for r in range(4)]
        dx_low, gg_a, *up = meet(dx_low, gg_a, *up)
    small = small_rows(gg_a, gg_f, bias, ti, heads_local)
    out_low_rows = jnp.where(is_first, dx_low, y.astype(BF))
    send = jnp.where(yi == 0, out_low_rows[rows:], out_low_rows[:rows])
    if near:
        up_run = [to_owner(up[r], r) for r in (1, 2, 3)]
        rows_got = y_swap(send)
        out_far = add_all(out[0][1], [run[1] for run in out_run]).astype(BF)
        out_got = y_swap(out_far)
        small = small + core_swap(small)
        rows_got, out_got, qkv_keep, qkv_send, small, *up_run = meet(
            rows_got, out_got, qkv_keep, qkv_send, small, *up_run
        )
        head_got = y_swap(qkv_send[:, :cut])
        more = [plus(up_keep[r, half:], up_got[r, half:]) for r in range(4)]
        more_run = [to_owner(more[r], r) for r in (1, 2, 3)]
        small = small + y_swap(small)
        head_got, small, *more_run = meet(head_got, small, *more_run)
        tail_got = y_swap(qkv_send[:, cut:])
        head = [plus(qkv_keep[r, :cut], head_got[r]) for r in range(4)]
        head_run = [to_owner(head[r], r) for r in (1, 2, 3)]
        small = small + lax.ppermute(small, "dp", [(i, i ^ 1) for i in range(4)])
        tail_got, small, down_run, out_got, *rest = meet(
            tail_got, small, down_run, out_got, *head_run, *gate_run, *out_run, *up_run, *more_run
        )
        head_run, gate_run, out_run, up_run, more_run = (rest[i : i + 3] for i in range(0, 15, 3))
        tail = [plus(qkv_keep[r, cut:], tail_got[r]) for r in range(4)]
        small = small + lax.ppermute(small, "dp", [(i, i ^ 2) for i in range(4)])
        small, *tail = meet(small, *tail)
        tail_run = [to_owner(tail[r], r) for r in (1, 2, 3)]
        g_down = down_run.astype(F32) + down[0].astype(F32)
        g_up = [add_all(up[0], up_run), add_all(more[0], more_run)]
        g_gu = jnp.stack([add_all(gate[0], gate_run), jnp.concatenate(g_up, axis=0)])
        g_out = add_all(out[0][0], [run[0] for run in out_run] + [out_got])
        g_qkv = jnp.concatenate([add_all(head[0], head_run), add_all(tail[0], tail_run)], axis=0)
    else:
        rows_got = y_swap(send)
        g_down = scatter_any(down_keep, down_send)
        g_gu = jnp.stack([scatter_any(gate_keep, gate_send), scatter_any(up_keep, up_send)])
        g_out = scatter_any(out_keep, out_send)
        g_qkv = scatter_any(qkv_keep, qkv_send)
        small = small_sum(small)

    out_rows = jnp.where(is_first, dx, y)
    keep = jnp.where(yi == 0, out_rows[:rows], out_rows[rows:])
    back = rows_got.astype(F32)
    boundary_out = jnp.where(yi == 0, jnp.stack([keep, back]), jnp.stack([back, keep]))[None]
    piece = model // (n * tn)
    gain_piece = lax.dynamic_slice_in_dim(
        small[:2], (lax.axis_index("dp") * tn + ti) * piece, piece, 1
    )
    bias_piece = lax.dynamic_slice_in_dim(
        small[2, : 8 * heads_local].reshape(-1, 2), ti * heads_local, heads_local, 0
    )
    return (
        boundary_out,
        g_qkv.reshape(3, width, cols).transpose(2, 0, 1)[None],
        g_out[None],
        g_gu.transpose(2, 0, 1)[None],
        g_down[None],
        gain_piece[None],
        bias_piece[None],
    )


def solution(mesh):
    placed = (
        P("section", "dp", "tensor", None),
        P("section", "dp", None, "tensor"),
        P("section", "tensor", "dp"),
        P("section", "dp", None, "tensor"),
        P("section", "tensor", "dp"),
        P("section", None, "dp"),
        P("section", "tensor", None),
        P("dp", None),
        P("dp", None),
        P("dp", None),
        P("dp", None),
    )
    return jax.shard_map(
        per_device,
        mesh=mesh,
        in_specs=placed,
        out_specs=(
            P("section", "dp", "tensor", None),
            P("section", "dp", None, "tensor"),
            P("section", "tensor", "dp"),
            P("section", "dp", None, "tensor"),
            P("section", "tensor", "dp"),
            P("section", None, ("dp", "tensor")),
            P("section", "tensor", None),
        ),
        check_vma=False,
    )
```

```python
import functools
import math

import jax
import jax.numpy as jnp
from jax import lax
from jax.experimental import pallas as pl
from jax.experimental.pallas import tpu as pltpu
from jax.sharding import PartitionSpec as P

EPS = 1e-05
BIG = 8192.0
LOG2E = 1.4426950408889634
BF = jnp.bfloat16
F32 = jnp.float32
HD = 64
ZB = 256
VMEM_MB = 56
N_VAR = 4
L_SEG = 8
L_PAD = 24
L_LSE = 25


def dot(a, b):
    return lax.dot_general(a, b, (((1,), (0,)), ((), ())), preferred_element_type=F32)


def dot_nt(a, b):
    return lax.dot_general(a, b, (((1,), (1,)), ((), ())), preferred_element_type=F32)


def dot_tn(a, b):
    return lax.dot_general(a, b, (((0,), (0,)), ((), ())), preferred_element_type=F32)


def params(mb=VMEM_MB):
    return pltpu.CompilerParams(
        dimension_semantics=("arbitrary",), vmem_limit_bytes=mb * 1024 * 1024
    )


def cost(flops, nbytes, trans=0):
    return pl.CostEstimate(flops=int(flops), bytes_accessed=int(nbytes), transcendentals=0)


def sds(shape, dtype):
    return jax.ShapeDtypeStruct(shape, dtype)


def whole(shape):
    zeros = (0,) * len(shape)
    return pl.BlockSpec(shape, lambda *_: zeros)


def head_sum(u):
    row = lax.broadcasted_iota(jnp.int32, (u.shape[1], u.shape[1]), 0) // HD
    col = lax.broadcasted_iota(jnp.int32, (u.shape[1], u.shape[1]), 1) // HD
    return dot(u.astype(BF), jnp.where(row == col, 1.0, 0.0).astype(BF))


def half_swap(u):
    lane = lax.broadcasted_iota(jnp.int32, u.shape, 1) % HD
    return jnp.where(lane < HD // 2, pltpu.roll(u, 128 - HD // 2, 1), pltpu.roll(u, HD // 2, 1))


def row_rms(x):
    return lax.rsqrt(jnp.mean(x * x, axis=-1, keepdims=True) + EPS)


def hbm():
    return pl.BlockSpec(memory_space=pl.ANY)


def smem():
    return pl.BlockSpec(memory_space=pltpu.SMEM)


def copies(refs, low, scratch, sems, t):
    rows = pl.ds(low, scratch.shape[2])
    return [
        pltpu.make_async_copy(
            refs[4 * (t // 2) + r].at[t % 2, rows], scratch.at[r, t], sems.at[r, t]
        )
        for r in range(4)
    ]


def start_all(refs, low, scratch, sems, shards=range(4)):
    for t in shards:
        for copy in copies(refs, low, scratch, sems, t):
            copy.start()


def wait_for(refs, low, scratch, sems, t):
    for fixed in range(4):

        @pl.when(t == fixed)
        def _():
            for copy in copies(refs, low, scratch, sems, fixed):
                copy.wait()


def weight_scratch(feats):
    return [pltpu.VMEM((4, 4, feats, ZB), BF), pltpu.SemaphoreType.DMA((4, 4))]


def place(zi_ref, r):
    return lax.rem(zi_ref[0] - r + 4, 4)


def block_store(ref, value):
    for z in range(4):
        ref[z] = value[:, z * ZB : (z + 1) * ZB]


def chunks(wide, step=ZB):
    return [slice(low, min(low + step, wide)) for low in range(0, wide, step)]


def block_load(ref):
    return jnp.concatenate([ref[z] for z in range(4)], axis=1)


def qkv_kernel(save, x_ref, gain_ref, zi_ref, cos_ref, sin_ref, *refs):
    weight, refs = refs[:8], refs[8:]
    if save:
        n_ref, q_ref, k_ref, v_ref, q0_ref, k0_ref, n_scr, w_ref, sems = refs
    else:
        q_ref, k_ref, v_ref, n_scr, w_ref, sems = refs
    t = pl.program_id(0)

    @pl.when(t == 0)
    def _():
        start_all(weight, 0, w_ref, sems, range(1))
        x = x_ref[...].astype(F32)
        n = (x * row_rms(x) * gain_ref[...]).astype(BF)
        block_store(n_scr, n)
        if save:
            n_ref[...] = n

    wait_for(weight, 0, w_ref, sems, t)

    @pl.when(t == 0)
    def _():
        start_all(weight, 0, w_ref, sems, range(1, 4))

    width = q_ref.shape[1]

    def project(which):
        cols = slice(which * width, (which + 1) * width)
        total = dot_nt(n_scr[place(zi_ref, 0)], w_ref[0, t, cols])
        for r in range(1, 4):
            total = total + dot_nt(n_scr[place(zi_ref, r)], w_ref[r, t, cols])
        return total

    cos, sin = cos_ref[...], sin_ref[...]
    for which, out in ((0, q_ref), (1, k_ref)):
        u = project(which)
        if save:
            kept = q0_ref if which == 0 else k0_ref
            kept[...] = u.astype(BF)
        un = u * lax.rsqrt(head_sum(u * u) * (1.0 / HD) + EPS)
        for pair in range(width // 128):
            at = slice(pair * 128, (pair + 1) * 128)
            out[:, at] = (un[:, at] * cos + half_swap(un[:, at]) * sin).astype(BF)
    v_ref[...] = project(2).astype(BF)


def qkv_call(save, x, gain, zi, w, feats, cos, sin):
    rows, model = x.shape
    width = feats // 3
    total = 4 * width
    col = pl.BlockSpec((rows, width), lambda t: (0, t))
    outs = [sds((rows, total), BF)] * 3
    specs = [col] * 3
    if save:
        outs = [sds((rows, model), BF)] + outs + [sds((rows, total), BF)] * 2
        specs = [whole((rows, model))] + specs + [col] * 2
    return pl.pallas_call(
        functools.partial(qkv_kernel, save),
        grid=(4,),
        in_specs=[whole((rows, model)), whole((1, model)), smem()]
        + [whole((rows, 128))] * 2
        + [hbm()] * 8,
        out_specs=specs,
        out_shape=outs,
        scratch_shapes=[pltpu.VMEM((4, rows, ZB), BF)] + weight_scratch(feats),
        compiler_params=params(),
        cost_estimate=cost(2 * rows * model * 3 * total, 6 * total * model + 16 * x.size),
    )(x, gain, zi, cos, sin, *w)


def other_core_spec(rows, pairs):
    half = pairs // 2
    return pl.BlockSpec((rows, 128), lambda p: (0, lax.rem(p + half, pairs)))


def pick(first, h, a, b):
    return jnp.where(first, a, b) if h == 0 else jnp.where(first, b, a)


def pick_low(first, h, a, b):
    mine = jnp.where(first, 1.0, 0.0) if h == 0 else jnp.where(first, 0.0, 1.0)
    low = mine.astype(BF)
    return a * low + b * (1.0 - mine).astype(BF)


def attend_kernel(
    scale, q_ref, ko_ref, kx_ref, vo_ref, vx_ref, aq_ref, ak_ref, hs_ref, add_ref, o_ref, l_ref
):
    rows = q_ref.shape[0]
    kb = 128
    first = lax.broadcasted_iota(jnp.int32, (1, 128), 1) < HD
    q = q_ref[...].astype(F32)
    base = aq_ref[...]
    raws = []
    for h in range(2):
        qh = pick(first, h, q, base * hs_ref[0, h : h + 1, :]).astype(BF)
        total = None
        for half, (k_ref, v_ref) in enumerate(((ko_ref, vo_ref), (kx_ref, vx_ref))):
            for block in range(rows // kb):
                at = slice(block * kb, (block + 1) * kb)
                kk = slice(half * rows + block * kb, half * rows + (block + 1) * kb)
                kh = pick_low(first, h, k_ref[at, :], ak_ref[kk, :])
                vh = pick_low(first, h, v_ref[at, :], BF(1.0))
                s = dot_nt(qh, kh)
                if half == 0:
                    s = s + add_ref[:, at]
                part = dot(jnp.exp2(s * scale).astype(BF), vh)
                total = part if total is None else total + part
        raws.append(total)
    sums = jnp.where(first, raws[1], raws[0])
    l_ref[...] = sums
    o_ref[...] = (jnp.where(first, raws[0], raws[1]) / pltpu.roll(sums, HD, 1)).astype(BF)


def attend_call(scale, q, k_own, k_oth, v_own, v_oth, aug_q, aug_k, head_scale, add_own):
    rows, total = q.shape
    pairs = total // 128
    col = pl.BlockSpec((rows, 128), lambda p: (0, p))
    far = other_core_spec(rows, pairs)
    return pl.pallas_call(
        functools.partial(attend_kernel, scale),
        grid=(pairs,),
        in_specs=[
            col,
            col,
            far,
            col,
            far,
            whole(aug_q.shape),
            whole(aug_k.shape),
            pl.BlockSpec((1, 2, 128), lambda p: (p, 0, 0)),
            whole(add_own.shape),
        ],
        out_specs=[col, col],
        out_shape=[sds((rows, total), BF), sds((rows, total), F32)],
        compiler_params=params(),
        cost_estimate=cost(
            4 * 2 * rows * rows * 2 * total, 20 * rows * total, rows * rows * 2 * pairs * 2
        ),
    )(q, k_own, k_oth, v_own, v_oth, aug_q, aug_k, head_scale, add_own)


def padded(hidden):
    return -(-2 * hidden // 128) * 128


def pair_scratch(parts, hidden):
    return [
        pltpu.VMEM((4, 2, parts * padded(hidden), ZB), BF),
        pltpu.SemaphoreType.DMA((4, 2, 2, parts)),
    ]


def pair_copies(refs, parts, scratch, sems, half):
    wide = scratch.shape[2] // parts
    hidden = refs[0].shape[1] // parts
    return [
        pltpu.make_async_copy(
            refs[4 * half + r].at[y, pl.ds(part * hidden, hidden)],
            scratch.at[r, half, pl.ds(part * wide + y * hidden, hidden)],
            sems.at[r, half, y, part],
        )
        for r in range(4)
        for y in range(2)
        for part in range(parts)
    ]


def pair_start(refs, parts, scratch, sems, halves=range(2)):
    wide = scratch.shape[2] // parts
    hidden = refs[0].shape[1] // parts
    for half in halves:
        for copy in pair_copies(refs, parts, scratch, sems, half):
            copy.start()
    blank = wide - 2 * hidden
    if blank:
        for half in halves:
            for r in range(4):
                for part in range(parts):
                    low = part * wide + 2 * hidden
                    scratch[r, half, low : low + blank] = jnp.zeros((blank, ZB), BF)


def pair_wait(refs, parts, scratch, sems, half):
    for fixed in range(2):

        @pl.when(half == fixed)
        def _():
            for copy in pair_copies(refs, parts, scratch, sems, fixed):
                copy.wait()


def near_far(rows, feats):
    return (
        pl.BlockSpec((1, rows, feats), lambda t: (jnp.minimum(t, 1), 0, 0)),
        pl.BlockSpec((1, rows, feats), lambda t: (jnp.maximum(t - 2, 0), 0, 0)),
    )


def put(is_near, near_ref, far_ref, value, at=...):
    @pl.when(is_near)
    def _():
        near_ref[at] = value

    @pl.when(jnp.logical_not(is_near))
    def _():
        far_ref[at] = value


def ffn_up_kernel(save, out_low, x_ref, o_ref, gain_ref, zi_ref, *refs):
    wo, wgu, refs = refs[:8], refs[8:16], refs[16:]
    if save:
        h_ref, zn_ref, zf_ref, n_ref, g_ref, u_ref = refs[:6]
    else:
        h_ref, zn_ref, zf_ref = refs[:3]
    n_scr, wo_ref, wo_sems, wgu_ref, wgu_sems, acc, z_scr = refs[-7:]
    wide = wgu_ref.shape[2] // 2
    half = pl.program_id(0)

    @pl.when(half == 0)
    def _():
        start_all(wo, out_low, wo_ref, wo_sems)
        pair_start(wgu, 2, wgu_ref, wgu_sems, range(1))
        width = wo_ref.shape[2]
        block_store(acc, x_ref[...].astype(F32))
        for s in range(4):
            for copy in copies(wo, out_low, wo_ref, wo_sems, s):
                copy.wait()
        pair_start(wgu, 2, wgu_ref, wgu_sems, range(1, 2))
        for r in range(4):
            z = place(zi_ref, r)
            h = acc[z]
            for s in range(4):
                h = h + dot(o_ref[:, s * width : (s + 1) * width], wo_ref[r, s])
            acc[z] = h
        h = block_load(acc)
        n = (h * row_rms(h) * gain_ref[...]).astype(BF)
        block_store(n_scr, n)
        h_ref[...] = h
        if save:
            n_ref[...] = n

    pair_wait(wgu, 2, wgu_ref, wgu_sems, half)
    for at in chunks(wide):
        total = []
        for part in range(2):
            cols = slice(part * wide + at.start, part * wide + at.stop)
            one = dot_nt(n_scr[place(zi_ref, 0)], wgu_ref[0, half, cols])
            for r in range(1, 4):
                one = one + dot_nt(n_scr[place(zi_ref, r)], wgu_ref[r, half, cols])
            total.append(one)
        gate, up = total
        z_scr[:, at] = (gate / (1.0 + jnp.exp(-gate)) * up).astype(BF)
        if save:
            g_ref[0, :, at] = gate.astype(BF)
            u_ref[0, :, at] = up.astype(BF)
    put(half == 0, zn_ref, zf_ref, z_scr[...])


def ffn_up_call(save, out_low, width, x, o, gain, zi, wo, wgu):
    rows, model = x.shape
    hidden = wgu[0].shape[1] // 2
    wide = padded(hidden)
    big = whole((rows, model))
    part = pl.BlockSpec((1, rows, wide), lambda t: (t, 0, 0))
    outs = [sds((rows, model), F32)] + [sds((rows, wide), BF)] * 2
    specs = [big, whole((rows, wide)), whole((rows, wide))]
    if save:
        outs += [sds((rows, model), BF)] + [sds((2, rows, wide), BF)] * 2
        specs += [big, part, part]
    return pl.pallas_call(
        functools.partial(ffn_up_kernel, save, out_low),
        grid=(2,),
        in_specs=[big, whole(o.shape), whole((1, model)), smem()] + [hbm()] * 16,
        out_specs=specs,
        out_shape=outs,
        scratch_shapes=[pltpu.VMEM((4, rows, ZB), BF)]
        + weight_scratch(width)
        + pair_scratch(2, hidden)
        + [pltpu.VMEM((4, rows, ZB), F32), pltpu.VMEM((rows, wide), BF)],
        compiler_params=params(),
        cost_estimate=cost(
            2 * rows * model * (8 * hidden + model), 16 * hidden * model + 20 * x.size
        ),
    )(x, o, gain, zi, *wo, *wgu)


def ffn_down_kernel(h_ref, zn_ref, zf_ref, zi_ref, *refs):
    weight, (y_ref, w_ref, sems, acc) = refs[:8], refs[8:]
    pair_start(weight, 1, w_ref, sems)
    for half, z_ref in enumerate((zn_ref, zf_ref)):
        for copy in pair_copies(weight, 1, w_ref, sems, half):
            copy.wait()
        for z in range(4):
            r = lax.rem(zi_ref[0] - z + 4, 4)
            at = slice(z * ZB, (z + 1) * ZB)
            part = dot(z_ref[...], w_ref[r, half])
            if half == 0:
                acc[:, at] = h_ref[:, at] + part
            else:
                y_ref[:, at] = (acc[:, at] + part).astype(y_ref.dtype)


def ffn_down_call(dtype, h, z_near, z_far, zi, wd):
    rows, model = h.shape
    hidden = wd[0].shape[1]
    vmem = pl.BlockSpec(memory_space=pltpu.VMEM)
    return pl.pallas_call(
        ffn_down_kernel,
        in_specs=[vmem] * 3 + [smem()] + [hbm()] * 8,
        out_specs=vmem,
        out_shape=sds((rows, model), dtype),
        scratch_shapes=pair_scratch(1, hidden) + [pltpu.VMEM((rows, model), F32)],
        compiler_params=pltpu.CompilerParams(vmem_limit_bytes=VMEM_MB * 1024 * 1024),
        cost_estimate=cost(2 * rows * model * 4 * hidden, 8 * hidden * model + 8 * h.size),
    )(h, z_near, z_far, zi, *wd)


def ffn_back_kernel(out_low, dy_ref, h_ref, g_ref, u_ref, gain_ref, zi_ref, *refs):
    wo, wgu, wd, refs = refs[:8], refs[8:16], refs[16:24], refs[24:]
    dh_ref, da_ref, do_ref, dgn_ref, dgf_ref, dun_ref, duf_ref, gg_ref = refs[:8]
    df_scr, acc, wo_ref, wo_sems, wgu_ref, wgu_sems, wd_ref, wd_sems, dg_scr, du_scr = refs[8:]
    wide = wd_ref.shape[2]
    half = pl.program_id(0)

    @pl.when(half == 0)
    def _():
        pair_start(wd, 1, wd_ref, wd_sems, range(1))
        block_store(df_scr, dy_ref[...])
        acc[...] = jnp.zeros_like(acc)

    pair_wait(wd, 1, wd_ref, wd_sems, half)

    @pl.when(half == 0)
    def _():
        pair_start(wgu, 2, wgu_ref, wgu_sems, range(1))
        pair_start(wd, 1, wd_ref, wd_sems, range(1, 2))
        pair_start(wgu, 2, wgu_ref, wgu_sems, range(1, 2))
        start_all(wo, out_low, wo_ref, wo_sems)

    for at in chunks(wide):
        dz = dot_nt(df_scr[place(zi_ref, 0)], wd_ref[0, half, at])
        for r in range(1, 4):
            dz = dz + dot_nt(df_scr[place(zi_ref, r)], wd_ref[r, half, at])
        gate = g_ref[0, :, at].astype(F32)
        up = u_ref[0, :, at].astype(F32)
        s = 1.0 / (1.0 + jnp.exp(-gate))
        dg_scr[:, at] = (dz * up * s * (1.0 + gate * (1.0 - s))).astype(BF)
        du_scr[:, at] = (dz * gate * s).astype(BF)
    dgate, dup = dg_scr[...], du_scr[...]
    put(half == 0, dgn_ref, dgf_ref, dgate)
    put(half == 0, dun_ref, duf_ref, dup)
    pair_wait(wgu, 2, wgu_ref, wgu_sems, half)
    for r in range(4):
        z = place(zi_ref, r)
        acc[z] = acc[z] + (
            dot(dgate, wgu_ref[r, half, :wide]) + dot(dup, wgu_ref[r, half, wide:])
        )

    @pl.when(half == 1)
    def _():
        h = h_ref[...]
        r = row_rms(h)
        hn = h * r
        dn = block_load(acc)
        gg_ref[...] = jnp.sum(dn * hn, axis=0, keepdims=True)
        dhat = dn * gain_ref[...]
        dh = dy_ref[...].astype(F32) + r * (
            dhat - hn * jnp.mean(dhat * hn, axis=-1, keepdims=True)
        )
        dh_ref[...] = dh
        da = dh.astype(BF)
        da_ref[...] = da
        block_store(df_scr, da)
        width = wo_ref.shape[2]
        for s in range(4):
            for copy in copies(wo, out_low, wo_ref, wo_sems, s):
                copy.wait()
        for s in range(4):
            part = dot_nt(df_scr[place(zi_ref, 0)], wo_ref[0, s])
            for q in range(1, 4):
                part = part + dot_nt(df_scr[place(zi_ref, q)], wo_ref[q, s])
            do_ref[:, s * width : (s + 1) * width] = part.astype(BF)


def ffn_back_call(out_low, width, dy, h, g, u, gain, zi, wo, wgu, wd):
    rows, model = dy.shape
    hidden = wd[0].shape[1]
    wide = g.shape[2]
    big = whole((rows, model))
    part = pl.BlockSpec((1, rows, wide), lambda t: (t, 0, 0))
    return pl.pallas_call(
        functools.partial(ffn_back_kernel, out_low),
        grid=(2,),
        in_specs=[big, big, part, part, whole((1, model)), smem()] + [hbm()] * 24,
        out_specs=[big, big, big] + [whole((rows, wide))] * 4 + [whole((1, model))],
        out_shape=[sds((rows, model), F32), sds((rows, model), BF), sds((rows, model), BF)]
        + [sds((rows, wide), BF)] * 4
        + [sds((1, model), F32)],
        scratch_shapes=[pltpu.VMEM((4, rows, ZB), BF), pltpu.VMEM((4, rows, ZB), F32)]
        + weight_scratch(width)
        + pair_scratch(2, hidden)
        + pair_scratch(1, hidden)
        + [pltpu.VMEM((rows, wide), BF)] * 2,
        compiler_params=params(57),
        cost_estimate=cost(
            2 * rows * model * (12 * hidden + model), 24 * hidden * model + 20 * dy.size
        ),
    )(dy, h, g, u, gain, zi, *wo, *wgu, *wd)


def split3(value):
    hi = value.astype(BF).astype(F32)
    mid = (value - hi).astype(BF).astype(F32)
    return hi, mid, value - hi - mid


def attend_back_kernel(
    scale, q_ref, ko_ref, kx_ref, vo_ref, vx_ref, do_ref, o_ref, l_ref, aq_ref, ak_ref, hs_ref,
    add_ref, var_ref, dq_ref, dko_ref, dkx_ref, dvo_ref, dvx_ref, bias_ref,
):
    rows = q_ref.shape[0]
    kb = 512
    first = lax.broadcasted_iota(jnp.int32, (1, 128), 1) < HD
    lane = lax.broadcasted_iota(jnp.int32, (1, 128), 1) % HD
    q = q_ref[...].astype(F32)
    do = do_ref[...].astype(F32)
    inner = do * o_ref[...].astype(F32)
    base = aq_ref[...]
    hi, mid, low = split3(jnp.log2(l_ref[...]) * (-1.0 / scale))
    lse = jnp.where(lane == L_LSE, hi, 0.0)
    lse = jnp.where(lane == L_LSE + 1, mid, lse)
    lse = jnp.where(lane == L_LSE + 2, low, lse)
    dq_t = []
    dk = [[], []]
    dv = [[], []]
    for h in range(2):
        qh = pick(first, h, q, base * hs_ref[0, h : h + 1, :] + lse).astype(BF)
        d = jnp.sum(pick(first, h, inner, 0.0), axis=-1, keepdims=True)
        dhi, dmid, dlow = split3(-d)
        d_aug = jnp.where(lane == 0, dhi, 0.0)
        d_aug = jnp.where(lane == 1, dmid, d_aug)
        d_aug = jnp.where(lane == 2, dlow, d_aug)
        doh = pick(first, h, do, d_aug).astype(BF)
        total = None
        for half, (k_ref, v_ref) in enumerate(((ko_ref, vo_ref), (kx_ref, vx_ref))):
            for block in range(rows // kb):
                at = slice(block * kb, (block + 1) * kb)
                kk = slice(half * rows + block * kb, half * rows + (block + 1) * kb)
                kh = pick_low(first, h, k_ref[at, :], ak_ref[kk, :])
                vh = pick_low(first, h, v_ref[at, :], BF(1.0))
                s = dot_nt(kh, qh)
                if half == 0:
                    s = s + add_ref[at, :]
                p = jnp.exp2(s * scale)
                ds = (p * dot_nt(vh, doh)).astype(BF)
                dv[h].append(dot(p.astype(BF), doh))
                dk[h].append(dot(ds, qh))
                part = dot_tn(kh, ds)
                total = part if total is None else total + part
        dq_t.append(total)
    scale_back = 1.0 / math.sqrt(HD)
    count = rows // kb
    for half, (dk_ref, dv_ref) in enumerate(((dko_ref, dvo_ref), (dkx_ref, dvx_ref))):
        for block in range(count):
            at = slice(block * kb, (block + 1) * kb)
            i = half * count + block
            dk_ref[at, :] = (jnp.where(first, dk[0][i], dk[1][i]) * scale_back).astype(dk_ref.dtype)
            dv_ref[at, :] = jnp.where(first, dv[0][i], dv[1][i]).astype(dv_ref.dtype)
    joined = jnp.concatenate([dq_t[0][:HD], dq_t[1][HD:]], axis=0)
    dq_ref[...] = (joined.T * scale_back).astype(BF)
    mine = var_ref[...]
    for h in range(2):
        begin = HD if h == 0 else 0
        r = dq_t[h][begin : begin + 8]
        same = jnp.sum(r * mine, axis=0, keepdims=True)
        every = jnp.sum(r[:N_VAR], axis=0, keepdims=True)
        bias_ref[0, 2 * h : 2 * h + 1, :] = same
        bias_ref[0, 2 * h + 1 : 2 * h + 2, :] = every - same


def attend_back_call(
    scale, span, q, k_own, k_oth, v_own, v_oth, do, o, sums, aug_q, aug_k, head_scale, add_own, var_q
):
    rows, total = q.shape
    every = total // 128
    low, high = span or (0, every)
    pairs = high - low
    total = pairs * 128
    col = pl.BlockSpec((rows, 128), lambda p: (0, p + low))
    far = pl.BlockSpec((rows, 128), lambda p: (0, lax.rem(p + low + every // 2, every)))
    out = pl.BlockSpec((rows, 128), lambda p: (0, p))
    out_far = other_core_spec(rows, pairs) if span is None else out
    return pl.pallas_call(
        functools.partial(attend_back_kernel, scale),
        grid=(pairs,),
        in_specs=[col, col, far, col, far, col, col, col]
        + [
            whole(aug_q.shape),
            whole(aug_k.shape),
            pl.BlockSpec((1, 2, 128), lambda p: (p + low, 0, 0)),
            whole(add_own.shape),
            whole(var_q.shape),
        ],
        out_specs=[out, out, out_far, out, out_far] + [pl.BlockSpec((1, 4, rows), lambda p: (p, 0, 0))],
        out_shape=[
            sds((rows, total), BF),
            sds((rows, total), BF),
            sds((rows, total), BF),
            sds((rows, total), BF),
            sds((rows, total), BF),
            sds((pairs, 4, rows), F32),
        ],
        compiler_params=params(),
        cost_estimate=cost(
            10 * 2 * rows * rows * 2 * total, 40 * rows * total, rows * rows * 2 * pairs * 2
        ),
    )(q, k_own, k_oth, v_own, v_oth, do, o, sums, aug_q, aug_k, head_scale, add_own, var_q)


def qkv_back_kernel(
    dq_ref, dk_ref, dkr_ref, dv_ref, dvr_ref, q0_ref, k0_ref, cos_ref, sin_ref, x_ref, dh_ref,
    gain_ref, zi_ref, *refs,
):
    weight, refs = refs[:8], refs[8:]
    dpn_ref, dpf_ref, dx_ref, dxl_ref, gg_ref, dp_scr, acc, w_ref, sems = refs
    width = dq_ref.shape[1]
    t = pl.program_id(0)

    @pl.when(t == 0)
    def _():
        start_all(weight, 0, w_ref, sems)
        acc[...] = jnp.zeros_like(acc)

    cos, sin = cos_ref[...], sin_ref[...]
    for which in range(2):
        u = (q0_ref if which == 0 else k0_ref)[...].astype(F32)
        r = lax.rsqrt(head_sum(u * u) * (1.0 / HD) + EPS)
        un = u * r
        turned = []
        for pair in range(width // 128):
            at = slice(pair * 128, (pair + 1) * 128)
            if which == 0:
                grad = dq_ref[:, at].astype(F32)
            else:
                grad = dk_ref[:, at].astype(F32) + dkr_ref[:, at].astype(F32)
            turned.append(grad * cos - half_swap(grad) * sin)
        grad = jnp.concatenate(turned, axis=1)
        out = r * (grad - un * (head_sum(grad * un) * (1.0 / HD)))
        dp_scr[:, which * width : (which + 1) * width] = out.astype(BF)
    dp_scr[:, 2 * width :] = (dv_ref[...].astype(F32) + dvr_ref[...].astype(F32)).astype(BF)
    wait_for(weight, 0, w_ref, sems, t)
    dp = dp_scr[...]
    put(t < 2, dpn_ref, dpf_ref, dp, 0)
    for r in range(4):
        z = place(zi_ref, r)
        acc[z] = acc[z] + dot(dp, w_ref[r, t])

    @pl.when(t == 3)
    def _():
        x = x_ref[...].astype(F32)
        r = row_rms(x)
        xn = x * r
        dn = block_load(acc)
        gg_ref[...] = jnp.sum(dn * xn, axis=0, keepdims=True)
        dhat = dn * gain_ref[...]
        dx = dh_ref[...] + r * (dhat - xn * jnp.mean(dhat * xn, axis=-1, keepdims=True))
        dx_ref[...] = dx
        dxl_ref[...] = dx.astype(BF)


def qkv_back_call(dq, dk, dkr, dv, dvr, q0, k0, cos, sin, x, dh, gain, zi, w, feats):
    rows, model = x.shape
    width = feats // 3
    big = whole((rows, model))
    col = pl.BlockSpec((rows, width), lambda t: (0, t))
    return pl.pallas_call(
        qkv_back_kernel,
        grid=(4,),
        in_specs=[col] * 7
        + [whole((rows, 128)), whole((rows, 128)), big, big, whole((1, model)), smem()]
        + [hbm()] * 8,
        out_specs=[*near_far(rows, feats), big, big, whole((1, model))],
        out_shape=[sds((2, rows, feats), BF)] * 2
        + [sds((rows, model), F32), sds((rows, model), BF), sds((1, model), F32)],
        scratch_shapes=[pltpu.VMEM((rows, feats), BF), pltpu.VMEM((4, rows, ZB), F32)]
        + weight_scratch(feats),
        compiler_params=params(),
        cost_estimate=cost(8 * rows * model * feats, 8 * feats * model + 40 * x.size),
    )(dq, dk, dkr, dv, dvr, q0, k0, cos, sin, x, dh, gain, zi, *w)


def wgrad_kernel(feats, zi_ref, ao_ref, bo_ref, ax_ref, bx_ref, keep_ref, send_ref):
    if len(ao_ref.shape) == 3:
        for i, out in ((1, send_ref), (0, keep_ref)):
            g = dot_tn(ao_ref[i], bo_ref[...]) + dot_tn(ax_ref[i], bx_ref[...])
            for z in range(4):
                out[lax.rem(zi_ref[0] - z + 4, 4)] = g[:, z * ZB : (z + 1) * ZB].astype(BF)
    else:
        g = dot_tn(ao_ref[...], bo_ref[...]) + dot_tn(ax_ref[...], bx_ref[...])
        for z in range(4):
            r = lax.rem(zi_ref[0] - z + 4, 4)
            at = slice(z * ZB, (z + 1) * ZB)
            keep_ref[r] = g[:feats, at].astype(BF)
            send_ref[r] = g[feats : 2 * feats, at].astype(BF)


def wgrad_call(zi, feats, a_own, b_own, a_oth, b_oth):
    rows, model = b_own.shape
    part = whole(a_oth.shape)
    big = whole((rows, model))
    out = whole((4, feats, ZB))
    return pl.pallas_call(
        functools.partial(wgrad_kernel, feats),
        grid=(1,),
        in_specs=[smem(), part, big, part, big],
        out_specs=[out, out],
        out_shape=[sds((4, feats, ZB), BF)] * 2,
        compiler_params=params(26),
        cost_estimate=cost(8 * rows * feats * model, 4 * feats * model),
    )(zi, a_own, b_own, a_oth, b_oth)


def core_swap(value):
    n = lax.axis_size("tensor")
    return lax.ppermute(value, "tensor", [(i, i ^ 1) for i in range(n)])


def y_swap(value):
    n = lax.axis_size("tensor")
    return lax.ppermute(value, "tensor", [(i, i ^ 2) for i in range(n)])


def ring(value):
    n = lax.axis_size("dp")
    return lax.ppermute(value, "dp", [(i, (i + 1) % n) for i in range(n)])


def gather_any(piece):
    ti = lax.axis_index("tensor")
    every = lax.all_gather(lax.all_gather(piece, "dp"), "tensor")
    tn, n, feats, cols = every.shape
    every = every.transpose(0, 2, 1, 3).reshape(tn, feats, n * cols // ZB, ZB)
    every = jnp.take(every, ti ^ jnp.array([0, 2, 1, 3]), axis=0)
    every = jnp.take(every, jnp.array([0, 3, 2, 1]), axis=2).transpose(2, 0, 1, 3)
    return [every[r, :2] for r in range(4)] + [every[r, 2:] for r in range(4)]


def meet(*values):
    return list(lax.optimization_barrier(values))


def after(value, *others):
    return lax.optimization_barrier((value, others))[0]


def to_owner(part, r):
    n = lax.axis_size("dp")
    return lax.ppermute(part, "dp", [(i, (i - r) % n) for i in range(n)])


def add_all(own, others):
    total = own.astype(F32)
    for other in others:
        total = total + other.astype(F32)
    return total


def scatter_any(keep, send):
    total = keep.astype(F32) + y_swap(send).astype(F32)
    total = jnp.take(total, jnp.array([0, 3, 2, 1]), axis=0)
    flat = total.transpose(1, 0, 2).reshape(total.shape[1], -1).astype(BF)
    return lax.psum_scatter(flat, "dp", scatter_dimension=1, tiled=True).astype(F32)


def plus(a, b):
    return (a.astype(F32) + b.astype(F32)).astype(BF)


def small_sum(value):
    n = lax.axis_size("dp")
    value = value + core_swap(value)
    value = value + y_swap(value)
    if n & (n - 1):
        return lax.psum(value, "dp")
    bit = 1
    while bit < n:
        value = value + lax.ppermute(value, "dp", [(i, i ^ bit) for i in range(n)])
        bit *= 2
    return value


def own_rows(row, core):
    quarters = row.reshape(2, 2, row.shape[0] // 4)
    own = lax.dynamic_index_in_dim(quarters, core, 1, keepdims=False).reshape(-1)
    oth = lax.dynamic_index_in_dim(quarters, 1 - core, 1, keepdims=False).reshape(-1)
    return own, oth


def tables(segment, variate, time_row, pad, core):
    seg_own, seg_oth = own_rows(segment, core)
    var_own, var_oth = own_rows(variate, core)
    pad_own, pad_oth = own_rows(pad, core)
    time_own, _ = own_rows(time_row, core)
    rows = seg_own.shape[0]
    half = HD // 2
    frequency = jnp.exp(-jnp.log(10000.0) * jnp.arange(half, dtype=F32) / half)
    phases = time_own.astype(F32)[:, None] * frequency[None, :]
    cos, sin = jnp.cos(phases), jnp.sin(phases)
    cos = jnp.concatenate([cos] * 4, axis=1)
    sin = jnp.concatenate([-sin, sin, -sin, sin], axis=1)
    lane = (jnp.arange(128, dtype=jnp.int32) % HD)[None, :]
    seg_k = jnp.concatenate([seg_own, seg_oth])[:, None]
    var_k = jnp.concatenate([var_own, var_oth])[:, None]
    pad_k = jnp.concatenate([jnp.ones_like(pad_own), pad_oth])[:, None]
    is_var = lane < 2 * N_VAR
    is_seg = (lane >= L_SEG) & (lane < L_PAD)
    is_lse = (lane >= L_LSE) & (lane < L_LSE + 3)
    aug_k = jnp.where(
        is_var,
        jnp.where(var_k == lane % N_VAR, 1.0, 0.0),
        jnp.where(
            is_seg,
            jnp.where(seg_k == lane - L_SEG, 0.0, -BIG),
            jnp.where(
                lane == L_PAD, jnp.where(pad_k == 1, 0.0, -BIG), jnp.where(is_lse, 1.0, 0.0)
            ),
        ),
    ).astype(BF)
    aug_q = jnp.where(
        is_var,
        jnp.where(var_own[:, None] == lane % N_VAR, 1.0, 0.0),
        jnp.where(
            is_seg,
            jnp.where(seg_own[:, None] == lane - L_SEG, 1.0, 0.0),
            jnp.where(lane == L_PAD, 1.0, 0.0),
        ),
    ).astype(F32)
    place = jnp.arange(rows, dtype=jnp.int32)
    neg = jnp.where(pad_own == 1, 0.0, -BIG).astype(F32)
    eye = place[:, None] == place[None, :]
    add_q = jnp.where(eye, 0.0, neg[None, :])
    add_k = jnp.where(eye, 0.0, neg[:, None])
    var_q = jnp.where(
        var_own[None, :] == jnp.arange(8, dtype=jnp.int32)[:, None], 1.0, 0.0
    ).astype(F32)
    return cos, sin, aug_q, aug_k, add_q, add_k, var_q


def head_scales(var_bias):
    lane = (jnp.arange(128, dtype=jnp.int32) % HD)[None, :]
    delta = (var_bias[:, 0] - var_bias[:, 1]) * math.sqrt(HD)
    hi = delta.astype(BF).astype(F32)
    low = (delta - hi).astype(BF).astype(F32)
    return jnp.where(
        lane < N_VAR, hi[:, None], jnp.where(lane < 2 * N_VAR, low[:, None], 1.0)
    ).reshape(-1, 2, 128)


def small_rows(gg_a, gg_f, bias, ti, heads_local):
    bias = bias.sum(axis=-1).reshape(4, 2 * heads_local)
    bias = jnp.take(bias, jnp.array([0, 2, 1, 3])[jnp.arange(4) ^ ti], axis=0).reshape(1, -1)
    bias = jnp.pad(bias, ((0, 0), (0, gg_a.shape[1] - bias.shape[1])))
    return jnp.concatenate([gg_a, gg_f, bias], axis=0)


def attend_part(scale, state, tab):
    q, k, v, k_oth, v_oth = state
    _, _, aug_q, aug_k, head_scale, add_q, _, _ = tab
    return attend_call(scale, q, k, k_oth, v, v_oth, aug_q, aug_k, head_scale, add_q)


def per_device(
    boundary, w_qkv, w_out, w_gate_up, w_down, norm_gains, variate_bias,
    segment_ids, variate_ids, time_ids, padding_mask,
):
    ti = lax.axis_index("tensor")
    tn = lax.axis_size("tensor")
    yi, core = ti // 2, ti % 2
    n = lax.axis_size("dp")
    is_first = lax.axis_index("section") == 0
    local = boundary[0]
    rows, model = local.shape[1:]
    scale = LOG2E / math.sqrt(HD)
    cols = w_qkv.shape[1]
    near = cols == ZB
    width = w_qkv.shape[3]
    hidden = w_gate_up.shape[3]
    heads_local = variate_bias.shape[1]
    zi = (lax.axis_index("dp") if near else 0) * jnp.ones((1,), jnp.int32)

    def row_of(array):
        return lax.dynamic_index_in_dim(array, yi, 0, keepdims=False)

    away = lax.dynamic_index_in_dim(local, 1 - yi, 0, keepdims=False).astype(BF)
    own = row_of(local).astype(BF)
    p_qkv = w_qkv[0].transpose(1, 2, 0).reshape(3 * width, cols)
    p_bias = jnp.pad(variate_bias[0].reshape(1, -1), ((0, 0), (0, cols - 2 * heads_local)))
    p_small = jnp.pad(jnp.concatenate([norm_gains[0], p_bias], axis=0), ((0, 13), (0, 0)))
    low = 3 * width
    out_low = low + 16
    p1 = jnp.concatenate([p_qkv, p_small, w_out[0]], axis=0)
    p2 = w_gate_up[0].transpose(1, 2, 0).reshape(2 * hidden, cols)
    p3 = w_down[0]

    def both_ends(came):
        return jnp.where(
            yi == 0, jnp.concatenate([own, came], axis=0), jnp.concatenate([came, own], axis=0)
        )

    tab = tables(
        row_of(segment_ids), row_of(variate_ids), row_of(time_ids), row_of(padding_mask), core
    )

    if near:
        a1, came = ring(p1), y_swap(away)
        a1, came, p1, p2, p3 = meet(a1, came, p1, p2, p3)
        a2, y0 = ring(a1), y_swap(p1)
        a1, a2, y0, p2, p3, *tab = meet(a1, a2, y0, p2, p3, *tab)
        ends = both_ends(came)
        a3, y1 = ring(a2), y_swap(a1)
        n1 = [jnp.stack([p1, y0])]
        f1 = [core_swap(n1[0])]
        a2, a3, y1, p2, p3, ends = meet(a2, a3, y1, p2, p3, ends)
        mid = p3.shape[0] // 32 * 16
        b1, y2, d0 = ring(p2), y_swap(a2), y_swap(p3[:mid])
        n1.append(jnp.stack([a1, y1]))
        f1.append(core_swap(n1[1]))
        a3, b1, y2, d0, p2, p3 = meet(a3, b1, y2, d0, p2, p3)
        b2, y3, d1 = ring(b1), y_swap(a3), y_swap(p3[mid:])
        n1.append(jnp.stack([a2, y2]))
        f1.append(core_swap(n1[2]))
        b1, b2, y3, p2, d0, d1 = meet(b1, b2, y3, p2, d0, d1)
        d0 = jnp.concatenate([d0, d1], axis=0)
        n1.append(jnp.stack([a3, y3]))
        f1.append(core_swap(n1[3]))
        w1 = n1 + f1
        b3, g0 = ring(b2), y_swap(p2)
    else:
        w1 = gather_any(p1)
        ends = both_ends(y_swap(away))
    gains = jnp.stack([w[0, low : low + 2] for w in w1[:4]])
    gains = jnp.take(gains, (zi[0] - jnp.arange(4)) % 4, axis=0)
    gains = gains.transpose(1, 0, 2).reshape(2, model).astype(F32)
    gain_a, gain_f = gains[:1], gains[1:]
    bias = [w[:, low + 2, : 2 * heads_local] for w in (w1[0], w1[4])]
    bias = jnp.concatenate(bias).reshape(4 * heads_local, 2).astype(F32)
    head_scale = head_scales(bias)
    cos, sin, aug_q, aug_k, add_q, add_k, var_q = tab
    tab = (cos, sin, aug_q, aug_k, head_scale, add_q, add_k, var_q)

    if near:
        b1, b2, b3, g0, d0 = meet(b1, b2, b3, g0, d0)
        n3 = [jnp.stack([p3, d0])]
        c1, g1 = ring(n3[0]), y_swap(b1)
        n2 = [jnp.stack([p2, g0])]
        f2 = [core_swap(n2[0])]
        f3 = [core_swap(n3[0])]
    q, k, v = qkv_call(False, ends, gain_a, zi, w1, low, cos, sin)
    if near:
        b2, b3, c1, g1, q, k, v = meet(b2, b3, c1, g1, q, k, v)
        c2, g2 = ring(c1), y_swap(b2)
    k_oth, v_oth = core_swap(k), core_swap(v)
    o, _ = attend_part(scale, (q, k, v, k_oth, v_oth), tab)
    if near:
        b3, c1, g1, c2, g2, o = meet(b3, c1, g1, c2, g2, o)
        c3, g3 = ring(c2), y_swap(b3)
        n2.append(jnp.stack([b1, g1]))
        f2.append(core_swap(n2[1]))
        f3.append(core_swap(c1))
        n2.append(jnp.stack([b2, g2]))
        f2.append(core_swap(n2[2]))
        f3.append(core_swap(c2))
        b3, c3, g3 = meet(b3, c3, g3)
        n2.append(jnp.stack([b3, g3]))
        f2.append(core_swap(n2[3]))
        f3.append(core_swap(c3))
        w2, w3 = n2 + f2, n3 + [c1, c2, c3] + f3
    else:
        w2, w3 = gather_any(p2), gather_any(p3)
    h, z_near, z_far = ffn_up_call(False, out_low, width, ends, o, gain_f, zi, w1, w2)
    y_low = ffn_down_call(BF, h, z_near, z_far, zi, w3)
    got = lax.ppermute(y_low, "section", [(0, 1)])

    x = jnp.where(is_first, ends, got)
    n1, q, k, v, q0, k0 = qkv_call(True, x, gain_a, zi, w1, low, cos, sin)
    k_oth, v_oth = core_swap(k), core_swap(v)
    o, sums = attend_part(scale, (q, k, v, k_oth, v_oth), tab)
    h, z_near, z_far, n2, g, u = ffn_up_call(True, out_low, width, x, o, gain_f, zi, w1, w2)
    y = ffn_down_call(F32, h, z_near, z_far, zi, w3)

    def qkv_back(dq, dk, dk_got, dv, dv_got, dh):
        return qkv_back_call(
            dq, dk, dk_got, dv, dv_got, q0, k0, cos, sin, x, dh, gain_a, zi, w1, low
        )

    dh, _, do = ffn_back_call(out_low, width, ends, h, g, u, gain_f, zi, w1, w2, w3)[:3]
    dq, dk, dk_send, dv, dv_send, _ = attend_back_call(
        scale, None, q, k, k_oth, v, v_oth, do, o, sums, aug_q, aug_k, head_scale, add_k, var_q
    )
    dx_low = qkv_back(dq, dk, core_swap(dk_send), dv, core_swap(dv_send), dh)[3]
    dx_low, z_far, n1_far, n2_far, o_far = meet(dx_low, z_far, n1, n2, o[:, 2 * width :])
    got = lax.ppermute(dx_low, "section", [(1, 0)])
    z_oth, n2_oth, n1_oth = core_swap(z_far), core_swap(n2_far), core_swap(n1_far)
    o_oth = core_swap(o_far)

    got, y, z_oth, n2_oth, n1_oth, o_oth = meet(got, y, z_oth, n2_oth, n1_oth, o_oth)

    df = jnp.where(is_first, got, ends)
    down_keep, down_send = wgrad_call(zi, hidden, z_near, df, z_oth, core_swap(df))
    df, down_keep, down_send = meet(df, down_keep, down_send)
    down_got = y_swap(down_send)
    back = ffn_back_call(out_low, width, df, h, g, u, gain_f, zi, w1, w2, w3)
    down_keep, down_got, *back = meet(down_keep, down_got, *back)
    dh, da, do, dg_near, dg_far, du_near, du_far, gg_f = back
    dg_oth, du_oth, da_oth = core_swap(dg_far), core_swap(du_far), core_swap(da)
    if near:
        down = [plus(down_keep[r], down_got[r]) for r in range(4)]
        down_run = ring(down[1])
    else:
        down_run = down_got
    dg_oth, du_oth, da_oth = meet(dg_oth, du_oth, da_oth)
    gate_keep, gate_send = wgrad_call(zi, hidden, dg_near, n2, dg_oth, n2_oth)
    down_run, do, gate_keep, gate_send, du_oth, da_oth = meet(
        down_run, do, gate_keep, gate_send, du_oth, da_oth
    )
    if near:
        gate_got = y_swap(gate_send)
        down_run = ring(plus(down_run, down[2]))
    out_keep, out_send = wgrad_call(zi, width, o, da, o_oth, da_oth)
    up_keep, up_send = wgrad_call(zi, hidden, du_near, n2, du_oth, n2_oth)
    do, out_keep, out_send, up_keep, up_send, down_run = meet(
        do, out_keep, out_send, up_keep, up_send, down_run
    )
    back = attend_back_call(
        scale, None, q, k, k_oth, v, v_oth, do, o, sums, aug_q, aug_k, head_scale, add_k, var_q
    )
    half = hidden * 3 // 128 * 16
    cut = width * 3 // 2
    if near:
        down_run = ring(plus(down_run, down[3]))
        out = [jnp.stack([out_keep[r], out_send[r]]) for r in range(4)]
        out_run = [to_owner(out[r], r) for r in (1, 2, 3)]
        gate_got, down_run, *rest = meet(gate_got, down_run, *out_run, *back)
        out_run, back = rest[:3], rest[3:]
    dq, dk, dk_send, dv, dv_send, bias = back
    dk_got, dv_got = core_swap(dk_send), core_swap(dv_send)
    if near:
        up_got = y_swap(up_send)
        gate = [plus(gate_keep[r], gate_got[r]) for r in range(4)]
        gate_run = [to_owner(gate[r], r) for r in (1, 2, 3)]
    back = qkv_back(dq, dk, dk_got, dv, dv_got, dh)
    if near:
        up_got, *rest = meet(up_got, *gate_run, *back)
        gate_run, back = rest[:3], rest[3:]
    dp_near, dp_far, dx, dx_low, gg_a = back
    dp_oth = core_swap(dp_far)
    qkv_keep, qkv_send = wgrad_call(zi, 3 * width, dp_near, n1, dp_oth, n1_oth)
    if near:
        up = [plus(up_keep[r, :half], up_got[r, :half]) for r in range(4)]
        dx_low, gg_a, *up = meet(dx_low, gg_a, *up)
    small = small_rows(gg_a, gg_f, bias, ti, heads_local)
    out_low_rows = jnp.where(is_first, dx_low, y.astype(BF))
    send = jnp.where(yi == 0, out_low_rows[rows:], out_low_rows[:rows])
    if near:
        up_run = [to_owner(up[r], r) for r in (1, 2, 3)]
        rows_got = y_swap(send)
        out_far = add_all(out[0][1], [run[1] for run in out_run]).astype(BF)
        out_got = y_swap(out_far)
        small = small + core_swap(small)
        rows_got, out_got, qkv_keep, qkv_send, small, *up_run = meet(
            rows_got, out_got, qkv_keep, qkv_send, small, *up_run
        )
        head_got = y_swap(qkv_send[:, :cut])
        more = [plus(up_keep[r, half:], up_got[r, half:]) for r in range(4)]
        more_run = [to_owner(more[r], r) for r in (1, 2, 3)]
        small = small + y_swap(small)
        head_got, small, *more_run = meet(head_got, small, *more_run)
        tail_got = y_swap(qkv_send[:, cut:])
        head = [plus(qkv_keep[r, :cut], head_got[r]) for r in range(4)]
        head_run = [to_owner(head[r], r) for r in (1, 2, 3)]
        small = small + lax.ppermute(small, "dp", [(i, i ^ 1) for i in range(4)])
        tail_got, small, down_run, out_got, *rest = meet(
            tail_got, small, down_run, out_got, *head_run, *gate_run, *out_run, *up_run, *more_run
        )
        head_run, gate_run, out_run, up_run, more_run = (rest[i : i + 3] for i in range(0, 15, 3))
        tail = [plus(qkv_keep[r, cut:], tail_got[r]) for r in range(4)]
        small = small + lax.ppermute(small, "dp", [(i, i ^ 2) for i in range(4)])
        small, *tail = meet(small, *tail)
        tail_run = [to_owner(tail[r], r) for r in (1, 2, 3)]
        g_down = down_run.astype(F32) + down[0].astype(F32)
        g_up = [add_all(up[0], up_run), add_all(more[0], more_run)]
        g_gu = jnp.stack([add_all(gate[0], gate_run), jnp.concatenate(g_up, axis=0)])
        g_out = add_all(out[0][0], [run[0] for run in out_run] + [out_got])
        g_qkv = jnp.concatenate([add_all(head[0], head_run), add_all(tail[0], tail_run)], axis=0)
    else:
        rows_got = y_swap(send)
        g_down = scatter_any(down_keep, down_send)
        g_gu = jnp.stack([scatter_any(gate_keep, gate_send), scatter_any(up_keep, up_send)])
        g_out = scatter_any(out_keep, out_send)
        g_qkv = scatter_any(qkv_keep, qkv_send)
        small = small_sum(small)

    out_rows = jnp.where(is_first, dx, y)
    keep = jnp.where(yi == 0, out_rows[:rows], out_rows[rows:])
    back = rows_got.astype(F32)
    boundary_out = jnp.where(yi == 0, jnp.stack([keep, back]), jnp.stack([back, keep]))[None]
    piece = model // (n * tn)
    gain_piece = lax.dynamic_slice_in_dim(
        small[:2], (lax.axis_index("dp") * tn + ti) * piece, piece, 1
    )
    bias_piece = lax.dynamic_slice_in_dim(
        small[2, : 8 * heads_local].reshape(-1, 2), ti * heads_local, heads_local, 0
    )
    return (
        boundary_out,
        g_qkv.reshape(3, width, cols).transpose(2, 0, 1)[None],
        g_out[None],
        g_gu.transpose(2, 0, 1)[None],
        g_down[None],
        gain_piece[None],
        bias_piece[None],
    )


def solution(mesh):
    placed = (
        P("section", "dp", "tensor", None),
        P("section", "dp", None, "tensor"),
        P("section", "tensor", "dp"),
        P("section", "dp", None, "tensor"),
        P("section", "tensor", "dp"),
        P("section", None, "dp"),
        P("section", "tensor", None),
        P("dp", None),
        P("dp", None),
        P("dp", None),
        P("dp", None),
    )
    return jax.shard_map(
        per_device,
        mesh=mesh,
        in_specs=placed,
        out_specs=(
            P("section", "dp", "tensor", None),
            P("section", "dp", None, "tensor"),
            P("section", "tensor", "dp"),
            P("section", "dp", None, "tensor"),
            P("section", "tensor", "dp"),
            P("section", None, ("dp", "tensor")),
            P("section", "tensor", None),
        ),
        check_vma=False,
    )
```

```python
import functools
import math

import jax
import jax.numpy as jnp
from jax import lax
from jax.experimental import pallas as pl
from jax.experimental.pallas import tpu as pltpu
from jax.sharding import PartitionSpec as P

EPS = 1e-05
BIG = 8192.0
LOG2E = 1.4426950408889634
BF = jnp.bfloat16
F32 = jnp.float32
HD = 64
ZB = 256
VMEM_MB = 56
N_VAR = 4
L_SEG = 8
L_PAD = 24
L_LSE = 25


def dot(a, b):
    return lax.dot_general(a, b, (((1,), (0,)), ((), ())), preferred_element_type=F32)


def dot_nt(a, b):
    return lax.dot_general(a, b, (((1,), (1,)), ((), ())), preferred_element_type=F32)


def dot_tn(a, b):
    return lax.dot_general(a, b, (((0,), (0,)), ((), ())), preferred_element_type=F32)


def params(mb=VMEM_MB):
    return pltpu.CompilerParams(
        dimension_semantics=("arbitrary",), vmem_limit_bytes=mb * 1024 * 1024
    )


def cost(flops, nbytes, trans=0):
    return pl.CostEstimate(flops=int(flops), bytes_accessed=int(nbytes), transcendentals=0)


def sds(shape, dtype):
    return jax.ShapeDtypeStruct(shape, dtype)


def whole(shape):
    zeros = (0,) * len(shape)
    return pl.BlockSpec(shape, lambda *_: zeros)


def head_sum(u):
    row = lax.broadcasted_iota(jnp.int32, (u.shape[1], u.shape[1]), 0) // HD
    col = lax.broadcasted_iota(jnp.int32, (u.shape[1], u.shape[1]), 1) // HD
    return dot(u.astype(BF), jnp.where(row == col, 1.0, 0.0).astype(BF))


def half_swap(u):
    lane = lax.broadcasted_iota(jnp.int32, u.shape, 1) % HD
    return jnp.where(lane < HD // 2, pltpu.roll(u, 128 - HD // 2, 1), pltpu.roll(u, HD // 2, 1))


def row_rms(x):
    return lax.rsqrt(jnp.mean(x * x, axis=-1, keepdims=True) + EPS)


def hbm():
    return pl.BlockSpec(memory_space=pl.ANY)


def smem():
    return pl.BlockSpec(memory_space=pltpu.SMEM)


def copies(refs, low, scratch, sems, t):
    rows = pl.ds(low, scratch.shape[2])
    return [
        pltpu.make_async_copy(
            refs[4 * (t // 2) + r].at[t % 2, rows], scratch.at[r, t], sems.at[r, t]
        )
        for r in range(4)
    ]


def start_all(refs, low, scratch, sems, shards=range(4)):
    for t in shards:
        for copy in copies(refs, low, scratch, sems, t):
            copy.start()


def wait_for(refs, low, scratch, sems, t):
    for fixed in range(4):

        @pl.when(t == fixed)
        def _():
            for copy in copies(refs, low, scratch, sems, fixed):
                copy.wait()


def weight_scratch(feats):
    return [pltpu.VMEM((4, 4, feats, ZB), BF), pltpu.SemaphoreType.DMA((4, 4))]


def place(zi_ref, r):
    return lax.rem(zi_ref[0] - r + 4, 4)


def block_store(ref, value):
    for z in range(4):
        ref[z] = value[:, z * ZB : (z + 1) * ZB]


def chunks(wide, step=ZB):
    return [slice(low, min(low + step, wide)) for low in range(0, wide, step)]


def block_load(ref):
    return jnp.concatenate([ref[z] for z in range(4)], axis=1)


def qkv_kernel(save, x_ref, gain_ref, zi_ref, cos_ref, sin_ref, *refs):
    weight, refs = refs[:8], refs[8:]
    if save:
        n_ref, q_ref, k_ref, v_ref, q0_ref, k0_ref, n_scr, w_ref, sems = refs
    else:
        q_ref, k_ref, v_ref, n_scr, w_ref, sems = refs
    t = pl.program_id(0)

    @pl.when(t == 0)
    def _():
        start_all(weight, 0, w_ref, sems, range(1))
        x = x_ref[...].astype(F32)
        n = (x * row_rms(x) * gain_ref[...]).astype(BF)
        block_store(n_scr, n)
        if save:
            n_ref[...] = n

    wait_for(weight, 0, w_ref, sems, t)

    @pl.when(t == 0)
    def _():
        start_all(weight, 0, w_ref, sems, range(1, 4))

    width = q_ref.shape[1]

    def project(which):
        cols = slice(which * width, (which + 1) * width)
        total = dot_nt(n_scr[place(zi_ref, 0)], w_ref[0, t, cols])
        for r in range(1, 4):
            total = total + dot_nt(n_scr[place(zi_ref, r)], w_ref[r, t, cols])
        return total

    cos, sin = cos_ref[...], sin_ref[...]
    for which, out in ((0, q_ref), (1, k_ref)):
        u = project(which)
        if save:
            kept = q0_ref if which == 0 else k0_ref
            kept[...] = u.astype(BF)
        un = u * lax.rsqrt(head_sum(u * u) * (1.0 / HD) + EPS)
        for pair in range(width // 128):
            at = slice(pair * 128, (pair + 1) * 128)
            out[:, at] = (un[:, at] * cos + half_swap(un[:, at]) * sin).astype(BF)
    v_ref[...] = project(2).astype(BF)


def qkv_call(save, x, gain, zi, w, feats, cos, sin):
    rows, model = x.shape
    width = feats // 3
    total = 4 * width
    col = pl.BlockSpec((rows, width), lambda t: (0, t))
    outs = [sds((rows, total), BF)] * 3
    specs = [col] * 3
    if save:
        outs = [sds((rows, model), BF)] + outs + [sds((rows, total), BF)] * 2
        specs = [whole((rows, model))] + specs + [col] * 2
    return pl.pallas_call(
        functools.partial(qkv_kernel, save),
        grid=(4,),
        in_specs=[whole((rows, model)), whole((1, model)), smem()]
        + [whole((rows, 128))] * 2
        + [hbm()] * 8,
        out_specs=specs,
        out_shape=outs,
        scratch_shapes=[pltpu.VMEM((4, rows, ZB), BF)] + weight_scratch(feats),
        compiler_params=params(),
        cost_estimate=cost(2 * rows * model * 3 * total, 6 * total * model + 16 * x.size),
    )(x, gain, zi, cos, sin, *w)


def other_core_spec(rows, pairs):
    half = pairs // 2
    return pl.BlockSpec((rows, 128), lambda p: (0, lax.rem(p + half, pairs)))


def pick(first, h, a, b):
    return jnp.where(first, a, b) if h == 0 else jnp.where(first, b, a)


def pick_low(first, h, a, b):
    mine = jnp.where(first, 1.0, 0.0) if h == 0 else jnp.where(first, 0.0, 1.0)
    low = mine.astype(BF)
    return a * low + b * (1.0 - mine).astype(BF)


def attend_kernel(
    scale, q_ref, ko_ref, kx_ref, vo_ref, vx_ref, aq_ref, ak_ref, hs_ref, add_ref, o_ref, l_ref
):
    rows = q_ref.shape[0]
    kb = 128
    first = lax.broadcasted_iota(jnp.int32, (1, 128), 1) < HD
    q = q_ref[...].astype(F32)
    base = aq_ref[...]
    raws = []
    for h in range(2):
        qh = pick(first, h, q, base * hs_ref[0, h : h + 1, :]).astype(BF)
        total = None
        for half, (k_ref, v_ref) in enumerate(((ko_ref, vo_ref), (kx_ref, vx_ref))):
            for block in range(rows // kb):
                at = slice(block * kb, (block + 1) * kb)
                kk = slice(half * rows + block * kb, half * rows + (block + 1) * kb)
                kh = pick_low(first, h, k_ref[at, :], ak_ref[kk, :])
                vh = pick_low(first, h, v_ref[at, :], BF(1.0))
                s = dot_nt(qh, kh)
                if half == 0:
                    s = s + add_ref[:, at]
                part = dot(jnp.exp2(s * scale).astype(BF), vh)
                total = part if total is None else total + part
        raws.append(total)
    sums = jnp.where(first, raws[1], raws[0])
    l_ref[...] = sums
    o_ref[...] = (jnp.where(first, raws[0], raws[1]) / pltpu.roll(sums, HD, 1)).astype(BF)


def attend_call(scale, q, k_own, k_oth, v_own, v_oth, aug_q, aug_k, head_scale, add_own):
    rows, total = q.shape
    pairs = total // 128
    col = pl.BlockSpec((rows, 128), lambda p: (0, p))
    far = other_core_spec(rows, pairs)
    return pl.pallas_call(
        functools.partial(attend_kernel, scale),
        grid=(pairs,),
        in_specs=[
            col,
            col,
            far,
            col,
            far,
            whole(aug_q.shape),
            whole(aug_k.shape),
            pl.BlockSpec((1, 2, 128), lambda p: (p, 0, 0)),
            whole(add_own.shape),
        ],
        out_specs=[col, col],
        out_shape=[sds((rows, total), BF), sds((rows, total), F32)],
        compiler_params=params(),
        cost_estimate=cost(
            4 * 2 * rows * rows * 2 * total, 20 * rows * total, rows * rows * 2 * pairs * 2
        ),
    )(q, k_own, k_oth, v_own, v_oth, aug_q, aug_k, head_scale, add_own)


def padded(hidden):
    return -(-2 * hidden // 128) * 128


def pair_scratch(parts, hidden):
    return [
        pltpu.VMEM((4, 2, parts * padded(hidden), ZB), BF),
        pltpu.SemaphoreType.DMA((4, 2, 2, parts)),
    ]


def pair_copies(refs, parts, scratch, sems, half):
    wide = scratch.shape[2] // parts
    hidden = refs[0].shape[1] // parts
    return [
        pltpu.make_async_copy(
            refs[4 * half + r].at[y, pl.ds(part * hidden, hidden)],
            scratch.at[r, half, pl.ds(part * wide + y * hidden, hidden)],
            sems.at[r, half, y, part],
        )
        for r in range(4)
        for y in range(2)
        for part in range(parts)
    ]


def pair_start(refs, parts, scratch, sems, halves=range(2)):
    wide = scratch.shape[2] // parts
    hidden = refs[0].shape[1] // parts
    for half in halves:
        for copy in pair_copies(refs, parts, scratch, sems, half):
            copy.start()
    blank = wide - 2 * hidden
    if blank:
        for half in halves:
            for r in range(4):
                for part in range(parts):
                    low = part * wide + 2 * hidden
                    scratch[r, half, low : low + blank] = jnp.zeros((blank, ZB), BF)


def pair_wait(refs, parts, scratch, sems, half):
    for fixed in range(2):

        @pl.when(half == fixed)
        def _():
            for copy in pair_copies(refs, parts, scratch, sems, fixed):
                copy.wait()


def near_far(rows, feats):
    return (
        pl.BlockSpec((1, rows, feats), lambda t: (jnp.minimum(t, 1), 0, 0)),
        pl.BlockSpec((1, rows, feats), lambda t: (jnp.maximum(t - 2, 0), 0, 0)),
    )


def put(is_near, near_ref, far_ref, value, at=...):
    @pl.when(is_near)
    def _():
        near_ref[at] = value

    @pl.when(jnp.logical_not(is_near))
    def _():
        far_ref[at] = value


def ffn_up_kernel(save, out_low, x_ref, o_ref, gain_ref, zi_ref, *refs):
    wo, wgu, refs = refs[:8], refs[8:16], refs[16:]
    if save:
        h_ref, zn_ref, zf_ref, n_ref, g_ref, u_ref = refs[:6]
    else:
        h_ref, zn_ref, zf_ref = refs[:3]
    n_scr, wo_ref, wo_sems, wgu_ref, wgu_sems, acc, z_scr = refs[-7:]
    wide = wgu_ref.shape[2] // 2
    half = pl.program_id(0)

    @pl.when(half == 0)
    def _():
        start_all(wo, out_low, wo_ref, wo_sems)
        pair_start(wgu, 2, wgu_ref, wgu_sems, range(1))
        width = wo_ref.shape[2]
        block_store(acc, x_ref[...].astype(F32))
        for s in range(4):
            for copy in copies(wo, out_low, wo_ref, wo_sems, s):
                copy.wait()
        pair_start(wgu, 2, wgu_ref, wgu_sems, range(1, 2))
        for r in range(4):
            z = place(zi_ref, r)
            h = acc[z]
            for s in range(4):
                h = h + dot(o_ref[:, s * width : (s + 1) * width], wo_ref[r, s])
            acc[z] = h
        h = block_load(acc)
        n = (h * row_rms(h) * gain_ref[...]).astype(BF)
        block_store(n_scr, n)
        h_ref[...] = h
        if save:
            n_ref[...] = n

    pair_wait(wgu, 2, wgu_ref, wgu_sems, half)
    for at in chunks(wide):
        total = []
        for part in range(2):
            cols = slice(part * wide + at.start, part * wide + at.stop)
            one = dot_nt(n_scr[place(zi_ref, 0)], wgu_ref[0, half, cols])
            for r in range(1, 4):
                one = one + dot_nt(n_scr[place(zi_ref, r)], wgu_ref[r, half, cols])
            total.append(one)
        gate, up = total
        z_scr[:, at] = (gate / (1.0 + jnp.exp(-gate)) * up).astype(BF)
        if save:
            g_ref[0, :, at] = gate.astype(BF)
            u_ref[0, :, at] = up.astype(BF)
    put(half == 0, zn_ref, zf_ref, z_scr[...])


def ffn_up_call(save, out_low, width, x, o, gain, zi, wo, wgu):
    rows, model = x.shape
    hidden = wgu[0].shape[1] // 2
    wide = padded(hidden)
    big = whole((rows, model))
    part = pl.BlockSpec((1, rows, wide), lambda t: (t, 0, 0))
    outs = [sds((rows, model), F32)] + [sds((rows, wide), BF)] * 2
    specs = [big, whole((rows, wide)), whole((rows, wide))]
    if save:
        outs += [sds((rows, model), BF)] + [sds((2, rows, wide), BF)] * 2
        specs += [big, part, part]
    return pl.pallas_call(
        functools.partial(ffn_up_kernel, save, out_low),
        grid=(2,),
        in_specs=[big, whole(o.shape), whole((1, model)), smem()] + [hbm()] * 16,
        out_specs=specs,
        out_shape=outs,
        scratch_shapes=[pltpu.VMEM((4, rows, ZB), BF)]
        + weight_scratch(width)
        + pair_scratch(2, hidden)
        + [pltpu.VMEM((4, rows, ZB), F32), pltpu.VMEM((rows, wide), BF)],
        compiler_params=params(),
        cost_estimate=cost(
            2 * rows * model * (8 * hidden + model), 16 * hidden * model + 20 * x.size
        ),
    )(x, o, gain, zi, *wo, *wgu)


def ffn_down_kernel(h_ref, zn_ref, zf_ref, zi_ref, *refs):
    weight, (y_ref, w_ref, sems) = refs[:8], refs[8:]
    pair_start(weight, 1, w_ref, sems)
    for half, z_ref in enumerate((zn_ref, zf_ref)):
        for copy in pair_copies(weight, 1, w_ref, sems, half):
            copy.wait()
    for z in range(4):
        r = lax.rem(zi_ref[0] - z + 4, 4)
        at = slice(z * ZB, (z + 1) * ZB)
        y = h_ref[:, at] + dot(zn_ref[...], w_ref[r, 0]) + dot(zf_ref[...], w_ref[r, 1])
        y_ref[:, at] = y.astype(y_ref.dtype)


def ffn_down_call(dtype, h, z_near, z_far, zi, wd):
    rows, model = h.shape
    hidden = wd[0].shape[1]
    vmem = pl.BlockSpec(memory_space=pltpu.VMEM)
    return pl.pallas_call(
        ffn_down_kernel,
        in_specs=[vmem] * 3 + [smem()] + [hbm()] * 8,
        out_specs=vmem,
        out_shape=sds((rows, model), dtype),
        scratch_shapes=pair_scratch(1, hidden),
        compiler_params=pltpu.CompilerParams(vmem_limit_bytes=VMEM_MB * 1024 * 1024),
        cost_estimate=cost(2 * rows * model * 4 * hidden, 8 * hidden * model + 8 * h.size),
    )(h, z_near, z_far, zi, *wd)


def ffn_back_kernel(out_low, dy_ref, h_ref, g_ref, u_ref, gain_ref, zi_ref, *refs):
    wo, wgu, wd, refs = refs[:8], refs[8:16], refs[16:24], refs[24:]
    dh_ref, da_ref, do_ref, dgn_ref, dgf_ref, dun_ref, duf_ref, gg_ref = refs[:8]
    df_scr, acc, wo_ref, wo_sems, wgu_ref, wgu_sems, wd_ref, wd_sems, dg_scr, du_scr = refs[8:]
    wide = wd_ref.shape[2]
    half = pl.program_id(0)

    @pl.when(half == 0)
    def _():
        pair_start(wd, 1, wd_ref, wd_sems, range(1))
        block_store(df_scr, dy_ref[...])
        acc[...] = jnp.zeros_like(acc)

    pair_wait(wd, 1, wd_ref, wd_sems, half)

    @pl.when(half == 0)
    def _():
        pair_start(wgu, 2, wgu_ref, wgu_sems, range(1))
        pair_start(wd, 1, wd_ref, wd_sems, range(1, 2))
        pair_start(wgu, 2, wgu_ref, wgu_sems, range(1, 2))
        start_all(wo, out_low, wo_ref, wo_sems)

    for at in chunks(wide):
        dz = dot_nt(df_scr[place(zi_ref, 0)], wd_ref[0, half, at])
        for r in range(1, 4):
            dz = dz + dot_nt(df_scr[place(zi_ref, r)], wd_ref[r, half, at])
        gate = g_ref[0, :, at].astype(F32)
        up = u_ref[0, :, at].astype(F32)
        s = 1.0 / (1.0 + jnp.exp(-gate))
        dg_scr[:, at] = (dz * up * s * (1.0 + gate * (1.0 - s))).astype(BF)
        du_scr[:, at] = (dz * gate * s).astype(BF)
    dgate, dup = dg_scr[...], du_scr[...]
    put(half == 0, dgn_ref, dgf_ref, dgate)
    put(half == 0, dun_ref, duf_ref, dup)
    pair_wait(wgu, 2, wgu_ref, wgu_sems, half)
    for r in range(4):
        z = place(zi_ref, r)
        acc[z] = acc[z] + (
            dot(dgate, wgu_ref[r, half, :wide]) + dot(dup, wgu_ref[r, half, wide:])
        )

    @pl.when(half == 1)
    def _():
        h = h_ref[...]
        r = row_rms(h)
        hn = h * r
        dn = block_load(acc)
        gg_ref[...] = jnp.sum(dn * hn, axis=0, keepdims=True)
        dhat = dn * gain_ref[...]
        dh = dy_ref[...].astype(F32) + r * (
            dhat - hn * jnp.mean(dhat * hn, axis=-1, keepdims=True)
        )
        dh_ref[...] = dh
        da = dh.astype(BF)
        da_ref[...] = da
        block_store(df_scr, da)
        width = wo_ref.shape[2]
        for s in range(4):
            for copy in copies(wo, out_low, wo_ref, wo_sems, s):
                copy.wait()
        for s in range(4):
            part = dot_nt(df_scr[place(zi_ref, 0)], wo_ref[0, s])
            for q in range(1, 4):
                part = part + dot_nt(df_scr[place(zi_ref, q)], wo_ref[q, s])
            do_ref[:, s * width : (s + 1) * width] = part.astype(BF)


def ffn_back_call(out_low, width, dy, h, g, u, gain, zi, wo, wgu, wd):
    rows, model = dy.shape
    hidden = wd[0].shape[1]
    wide = g.shape[2]
    big = whole((rows, model))
    part = pl.BlockSpec((1, rows, wide), lambda t: (t, 0, 0))
    return pl.pallas_call(
        functools.partial(ffn_back_kernel, out_low),
        grid=(2,),
        in_specs=[big, big, part, part, whole((1, model)), smem()] + [hbm()] * 24,
        out_specs=[big, big, big] + [whole((rows, wide))] * 4 + [whole((1, model))],
        out_shape=[sds((rows, model), F32), sds((rows, model), BF), sds((rows, model), BF)]
        + [sds((rows, wide), BF)] * 4
        + [sds((1, model), F32)],
        scratch_shapes=[pltpu.VMEM((4, rows, ZB), BF), pltpu.VMEM((4, rows, ZB), F32)]
        + weight_scratch(width)
        + pair_scratch(2, hidden)
        + pair_scratch(1, hidden)
        + [pltpu.VMEM((rows, wide), BF)] * 2,
        compiler_params=params(57),
        cost_estimate=cost(
            2 * rows * model * (12 * hidden + model), 24 * hidden * model + 20 * dy.size
        ),
    )(dy, h, g, u, gain, zi, *wo, *wgu, *wd)


def split3(value):
    hi = value.astype(BF).astype(F32)
    mid = (value - hi).astype(BF).astype(F32)
    return hi, mid, value - hi - mid


def attend_back_kernel(
    scale, q_ref, ko_ref, kx_ref, vo_ref, vx_ref, do_ref, o_ref, l_ref, aq_ref, ak_ref, hs_ref,
    add_ref, var_ref, dq_ref, dko_ref, dkx_ref, dvo_ref, dvx_ref, bias_ref,
):
    rows = q_ref.shape[0]
    kb = 512
    first = lax.broadcasted_iota(jnp.int32, (1, 128), 1) < HD
    lane = lax.broadcasted_iota(jnp.int32, (1, 128), 1) % HD
    q = q_ref[...].astype(F32)
    do = do_ref[...].astype(F32)
    inner = do * o_ref[...].astype(F32)
    base = aq_ref[...]
    hi, mid, low = split3(jnp.log2(l_ref[...]) * (-1.0 / scale))
    lse = jnp.where(lane == L_LSE, hi, 0.0)
    lse = jnp.where(lane == L_LSE + 1, mid, lse)
    lse = jnp.where(lane == L_LSE + 2, low, lse)
    dq_t = []
    dk = [[], []]
    dv = [[], []]
    for h in range(2):
        qh = pick(first, h, q, base * hs_ref[0, h : h + 1, :] + lse).astype(BF)
        d = jnp.sum(pick(first, h, inner, 0.0), axis=-1, keepdims=True)
        dhi, dmid, dlow = split3(-d)
        d_aug = jnp.where(lane == 0, dhi, 0.0)
        d_aug = jnp.where(lane == 1, dmid, d_aug)
        d_aug = jnp.where(lane == 2, dlow, d_aug)
        doh = pick(first, h, do, d_aug).astype(BF)
        total = None
        for half, (k_ref, v_ref) in enumerate(((ko_ref, vo_ref), (kx_ref, vx_ref))):
            for block in range(rows // kb):
                at = slice(block * kb, (block + 1) * kb)
                kk = slice(half * rows + block * kb, half * rows + (block + 1) * kb)
                kh = pick_low(first, h, k_ref[at, :], ak_ref[kk, :])
                vh = pick_low(first, h, v_ref[at, :], BF(1.0))
                s = dot_nt(kh, qh)
                if half == 0:
                    s = s + add_ref[at, :]
                p = jnp.exp2(s * scale)
                ds = (p * dot_nt(vh, doh)).astype(BF)
                dv[h].append(dot(p.astype(BF), doh))
                dk[h].append(dot(ds, qh))
                part = dot_tn(kh, ds)
                total = part if total is None else total + part
        dq_t.append(total)
    scale_back = 1.0 / math.sqrt(HD)
    count = rows // kb
    for half, (dk_ref, dv_ref) in enumerate(((dko_ref, dvo_ref), (dkx_ref, dvx_ref))):
        for block in range(count):
            at = slice(block * kb, (block + 1) * kb)
            i = half * count + block
            dk_ref[at, :] = (jnp.where(first, dk[0][i], dk[1][i]) * scale_back).astype(dk_ref.dtype)
            dv_ref[at, :] = jnp.where(first, dv[0][i], dv[1][i]).astype(dv_ref.dtype)
    joined = jnp.concatenate([dq_t[0][:HD], dq_t[1][HD:]], axis=0)
    dq_ref[...] = (joined.T * scale_back).astype(BF)
    mine = var_ref[...]
    for h in range(2):
        begin = HD if h == 0 else 0
        r = dq_t[h][begin : begin + 8]
        same = jnp.sum(r * mine, axis=0, keepdims=True)
        every = jnp.sum(r[:N_VAR], axis=0, keepdims=True)
        bias_ref[0, 2 * h : 2 * h + 1, :] = same
        bias_ref[0, 2 * h + 1 : 2 * h + 2, :] = every - same


def attend_back_call(
    scale, span, q, k_own, k_oth, v_own, v_oth, do, o, sums, aug_q, aug_k, head_scale, add_own, var_q
):
    rows, total = q.shape
    every = total // 128
    low, high = span or (0, every)
    pairs = high - low
    total = pairs * 128
    col = pl.BlockSpec((rows, 128), lambda p: (0, p + low))
    far = pl.BlockSpec((rows, 128), lambda p: (0, lax.rem(p + low + every // 2, every)))
    out = pl.BlockSpec((rows, 128), lambda p: (0, p))
    out_far = other_core_spec(rows, pairs) if span is None else out
    return pl.pallas_call(
        functools.partial(attend_back_kernel, scale),
        grid=(pairs,),
        in_specs=[col, col, far, col, far, col, col, col]
        + [
            whole(aug_q.shape),
            whole(aug_k.shape),
            pl.BlockSpec((1, 2, 128), lambda p: (p + low, 0, 0)),
            whole(add_own.shape),
            whole(var_q.shape),
        ],
        out_specs=[out, out, out_far, out, out_far] + [pl.BlockSpec((1, 4, rows), lambda p: (p, 0, 0))],
        out_shape=[
            sds((rows, total), BF),
            sds((rows, total), BF),
            sds((rows, total), BF),
            sds((rows, total), BF),
            sds((rows, total), BF),
            sds((pairs, 4, rows), F32),
        ],
        compiler_params=params(),
        cost_estimate=cost(
            10 * 2 * rows * rows * 2 * total, 40 * rows * total, rows * rows * 2 * pairs * 2
        ),
    )(q, k_own, k_oth, v_own, v_oth, do, o, sums, aug_q, aug_k, head_scale, add_own, var_q)


def qkv_back_kernel(
    dq_ref, dk_ref, dkr_ref, dv_ref, dvr_ref, q0_ref, k0_ref, cos_ref, sin_ref, x_ref, dh_ref,
    gain_ref, zi_ref, *refs,
):
    weight, refs = refs[:8], refs[8:]
    dpn_ref, dpf_ref, dx_ref, dxl_ref, gg_ref, dp_scr, acc, w_ref, sems = refs
    width = dq_ref.shape[1]
    t = pl.program_id(0)

    @pl.when(t == 0)
    def _():
        start_all(weight, 0, w_ref, sems, range(1))
        acc[...] = jnp.zeros_like(acc)

    cos, sin = cos_ref[...], sin_ref[...]
    for which in range(2):
        u = (q0_ref if which == 0 else k0_ref)[...].astype(F32)
        r = lax.rsqrt(head_sum(u * u) * (1.0 / HD) + EPS)
        un = u * r
        turned = []
        for pair in range(width // 128):
            at = slice(pair * 128, (pair + 1) * 128)
            if which == 0:
                grad = dq_ref[:, at].astype(F32)
            else:
                grad = dk_ref[:, at].astype(F32) + dkr_ref[:, at].astype(F32)
            turned.append(grad * cos - half_swap(grad) * sin)
        grad = jnp.concatenate(turned, axis=1)
        out = r * (grad - un * (head_sum(grad * un) * (1.0 / HD)))
        dp_scr[:, which * width : (which + 1) * width] = out.astype(BF)
    dp_scr[:, 2 * width :] = (dv_ref[...].astype(F32) + dvr_ref[...].astype(F32)).astype(BF)
    wait_for(weight, 0, w_ref, sems, t)

    @pl.when(t == 0)
    def _():
        start_all(weight, 0, w_ref, sems, range(1, 4))

    dp = dp_scr[...]
    put(t < 2, dpn_ref, dpf_ref, dp, 0)
    for r in range(4):
        z = place(zi_ref, r)
        acc[z] = acc[z] + dot(dp, w_ref[r, t])

    @pl.when(t == 3)
    def _():
        x = x_ref[...].astype(F32)
        r = row_rms(x)
        xn = x * r
        dn = block_load(acc)
        gg_ref[...] = jnp.sum(dn * xn, axis=0, keepdims=True)
        dhat = dn * gain_ref[...]
        dx = dh_ref[...] + r * (dhat - xn * jnp.mean(dhat * xn, axis=-1, keepdims=True))
        dx_ref[...] = dx
        dxl_ref[...] = dx.astype(BF)


def qkv_back_call(dq, dk, dkr, dv, dvr, q0, k0, cos, sin, x, dh, gain, zi, w, feats):
    rows, model = x.shape
    width = feats // 3
    big = whole((rows, model))
    col = pl.BlockSpec((rows, width), lambda t: (0, t))
    return pl.pallas_call(
        qkv_back_kernel,
        grid=(4,),
        in_specs=[col] * 7
        + [whole((rows, 128)), whole((rows, 128)), big, big, whole((1, model)), smem()]
        + [hbm()] * 8,
        out_specs=[*near_far(rows, feats), big, big, whole((1, model))],
        out_shape=[sds((2, rows, feats), BF)] * 2
        + [sds((rows, model), F32), sds((rows, model), BF), sds((1, model), F32)],
        scratch_shapes=[pltpu.VMEM((rows, feats), BF), pltpu.VMEM((4, rows, ZB), F32)]
        + weight_scratch(feats),
        compiler_params=params(),
        cost_estimate=cost(8 * rows * model * feats, 8 * feats * model + 40 * x.size),
    )(dq, dk, dkr, dv, dvr, q0, k0, cos, sin, x, dh, gain, zi, *w)


def wgrad_kernel(feats, zi_ref, ao_ref, bo_ref, ax_ref, bx_ref, keep_ref, send_ref):
    if len(ao_ref.shape) == 3:
        for i, out in ((1, send_ref), (0, keep_ref)):
            g = dot_tn(ao_ref[i], bo_ref[...]) + dot_tn(ax_ref[i], bx_ref[...])
            for z in range(4):
                out[lax.rem(zi_ref[0] - z + 4, 4)] = g[:, z * ZB : (z + 1) * ZB].astype(BF)
    else:
        g = dot_tn(ao_ref[...], bo_ref[...]) + dot_tn(ax_ref[...], bx_ref[...])
        for z in range(4):
            r = lax.rem(zi_ref[0] - z + 4, 4)
            at = slice(z * ZB, (z + 1) * ZB)
            keep_ref[r] = g[:feats, at].astype(BF)
            send_ref[r] = g[feats : 2 * feats, at].astype(BF)


def wgrad_call(zi, feats, a_own, b_own, a_oth, b_oth):
    rows, model = b_own.shape
    part = whole(a_oth.shape)
    big = whole((rows, model))
    out = whole((4, feats, ZB))
    return pl.pallas_call(
        functools.partial(wgrad_kernel, feats),
        grid=(1,),
        in_specs=[smem(), part, big, part, big],
        out_specs=[out, out],
        out_shape=[sds((4, feats, ZB), BF)] * 2,
        compiler_params=params(26),
        cost_estimate=cost(8 * rows * feats * model, 4 * feats * model),
    )(zi, a_own, b_own, a_oth, b_oth)


def core_swap(value):
    n = lax.axis_size("tensor")
    return lax.ppermute(value, "tensor", [(i, i ^ 1) for i in range(n)])


def y_swap(value):
    n = lax.axis_size("tensor")
    return lax.ppermute(value, "tensor", [(i, i ^ 2) for i in range(n)])


def ring(value):
    n = lax.axis_size("dp")
    return lax.ppermute(value, "dp", [(i, (i + 1) % n) for i in range(n)])


def gather_any(piece):
    ti = lax.axis_index("tensor")
    every = lax.all_gather(lax.all_gather(piece, "dp"), "tensor")
    tn, n, feats, cols = every.shape
    every = every.transpose(0, 2, 1, 3).reshape(tn, feats, n * cols // ZB, ZB)
    every = jnp.take(every, ti ^ jnp.array([0, 2, 1, 3]), axis=0)
    every = jnp.take(every, jnp.array([0, 3, 2, 1]), axis=2).transpose(2, 0, 1, 3)
    return [every[r, :2] for r in range(4)] + [every[r, 2:] for r in range(4)]


def meet(*values):
    return list(lax.optimization_barrier(values))


def after(value, *others):
    return lax.optimization_barrier((value, others))[0]


def to_owner(part, r):
    n = lax.axis_size("dp")
    return lax.ppermute(part, "dp", [(i, (i - r) % n) for i in range(n)])


def add_all(own, others):
    total = own.astype(F32)
    for other in others:
        total = total + other.astype(F32)
    return total


def scatter_any(keep, send):
    total = keep.astype(F32) + y_swap(send).astype(F32)
    total = jnp.take(total, jnp.array([0, 3, 2, 1]), axis=0)
    flat = total.transpose(1, 0, 2).reshape(total.shape[1], -1).astype(BF)
    return lax.psum_scatter(flat, "dp", scatter_dimension=1, tiled=True).astype(F32)


def plus(a, b):
    return (a.astype(F32) + b.astype(F32)).astype(BF)


def small_sum(value):
    n = lax.axis_size("dp")
    value = value + core_swap(value)
    value = value + y_swap(value)
    if n & (n - 1):
        return lax.psum(value, "dp")
    bit = 1
    while bit < n:
        value = value + lax.ppermute(value, "dp", [(i, i ^ bit) for i in range(n)])
        bit *= 2
    return value


def own_rows(row, core):
    quarters = row.reshape(2, 2, row.shape[0] // 4)
    own = lax.dynamic_index_in_dim(quarters, core, 1, keepdims=False).reshape(-1)
    oth = lax.dynamic_index_in_dim(quarters, 1 - core, 1, keepdims=False).reshape(-1)
    return own, oth


def tables(segment, variate, time_row, pad, core):
    seg_own, seg_oth = own_rows(segment, core)
    var_own, var_oth = own_rows(variate, core)
    pad_own, pad_oth = own_rows(pad, core)
    time_own, _ = own_rows(time_row, core)
    rows = seg_own.shape[0]
    half = HD // 2
    frequency = jnp.exp(-jnp.log(10000.0) * jnp.arange(half, dtype=F32) / half)
    phases = time_own.astype(F32)[:, None] * frequency[None, :]
    cos, sin = jnp.cos(phases), jnp.sin(phases)
    cos = jnp.concatenate([cos] * 4, axis=1)
    sin = jnp.concatenate([-sin, sin, -sin, sin], axis=1)
    lane = (jnp.arange(128, dtype=jnp.int32) % HD)[None, :]
    seg_k = jnp.concatenate([seg_own, seg_oth])[:, None]
    var_k = jnp.concatenate([var_own, var_oth])[:, None]
    pad_k = jnp.concatenate([jnp.ones_like(pad_own), pad_oth])[:, None]
    is_var = lane < 2 * N_VAR
    is_seg = (lane >= L_SEG) & (lane < L_PAD)
    is_lse = (lane >= L_LSE) & (lane < L_LSE + 3)
    aug_k = jnp.where(
        is_var,
        jnp.where(var_k == lane % N_VAR, 1.0, 0.0),
        jnp.where(
            is_seg,
            jnp.where(seg_k == lane - L_SEG, 0.0, -BIG),
            jnp.where(
                lane == L_PAD, jnp.where(pad_k == 1, 0.0, -BIG), jnp.where(is_lse, 1.0, 0.0)
            ),
        ),
    ).astype(BF)
    aug_q = jnp.where(
        is_var,
        jnp.where(var_own[:, None] == lane % N_VAR, 1.0, 0.0),
        jnp.where(
            is_seg,
            jnp.where(seg_own[:, None] == lane - L_SEG, 1.0, 0.0),
            jnp.where(lane == L_PAD, 1.0, 0.0),
        ),
    ).astype(F32)
    place = jnp.arange(rows, dtype=jnp.int32)
    neg = jnp.where(pad_own == 1, 0.0, -BIG).astype(F32)
    eye = place[:, None] == place[None, :]
    add_q = jnp.where(eye, 0.0, neg[None, :])
    add_k = jnp.where(eye, 0.0, neg[:, None])
    var_q = jnp.where(
        var_own[None, :] == jnp.arange(8, dtype=jnp.int32)[:, None], 1.0, 0.0
    ).astype(F32)
    return cos, sin, aug_q, aug_k, add_q, add_k, var_q


def head_scales(var_bias):
    lane = (jnp.arange(128, dtype=jnp.int32) % HD)[None, :]
    delta = (var_bias[:, 0] - var_bias[:, 1]) * math.sqrt(HD)
    hi = delta.astype(BF).astype(F32)
    low = (delta - hi).astype(BF).astype(F32)
    return jnp.where(
        lane < N_VAR, hi[:, None], jnp.where(lane < 2 * N_VAR, low[:, None], 1.0)
    ).reshape(-1, 2, 128)


def small_rows(gg_a, gg_f, bias, ti, heads_local):
    bias = bias.sum(axis=-1).reshape(4, 2 * heads_local)
    bias = jnp.take(bias, jnp.array([0, 2, 1, 3])[jnp.arange(4) ^ ti], axis=0).reshape(1, -1)
    bias = jnp.pad(bias, ((0, 0), (0, gg_a.shape[1] - bias.shape[1])))
    return jnp.concatenate([gg_a, gg_f, bias], axis=0)


def attend_part(scale, state, tab):
    q, k, v, k_oth, v_oth = state
    _, _, aug_q, aug_k, head_scale, add_q, _, _ = tab
    return attend_call(scale, q, k, k_oth, v, v_oth, aug_q, aug_k, head_scale, add_q)


def per_device(
    boundary, w_qkv, w_out, w_gate_up, w_down, norm_gains, variate_bias,
    segment_ids, variate_ids, time_ids, padding_mask,
):
    ti = lax.axis_index("tensor")
    tn = lax.axis_size("tensor")
    yi, core = ti // 2, ti % 2
    n = lax.axis_size("dp")
    is_first = lax.axis_index("section") == 0
    local = boundary[0]
    rows, model = local.shape[1:]
    scale = LOG2E / math.sqrt(HD)
    cols = w_qkv.shape[1]
    near = cols == ZB
    width = w_qkv.shape[3]
    hidden = w_gate_up.shape[3]
    heads_local = variate_bias.shape[1]
    zi = (lax.axis_index("dp") if near else 0) * jnp.ones((1,), jnp.int32)

    def row_of(array):
        return lax.dynamic_index_in_dim(array, yi, 0, keepdims=False)

    away = lax.dynamic_index_in_dim(local, 1 - yi, 0, keepdims=False).astype(BF)
    own = row_of(local).astype(BF)
    p_qkv = w_qkv[0].transpose(1, 2, 0).reshape(3 * width, cols)
    p_bias = jnp.pad(variate_bias[0].reshape(1, -1), ((0, 0), (0, cols - 2 * heads_local)))
    p_small = jnp.pad(jnp.concatenate([norm_gains[0], p_bias], axis=0), ((0, 13), (0, 0)))
    low = 3 * width
    out_low = low + 16
    p1 = jnp.concatenate([p_qkv, p_small, w_out[0]], axis=0)
    p2 = w_gate_up[0].transpose(1, 2, 0).reshape(2 * hidden, cols)
    p3 = w_down[0]

    def both_ends(came):
        return jnp.where(
            yi == 0, jnp.concatenate([own, came], axis=0), jnp.concatenate([came, own], axis=0)
        )

    tab = tables(
        row_of(segment_ids), row_of(variate_ids), row_of(time_ids), row_of(padding_mask), core
    )

    if near:
        a1, came = ring(p1), y_swap(away)
        a1, came, p1, p2, p3 = meet(a1, came, p1, p2, p3)
        a2, y0 = ring(a1), y_swap(p1)
        a1, a2, y0, p2, p3, *tab = meet(a1, a2, y0, p2, p3, *tab)
        ends = both_ends(came)
        a3, y1 = ring(a2), y_swap(a1)
        n1 = [jnp.stack([p1, y0])]
        f1 = [core_swap(n1[0])]
        a2, a3, y1, p2, p3, ends = meet(a2, a3, y1, p2, p3, ends)
        mid = p3.shape[0] // 32 * 16
        b1, y2, d0 = ring(p2), y_swap(a2), y_swap(p3[:mid])
        n1.append(jnp.stack([a1, y1]))
        f1.append(core_swap(n1[1]))
        a3, b1, y2, d0, p2, p3 = meet(a3, b1, y2, d0, p2, p3)
        b2, y3, d1 = ring(b1), y_swap(a3), y_swap(p3[mid:])
        n1.append(jnp.stack([a2, y2]))
        f1.append(core_swap(n1[2]))
        b1, b2, y3, p2, d0, d1 = meet(b1, b2, y3, p2, d0, d1)
        d0 = jnp.concatenate([d0, d1], axis=0)
        n1.append(jnp.stack([a3, y3]))
        f1.append(core_swap(n1[3]))
        w1 = n1 + f1
        b3, g0 = ring(b2), y_swap(p2)
    else:
        w1 = gather_any(p1)
        ends = both_ends(y_swap(away))
    gains = jnp.stack([w[0, low : low + 2] for w in w1[:4]])
    gains = jnp.take(gains, (zi[0] - jnp.arange(4)) % 4, axis=0)
    gains = gains.transpose(1, 0, 2).reshape(2, model).astype(F32)
    gain_a, gain_f = gains[:1], gains[1:]
    bias = [w[:, low + 2, : 2 * heads_local] for w in (w1[0], w1[4])]
    bias = jnp.concatenate(bias).reshape(4 * heads_local, 2).astype(F32)
    head_scale = head_scales(bias)
    cos, sin, aug_q, aug_k, add_q, add_k, var_q = tab
    tab = (cos, sin, aug_q, aug_k, head_scale, add_q, add_k, var_q)

    if near:
        b1, b2, b3, g0, d0 = meet(b1, b2, b3, g0, d0)
        n3 = [jnp.stack([p3, d0])]
        c1, g1 = ring(n3[0]), y_swap(b1)
        n2 = [jnp.stack([p2, g0])]
        f2 = [core_swap(n2[0])]
        f3 = [core_swap(n3[0])]
    q, k, v = qkv_call(False, ends, gain_a, zi, w1, low, cos, sin)
    if near:
        b2, b3, c1, g1, q, k, v = meet(b2, b3, c1, g1, q, k, v)
        c2, g2 = ring(c1), y_swap(b2)
    k_oth, v_oth = core_swap(k), core_swap(v)
    o, _ = attend_part(scale, (q, k, v, k_oth, v_oth), tab)
    if near:
        b3, c1, g1, c2, g2, o = meet(b3, c1, g1, c2, g2, o)
        c3, g3 = ring(c2), y_swap(b3)
        n2.append(jnp.stack([b1, g1]))
        f2.append(core_swap(n2[1]))
        f3.append(core_swap(c1))
        n2.append(jnp.stack([b2, g2]))
        f2.append(core_swap(n2[2]))
        f3.append(core_swap(c2))
        b3, c3, g3 = meet(b3, c3, g3)
        n2.append(jnp.stack([b3, g3]))
        f2.append(core_swap(n2[3]))
        f3.append(core_swap(c3))
        w2, w3 = n2 + f2, n3 + [c1, c2, c3] + f3
    else:
        w2, w3 = gather_any(p2), gather_any(p3)
    h, z_near, z_far = ffn_up_call(False, out_low, width, ends, o, gain_f, zi, w1, w2)
    y_low = ffn_down_call(BF, h, z_near, z_far, zi, w3)
    got = lax.ppermute(y_low, "section", [(0, 1)])

    x = jnp.where(is_first, ends, got)
    n1, q, k, v, q0, k0 = qkv_call(True, x, gain_a, zi, w1, low, cos, sin)
    k_oth, v_oth = core_swap(k), core_swap(v)
    o, sums = attend_part(scale, (q, k, v, k_oth, v_oth), tab)
    h, z_near, z_far, n2, g, u = ffn_up_call(True, out_low, width, x, o, gain_f, zi, w1, w2)
    y = ffn_down_call(F32, h, z_near, z_far, zi, w3)

    def qkv_back(dq, dk, dk_got, dv, dv_got, dh):
        return qkv_back_call(
            dq, dk, dk_got, dv, dv_got, q0, k0, cos, sin, x, dh, gain_a, zi, w1, low
        )

    dh, _, do = ffn_back_call(out_low, width, ends, h, g, u, gain_f, zi, w1, w2, w3)[:3]
    dq, dk, dk_send, dv, dv_send, _ = attend_back_call(
        scale, None, q, k, k_oth, v, v_oth, do, o, sums, aug_q, aug_k, head_scale, add_k, var_q
    )
    dx_low = qkv_back(dq, dk, core_swap(dk_send), dv, core_swap(dv_send), dh)[3]
    dx_low, z_far, n1_far, n2_far, o_far = meet(dx_low, z_far, n1, n2, o[:, 2 * width :])
    got = lax.ppermute(dx_low, "section", [(1, 0)])
    z_oth, n2_oth, n1_oth = core_swap(z_far), core_swap(n2_far), core_swap(n1_far)
    o_oth = core_swap(o_far)

    got, y, z_oth, n2_oth, n1_oth, o_oth = meet(got, y, z_oth, n2_oth, n1_oth, o_oth)

    df = jnp.where(is_first, got, ends)
    down_keep, down_send = wgrad_call(zi, hidden, z_near, df, z_oth, core_swap(df))
    df, down_keep, down_send = meet(df, down_keep, down_send)
    down_got = y_swap(down_send)
    back = ffn_back_call(out_low, width, df, h, g, u, gain_f, zi, w1, w2, w3)
    down_keep, down_got, *back = meet(down_keep, down_got, *back)
    dh, da, do, dg_near, dg_far, du_near, du_far, gg_f = back
    dg_oth, du_oth, da_oth = core_swap(dg_far), core_swap(du_far), core_swap(da)
    if near:
        down = [plus(down_keep[r], down_got[r]) for r in range(4)]
        down_run = ring(down[1])
    else:
        down_run = down_got
    dg_oth, du_oth, da_oth = meet(dg_oth, du_oth, da_oth)
    gate_keep, gate_send = wgrad_call(zi, hidden, dg_near, n2, dg_oth, n2_oth)
    down_run, do, gate_keep, gate_send, du_oth, da_oth = meet(
        down_run, do, gate_keep, gate_send, du_oth, da_oth
    )
    if near:
        gate_got = y_swap(gate_send)
        down_run = ring(plus(down_run, down[2]))
    out_keep, out_send = wgrad_call(zi, width, o, da, o_oth, da_oth)
    up_keep, up_send = wgrad_call(zi, hidden, du_near, n2, du_oth, n2_oth)
    do, out_keep, out_send, up_keep, up_send, down_run = meet(
        do, out_keep, out_send, up_keep, up_send, down_run
    )
    back = attend_back_call(
        scale, None, q, k, k_oth, v, v_oth, do, o, sums, aug_q, aug_k, head_scale, add_k, var_q
    )
    half = hidden // 32 * 16
    cut = width * 3 // 2
    if near:
        down_run = ring(plus(down_run, down[3]))
        out = [jnp.stack([out_keep[r], out_send[r]]) for r in range(4)]
        out_run = [to_owner(out[r], r) for r in (1, 2, 3)]
        gate_got, down_run, *rest = meet(gate_got, down_run, *out_run, *back)
        out_run, back = rest[:3], rest[3:]
    dq, dk, dk_send, dv, dv_send, bias = back
    dk_got, dv_got = core_swap(dk_send), core_swap(dv_send)
    if near:
        up_got = y_swap(up_send)
        gate = [plus(gate_keep[r], gate_got[r]) for r in range(4)]
        gate_run = [to_owner(gate[r], r) for r in (1, 2, 3)]
    back = qkv_back(dq, dk, dk_got, dv, dv_got, dh)
    if near:
        up_got, *rest = meet(up_got, *gate_run, *back)
        gate_run, back = rest[:3], rest[3:]
    dp_near, dp_far, dx, dx_low, gg_a = back
    dp_oth = core_swap(dp_far)
    qkv_keep, qkv_send = wgrad_call(zi, 3 * width, dp_near, n1, dp_oth, n1_oth)
    if near:
        up = [plus(up_keep[r, :half], up_got[r, :half]) for r in range(4)]
        dx_low, gg_a, *up = meet(dx_low, gg_a, *up)
    small = small_rows(gg_a, gg_f, bias, ti, heads_local)
    out_low_rows = jnp.where(is_first, dx_low, y.astype(BF))
    send = jnp.where(yi == 0, out_low_rows[rows:], out_low_rows[:rows])
    if near:
        up_run = [to_owner(up[r], r) for r in (1, 2, 3)]
        rows_got = y_swap(send)
        out_far = add_all(out[0][1], [run[1] for run in out_run]).astype(BF)
        out_got = y_swap(out_far)
        small = small + core_swap(small)
        rows_got, out_got, qkv_keep, qkv_send, small, *up_run = meet(
            rows_got, out_got, qkv_keep, qkv_send, small, *up_run
        )
        head_got = y_swap(qkv_send[:, :cut])
        more = [plus(up_keep[r, half:], up_got[r, half:]) for r in range(4)]
        more_run = [to_owner(more[r], r) for r in (1, 2, 3)]
        small = small + y_swap(small)
        head_got, small, *more_run = meet(head_got, small, *more_run)
        tail_got = y_swap(qkv_send[:, cut:])
        head = [plus(qkv_keep[r, :cut], head_got[r]) for r in range(4)]
        head_run = [to_owner(head[r], r) for r in (1, 2, 3)]
        small = small + lax.ppermute(small, "dp", [(i, i ^ 1) for i in range(4)])
        tail_got, small, down_run, out_got, *rest = meet(
            tail_got, small, down_run, out_got, *head_run, *gate_run, *out_run, *up_run, *more_run
        )
        head_run, gate_run, out_run, up_run, more_run = (rest[i : i + 3] for i in range(0, 15, 3))
        tail = [plus(qkv_keep[r, cut:], tail_got[r]) for r in range(4)]
        small = small + lax.ppermute(small, "dp", [(i, i ^ 2) for i in range(4)])
        small, *tail = meet(small, *tail)
        tail_run = [to_owner(tail[r], r) for r in (1, 2, 3)]
        g_down = down_run.astype(F32) + down[0].astype(F32)
        g_up = [add_all(up[0], up_run), add_all(more[0], more_run)]
        g_gu = jnp.stack([add_all(gate[0], gate_run), jnp.concatenate(g_up, axis=0)])
        g_out = add_all(out[0][0], [run[0] for run in out_run] + [out_got])
        g_qkv = jnp.concatenate([add_all(head[0], head_run), add_all(tail[0], tail_run)], axis=0)
    else:
        rows_got = y_swap(send)
        g_down = scatter_any(down_keep, down_send)
        g_gu = jnp.stack([scatter_any(gate_keep, gate_send), scatter_any(up_keep, up_send)])
        g_out = scatter_any(out_keep, out_send)
        g_qkv = scatter_any(qkv_keep, qkv_send)
        small = small_sum(small)

    out_rows = jnp.where(is_first, dx, y)
    keep = jnp.where(yi == 0, out_rows[:rows], out_rows[rows:])
    back = rows_got.astype(F32)
    boundary_out = jnp.where(yi == 0, jnp.stack([keep, back]), jnp.stack([back, keep]))[None]
    piece = model // (n * tn)
    gain_piece = lax.dynamic_slice_in_dim(
        small[:2], (lax.axis_index("dp") * tn + ti) * piece, piece, 1
    )
    bias_piece = lax.dynamic_slice_in_dim(
        small[2, : 8 * heads_local].reshape(-1, 2), ti * heads_local, heads_local, 0
    )
    return (
        boundary_out,
        g_qkv.reshape(3, width, cols).transpose(2, 0, 1)[None],
        g_out[None],
        g_gu.transpose(2, 0, 1)[None],
        g_down[None],
        gain_piece[None],
        bias_piece[None],
    )


def solution(mesh):
    placed = (
        P("section", "dp", "tensor", None),
        P("section", "dp", None, "tensor"),
        P("section", "tensor", "dp"),
        P("section", "dp", None, "tensor"),
        P("section", "tensor", "dp"),
        P("section", None, "dp"),
        P("section", "tensor", None),
        P("dp", None),
        P("dp", None),
        P("dp", None),
        P("dp", None),
    )
    return jax.shard_map(
        per_device,
        mesh=mesh,
        in_specs=placed,
        out_specs=(
            P("section", "dp", "tensor", None),
            P("section", "dp", None, "tensor"),
            P("section", "tensor", "dp"),
            P("section", "dp", None, "tensor"),
            P("section", "tensor", "dp"),
            P("section", None, ("dp", "tensor")),
            P("section", "tensor", None),
        ),
        check_vma=False,
    )
```
